32 devices in a mesh: fsdp: 16 (over z, y, x), tp: 2 (over core).
Axes of the slice: x: 2, y: 2, z: 4, core: 2. Of those that a mesh axis runs over, the one named last changes fastest.
Arguments:
- tokens: bfloat16 [8192, 2048], P(('fsdp', 'tp')), may hold values from -6 to 6
- cotangent: bfloat16 [8192, 2048], P(('fsdp', 'tp')), may hold values from -6 to 6
- segment: int32 [8192], replicated, may hold values from 0 to 8, as said below
- position: int32 [8192], replicated, may hold values from 0 to 1151, as said below
- clip_limit: float32 [8], P('tp'), may hold values from 2.5 to 8
- attn_gain: bfloat16 [2048], P('fsdp'), may hold values from 0.5 to 1.5
- query_weight: bfloat16 [2048, 2048], P('fsdp', 'tp'), may hold values from -0.125 to 0.125
- key_weight: bfloat16 [2048, 1024], P('fsdp', 'tp'), may hold values from -0.125 to 0.125
- value_weight: bfloat16 [2048, 1024], P('fsdp', 'tp'), may hold values from -0.125 to 0.125
- output_weight: bfloat16 [2048, 2048], P('fsdp', 'tp'), may hold values from -1 to 1
- mlp_gain: bfloat16 [2048], P('fsdp'), may hold values from 0.5 to 1.5
- gate_weight: bfloat16 [2048, 8192], P('fsdp', 'tp'), may hold values from -0.125 to 0.125
- up_weight: bfloat16 [2048, 8192], P('fsdp', 'tp'), may hold values from -0.125 to 0.125
- down_weight: bfloat16 [2048, 8192], P('fsdp', 'tp'), may hold values from -0.0625 to 0.0625
Outputs:
- block_out: bfloat16 [8192, 2048], P(('fsdp', 'tp'))
- tokens_grad: float32 [8192, 2048], P(('fsdp', 'tp'))
- attn_gain_grad: float32 [2048], P('fsdp')
- query_grad: float32 [2048, 2048], P('fsdp', 'tp')
- key_grad: float32 [2048, 1024], P('fsdp', 'tp')
- value_grad: float32 [2048, 1024], P('fsdp', 'tp')
- output_grad: float32 [2048, 2048], P('fsdp', 'tp')
- mlp_gain_grad: float32 [2048], P('fsdp')
- gate_grad: float32 [2048, 8192], P('fsdp', 'tp')
- up_grad: float32 [2048, 8192], P('fsdp', 'tp')
- down_grad: float32 [2048, 8192], P('fsdp', 'tp')
- head_maxima: float32 [8], P('tp')
- query_clipped: bfloat16 [2048, 2048], P('fsdp', 'tp')
- key_clipped: bfloat16 [2048, 1024], P('fsdp', 'tp')
The draws below stay inside these ranges and needn't reach their ends.
Inputs may be any that keep to these rules, and one draw needn't show every extreme that they name: Each group of 2048 consecutive tokens is made of aligned blocks of 128 tokens of one segment: 0 is the group's prompt and 1 to 8 its continuations, each holding one block; each aligned block of 512 tokens of a group holds at least one prompt block. `position`: the prompt block number b of a group holds positions b * 128 to b * 128 + 127 in order; a continuation's tokens hold 1024 to 1151 in order.
All inputs are finite; a program needn't handle non-finite values.
Results may differ from the reference program's by a relative error of at most 0.014.
Values may be sent and summed in bfloat16 or wider, within the bound.
No kernel may reach another device: no remote copies, remote signals or barrier semaphores. Data moves between devices by JAX's collectives and lax.ppermute only.
A program may use at most 320 MiB of HBM per device.

```python
import jax
import jax.numpy as jnp
from jax import lax

D = 2048
HQ = 8
HK = 4
HS = 256
FF = 8192
CONT = 128
PROMPT = 1024
TOK_DEV = 512
GROUP = 2048
TOKENS = 8192
GROUPS = 4


def group_layout(key):
    block_total = GROUP // CONT
    prompt_blocks = PROMPT // CONT
    blocks_device = TOK_DEV // CONT
    group_devices = GROUP // TOK_DEV

    def one_group(group_key):
        split_keys = jax.random.split(group_key, 4)
        prompt_order = jax.random.permutation(split_keys[0], prompt_blocks).astype(jnp.int32)
        cont_order = (prompt_blocks + jax.random.permutation(split_keys[1], block_total - prompt_blocks)).astype(jnp.int32)
        offsets = jax.random.randint(split_keys[2], (group_devices,), 0, blocks_device)
        forced_slots = jnp.arange(group_devices, dtype=jnp.int32) * blocks_device + offsets
        forced_flag = jnp.zeros((block_total,), jnp.int32).at[forced_slots].set(1)
        free_slots = jnp.argsort(forced_flag, stable=True)[:block_total - group_devices]
        remaining = jax.random.permutation(split_keys[3], jnp.concatenate([prompt_order[group_devices:], cont_order]))
        content = jnp.zeros((block_total,), jnp.int32).at[forced_slots].set(prompt_order[:group_devices])
        return content.at[free_slots].set(remaining)
    blocks = jax.vmap(one_group)(jax.random.split(key, GROUPS))
    block_ids = jnp.repeat(blocks.reshape(-1), CONT)
    within = jnp.tile(jnp.arange(CONT, dtype=jnp.int32), GROUPS * block_total)
    return (block_ids, within, prompt_blocks)


def draw_segment(key, part):
    block_ids, within, prompt_blocks = group_layout(key)
    return jnp.where(block_ids < prompt_blocks, 0, block_ids - prompt_blocks + 1).astype(jnp.int32)


def draw_position(key, part):
    block_ids, within, prompt_blocks = group_layout(key)
    return jnp.where(block_ids < prompt_blocks, block_ids * CONT + within, PROMPT + within).astype(jnp.int32)


def block_scale(key, dims, cuts, smallest, largest):
    level, own = 1.0, jax.random.fold_in(key, 6)
    for dim, parts in cuts:
        steps = jnp.exp(jax.random.uniform(jax.random.fold_in(own, dim), (parts,), jnp.float32, smallest / len(cuts), largest / len(cuts)))
        level = level * jnp.repeat(steps, dims[dim] // parts).reshape([-1 if axis == dim else 1 for axis in range(len(dims))])
    return level


def normal_values(stream_key, extent, width, most, pieces=(), kind=jnp.bfloat16):
    level = block_scale(stream_key, extent, pieces, -0.22, 0.18) if pieces else 1.0
    drawn = jax.random.normal(stream_key, extent, jnp.float32) * width * level
    return jnp.minimum(jnp.maximum(drawn, -most), most).astype(kind)


def setup_inputs(seed: int = 0) -> dict:
    arg_keys = jax.random.split(jax.random.key(seed), 15)
    tokens = normal_values(arg_keys[0], (TOKENS, D), 1.0, 6.0, ((0, 32),))
    cotangent = normal_values(arg_keys[1], (TOKENS, D), 1.0, 6.0, ((0, 32),))
    segment = draw_segment(jax.random.fold_in(arg_keys[14], 71), 0)
    position = draw_position(jax.random.fold_in(arg_keys[14], 71), 0)
    clip_limit = jnp.clip(2.5 + 5.5 * jax.random.uniform(arg_keys[4], (HQ,), jnp.float32) ** block_scale(arg_keys[4], (HQ,), ((0, 2),), -0.2, 0.2), 2.5, 8.0)
    attn_gain = jnp.clip(1.0 + 0.1 * jax.random.normal(arg_keys[5], (D,), jnp.float32), 0.5, 1.5).astype(jnp.bfloat16)
    query_weight = normal_values(arg_keys[6], (D, HQ * HS), D ** -0.5, 0.125, ((0, 16), (1, 2)))
    key_weight = normal_values(arg_keys[7], (D, HK * HS), D ** -0.5, 0.125, ((0, 16), (1, 2)))
    value_weight = normal_values(arg_keys[8], (D, HK * HS), D ** -0.5, 0.125, ((0, 16), (1, 2)))
    output_weight = normal_values(arg_keys[9], (D, HQ * HS), (HQ * HS // 64) ** -0.5, 1.0, ((0, 16), (1, 2)))
    mlp_gain = jnp.clip(1.0 + 0.1 * jax.random.normal(arg_keys[10], (D,), jnp.float32), 0.5, 1.5).astype(jnp.bfloat16)
    gate_weight = normal_values(arg_keys[11], (D, FF), D ** -0.5, 0.125, ((0, 16), (1, 2)))
    up_weight = normal_values(arg_keys[12], (D, FF), D ** -0.5, 0.125, ((0, 16), (1, 2)))
    down_weight = normal_values(arg_keys[13], (D, FF), FF ** -0.5, 0.0625, ((0, 16), (1, 2)))
    return dict(tokens=tokens, cotangent=cotangent, segment=segment, position=position, clip_limit=clip_limit, attn_gain=attn_gain, query_weight=query_weight, key_weight=key_weight, value_weight=value_weight, output_weight=output_weight, mlp_gain=mlp_gain, gate_weight=gate_weight, up_weight=up_weight, down_weight=down_weight)


@jax.custom_vjp
def low(v):
    return lax.optimization_barrier(v.astype(jnp.bfloat16)).astype(jnp.float32)

@jax.custom_vjp
def low_back(v):
    return v

def low_keep(v):
    return (low(v), None)

def low_pass(kept, grad):
    return (grad,)

def back_keep(v):
    return (v, None)

def back_low(kept, grad):
    return (low(grad),)
low.defvjp(low_keep, low_pass)
low_back.defvjp(back_keep, back_low)
epsilon = 1e-05
theta_base = 1000042.0
masked_value = -1e+30
highest = lax.Precision.HIGHEST

def matmul(left, right):
    return jnp.dot(left, right, precision=highest)

def times_transposed(left, right):
    return lax.dot_general(left, right, (((1,), (1,)), ((), ())), precision=highest)

def rms_scale(values, gain):
    inverse = lax.rsqrt(lax.optimization_barrier(jnp.mean(values * values, axis=-1, keepdims=True)) + epsilon)
    return values * inverse * gain

def rope_tables(positions, head_size):
    half_size = head_size // 2
    indices = jnp.arange(half_size, dtype=jnp.float32)
    inverse = theta_base ** (-2.0 * indices / head_size)
    angles = positions.astype(jnp.float32)[:, None] * inverse[None, :]
    return (jnp.cos(angles), jnp.sin(angles))

def rotate(vectors, cos_table, sin_table):
    half_size = vectors.shape[-1] // 2
    front_half = vectors[..., :half_size]
    back_half = vectors[..., half_size:]
    cos_rows = cos_table[:, None, :]
    sin_rows = sin_table[:, None, :]
    return jnp.concatenate([front_half * cos_rows - back_half * sin_rows, back_half * cos_rows + front_half * sin_rows], axis=-1)

def group_attention(query, keys, values, seg_ids, pos_ids):
    repeats = HQ // HK
    query_heads = query.reshape(GROUP, HK, repeats, HS)
    scores = jnp.einsum('ikrd,jkd->krij', query_heads, keys, precision=highest) * HS ** (-0.5)
    scores = low_back(scores)
    same_segment = (seg_ids[None, :] == seg_ids[:, None]) & (pos_ids[None, :] <= pos_ids[:, None])
    prompt_keys = (seg_ids[None, :] == 0) & (seg_ids[:, None] != 0)
    allowed = same_segment | prompt_keys
    masked = jnp.where(allowed[None, None], scores, masked_value)
    peaks = lax.optimization_barrier(jnp.max(masked, axis=(2, 3))).reshape(HQ)
    attention = low(jax.nn.softmax(masked, axis=-1))
    mixed = jnp.einsum('krij,jkd->ikrd', attention, values, precision=highest)
    return (mixed.reshape(GROUP, HQ * HS), peaks)

def one_group(group_items):
    return group_attention(*group_items)

def attend_all(query, keys, values, segment, position):
    group_items = (query.reshape(GROUPS, GROUP, HQ, HS), keys.reshape(GROUPS, GROUP, HK, HS), values.reshape(GROUPS, GROUP, HK, HS), segment.reshape(GROUPS, GROUP), position.reshape(GROUPS, GROUP))
    mixed, peaks = lax.map(jax.checkpoint(one_group), group_items)
    return (mixed.reshape(TOKENS, HQ * HS), lax.optimization_barrier(jnp.max(peaks, axis=0)))

def forward(tokens_f, attn_gain, query_weight, key_weight, value_weight, output_weight, mlp_gain, gate_weight, up_weight, down_weight, cos_table, sin_table, segment, position):
    normed = low(rms_scale(tokens_f, attn_gain))
    query_pre = low_back(matmul(normed, query_weight)).reshape(TOKENS, HQ, HS)
    query = low(rotate(query_pre, cos_table, sin_table))
    key_pre = low_back(matmul(normed, key_weight)).reshape(TOKENS, HK, HS)
    keys = low(rotate(key_pre, cos_table, sin_table))
    values = low(low_back(matmul(normed, value_weight))).reshape(TOKENS, HK, HS)
    mixed, peaks = attend_all(query, keys, values, segment, position)
    mixed = low(low_back(mixed))
    attn_out = low_back(times_transposed(mixed, output_weight))
    hidden_state = tokens_f + attn_out
    normed_mlp = low(rms_scale(hidden_state, mlp_gain))
    gate = low_back(matmul(normed_mlp, gate_weight))
    upward = low_back(matmul(normed_mlp, up_weight))
    inner = low(jax.nn.silu(gate) * upward)
    mlp_out = low_back(times_transposed(inner, down_weight))
    return (hidden_state + mlp_out, peaks)

def reference(tokens, cotangent, segment, position, clip_limit, attn_gain, query_weight, key_weight, value_weight, output_weight, mlp_gain, gate_weight, up_weight, down_weight):
    floats = [array.astype(jnp.float32) for array in (tokens, attn_gain, query_weight, key_weight, value_weight, output_weight, mlp_gain, gate_weight, up_weight, down_weight)]
    cos_table, sin_table = rope_tables(position, HS)

    def forward_of(*weights):
        return forward(*weights, cos_table, sin_table, segment, position)
    output, pullback, head_maxima = jax.vjp(forward_of, *floats, has_aux=True)
    grads = pullback(cotangent.astype(jnp.float32))
    factor = clip_limit / jnp.maximum(head_maxima, clip_limit)
    query_scale = jnp.repeat(jnp.sqrt(factor), HS)
    key_factor = lax.optimization_barrier(jnp.min(factor.reshape(HK, HQ // HK), axis=1))
    key_scale = jnp.repeat(jnp.sqrt(key_factor), HS)
    query_clipped = (floats[2] * query_scale[None, :]).astype(jnp.bfloat16)
    key_clipped = (floats[3] * key_scale[None, :]).astype(jnp.bfloat16)
    return (output.astype(jnp.bfloat16), grads[0], grads[1], grads[2], grads[3], grads[4], grads[5], grads[6], grads[7], grads[8], grads[9], head_maxima, query_clipped, key_clipped)
```

```python
import jax
import jax.numpy as jnp
from jax import lax
from jax.sharding import Mesh, PartitionSpec as P

HS = 256
GROUP = 2048

epsilon = 1e-05
theta_base = 1000042.0
masked_value = -1e30

bf16 = jnp.bfloat16
f32 = jnp.float32
PLANE = ("row", "col")
FSDP = ("group", "row", "col")


def product(left, right):
    return jnp.dot(left, right, preferred_element_type=f32)


def times_transposed(left, right):
    return lax.dot_general(left, right, (((1,), (1,)), ((), ())), preferred_element_type=f32)


def outer_sum(left, right):
    return lax.dot_general(left, right, (((0,), (0,)), ((), ())), preferred_element_type=f32)


def take(array, index, axis=0):
    return lax.dynamic_index_in_dim(array, index, axis, keepdims=False)


def swap(block, axis):
    return lax.ppermute(block, axis, [(0, 1), (1, 0)])


def swap_plane(block, distance):
    return lax.ppermute(block, PLANE, [(i, i ^ distance) for i in range(4)])


def plane_gather(rows):
    return lax.all_gather(rows, ("row", "col", "tp"), axis=0, tiled=True)


def plane_reduce(partial, row, col, core):
    width = partial.shape[1]
    rows = partial.shape[0] // 8
    parts = partial.astype(bf16).reshape(4, 2, rows, width)
    received = swap(take(parts, 1 - core, 1), "tp")
    summed = (take(parts, core, 1).astype(f32) + received.astype(f32)).astype(bf16)
    summed = summed.reshape(2, 2, rows, width)
    half = width // 2
    first, second = summed[..., :half], summed[..., half:]
    got_first = swap(take(first, 1 - col, 1), "col")
    got_second = swap(take(second, 1 - row, 0), "row")
    sum_first = take(first, col, 1).astype(f32) + got_first.astype(f32)
    sum_second = take(second, row, 0).astype(f32) + got_second.astype(f32)
    got_first = swap(take(sum_first, 1 - row).astype(bf16), "row")
    got_second = swap(take(sum_second, 1 - col).astype(bf16), "col")
    return jnp.concatenate(
        [
            take(sum_first, row) + got_first.astype(f32),
            take(sum_second, col) + got_second.astype(f32),
        ],
        axis=1,
    )


def line_reduce(blocks, groups, index):
    up = down = None
    for step in range(1, groups):
        out_up = take(blocks, jnp.minimum(index + groups - step, groups - 1))
        out_down = take(blocks, jnp.maximum(index - groups + step, 0))
        if up is not None:
            out_up = (out_up.astype(f32) + up.astype(f32)).astype(bf16)
            out_down = (out_down.astype(f32) + down.astype(f32)).astype(bf16)
        senders = range(min(step, groups - 1))
        up = lax.ppermute(out_up, "group", [(j, j + 1) for j in senders])
        down = lax.ppermute(
            out_down, "group", [(groups - 1 - j, groups - 2 - j) for j in senders]
        )
    return take(blocks, index).astype(f32) + up.astype(f32) + down.astype(f32)


def plane_exchange(make, member):
    own = make(member)
    result = jnp.zeros((4,) + own.shape, own.dtype)
    result = lax.dynamic_update_index_in_dim(result, own, member, 0)
    for distance in (1, 2, 3):
        got = swap_plane(make(member ^ distance), distance)
        result = lax.dynamic_update_index_in_dim(result, got, member ^ distance, 0)
    return result


def rms_inverse(values):
    return lax.rsqrt(jnp.mean(values * values, axis=-1, keepdims=True) + epsilon)


def rope_tables(positions):
    half_size = HS // 2
    indices = jnp.arange(half_size, dtype=f32)
    inverse = theta_base ** (-2.0 * indices / HS)
    angles = positions.astype(f32)[:, None] * inverse[None, :]
    return jnp.cos(angles), jnp.sin(angles)


def rotate(vectors, cos, sin):
    front, back = vectors[:, : HS // 2], vectors[:, HS // 2 :]
    return jnp.concatenate([front * cos - back * sin, back * cos + front * sin], axis=-1)


def unrotate(grads, cos, sin):
    front, back = grads[:, : HS // 2], grads[:, HS // 2 :]
    return jnp.concatenate([front * cos + back * sin, back * cos - front * sin], axis=-1)


def local(
    tokens,
    cotangent,
    segment,
    position,
    clip_limit,
    attn_gain,
    query_weight,
    key_weight,
    value_weight,
    output_weight,
    mlp_gain,
    gate_weight,
    up_weight,
    down_weight,
):
    groups = lax.axis_size("group")
    group = lax.axis_index("group")
    row = lax.axis_index("row")
    col = lax.axis_index("col")
    core = lax.axis_index("tp")
    member = row * 2 + col
    own_rows = query_weight.shape[0]
    hidden_own = gate_weight.shape[1] // 4
    seg = lax.dynamic_slice_in_dim(segment, group * GROUP, GROUP)
    pos = lax.dynamic_slice_in_dim(position, group * GROUP, GROUP)
    scale = HS ** (-0.5)

    gain_attn = attn_gain.astype(f32)[:, None]
    gain_mlp = mlp_gain.astype(f32)[:, None]
    query_gained = (query_weight.astype(f32) * gain_attn).astype(bf16)
    key_gained = (key_weight.astype(f32) * gain_attn).astype(bf16)
    value_gained = (value_weight.astype(f32) * gain_attn).astype(bf16)
    gate_gained = (gate_weight.astype(f32) * gain_mlp).astype(bf16)
    up_gained = (up_weight.astype(f32) * gain_mlp).astype(bf16)

    def columns(array, index, width):
        return lax.dynamic_slice_in_dim(array, index * width, width, 1)

    def attention_block(m):
        return jnp.concatenate(
            [
                columns(query_gained, m, HS),
                columns(key_gained, m // 2, HS),
                columns(value_gained, m // 2, HS),
                columns(output_weight, m, HS),
            ],
            axis=1,
        )

    def mlp_block(m):
        return jnp.concatenate(
            [columns(a, m, hidden_own) for a in (gate_gained, up_gained, down_weight)], axis=1
        )

    def collect(make):
        blocks = plane_exchange(make, member)
        width = blocks.shape[-1]
        return lax.all_gather(blocks.reshape(4 * own_rows, width), "group", axis=0, tiled=True)

    tokens_all = plane_gather(tokens)
    attn_weights = collect(attention_block)
    mlp_weights = collect(mlp_block)
    cot_all = plane_gather(cotangent)

    tokens_f = tokens.astype(f32)
    all_f = tokens_all.astype(f32)
    unit_all = (all_f * rms_inverse(all_f)).astype(bf16)
    inverse_attn = rms_inverse(tokens_f)
    unit_attn = tokens_f * inverse_attn
    qkv_weight = attn_weights[:, : 3 * HS]
    out_weight = attn_weights[:, 3 * HS :]
    cos, sin = rope_tables(pos)
    qkv = product(unit_all, qkv_weight)
    query = rotate(qkv[:, :HS], cos, sin).astype(bf16)
    keys = rotate(qkv[:, HS : 2 * HS], cos, sin).astype(bf16)
    vals = qkv[:, 2 * HS :].astype(bf16)

    same = (seg[None, :] == seg[:, None]) & (pos[None, :] <= pos[:, None])
    allowed = same | ((seg[None, :] == 0) & (seg[:, None] != 0))

    scores = jnp.where(allowed, times_transposed(query, keys) * scale, masked_value)
    peak = jnp.max(scores, axis=1, keepdims=True)
    exponent = jnp.exp(scores - peak)
    total = jnp.sum(exponent, axis=1, keepdims=True)
    probs = (exponent / total).astype(bf16)
    logsum = peak + jnp.log(total)
    mixed = product(probs, vals).astype(bf16)

    slot = jnp.arange(4) == member
    head_top = jnp.where(slot, jnp.max(peak), masked_value)
    head_top = lax.pmax(head_top, FSDP)

    attn_out = plane_reduce(times_transposed(mixed, out_weight), row, col, core)
    hidden = tokens_f + attn_out
    inverse_mlp = rms_inverse(hidden)
    unit_mlp = hidden * inverse_mlp
    unit_mlp_all = plane_gather(unit_mlp.astype(bf16))

    gate_full = mlp_weights[:, :hidden_own]
    up_full = mlp_weights[:, hidden_own : 2 * hidden_own]
    down_full = mlp_weights[:, 2 * hidden_own :]
    gate = product(unit_mlp_all, gate_full)
    upward = product(unit_mlp_all, up_full)
    d_inner = product(cot_all, down_full)
    sig = jax.nn.sigmoid(gate)
    silu = gate * sig
    inner = (silu * upward).astype(bf16)
    d_gate = (d_inner * upward * sig * (1.0 + gate * (1.0 - sig))).astype(bf16)
    d_up = (d_inner * silu).astype(bf16)
    scaled = plane_reduce(
        times_transposed(d_gate, gate_full) + times_transposed(d_up, up_full), row, col, core
    )
    cot_f = cotangent.astype(f32)
    d_hidden = cot_f + inverse_mlp * (
        scaled - unit_mlp * jnp.mean(scaled * unit_mlp, axis=-1, keepdims=True)
    )
    d_attn_all = plane_gather(d_hidden.astype(bf16))
    block_out = (
        hidden + plane_reduce(times_transposed(inner, down_full), row, col, core)
    ).astype(bf16)

    def send_grads(partial):
        width = partial.shape[1]
        blocks = partial.astype(bf16).reshape(groups, 4 * own_rows, width)
        reduced = line_reduce(blocks, groups, group).astype(bf16).reshape(4, own_rows, width)
        return plane_exchange(lambda m: take(reduced, m), member)

    mlp_grads = send_grads(
        jnp.concatenate(
            [
                outer_sum(unit_mlp_all, d_gate).astype(bf16),
                outer_sum(unit_mlp_all, d_up).astype(bf16),
                outer_sum(cot_all, inner).astype(bf16),
            ],
            axis=1,
        )
    )

    d_mixed = product(d_attn_all, out_weight).astype(bf16)
    scores = jnp.where(allowed, times_transposed(query, keys) * scale, masked_value)
    probs_f = jnp.exp(scores - logsum)
    d_probs = times_transposed(d_mixed, vals)
    row_inner = jnp.sum(probs_f * d_probs, axis=1, keepdims=True)
    d_scores = (probs_f * (d_probs - row_inner)).astype(bf16)
    d_vals = outer_sum(probs_f.astype(bf16), d_mixed)
    d_query = product(d_scores, keys) * scale
    d_keys = outer_sum(d_scores, query) * scale
    d_qkv = jnp.concatenate(
        [
            unrotate(d_query, cos, sin).astype(bf16),
            unrotate(d_keys, cos, sin).astype(bf16),
            d_vals.astype(bf16),
        ],
        axis=1,
    )
    scaled = plane_reduce(times_transposed(d_qkv, qkv_weight), row, col, core)
    tokens_grad = d_hidden + inverse_attn * (
        scaled - unit_attn * jnp.mean(scaled * unit_attn, axis=-1, keepdims=True)
    )
    attn_grads = send_grads(
        jnp.concatenate(
            [
                outer_sum(unit_all, d_qkv).astype(bf16),
                outer_sum(d_attn_all, mixed).astype(bf16),
            ],
            axis=1,
        )
    )

    def wide(grads, start, width):
        part = grads[:, :, start : start + width].astype(f32)
        return part.transpose(1, 0, 2).reshape(own_rows, 4 * width)

    def paired(grads, start):
        part = grads[:, :, start : start + HS].astype(f32).reshape(2, 2, own_rows, HS)
        return jnp.sum(part, axis=1).transpose(1, 0, 2).reshape(own_rows, 2 * HS)

    query_raw = wide(attn_grads, 0, HS)
    key_raw = paired(attn_grads, HS)
    value_raw = paired(attn_grads, 2 * HS)
    output_grad = wide(attn_grads, 3 * HS, HS)
    gate_raw = wide(mlp_grads, 0, hidden_own)
    up_raw = wide(mlp_grads, hidden_own, hidden_own)
    down_grad = wide(mlp_grads, 2 * hidden_own, hidden_own)

    def gain_sum(weight, grad):
        return jnp.sum(weight.astype(f32) * grad, axis=1)

    gains = jnp.stack(
        [
            gain_sum(query_weight, query_raw)
            + gain_sum(key_weight, key_raw)
            + gain_sum(value_weight, value_raw),
            gain_sum(gate_weight, gate_raw) + gain_sum(up_weight, up_raw),
        ]
    )
    gains = gains + swap(gains, "tp")

    factor = clip_limit / jnp.maximum(head_top, clip_limit)
    query_scale = jnp.repeat(jnp.sqrt(factor), HS)
    key_factor = jnp.min(factor.reshape(2, 2), axis=1)
    key_scale = jnp.repeat(jnp.sqrt(key_factor), HS)
    query_clipped = (query_weight.astype(f32) * query_scale[None, :]).astype(bf16)
    key_clipped = (key_weight.astype(f32) * key_scale[None, :]).astype(bf16)
    return (
        block_out,
        tokens_grad,
        gains[0],
        query_raw * gain_attn,
        key_raw * gain_attn,
        value_raw * gain_attn,
        output_grad,
        gains[1],
        gate_raw * gain_mlp,
        up_raw * gain_mlp,
        down_grad,
        head_top,
        query_clipped,
        key_clipped,
    )


def solution(mesh):
    shape = (mesh.shape["fsdp"] // 4, 2, 2, mesh.shape["tp"])
    fine = Mesh(mesh.devices.reshape(shape), ("group", "row", "col", "tp"))
    rows = P(("group", "row", "col", "tp"), None)
    weight = P(FSDP, "tp")
    gain = P(FSDP)
    heads = P("tp")
    return jax.shard_map(
        local,
        mesh=fine,
        in_specs=(
            rows, rows, P(), P(), heads, gain, weight, weight, weight, weight,
            gain, weight, weight, weight,
        ),
        out_specs=(
            rows, rows, gain, weight, weight, weight, weight, gain, weight, weight, weight,
            heads, weight, weight,
        ),
        check_vma=False,
    )
```

```python
import functools

import jax
import jax.numpy as jnp
from jax import lax
from jax.experimental import pallas as pl
from jax.experimental.pallas import tpu as pltpu
from jax.sharding import Mesh, PartitionSpec as P

HS = 256
GROUP = 2048
CHUNKS = 4

epsilon = 1e-05
theta_base = 1000042.0
masked_value = -1e30

bf16 = jnp.bfloat16
f32 = jnp.float32
PLANE = ("row", "col")
FSDP = ("group", "row", "col")
VMEM_LIMIT = 48 * 1024 * 1024


def product(left, right):
    return jnp.dot(left, right, preferred_element_type=f32)


def times_transposed(left, right):
    return lax.dot_general(left, right, (((1,), (1,)), ((), ())), preferred_element_type=f32)


def outer_sum(left, right):
    return lax.dot_general(left, right, (((0,), (0,)), ((), ())), preferred_element_type=f32)


def take(array, index, axis=0):
    return lax.dynamic_index_in_dim(array, index, axis, keepdims=False)


def swap(block, axis):
    return lax.ppermute(block, axis, [(0, 1), (1, 0)])


def swap_plane(block, distance):
    return lax.ppermute(block, PLANE, [(i, i ^ distance) for i in range(4)])


def combine_all(values, groups, combine):
    distance = 1
    while distance < 4 * groups:
        route = [(i, i ^ distance) for i in range(4 * groups)]
        values = combine(values, lax.ppermute(values, FSDP, route))
        distance *= 2
    return values


def plane_gather(own):
    half = own.shape[0] // 2
    across = swap(own, "col")
    along = swap(own, "row")
    far_front = swap(across[:half], "row")
    far_back = swap(along[half:], "col")
    mine = [own, across, along, far_front, far_back]
    return jnp.concatenate(mine + [swap(piece, "tp") for piece in mine], axis=0)


def plane_reduce(partial):
    def chip_sum(half):
        received = swap(partial(1, half).astype(bf16), "tp")
        total = partial(0, half).astype(f32) + received.astype(f32)
        return total.reshape((4, total.shape[0] // 4, total.shape[1]))

    first = chip_sum(0)
    got = swap(jnp.stack([first[1], first[3]]).astype(bf16), "col").astype(f32)
    second = chip_sum(1)
    got_second = swap(second[2:].astype(bf16), "row").astype(f32)
    last = swap((first[2] + got[1]).astype(bf16), "row").astype(f32)
    last_second = swap((second[1] + got_second[1]).astype(bf16), "col").astype(f32)
    return jnp.concatenate(
        [first[0] + got[0] + last, second[0] + got_second[0] + last_second], axis=1
    )


def line_reduce(blocks, groups, index):
    up = down = None
    for step in range(1, groups):
        out_up = take(blocks, jnp.minimum(index + groups - step, groups - 1))
        out_down = take(blocks, jnp.maximum(index - groups + step, 0))
        if up is not None:
            out_up = (out_up.astype(f32) + up.astype(f32)).astype(bf16)
            out_down = (out_down.astype(f32) + down.astype(f32)).astype(bf16)
        senders = range(min(step, groups - 1))
        up = lax.ppermute(out_up, "group", [(j, j + 1) for j in senders])
        down = lax.ppermute(
            out_down, "group", [(groups - 1 - j, groups - 2 - j) for j in senders]
        )
    return take(blocks, index).astype(f32) + up.astype(f32) + down.astype(f32)


def plane_exchange(make, member):
    own = make(member)
    result = jnp.zeros((4,) + own.shape, own.dtype)
    result = lax.dynamic_update_index_in_dim(result, own, member, 0)
    for distance in (1, 2, 3):
        got = swap_plane(make(member ^ distance), distance)
        result = lax.dynamic_update_index_in_dim(result, got, member ^ distance, 0)
    return result


def rms_inverse(values):
    return lax.rsqrt(jnp.mean(values * values, axis=-1, keepdims=True) + epsilon)


def rope_tables(positions):
    half_size = HS // 2
    indices = jnp.arange(half_size, dtype=f32)
    inverse = theta_base ** (-2.0 * indices / HS)
    angles = positions.astype(f32)[:, None] * inverse[None, :]
    return jnp.cos(angles), jnp.sin(angles)


def rotate(vectors, cos, sin):
    front, back = vectors[:, : HS // 2], vectors[:, HS // 2 :]
    return jnp.concatenate([front * cos - back * sin, back * cos + front * sin], axis=-1)


def unrotate(grads, cos, sin):
    front, back = grads[:, : HS // 2], grads[:, HS // 2 :]
    return jnp.concatenate([front * cos + back * sin, back * cos - front * sin], axis=-1)


def mlp_kernel(width, normed_ref, cot_ref, weight_ref, inner_ref, grads_ref):
    both = product(normed_ref[...], weight_ref[:, : 2 * width])
    d_inner = product(cot_ref[...], weight_ref[:, 2 * width :])
    gate, upward = both[:, :width], both[:, width:]
    sig = 1.0 / (1.0 + jnp.exp(-gate))
    silu = gate * sig
    inner_ref[...] = (silu * upward).astype(bf16)
    d_gate = d_inner * upward * sig * (1.0 + gate * (1.0 - sig))
    grads_ref[...] = jnp.concatenate([d_gate, d_inner * silu], axis=1).astype(bf16)


def mlp_chunk(normed, cot, weight):
    tokens, features = normed.shape
    width = weight.shape[1] // 3
    tile = 256
    return pl.pallas_call(
        functools.partial(mlp_kernel, width),
        grid=(tokens // tile,),
        in_specs=[
            pl.BlockSpec((tile, features), lambda i: (i, 0)),
            pl.BlockSpec((tile, features), lambda i: (i, 0)),
            pl.BlockSpec((features, 3 * width), lambda i: (0, 0)),
        ],
        out_specs=[
            pl.BlockSpec((tile, width), lambda i: (i, 0)),
            pl.BlockSpec((tile, 2 * width), lambda i: (i, 0)),
        ],
        out_shape=[
            jax.ShapeDtypeStruct((tokens, width), bf16),
            jax.ShapeDtypeStruct((tokens, 2 * width), bf16),
        ],
        cost_estimate=pl.CostEstimate(
            flops=6 * tokens * features * width,
            bytes_accessed=2 * features * (2 * tokens + 3 * width),
            transcendentals=tokens * width,
        ),
        compiler_params=pltpu.CompilerParams(vmem_limit_bytes=VMEM_LIMIT),
        name="mlp_chunk",
    )(normed, cot, weight)


def sum_kernel(count, *refs):
    lefts, rights, out_ref = refs[:count], refs[count : 2 * count], refs[2 * count]
    total = times_transposed(lefts[0][...], rights[0][...])
    for left, right in zip(lefts[1:], rights[1:]):
        total += times_transposed(left[...], right[...])
    out_ref[...] = total.astype(out_ref.dtype)


def chunk_sum(lefts, rights, column, part, half, dtype):
    count = len(lefts)
    tokens, width = lefts[0].shape
    features = rights[0].shape[0] // 2
    rows = tokens // 2
    tile = 256
    steps = rows // tile
    return pl.pallas_call(
        functools.partial(sum_kernel, count),
        grid=(steps,),
        in_specs=[pl.BlockSpec((tile, width), lambda i: (part * steps + i, 0))] * count
        + [pl.BlockSpec((features, width), lambda i: (half, column))] * count,
        out_specs=pl.BlockSpec((tile, features), lambda i: (i, 0)),
        out_shape=jax.ShapeDtypeStruct((rows, features), dtype),
        cost_estimate=pl.CostEstimate(
            flops=2 * rows * features * width * count,
            bytes_accessed=2 * count * width * (rows + features) + 4 * rows * features,
            transcendentals=0,
        ),
        compiler_params=pltpu.CompilerParams(vmem_limit_bytes=VMEM_LIMIT),
        name="chunk_sum",
    )(*lefts, *rights)


def local(
    tokens,
    cotangent,
    segment,
    position,
    clip_limit,
    attn_gain,
    query_weight,
    key_weight,
    value_weight,
    output_weight,
    mlp_gain,
    gate_weight,
    up_weight,
    down_weight,
):
    groups = lax.axis_size("group")
    group = lax.axis_index("group")
    core = lax.axis_index("tp")
    member = lax.axis_index(PLANE)
    token_rows = tokens.shape[0]
    own_rows, features = query_weight.shape[0], tokens.shape[1]
    width = gate_weight.shape[1] // 4 // CHUNKS
    scale = HS ** (-0.5)

    def own_order(array):
        parts = []
        for j in range(2):
            for k in range(4):
                start = group * GROUP + (member ^ k) * (2 * token_rows) + (core ^ j) * token_rows
                parts.append(lax.dynamic_slice_in_dim(array, start, token_rows))
        return jnp.concatenate(parts)

    def columns(array, start, count):
        return lax.dynamic_slice_in_dim(array, start, count, 1)

    def collect(make):
        blocks = plane_exchange(make, member)
        flat = blocks.reshape(4 * own_rows, blocks.shape[-1])
        return lax.all_gather(flat, "group", axis=0, tiled=True)

    def qkv_block(m):
        return jnp.concatenate(
            [
                columns(query_weight, m * HS, HS),
                columns(key_weight, m // 2 * HS, HS),
                columns(value_weight, m // 2 * HS, HS),
            ],
            axis=1,
        )

    def mlp_block(chunk, m):
        start = (m * CHUNKS + chunk) * width
        return jnp.concatenate(
            [columns(a, start, width) for a in (gate_weight, up_weight, down_weight)], axis=1
        )

    qkv_weight = collect(qkv_block)
    tokens_all = plane_gather(tokens)
    out_weight = collect(lambda m: columns(output_weight, m * HS, HS))
    mlp_weights = [collect(functools.partial(mlp_block, n)) for n in range(CHUNKS)]

    index = lax.axis_index(FSDP)
    gains = jnp.stack([attn_gain, mlp_gain])[:, None, :]
    gains = jnp.where(jnp.arange(4 * groups)[None, :, None] == index, gains, 0)
    gains = combine_all(gains, groups, lambda a, b: a + b).reshape(2, features).astype(f32)
    gain_attn, gain_mlp = gains[0], gains[1]

    tokens_f = tokens.astype(f32)
    all_f = tokens_all.astype(f32)
    normed_all = (all_f * rms_inverse(all_f) * gain_attn).astype(bf16)
    inverse_attn = rms_inverse(tokens_f)
    unit_attn = tokens_f * inverse_attn
    seg, pos = own_order(segment), own_order(position)
    cos, sin = rope_tables(pos)
    qkv = product(normed_all, qkv_weight)
    query = rotate(qkv[:, :HS], cos, sin).astype(bf16)
    keys = rotate(qkv[:, HS : 2 * HS], cos, sin).astype(bf16)
    vals = qkv[:, 2 * HS :].astype(bf16)

    same = (seg[None, :] == seg[:, None]) & (pos[None, :] <= pos[:, None])
    allowed = same | ((seg[None, :] == 0) & (seg[:, None] != 0))

    scores = jnp.where(allowed, times_transposed(query, keys) * scale, masked_value)
    peak = jnp.max(scores, axis=1, keepdims=True)
    exponent = jnp.exp(scores - peak)
    total = jnp.sum(exponent, axis=1, keepdims=True)
    probs = (exponent / total).astype(bf16)
    logsum = peak + jnp.log(total)
    mixed = product(probs, vals).astype(bf16)

    head_top = jnp.where(jnp.arange(4) == member, jnp.max(peak), masked_value)
    head_top = combine_all(head_top, groups, jnp.maximum)

    def projected(left, right):
        rows, half = left.shape[0] // 2, right.shape[0] // 2
        return lambda j, h: times_transposed(
            left[j * rows : (j + 1) * rows], right[h * half : (h + 1) * half]
        )

    attn_out = plane_reduce(projected(mixed, out_weight))
    hidden = tokens_f + attn_out
    inverse_mlp = rms_inverse(hidden)
    unit_mlp = hidden * inverse_mlp
    normed_mlp = plane_gather((unit_mlp * gain_mlp).astype(bf16))
    cot_all = plane_gather(cotangent)

    inners, d_boths, mlp_grads = [], [], []
    for n in range(CHUNKS):
        inner, d_both = mlp_chunk(normed_mlp, cot_all, mlp_weights[n])
        inners.append(inner)
        d_boths.append(d_both)
    d_normed = plane_reduce(
        lambda j, h: chunk_sum(d_boths, mlp_weights, 0, j, h, bf16 if j else f32)
    )
    cot_f = cotangent.astype(f32)
    scaled = d_normed * gain_mlp
    d_hidden = cot_f + inverse_mlp * (
        scaled - unit_mlp * jnp.mean(scaled * unit_mlp, axis=-1, keepdims=True)
    )
    d_attn_all = plane_gather(d_hidden.astype(bf16))

    def send_grads(partial):
        blocks = partial.astype(bf16).reshape(groups, 4 * own_rows, partial.shape[1])
        reduced = line_reduce(blocks, groups, group).astype(bf16)
        reduced = reduced.reshape(4, own_rows, partial.shape[1])
        return plane_exchange(lambda m: take(reduced, m), member)

    both_grads, down_grads = [], []
    for n in range(CHUNKS):
        both_grads.append(send_grads(outer_sum(normed_mlp, d_boths[n])))
        down_grads.append(send_grads(outer_sum(cot_all, inners[n])))
    block_out = (
        hidden
        + plane_reduce(lambda j, h: chunk_sum(inners, mlp_weights, 2, j, h, bf16 if j else f32))
    ).astype(bf16)

    d_mixed = product(d_attn_all, out_weight).astype(bf16)
    scores = jnp.where(allowed, times_transposed(query, keys) * scale, masked_value)
    probs_f = jnp.exp(scores - logsum)
    d_probs = times_transposed(d_mixed, vals)
    row_inner = jnp.sum(probs_f * d_probs, axis=1, keepdims=True)
    d_scores = (probs_f * (d_probs - row_inner)).astype(bf16)
    d_vals = outer_sum(probs_f.astype(bf16), d_mixed)
    d_query = product(d_scores, keys) * scale
    d_keys = outer_sum(d_scores, query) * scale
    d_qkv = jnp.concatenate(
        [
            unrotate(d_query, cos, sin).astype(bf16),
            unrotate(d_keys, cos, sin).astype(bf16),
            d_vals.astype(bf16),
        ],
        axis=1,
    )
    output_grads = send_grads(outer_sum(d_attn_all, mixed))
    d_normed = plane_reduce(projected(d_qkv, qkv_weight))
    qkv_grads = send_grads(outer_sum(normed_all, d_qkv))
    scaled = d_normed * gain_attn
    tokens_grad = d_hidden + inverse_attn * (
        scaled - unit_attn * jnp.mean(scaled * unit_attn, axis=-1, keepdims=True)
    )

    def wide(grads, start, count):
        part = grads[:, :, start : start + count].astype(f32)
        return part.transpose(1, 0, 2).reshape(own_rows, 4 * count)

    def paired(grads, start):
        part = grads[:, :, start : start + HS].astype(f32).reshape(2, 2, own_rows, HS)
        return jnp.sum(part, axis=1).transpose(1, 0, 2).reshape(own_rows, 2 * HS)

    def chunked(parts, start):
        part = jnp.stack([g[:, :, start : start + width] for g in parts], axis=1).astype(f32)
        return part.transpose(2, 0, 1, 3).reshape(own_rows, 4 * CHUNKS * width)

    query_grad = wide(qkv_grads, 0, HS)
    key_grad = paired(qkv_grads, HS)
    value_grad = paired(qkv_grads, 2 * HS)
    output_grad = wide(output_grads, 0, HS)
    gate_grad = chunked(both_grads, 0)
    up_grad = chunked(both_grads, width)
    down_grad = chunked(down_grads, 0)

    def gain_sum(weight, grad):
        return jnp.sum(weight.astype(f32) * grad, axis=1)

    gain_grads = jnp.stack(
        [
            gain_sum(query_weight, query_grad)
            + gain_sum(key_weight, key_grad)
            + gain_sum(value_weight, value_grad),
            gain_sum(gate_weight, gate_grad) + gain_sum(up_weight, up_grad),
        ]
    )
    gain_grads = gain_grads + swap(gain_grads, "tp")
    attn_gain_grad = gain_grads[0] / attn_gain.astype(f32)
    mlp_gain_grad = gain_grads[1] / mlp_gain.astype(f32)

    factor = clip_limit / jnp.maximum(head_top, clip_limit)
    query_scale = jnp.repeat(jnp.sqrt(factor), HS)
    key_factor = jnp.min(factor.reshape(2, 2), axis=1)
    key_scale = jnp.repeat(jnp.sqrt(key_factor), HS)
    query_clipped = (query_weight.astype(f32) * query_scale[None, :]).astype(bf16)
    key_clipped = (key_weight.astype(f32) * key_scale[None, :]).astype(bf16)
    return (
        block_out,
        tokens_grad,
        attn_gain_grad,
        query_grad,
        key_grad,
        value_grad,
        output_grad,
        mlp_gain_grad,
        gate_grad,
        up_grad,
        down_grad,
        head_top,
        query_clipped,
        key_clipped,
    )


def solution(mesh):
    shape = (mesh.shape["fsdp"] // 4, 2, 2, mesh.shape["tp"])
    fine = Mesh(mesh.devices.reshape(shape), ("group", "row", "col", "tp"))
    rows = P(("group", "row", "col", "tp"), None)
    weight = P(FSDP, "tp")
    gain = P(FSDP)
    heads = P("tp")
    return jax.shard_map(
        local,
        mesh=fine,
        in_specs=(
            rows, rows, P(), P(), heads, gain, weight, weight, weight, weight,
            gain, weight, weight, weight,
        ),
        out_specs=(
            rows, rows, gain, weight, weight, weight, weight, gain, weight, weight, weight,
            heads, weight, weight,
        ),
        check_vma=False,
    )
```

```python
import functools

import jax
import jax.numpy as jnp
from jax import lax
from jax.experimental import pallas as pl
from jax.experimental.pallas import tpu as pltpu
from jax.sharding import Mesh, PartitionSpec as P

HS = 256
GROUP = 2048
CHUNKS = 4

epsilon = 1e-05
theta_base = 1000042.0
masked_value = -1e30

bf16 = jnp.bfloat16
f32 = jnp.float32
PLANE = ("row", "col")
FSDP = ("group", "row", "col")
VMEM_LIMIT = 48 * 1024 * 1024


def product(left, right):
    return jnp.dot(left, right, preferred_element_type=f32)


def times_transposed(left, right):
    return lax.dot_general(left, right, (((1,), (1,)), ((), ())), preferred_element_type=f32)


def outer_sum(left, right):
    return lax.dot_general(left, right, (((0,), (0,)), ((), ())), preferred_element_type=f32)


def take(array, index, axis=0):
    return lax.dynamic_index_in_dim(array, index, axis, keepdims=False)


def swap(block, axis):
    return lax.ppermute(block, axis, [(0, 1), (1, 0)])


def swap_plane(block, distance):
    return lax.ppermute(block, PLANE, [(i, i ^ distance) for i in range(4)])


def after(value, *others):
    return lax.optimization_barrier((value,) + others)[0]


def combine_all(values, groups, combine):
    distance = 1
    while distance < 4 * groups:
        route = [(i, i ^ distance) for i in range(4 * groups)]
        values = combine(values, lax.ppermute(values, FSDP, route))
        distance *= 2
    return values


def plane_neighbours(own):
    return swap(own, "col"), swap(own, "row")


def plane_gather(own, neighbours=None):
    half = own.shape[0] // 2
    across, along = neighbours or plane_neighbours(own)
    far_front = swap(across[:half], "row")
    far_back = swap(along[half:], "col")
    mine = [own, across, along, far_front, far_back]
    return jnp.concatenate(mine + [swap(piece, "tp") for piece in mine], axis=0)


def plane_reduce(partial):
    def chip_sum(half):
        received = swap(partial(1, half).astype(bf16), "tp")
        total = partial(0, half).astype(f32) + received.astype(f32)
        return total.reshape((4, total.shape[0] // 4, total.shape[1]))

    first = chip_sum(0)
    got = swap(jnp.stack([first[1], first[3]]).astype(bf16), "col").astype(f32)
    second = chip_sum(1)
    got_second = swap(second[2:].astype(bf16), "row").astype(f32)
    last = swap((first[2] + got[1]).astype(bf16), "row").astype(f32)
    last_second = swap((second[1] + got_second[1]).astype(bf16), "col").astype(f32)
    return jnp.concatenate(
        [first[0] + got[0] + last, second[0] + got_second[0] + last_second], axis=1
    )


def plane_exchange(make, member):
    own = make(member)
    result = jnp.zeros((4,) + own.shape, own.dtype)
    result = lax.dynamic_update_index_in_dim(result, own, member, 0)
    for distance in (1, 2, 3):
        got = swap_plane(make(member ^ distance), distance)
        result = lax.dynamic_update_index_in_dim(result, got, member ^ distance, 0)
    return result


def rms_inverse(values):
    return lax.rsqrt(jnp.mean(values * values, axis=-1, keepdims=True) + epsilon)


def rope_tables(positions):
    half_size = HS // 2
    indices = jnp.arange(half_size, dtype=f32)
    inverse = theta_base ** (-2.0 * indices / HS)
    angles = positions.astype(f32)[:, None] * inverse[None, :]
    return jnp.cos(angles), jnp.sin(angles)


def rotate(vectors, cos, sin):
    front, back = vectors[:, : HS // 2], vectors[:, HS // 2 :]
    return jnp.concatenate([front * cos - back * sin, back * cos + front * sin], axis=-1)


def unrotate(grads, cos, sin):
    front, back = grads[:, : HS // 2], grads[:, HS // 2 :]
    return jnp.concatenate([front * cos + back * sin, back * cos - front * sin], axis=-1)


def mlp_kernel(width, normed_ref, cot_ref, weight_ref, inner_ref, grads_ref):
    both = product(normed_ref[...], weight_ref[:, : 2 * width])
    d_inner = product(cot_ref[...], weight_ref[:, 2 * width :])
    gate, upward = both[:, :width], both[:, width:]
    sig = 1.0 / (1.0 + jnp.exp(-gate))
    silu = gate * sig
    inner_ref[...] = (silu * upward).astype(bf16)
    d_gate = d_inner * upward * sig * (1.0 + gate * (1.0 - sig))
    grads_ref[...] = jnp.concatenate([d_gate, d_inner * silu], axis=1).astype(bf16)


def mlp_chunk(normed, cot, weight):
    tokens, features = normed.shape
    width = weight.shape[1] // 3
    tile = 256
    return pl.pallas_call(
        functools.partial(mlp_kernel, width),
        grid=(tokens // tile,),
        in_specs=[
            pl.BlockSpec((tile, features), lambda i: (i, 0)),
            pl.BlockSpec((tile, features), lambda i: (i, 0)),
            pl.BlockSpec((features, 3 * width), lambda i: (0, 0)),
        ],
        out_specs=[
            pl.BlockSpec((tile, width), lambda i: (i, 0)),
            pl.BlockSpec((tile, 2 * width), lambda i: (i, 0)),
        ],
        out_shape=[
            jax.ShapeDtypeStruct((tokens, width), bf16),
            jax.ShapeDtypeStruct((tokens, 2 * width), bf16),
        ],
        cost_estimate=pl.CostEstimate(
            flops=6 * tokens * features * width,
            bytes_accessed=2 * features * (2 * tokens + 3 * width),
            transcendentals=tokens * width,
        ),
        compiler_params=pltpu.CompilerParams(vmem_limit_bytes=VMEM_LIMIT),
        name="mlp_chunk",
    )(normed, cot, weight)


def sum_kernel(count, *refs):
    lefts, rights, out_ref = refs[:count], refs[count : 2 * count], refs[2 * count]
    total = times_transposed(lefts[0][...], rights[0][...])
    for left, right in zip(lefts[1:], rights[1:]):
        total += times_transposed(left[...], right[...])
    out_ref[...] = total.astype(out_ref.dtype)


def chunk_sum(lefts, rights, column, part, half, dtype):
    count = len(lefts)
    tokens, width = lefts[0].shape
    features = rights[0].shape[0] // 2
    rows = tokens // 2
    tile = 256
    steps = rows // tile
    return pl.pallas_call(
        functools.partial(sum_kernel, count),
        grid=(steps,),
        in_specs=[pl.BlockSpec((tile, width), lambda i: (part * steps + i, 0))] * count
        + [pl.BlockSpec((features, width), lambda i: (half, column))] * count,
        out_specs=pl.BlockSpec((tile, features), lambda i: (i, 0)),
        out_shape=jax.ShapeDtypeStruct((rows, features), dtype),
        cost_estimate=pl.CostEstimate(
            flops=2 * rows * features * width * count,
            bytes_accessed=2 * count * width * (rows + features) + 4 * rows * features,
            transcendentals=0,
        ),
        compiler_params=pltpu.CompilerParams(vmem_limit_bytes=VMEM_LIMIT),
        name="chunk_sum",
    )(*lefts, *rights)


def grads_kernel(normed_ref, cot_ref, both_ref, inner_ref, out_ref):
    width = inner_ref.shape[1]
    out_ref[:, : 2 * width] = outer_sum(normed_ref[...], both_ref[...]).astype(bf16)
    out_ref[:, 2 * width :] = outer_sum(cot_ref[...], inner_ref[...]).astype(bf16)


def mlp_grads(normed, cot, both, inner):
    tokens, features = normed.shape
    width = inner.shape[1]
    tile = 256
    return pl.pallas_call(
        grads_kernel,
        grid=(features // tile,),
        in_specs=[
            pl.BlockSpec((tokens, tile), lambda i: (0, i)),
            pl.BlockSpec((tokens, tile), lambda i: (0, i)),
            pl.BlockSpec((tokens, 2 * width), lambda i: (0, 0)),
            pl.BlockSpec((tokens, width), lambda i: (0, 0)),
        ],
        out_specs=pl.BlockSpec((tile, 3 * width), lambda i: (i, 0)),
        out_shape=jax.ShapeDtypeStruct((features, 3 * width), bf16),
        cost_estimate=pl.CostEstimate(
            flops=6 * tokens * features * width,
            bytes_accessed=2 * (2 * tokens * features + 3 * width * (tokens + features)),
            transcendentals=0,
        ),
        compiler_params=pltpu.CompilerParams(vmem_limit_bytes=VMEM_LIMIT),
        name="mlp_grads",
    )(normed, cot, both, inner)


def local(
    tokens,
    cotangent,
    segment,
    position,
    clip_limit,
    attn_gain,
    query_weight,
    key_weight,
    value_weight,
    output_weight,
    mlp_gain,
    gate_weight,
    up_weight,
    down_weight,
):
    groups = lax.axis_size("group")
    group = lax.axis_index("group")
    core = lax.axis_index("tp")
    member = lax.axis_index(PLANE)
    token_rows = tokens.shape[0]
    own_rows, features = query_weight.shape[0], tokens.shape[1]
    width = gate_weight.shape[1] // 4 // CHUNKS
    scale = HS ** (-0.5)

    def own_order(array):
        parts = []
        for j in range(2):
            for k in range(4):
                start = group * GROUP + (member ^ k) * (2 * token_rows) + (core ^ j) * token_rows
                parts.append(lax.dynamic_slice_in_dim(array, start, token_rows))
        return jnp.concatenate(parts)

    def columns(array, start, count):
        return lax.dynamic_slice_in_dim(array, start, count, 1)

    def exchange(make):
        blocks = plane_exchange(make, member)
        return blocks.reshape(4 * own_rows, blocks.shape[-1])

    def collect(blocks):
        return lax.all_gather(blocks, "group", axis=0, tiled=True)

    def qkv_block(m):
        return jnp.concatenate(
            [
                columns(query_weight, m * HS, HS),
                columns(key_weight, m // 2 * HS, HS),
                columns(value_weight, m // 2 * HS, HS),
            ],
            axis=1,
        )

    qkv_blocks = exchange(qkv_block)
    qkv_weight = collect(qkv_blocks)
    late_output = after(output_weight, qkv_blocks)
    out_blocks = exchange(lambda m: columns(late_output, m * HS, HS))
    out_weight = collect(out_blocks)
    late_tokens = after(tokens, qkv_blocks)
    neighbours = plane_neighbours(late_tokens)
    tokens_all = plane_gather(late_tokens, neighbours)

    def mlp_blocks(chunk, waits):
        weights = [after(a, *waits) for a in (gate_weight, up_weight, down_weight)]

        def block(m):
            start = (m * CHUNKS + chunk) * width
            return jnp.concatenate([columns(a, start, width) for a in weights], axis=1)

        return exchange(block)

    chunk_blocks = [mlp_blocks(0, neighbours)]
    for n in range(1, CHUNKS):
        chunk_blocks.append(mlp_blocks(n, (chunk_blocks[0], tokens_all)))
    mlp_weights = [collect(blocks) for blocks in chunk_blocks]
    cot_all = plane_gather(after(cotangent, *chunk_blocks))

    index = lax.axis_index(FSDP)
    gains = jnp.stack([attn_gain, mlp_gain])[:, None, :]
    gains = jnp.where(jnp.arange(4 * groups)[None, :, None] == index, gains, 0)
    gains = combine_all(gains, groups, lambda a, b: a + b).reshape(2, features).astype(f32)
    gain_attn, gain_mlp = gains[0], gains[1]

    tokens_f = tokens.astype(f32)
    all_f = tokens_all.astype(f32)
    normed_all = (all_f * rms_inverse(all_f) * gain_attn).astype(bf16)
    inverse_attn = rms_inverse(tokens_f)
    unit_attn = tokens_f * inverse_attn
    seg, pos = own_order(segment), own_order(position)
    cos, sin = rope_tables(pos)
    qkv = product(normed_all, qkv_weight)
    query = rotate(qkv[:, :HS], cos, sin).astype(bf16)
    keys = rotate(qkv[:, HS : 2 * HS], cos, sin).astype(bf16)
    vals = qkv[:, 2 * HS :].astype(bf16)

    same = (seg[None, :] == seg[:, None]) & (pos[None, :] <= pos[:, None])
    allowed = same | ((seg[None, :] == 0) & (seg[:, None] != 0))

    scores = jnp.where(allowed, times_transposed(query, keys) * scale, masked_value)
    peak = jnp.max(scores, axis=1, keepdims=True)
    exponent = jnp.exp(scores - peak)
    total = jnp.sum(exponent, axis=1, keepdims=True)
    probs = (exponent / total).astype(bf16)
    logsum = peak + jnp.log(total)
    mixed = product(probs, vals).astype(bf16)

    head_top = jnp.where(jnp.arange(4) == member, jnp.max(peak), masked_value)
    head_top = combine_all(head_top, groups, jnp.maximum)

    def projected(left, right):
        rows, half = left.shape[0] // 2, right.shape[0] // 2
        return lambda j, h: times_transposed(
            left[j * rows : (j + 1) * rows], right[h * half : (h + 1) * half]
        )

    attn_out = plane_reduce(projected(mixed, out_weight))
    hidden = tokens_f + attn_out
    inverse_mlp = rms_inverse(hidden)
    unit_mlp = hidden * inverse_mlp
    normed_mlp = plane_gather((unit_mlp * gain_mlp).astype(bf16))

    inners, d_boths = [], []
    for n in range(CHUNKS):
        inner, d_both = mlp_chunk(normed_mlp, cot_all, mlp_weights[n])
        inners.append(inner)
        d_boths.append(d_both)
    sums = {
        (j, h): chunk_sum(d_boths, mlp_weights, 0, j, h, bf16 if j else f32)
        for h in range(2)
        for j in (1, 0)
    }
    d_normed = plane_reduce(lambda j, h: sums[j, h])
    cot_f = cotangent.astype(f32)
    scaled = d_normed * gain_mlp
    d_hidden = cot_f + inverse_mlp * (
        scaled - unit_mlp * jnp.mean(scaled * unit_mlp, axis=-1, keepdims=True)
    )
    d_attn_all = plane_gather(d_hidden.astype(bf16))

    def line_sum(partial):
        return lax.psum_scatter(partial, "group", scatter_dimension=0, tiled=True)

    def send_grads(reduced):
        reduced = reduced.reshape(4, own_rows, reduced.shape[1])
        return plane_exchange(lambda m: take(reduced, m), member)

    chunk_grads = []
    for n in range(CHUNKS):
        inner = inners[n] if n < CHUNKS - 1 else after(inners[n], *sums.values())
        chunk_grads.append(line_sum(mlp_grads(normed_mlp, cot_all, d_boths[n], inner)))
    late_inners = [after(inner, d_attn_all) for inner in inners]
    block_out = (
        hidden
        + plane_reduce(
            lambda j, h: chunk_sum(late_inners, mlp_weights, 2, j, h, bf16 if j else f32)
        )
    ).astype(bf16)

    d_mixed = product(d_attn_all, out_weight).astype(bf16)
    scores = jnp.where(allowed, times_transposed(query, keys) * scale, masked_value)
    probs_f = jnp.exp(scores - logsum)
    d_probs = times_transposed(d_mixed, vals)
    row_inner = jnp.sum(probs_f * d_probs, axis=1, keepdims=True)
    d_scores = (probs_f * (d_probs - row_inner)).astype(bf16)
    d_vals = outer_sum(probs_f.astype(bf16), d_mixed)
    d_query = product(d_scores, keys) * scale
    d_keys = outer_sum(d_scores, query) * scale
    d_qkv = jnp.concatenate(
        [
            unrotate(d_query, cos, sin).astype(bf16),
            unrotate(d_keys, cos, sin).astype(bf16),
            d_vals.astype(bf16),
        ],
        axis=1,
    )
    output_sum = line_sum(outer_sum(d_attn_all, mixed).astype(bf16))
    d_normed = plane_reduce(projected(d_qkv, qkv_weight))
    qkv_sum = line_sum(outer_sum(normed_all, d_qkv).astype(bf16))
    scaled = d_normed * gain_attn
    tokens_grad = d_hidden + inverse_attn * (
        scaled - unit_attn * jnp.mean(scaled * unit_attn, axis=-1, keepdims=True)
    )

    mlp_parts = [send_grads(reduced) for reduced in chunk_grads]
    output_grads = send_grads(output_sum)
    qkv_grads = send_grads(qkv_sum)

    def wide(grads, start, count):
        part = grads[:, :, start : start + count].astype(f32)
        return part.transpose(1, 0, 2).reshape(own_rows, 4 * count)

    def paired(grads, start):
        part = grads[:, :, start : start + HS].astype(f32).reshape(2, 2, own_rows, HS)
        return jnp.sum(part, axis=1).transpose(1, 0, 2).reshape(own_rows, 2 * HS)

    def chunked(parts, start):
        part = jnp.stack([g[:, :, start : start + width] for g in parts], axis=1).astype(f32)
        return part.transpose(2, 0, 1, 3).reshape(own_rows, 4 * CHUNKS * width)

    query_grad = wide(qkv_grads, 0, HS)
    key_grad = paired(qkv_grads, HS)
    value_grad = paired(qkv_grads, 2 * HS)
    output_grad = wide(output_grads, 0, HS)
    gate_grad = chunked(mlp_parts, 0)
    up_grad = chunked(mlp_parts, width)
    down_grad = chunked(mlp_parts, 2 * width)

    def gain_sum(weight, grad):
        return jnp.sum(weight.astype(f32) * grad, axis=1)

    gain_grads = jnp.stack(
        [
            gain_sum(query_weight, query_grad)
            + gain_sum(key_weight, key_grad)
            + gain_sum(value_weight, value_grad),
            gain_sum(gate_weight, gate_grad) + gain_sum(up_weight, up_grad),
        ]
    )
    gain_grads = gain_grads + swap(gain_grads, "tp")
    attn_gain_grad = gain_grads[0] / attn_gain.astype(f32)
    mlp_gain_grad = gain_grads[1] / mlp_gain.astype(f32)

    factor = clip_limit / jnp.maximum(head_top, clip_limit)
    query_scale = jnp.repeat(jnp.sqrt(factor), HS)
    key_factor = jnp.min(factor.reshape(2, 2), axis=1)
    key_scale = jnp.repeat(jnp.sqrt(key_factor), HS)
    query_clipped = (query_weight.astype(f32) * query_scale[None, :]).astype(bf16)
    key_clipped = (key_weight.astype(f32) * key_scale[None, :]).astype(bf16)
    return (
        block_out,
        tokens_grad,
        attn_gain_grad,
        query_grad,
        key_grad,
        value_grad,
        output_grad,
        mlp_gain_grad,
        gate_grad,
        up_grad,
        down_grad,
        head_top,
        query_clipped,
        key_clipped,
    )


def solution(mesh):
    shape = (mesh.shape["fsdp"] // 4, 2, 2, mesh.shape["tp"])
    fine = Mesh(mesh.devices.reshape(shape), ("group", "row", "col", "tp"))
    rows = P(("group", "row", "col", "tp"), None)
    weight = P(FSDP, "tp")
    gain = P(FSDP)
    heads = P("tp")
    return jax.shard_map(
        local,
        mesh=fine,
        in_specs=(
            rows, rows, P(), P(), heads, gain, weight, weight, weight, weight,
            gain, weight, weight, weight,
        ),
        out_specs=(
            rows, rows, gain, weight, weight, weight, weight, gain, weight, weight, weight,
            heads, weight, weight,
        ),
        check_vma=False,
    )
```

```python
import functools

import jax
import jax.numpy as jnp
from jax import lax
from jax.experimental import pallas as pl
from jax.experimental.pallas import tpu as pltpu
from jax.sharding import Mesh, PartitionSpec as P

HS = 256
GROUP = 2048
CHUNKS = 2
BLOCK = 128

epsilon = 1e-05
theta_base = 1000042.0
masked_value = -1e30

bf16 = jnp.bfloat16
f32 = jnp.float32
PLANE = ("row", "col")
FSDP = ("group", "row", "col")
VMEM_LIMIT = 48 * 1024 * 1024


def product(left, right):
    return jnp.dot(left, right, preferred_element_type=f32)


def times_transposed(left, right):
    return lax.dot_general(left, right, (((1,), (1,)), ((), ())), preferred_element_type=f32)


def outer_sum(left, right):
    return lax.dot_general(left, right, (((0,), (0,)), ((), ())), preferred_element_type=f32)


def take(array, index, axis=0):
    return lax.dynamic_index_in_dim(array, index, axis, keepdims=False)


def swap(block, axis):
    return lax.ppermute(block, axis, [(0, 1), (1, 0)])


def swap_plane(block, distance):
    return lax.ppermute(block, PLANE, [(i, i ^ distance) for i in range(4)])


def after(value, *others):
    return lax.optimization_barrier((value,) + others)[0]


def combine_all(values, groups, combine):
    distance = 1
    while distance < 4 * groups:
        route = [(i, i ^ distance) for i in range(4 * groups)]
        values = combine(values, lax.ppermute(values, FSDP, route))
        distance *= 2
    return values


def pack_kernel(count, *refs):
    out_ref, sems = refs[count], refs[count + 1]
    copies, start = [], 0
    for i in range(count):
        rows = refs[i].shape[0]
        copy = pltpu.make_async_copy(refs[i], out_ref.at[pl.ds(start, rows)], sems.at[i])
        copy.start()
        copies.append(copy)
        start += rows
    for copy in copies:
        copy.wait()


def pack(pieces):
    rows, width = sum(p.shape[0] for p in pieces), pieces[0].shape[1]
    count = len(pieces)
    return pl.pallas_call(
        functools.partial(pack_kernel, count),
        in_specs=[pl.BlockSpec(memory_space=pl.ANY)] * count,
        out_specs=pl.BlockSpec(memory_space=pl.ANY),
        out_shape=jax.ShapeDtypeStruct((rows, width), pieces[0].dtype),
        scratch_shapes=[pltpu.SemaphoreType.DMA((count,))],
        cost_estimate=pl.CostEstimate(
            flops=0, bytes_accessed=4 * rows * width, transcendentals=0
        ),
        name="pack",
    )(*pieces)


def plane_neighbours(own):
    return swap(own, "col"), swap(own, "row")


def plane_gather(own, neighbours=None, wait=()):
    half = own.shape[0] // 2
    across, along = neighbours or plane_neighbours(own)
    far_front = swap(after(across[:half], *wait), "row")
    far_back = swap(after(along[half:], *wait), "col")
    mine = [own, across, along, far_front, far_back]
    return pack(mine + [swap(piece, "tp") for piece in mine])


def plane_reduce(partial, wait=()):
    def chip_sum(half):
        received = swap(partial(1, half).astype(bf16), "tp")
        total = partial(0, half).astype(f32) + received.astype(f32)
        return total.reshape((4, total.shape[0] // 4, total.shape[1]))

    first = chip_sum(0)
    got = swap(after(jnp.stack([first[1], first[3]]).astype(bf16), *wait), "col").astype(f32)
    second = chip_sum(1)
    got_second = swap(after(second[2:].astype(bf16), *wait), "row").astype(f32)
    last = swap((first[2] + got[1]).astype(bf16), "row").astype(f32)
    last_second = swap((second[1] + got_second[1]).astype(bf16), "col").astype(f32)
    return jnp.concatenate(
        [first[0] + got[0] + last, second[0] + got_second[0] + last_second], axis=1
    )


def line_reduce(blocks, groups, index):
    up = down = None
    for step in range(1, groups):
        out_up = take(blocks, jnp.minimum(index + groups - step, groups - 1))
        out_down = take(blocks, jnp.maximum(index - groups + step, 0))
        if up is not None:
            out_up = (out_up.astype(f32) + up.astype(f32)).astype(bf16)
            out_down = (out_down.astype(f32) + down.astype(f32)).astype(bf16)
        senders = range(min(step, groups - 1))
        up = lax.ppermute(out_up, "group", [(j, j + 1) for j in senders])
        down = lax.ppermute(
            out_down, "group", [(groups - 1 - j, groups - 2 - j) for j in senders]
        )
    return (take(blocks, index).astype(f32) + up.astype(f32) + down.astype(f32)).astype(bf16)


def plane_exchange(make, member):
    own = make(member)
    result = jnp.zeros((4,) + own.shape, own.dtype)
    result = lax.dynamic_update_index_in_dim(result, own, member, 0)
    for distance in (1, 2, 3):
        got = swap_plane(make(member ^ distance), distance)
        result = lax.dynamic_update_index_in_dim(result, got, member ^ distance, 0)
    return result


def rms_inverse(values):
    return lax.rsqrt(jnp.mean(values * values, axis=-1, keepdims=True) + epsilon)


def rope_tables(positions):
    half_size = HS // 2
    indices = jnp.arange(half_size, dtype=f32)
    inverse = theta_base ** (-2.0 * indices / HS)
    angles = positions.astype(f32)[:, None] * inverse[None, :]
    return jnp.cos(angles), jnp.sin(angles)


def rotate(vectors, cos, sin):
    front, back = vectors[:, : HS // 2], vectors[:, HS // 2 :]
    return jnp.concatenate([front * cos - back * sin, back * cos + front * sin], axis=-1)


def unrotate(grads, cos, sin):
    front, back = grads[:, : HS // 2], grads[:, HS // 2 :]
    return jnp.concatenate([front * cos + back * sin, back * cos - front * sin], axis=-1)


def mlp_kernel(width, normed_ref, cot_ref, weight_ref, inner_ref, grads_ref):
    both = product(normed_ref[...], weight_ref[:, : 2 * width])
    d_inner = product(cot_ref[...], weight_ref[:, 2 * width :])
    gate, upward = both[:, :width], both[:, width:]
    sig = 1.0 / (1.0 + jnp.exp(-gate))
    silu = gate * sig
    inner_ref[...] = (silu * upward).astype(bf16)
    d_gate = d_inner * upward * sig * (1.0 + gate * (1.0 - sig))
    grads_ref[...] = jnp.concatenate([d_gate, d_inner * silu], axis=1).astype(bf16)


def mlp_chunk(normed, cot, weight):
    tokens, features = normed.shape
    width = weight.shape[1] // 3
    tile = 256
    return pl.pallas_call(
        functools.partial(mlp_kernel, width),
        grid=(tokens // tile,),
        in_specs=[
            pl.BlockSpec((tile, features), lambda i: (i, 0)),
            pl.BlockSpec((tile, features), lambda i: (i, 0)),
            pl.BlockSpec((features, 3 * width), lambda i: (0, 0)),
        ],
        out_specs=[
            pl.BlockSpec((tile, width), lambda i: (i, 0)),
            pl.BlockSpec((tile, 2 * width), lambda i: (i, 0)),
        ],
        out_shape=[
            jax.ShapeDtypeStruct((tokens, width), bf16),
            jax.ShapeDtypeStruct((tokens, 2 * width), bf16),
        ],
        cost_estimate=pl.CostEstimate(
            flops=6 * tokens * features * width,
            bytes_accessed=2 * features * (2 * tokens + 3 * width),
            transcendentals=tokens * width,
        ),
        compiler_params=pltpu.CompilerParams(vmem_limit_bytes=VMEM_LIMIT),
        name="mlp_chunk",
    )(normed, cot, weight)


def sum_kernel(count, *refs):
    lefts, rights, out_ref = refs[:count], refs[count : 2 * count], refs[-1]
    total = times_transposed(lefts[0][...], rights[0][...])
    for left, right in zip(lefts[1:], rights[1:]):
        total += times_transposed(left[...], right[...])
    for base in refs[2 * count : -1]:
        total += base[...].astype(f32)
    out_ref[...] = total.astype(out_ref.dtype)


def chunk_sum(lefts, rights, column, part, half, dtype, base=()):
    count = len(lefts)
    tokens, width = lefts[0].shape
    features = rights[0].shape[0] // 2
    rows = tokens // 2
    tile = 512
    steps = rows // tile
    return pl.pallas_call(
        functools.partial(sum_kernel, count),
        grid=(steps,),
        in_specs=[pl.BlockSpec((tile, width), lambda i: (part * steps + i, 0))] * count
        + [pl.BlockSpec((features, width), lambda i: (half, column))] * count
        + [pl.BlockSpec((tile, features), lambda i: (i, 0))] * len(base),
        out_specs=pl.BlockSpec((tile, features), lambda i: (i, 0)),
        out_shape=jax.ShapeDtypeStruct((rows, features), dtype),
        cost_estimate=pl.CostEstimate(
            flops=2 * rows * features * width * count,
            bytes_accessed=2 * count * width * (rows + features) + 4 * rows * features,
            transcendentals=0,
        ),
        compiler_params=pltpu.CompilerParams(vmem_limit_bytes=VMEM_LIMIT),
        name="chunk_sum",
    )(*lefts, *rights, *base)


def grads_kernel(first_ref, second_ref, right_ref, other_ref, out_ref):
    width = right_ref.shape[1]
    out_ref[:, :width] = outer_sum(first_ref[...], right_ref[...]).astype(bf16)
    out_ref[:, width:] = outer_sum(second_ref[...], other_ref[...]).astype(bf16)


def weight_grads(first, second, right, other):
    tokens, features = first.shape
    width, rest = right.shape[1], other.shape[1]
    tile = 256
    return pl.pallas_call(
        grads_kernel,
        grid=(features // tile,),
        in_specs=[
            pl.BlockSpec((tokens, tile), lambda i: (0, i)),
            pl.BlockSpec((tokens, tile), lambda i: (0, i)),
            pl.BlockSpec((tokens, width), lambda i: (0, 0)),
            pl.BlockSpec((tokens, rest), lambda i: (0, 0)),
        ],
        out_specs=pl.BlockSpec((tile, width + rest), lambda i: (i, 0)),
        out_shape=jax.ShapeDtypeStruct((features, width + rest), bf16),
        cost_estimate=pl.CostEstimate(
            flops=2 * tokens * features * (width + rest),
            bytes_accessed=2 * (2 * tokens * features + (width + rest) * (tokens + features)),
            transcendentals=0,
        ),
        compiler_params=pltpu.CompilerParams(vmem_limit_bytes=VMEM_LIMIT),
        name="weight_grads",
    )(first, second, right, other)


def project_kernel(place_ref, normed_ref, weight_ref, cos_ref, sin_ref, q_ref, k_ref, v_ref):
    step = pl.program_id(0)
    cos, sin = cos_ref[...], sin_ref[...]
    qkv = product(normed_ref[...], weight_ref[...])
    query = rotate(qkv[:, :HS], cos, sin).astype(bf16) * HS ** (-0.5)
    keys = rotate(qkv[:, HS : 2 * HS], cos, sin).astype(bf16)
    vals = qkv[:, 2 * HS :].astype(bf16)
    blocks = normed_ref.shape[0] // BLOCK
    for b in range(blocks):
        rows = pl.ds(pl.multiple_of(place_ref[step * blocks + b] * BLOCK, BLOCK), BLOCK)
        part = slice(b * BLOCK, (b + 1) * BLOCK)
        q_ref[rows, :] = query[part]
        k_ref[rows, :] = keys[part]
        v_ref[rows, :] = vals[part]


def project(place, normed, weight, cos, sin):
    tokens, features = normed.shape
    tile = 256
    whole = pl.BlockSpec((tokens, HS), lambda i, place: (0, 0))
    return pl.pallas_call(
        project_kernel,
        grid_spec=pltpu.PrefetchScalarGridSpec(
            num_scalar_prefetch=1,
            grid=(tokens // tile,),
            in_specs=[
                pl.BlockSpec((tile, features), lambda i, place: (i, 0)),
                pl.BlockSpec((features, 3 * HS), lambda i, place: (0, 0)),
                pl.BlockSpec((tile, HS // 2), lambda i, place: (i, 0)),
                pl.BlockSpec((tile, HS // 2), lambda i, place: (i, 0)),
            ],
            out_specs=[whole] * 3,
        ),
        out_shape=[jax.ShapeDtypeStruct((tokens, HS), bf16)] * 3,
        cost_estimate=pl.CostEstimate(
            flops=6 * tokens * features * HS,
            bytes_accessed=2 * features * (tokens + 3 * HS) + 10 * tokens * HS,
            transcendentals=0,
        ),
        compiler_params=pltpu.CompilerParams(vmem_limit_bytes=VMEM_LIMIT),
        name="project",
    )(place, normed, weight, cos, sin)


TILE = 256


def tile_masks():
    rows = lax.broadcasted_iota(jnp.int32, (TILE, TILE), 0)
    cols = lax.broadcasted_iota(jnp.int32, (TILE, TILE), 1)
    causal = rows >= cols
    return causal, causal & (rows // BLOCK == cols // BLOCK)


def block_rows(order_ref, index):
    return pl.ds(pl.multiple_of(order_ref[index] * BLOCK, BLOCK), BLOCK)


def forward_kernel(order_ref, q_ref, k_ref, v_ref, mixed_ref, lse_ref, peak_ref):
    causal, inside = tile_masks()
    prompt = GROUP // 2
    top = jnp.full((TILE, 1), masked_value, f32)
    for i in range(GROUP // TILE):
        rows = slice(i * TILE, (i + 1) * TILE)
        past = min(i * TILE, prompt)
        query = q_ref[rows, :]
        near = times_transposed(query, k_ref[rows, :])
        near = jnp.where(causal if i * TILE < prompt else inside, near, masked_value)
        peak = jnp.max(near, axis=1, keepdims=True)
        if past:
            far = times_transposed(query, k_ref[:past, :])
            peak = jnp.maximum(peak, jnp.max(far, axis=1, keepdims=True))
            far = jnp.exp(far - peak)
        near = jnp.exp(near - peak)
        total = jnp.sum(near, axis=1, keepdims=True)
        if past:
            total += jnp.sum(far, axis=1, keepdims=True)
        share = 1.0 / total
        mixed = product((near * share).astype(bf16), v_ref[rows, :])
        if past:
            mixed += product((far * share).astype(bf16), v_ref[:past, :])
        mixed = mixed.astype(bf16)
        for b in range(TILE // BLOCK):
            mixed_ref[block_rows(order_ref, i * (TILE // BLOCK) + b), :] = mixed[
                b * BLOCK : (b + 1) * BLOCK
            ]
        lse_ref[rows, :] = peak + jnp.log(total)
        top = jnp.maximum(top, peak)
    peak_ref[...] = jnp.full(peak_ref.shape, jnp.max(top), f32)


def attention_forward(order, query, keys, vals):
    whole = pl.BlockSpec(memory_space=pltpu.VMEM)
    return pl.pallas_call(
        forward_kernel,
        in_specs=[pl.BlockSpec(memory_space=pltpu.SMEM), whole, whole, whole],
        out_specs=[whole] * 3,
        out_shape=[
            jax.ShapeDtypeStruct((GROUP, HS), bf16),
            jax.ShapeDtypeStruct((GROUP, 1), f32),
            jax.ShapeDtypeStruct((8, 128), f32),
        ],
        cost_estimate=pl.CostEstimate(
            flops=2 * GROUP * GROUP * HS,
            bytes_accessed=8 * GROUP * HS,
            transcendentals=GROUP * GROUP // 2,
        ),
        compiler_params=pltpu.CompilerParams(vmem_limit_bytes=VMEM_LIMIT),
        name="attention_forward",
    )(order, query, keys, vals)


def backward_kernel(
    order_ref, q_ref, k_ref, v_ref, lse_ref, mixed_ref, cos_ref, sin_ref, out_ref, dk_ref, dv_ref
):
    causal, inside = tile_masks()
    prompt = GROUP // 2
    blocks = TILE // BLOCK

    def back(grad, index):
        rows = block_rows(order_ref, index)
        return rows, unrotate(grad, cos_ref[rows, :], sin_ref[rows, :]).astype(bf16)

    for i in range(GROUP // TILE):
        rows = slice(i * TILE, (i + 1) * TILE)
        past = min(i * TILE, prompt)
        query, lse = q_ref[rows, :], lse_ref[rows, :]
        d_mixed = jnp.concatenate(
            [mixed_ref[block_rows(order_ref, i * blocks + b), :] for b in range(blocks)], axis=0
        )
        near = times_transposed(query, k_ref[rows, :])
        near = jnp.where(causal if i * TILE < prompt else inside, near, masked_value)
        near = jnp.exp(near - lse)
        d_near = times_transposed(d_mixed, v_ref[rows, :])
        inner = jnp.sum(near * d_near, axis=1, keepdims=True)
        if past:
            far = jnp.exp(times_transposed(query, k_ref[:past, :]) - lse)
            d_far = times_transposed(d_mixed, v_ref[:past, :])
            inner += jnp.sum(far * d_far, axis=1, keepdims=True)
        d_near = (near * (d_near - inner)).astype(bf16)
        d_query = product(d_near, k_ref[rows, :])
        dk_ref[rows, :] = outer_sum(d_near, query)
        dv_ref[rows, :] = outer_sum(near.astype(bf16), d_mixed)
        if past:
            d_far = (far * (d_far - inner)).astype(bf16)
            d_query += product(d_far, k_ref[:past, :])
            dk_ref[:past, :] += outer_sum(d_far, query)
            dv_ref[:past, :] += outer_sum(far.astype(bf16), d_mixed)
        d_query = d_query * HS ** (-0.5)
        for b in range(blocks):
            where, grad = back(d_query[b * BLOCK : (b + 1) * BLOCK], i * blocks + b)
            out_ref[where, :HS] = grad
    for c in range(GROUP // BLOCK):
        part = slice(c * BLOCK, (c + 1) * BLOCK)
        where, grad = back(dk_ref[part, :], c)
        out_ref[where, HS : 2 * HS] = grad
        out_ref[where, 2 * HS :] = dv_ref[part, :].astype(bf16)


def attention_backward(order, query, keys, vals, lse, d_mixed, cos, sin):
    whole = pl.BlockSpec(memory_space=pltpu.VMEM)
    return pl.pallas_call(
        backward_kernel,
        in_specs=[pl.BlockSpec(memory_space=pltpu.SMEM)] + [whole] * 7,
        out_specs=whole,
        out_shape=jax.ShapeDtypeStruct((GROUP, 3 * HS), bf16),
        scratch_shapes=[pltpu.VMEM((GROUP, HS), f32), pltpu.VMEM((GROUP, HS), f32)],
        cost_estimate=pl.CostEstimate(
            flops=5 * GROUP * GROUP * HS,
            bytes_accessed=20 * GROUP * HS,
            transcendentals=GROUP * GROUP // 2,
        ),
        compiler_params=pltpu.CompilerParams(vmem_limit_bytes=VMEM_LIMIT),
        name="attention_backward",
    )(order, query, keys, vals, lse, d_mixed, cos, sin)


def local(
    tokens,
    cotangent,
    segment,
    position,
    clip_limit,
    attn_gain,
    query_weight,
    key_weight,
    value_weight,
    output_weight,
    mlp_gain,
    gate_weight,
    up_weight,
    down_weight,
):
    groups = lax.axis_size("group")
    group = lax.axis_index("group")
    core = lax.axis_index("tp")
    member = lax.axis_index(PLANE)
    token_rows = tokens.shape[0]
    own_rows, features = query_weight.shape[0], tokens.shape[1]
    width = gate_weight.shape[1] // 4 // CHUNKS

    def own_order(array):
        parts = []
        for j in range(2):
            for k in range(4):
                start = group * GROUP + (member ^ k) * (2 * token_rows) + (core ^ j) * token_rows
                parts.append(lax.dynamic_slice_in_dim(array, start, token_rows))
        return jnp.concatenate(parts)

    def columns(array, start, count):
        return lax.dynamic_slice_in_dim(array, start, count, 1)

    def exchange(make):
        blocks = plane_exchange(make, member)
        return blocks.reshape(4 * own_rows, blocks.shape[-1])

    def collect(blocks):
        return lax.all_gather(blocks, "group", axis=0, tiled=True)

    def attention_block(m):
        return jnp.concatenate(
            [
                columns(query_weight, m * HS, HS),
                columns(key_weight, m // 2 * HS, HS),
                columns(value_weight, m // 2 * HS, HS),
                columns(output_weight, m * HS, HS),
            ],
            axis=1,
        )

    def mlp_blocks(chunk, waits):
        weights = [after(a, *waits) for a in (gate_weight, up_weight, down_weight)]

        def block(m):
            start = (m * CHUNKS + chunk) * width
            return jnp.concatenate([columns(a, start, width) for a in weights], axis=1)

        return exchange(block)

    index = lax.axis_index(FSDP)
    gains = jnp.stack([attn_gain, mlp_gain])[:, None, :]
    gains = jnp.where(jnp.arange(4 * groups)[None, :, None] == index, gains, 0)
    gains = combine_all(gains, groups, lambda a, b: a + b).reshape(2, features)
    attn_blocks = exchange(attention_block)
    attn_weights = collect(attn_blocks)
    late_tokens = after(tokens, attn_blocks)
    neighbours = plane_neighbours(late_tokens)
    tokens_all = plane_gather(late_tokens, neighbours, (gains,))
    chunk_blocks = [mlp_blocks(0, neighbours)]
    cot_all = plane_gather(after(cotangent, chunk_blocks[0], tokens_all))
    for n in range(1, CHUNKS):
        chunk_blocks.append(mlp_blocks(n, (cot_all,)))
    mlp_weights = [collect(blocks) for blocks in chunk_blocks]
    gain_attn, gain_mlp = gains[0].astype(f32), gains[1].astype(f32)

    tokens_f = tokens.astype(f32)
    all_f = tokens_all.astype(f32)
    normed_all = (all_f * rms_inverse(all_f) * gain_attn).astype(bf16)
    inverse_attn = rms_inverse(tokens_f)
    unit_attn = tokens_f * inverse_attn
    seg, pos = own_order(segment), own_order(position)
    cos, sin = rope_tables(pos)
    seg_blocks, pos_blocks = seg[::BLOCK], pos[::BLOCK]
    half_blocks = GROUP // BLOCK // 2
    place = jnp.where(seg_blocks == 0, pos_blocks // BLOCK, half_blocks - 1 + seg_blocks)
    labels = jnp.arange(2 * half_blocks, dtype=jnp.int32)
    order = jnp.sum(jnp.where(place[None, :] == labels[:, None], labels[None, :], 0), axis=1)
    query, keys, vals = project(place, normed_all, attn_weights, cos, sin)
    mixed, logsum, peak = attention_forward(order, query, keys, vals)

    head_top = jnp.where(jnp.arange(4) == member, peak[0, :4], masked_value)
    head_top = combine_all(head_top, groups, jnp.maximum)

    def projected(left, column):
        return lambda j, h: chunk_sum([left], [attn_weights], column, j, h, bf16 if j else f32)

    attn_out = plane_reduce(projected(mixed, 3))
    hidden = tokens_f + attn_out
    inverse_mlp = rms_inverse(hidden)
    unit_mlp = hidden * inverse_mlp
    normed_mlp = plane_gather((unit_mlp * gain_mlp).astype(bf16))

    inners, d_boths = [], []
    for n in range(CHUNKS):
        inner, d_both = mlp_chunk(normed_mlp, cot_all, mlp_weights[n])
        inners.append(inner)
        d_boths.append(d_both)
    parts = [(j, h) for h in range(2) for j in (1, 0)]
    early = {
        (j, h): chunk_sum(d_boths[:-1], mlp_weights[:-1], 0, j, h, f32) for j, h in parts
    }
    sums = {
        (j, h): chunk_sum(
            d_boths[-1:], mlp_weights[-1:], 0, j, h, bf16 if j else f32, (early[j, h],)
        )
        for j, h in parts
    }
    d_normed = plane_reduce(lambda j, h: sums[j, h])
    cot_f = cotangent.astype(f32)
    scaled = d_normed * gain_mlp
    d_hidden = cot_f + inverse_mlp * (
        scaled - unit_mlp * jnp.mean(scaled * unit_mlp, axis=-1, keepdims=True)
    )
    d_attn_all = plane_gather(d_hidden.astype(bf16))

    def line_sum(partial):
        return lax.psum_scatter(partial, "group", scatter_dimension=0, tiled=True)

    def send_grads(reduced):
        reduced = reduced.reshape(4, own_rows, reduced.shape[1])
        return plane_exchange(lambda m: take(reduced, m), member)

    chunk_grads = []
    for n in range(CHUNKS):
        last = n == CHUNKS - 1
        inner = after(inners[n], *sums.values()) if last else inners[n]
        grads = weight_grads(normed_mlp, cot_all, d_boths[n], inner)
        if last:
            chunk_grads.append(line_sum(grads))
        else:
            blocks = grads.reshape(groups, 4 * own_rows, grads.shape[1])
            chunk_grads.append(line_reduce(blocks, groups, group))
    late_inners = [after(inner, *sums.values()) for inner in inners]
    block_out = (
        hidden
        + plane_reduce(
            lambda j, h: chunk_sum(late_inners, mlp_weights, 2, j, h, bf16 if j else f32),
            (d_attn_all,),
        )
    ).astype(bf16)

    d_mixed = product(d_attn_all, attn_weights[:, 3 * HS :]).astype(bf16)
    d_qkv = attention_backward(order, query, keys, vals, logsum, d_mixed, cos, sin)
    attn_sum = line_sum(weight_grads(normed_all, d_attn_all, d_qkv, mixed))
    d_normed = plane_reduce(projected(d_qkv, 0))
    scaled = d_normed * gain_attn
    tokens_grad = d_hidden + inverse_attn * (
        scaled - unit_attn * jnp.mean(scaled * unit_attn, axis=-1, keepdims=True)
    )

    mlp_parts = [send_grads(after(reduced, d_attn_all)) for reduced in chunk_grads[:-1]]
    mlp_parts.append(send_grads(after(chunk_grads[-1], d_normed)))
    attn_grads = send_grads(attn_sum)

    def wide(grads, start, count):
        part = grads[:, :, start : start + count].astype(f32)
        return part.transpose(1, 0, 2).reshape(own_rows, 4 * count)

    def paired(grads, start):
        part = grads[:, :, start : start + HS].astype(f32).reshape(2, 2, own_rows, HS)
        return jnp.sum(part, axis=1).transpose(1, 0, 2).reshape(own_rows, 2 * HS)

    def chunked(parts, start):
        part = jnp.stack([g[:, :, start : start + width] for g in parts], axis=1).astype(f32)
        return part.transpose(2, 0, 1, 3).reshape(own_rows, 4 * CHUNKS * width)

    query_grad = wide(attn_grads, 0, HS)
    key_grad = paired(attn_grads, HS)
    value_grad = paired(attn_grads, 2 * HS)
    output_grad = wide(attn_grads, 3 * HS, HS)
    gate_grad = chunked(mlp_parts, 0)
    up_grad = chunked(mlp_parts, width)
    down_grad = chunked(mlp_parts, 2 * width)

    def gain_sum(weight, grad):
        return jnp.sum(weight.astype(f32) * grad, axis=1)

    gain_grads = jnp.stack(
        [
            gain_sum(query_weight, query_grad)
            + gain_sum(key_weight, key_grad)
            + gain_sum(value_weight, value_grad),
            gain_sum(gate_weight, gate_grad) + gain_sum(up_weight, up_grad),
        ]
    )
    gain_grads = gain_grads + swap(gain_grads, "tp")
    attn_gain_grad = gain_grads[0] / attn_gain.astype(f32)
    mlp_gain_grad = gain_grads[1] / mlp_gain.astype(f32)

    factor = clip_limit / jnp.maximum(head_top, clip_limit)
    query_scale = jnp.repeat(jnp.sqrt(factor), HS)
    key_factor = jnp.min(factor.reshape(2, 2), axis=1)
    key_scale = jnp.repeat(jnp.sqrt(key_factor), HS)
    query_clipped = (query_weight.astype(f32) * query_scale[None, :]).astype(bf16)
    key_clipped = (key_weight.astype(f32) * key_scale[None, :]).astype(bf16)
    return (
        block_out,
        tokens_grad,
        attn_gain_grad,
        query_grad,
        key_grad,
        value_grad,
        output_grad,
        mlp_gain_grad,
        gate_grad,
        up_grad,
        down_grad,
        head_top,
        query_clipped,
        key_clipped,
    )


def solution(mesh):
    shape = (mesh.shape["fsdp"] // 4, 2, 2, mesh.shape["tp"])
    fine = Mesh(mesh.devices.reshape(shape), ("group", "row", "col", "tp"))
    rows = P(("group", "row", "col", "tp"), None)
    weight = P(FSDP, "tp")
    gain = P(FSDP)
    heads = P("tp")
    return jax.shard_map(
        local,
        mesh=fine,
        in_specs=(
            rows, rows, P(), P(), heads, gain, weight, weight, weight, weight,
            gain, weight, weight, weight,
        ),
        out_specs=(
            rows, rows, gain, weight, weight, weight, weight, gain, weight, weight, weight,
            heads, weight, weight,
        ),
        check_vma=False,
    )
```

```python
import functools

import jax
import jax.numpy as jnp
from jax import lax
from jax.experimental import pallas as pl
from jax.experimental.pallas import tpu as pltpu
from jax.sharding import Mesh, PartitionSpec as P

HS = 256
GROUP = 2048
SIXTEENTHS = (10, 6)
BLOCK = 128

epsilon = 1e-05
theta_base = 1000042.0
masked_value = -1e30

bf16 = jnp.bfloat16
f32 = jnp.float32
PLANE = ("row", "col")
FSDP = ("group", "row", "col")
VMEM_LIMIT = 48 * 1024 * 1024


def product(left, right):
    return jnp.dot(left, right, preferred_element_type=f32)


def times_transposed(left, right):
    return lax.dot_general(left, right, (((1,), (1,)), ((), ())), preferred_element_type=f32)


def outer_sum(left, right):
    return lax.dot_general(left, right, (((0,), (0,)), ((), ())), preferred_element_type=f32)


def take(array, index, axis=0):
    return lax.dynamic_index_in_dim(array, index, axis, keepdims=False)


def swap(block, axis):
    return lax.ppermute(block, axis, [(0, 1), (1, 0)])


def swap_plane(block, distance):
    return lax.ppermute(block, PLANE, [(i, i ^ distance) for i in range(4)])


def after(value, *others):
    return lax.optimization_barrier((value,) + others)[0]


def combine_all(values, groups, combine):
    distance = 1
    while distance < 4 * groups:
        route = [(i, i ^ distance) for i in range(4 * groups)]
        values = combine(values, lax.ppermute(values, FSDP, route))
        distance *= 2
    return values


def pack_kernel(count, *refs):
    out_ref, sems = refs[count], refs[count + 1]
    copies, start = [], 0
    for i in range(count):
        rows = refs[i].shape[0]
        copy = pltpu.make_async_copy(refs[i], out_ref.at[pl.ds(start, rows)], sems.at[i])
        copy.start()
        copies.append(copy)
        start += rows
    for copy in copies:
        copy.wait()


def pack(pieces):
    rows, width = sum(p.shape[0] for p in pieces), pieces[0].shape[1]
    count = len(pieces)
    return pl.pallas_call(
        functools.partial(pack_kernel, count),
        in_specs=[pl.BlockSpec(memory_space=pl.ANY)] * count,
        out_specs=pl.BlockSpec(memory_space=pltpu.VMEM),
        out_shape=jax.ShapeDtypeStruct((rows, width), pieces[0].dtype),
        scratch_shapes=[pltpu.SemaphoreType.DMA((count,))],
        cost_estimate=pl.CostEstimate(
            flops=0, bytes_accessed=4 * rows * width, transcendentals=0
        ),
        compiler_params=pltpu.CompilerParams(vmem_limit_bytes=VMEM_LIMIT),
        name="pack",
    )(*pieces)


def plane_neighbours(own):
    return swap(own, "col"), swap(own, "row")


def plane_pieces(own, neighbours=None, wait=()):
    half = own.shape[0] // 2
    across, along = neighbours or plane_neighbours(own)
    far_front = swap(after(across[:half], *wait), "row")
    far_back = swap(after(along[half:], *wait), "col")
    mine = [own, across, along, far_front, far_back]
    return mine + [swap(piece, "tp") for piece in mine]


def plane_reduce(partial, wait=()):
    def chip_sum(half):
        received = swap(partial(1, half).astype(bf16), "tp")
        total = partial(0, half).astype(f32) + received.astype(f32)
        return total.reshape((4, total.shape[0] // 4, total.shape[1]))

    first = chip_sum(0)
    arrived = swap(after(jnp.stack([first[1], first[3]]).astype(bf16), *wait), "col")
    second = chip_sum(1)
    arrived_second = swap(after(second[2:].astype(bf16), *wait), "row")
    got, got_second = arrived.astype(f32), arrived_second.astype(f32)
    last = swap((first[2] + got[1]).astype(bf16), "row").astype(f32)
    last_second = swap((second[1] + got_second[1]).astype(bf16), "col").astype(f32)
    total = jnp.concatenate(
        [first[0] + got[0] + last, second[0] + got_second[0] + last_second], axis=1
    )
    return total, (arrived, arrived_second)


def line_reduce(blocks, groups, index):
    up = down = None
    for step in range(1, groups):
        out_up = take(blocks, jnp.minimum(index + groups - step, groups - 1))
        out_down = take(blocks, jnp.maximum(index - groups + step, 0))
        if up is not None:
            out_up = (out_up.astype(f32) + up.astype(f32)).astype(bf16)
            out_down = (out_down.astype(f32) + down.astype(f32)).astype(bf16)
        senders = range(min(step, groups - 1))
        up = lax.ppermute(out_up, "group", [(j, j + 1) for j in senders])
        down = lax.ppermute(
            out_down, "group", [(groups - 1 - j, groups - 2 - j) for j in senders]
        )
    return (take(blocks, index).astype(f32) + up.astype(f32) + down.astype(f32)).astype(bf16)


def split_kernel(spans, member_ref, *refs):
    sources, outs = refs[: len(spans)], refs[len(spans) :]
    for k in range(4):
        target = member_ref[0] ^ k
        column = 0
        for source, (offset, stride, width, shift) in zip(sources, spans):
            start = pl.multiple_of((target >> shift) * stride + offset, 128)
            outs[k][:, column : column + width] = source[:, pl.ds(start, width)]
            column += width


def split(member, sources, spans):
    rows, width = sources[0].shape[0], sum(span[2] for span in spans)
    whole = pl.BlockSpec(memory_space=pltpu.VMEM)
    return pl.pallas_call(
        functools.partial(split_kernel, spans),
        in_specs=[pl.BlockSpec(memory_space=pltpu.SMEM)] + [whole] * len(sources),
        out_specs=[whole] * 4,
        out_shape=[jax.ShapeDtypeStruct((rows, width), bf16)] * 4,
        cost_estimate=pl.CostEstimate(
            flops=0, bytes_accessed=16 * rows * width, transcendentals=0
        ),
        compiler_params=pltpu.CompilerParams(vmem_limit_bytes=VMEM_LIMIT),
        name="split",
    )(member, *sources)


def place_kernel(member_ref, *refs):
    rows = refs[0].shape[0]
    for k in range(4):
        start = pl.multiple_of((member_ref[0] ^ k) * rows, rows)
        refs[4][pl.ds(start, rows), :] = refs[k][...]


def place_rows(member, pieces):
    rows, width = pieces[0].shape
    whole = pl.BlockSpec(memory_space=pltpu.VMEM)
    return pl.pallas_call(
        place_kernel,
        in_specs=[pl.BlockSpec(memory_space=pltpu.SMEM)] + [whole] * 4,
        out_specs=whole,
        out_shape=jax.ShapeDtypeStruct((4 * rows, width), bf16),
        cost_estimate=pl.CostEstimate(
            flops=0, bytes_accessed=16 * rows * width, transcendentals=0
        ),
        compiler_params=pltpu.CompilerParams(vmem_limit_bytes=VMEM_LIMIT),
        name="place_rows",
    )(member, *pieces)


def pick_kernel(member_ref, source_ref, *outs):
    rows = outs[0].shape[0]
    for k in range(4):
        start = pl.multiple_of((member_ref[0] ^ k) * rows, rows)
        outs[k][...] = source_ref[pl.ds(start, rows), :]


def pick_rows(member, source):
    rows, width = source.shape[0] // 4, source.shape[1]
    whole = pl.BlockSpec(memory_space=pltpu.VMEM)
    return pl.pallas_call(
        pick_kernel,
        in_specs=[pl.BlockSpec(memory_space=pltpu.SMEM), whole],
        out_specs=[whole] * 4,
        out_shape=[jax.ShapeDtypeStruct((rows, width), bf16)] * 4,
        cost_estimate=pl.CostEstimate(
            flops=0, bytes_accessed=16 * rows * width, transcendentals=0
        ),
        compiler_params=pltpu.CompilerParams(vmem_limit_bytes=VMEM_LIMIT),
        name="pick_rows",
    )(member, source)


def swap_all(pieces):
    return [pieces[0]] + [swap_plane(pieces[k], k) for k in (1, 2, 3)]


def mlp_final_kernel(chunks, stride, member_ref, gate_w_ref, up_w_ref, *refs):
    pieces, outs, gain_ref = refs[:-4], refs[-4:-1], refs[-1]
    for n, (offset, width) in enumerate(chunks):
        for k in range(4):
            column = pl.multiple_of((member_ref[0] ^ k) * stride + offset, 128)
            for i in range(3):
                part = pieces[4 * n + k][:, i * width : (i + 1) * width]
                outs[i][:, pl.ds(column, width)] = part.astype(f32)
    gain_ref[...] = jnp.sum(
        gate_w_ref[...].astype(f32) * outs[0][...] + up_w_ref[...].astype(f32) * outs[1][...],
        axis=1,
        keepdims=True,
    )


def mlp_final(member, gate_weight, up_weight, chunks, parts):
    rows, hidden = gate_weight.shape
    pieces = [piece for part in parts for piece in part]
    whole = pl.BlockSpec(memory_space=pltpu.VMEM)
    return pl.pallas_call(
        functools.partial(mlp_final_kernel, chunks, hidden // 4),
        in_specs=[pl.BlockSpec(memory_space=pltpu.SMEM)] + [whole] * (2 + len(pieces)),
        out_specs=[whole] * 4,
        out_shape=[jax.ShapeDtypeStruct((rows, hidden), f32)] * 3
        + [jax.ShapeDtypeStruct((rows, 1), f32)],
        cost_estimate=pl.CostEstimate(
            flops=4 * rows * hidden, bytes_accessed=22 * rows * hidden, transcendentals=0
        ),
        compiler_params=pltpu.CompilerParams(vmem_limit_bytes=VMEM_LIMIT),
        name="mlp_final",
    )(member, gate_weight, up_weight, *pieces)


def attention_final_kernel(member_ref, qw_ref, kw_ref, vw_ref, *refs):
    qkv, out = refs[:4], refs[4:8]
    q_ref, k_ref, v_ref, o_ref, gain_ref = refs[8:]
    member = member_ref[0]
    for k in range(4):
        columns = pl.ds(pl.multiple_of((member ^ k) * HS, HS), HS)
        q_ref[:, columns] = qkv[k][:, :HS].astype(f32)
        o_ref[:, columns] = out[k][...].astype(f32)
    for h in range(2):
        columns = pl.ds(pl.multiple_of(((member >> 1) ^ h) * HS, HS), HS)
        both = qkv[2 * h][:, HS:].astype(f32) + qkv[2 * h + 1][:, HS:].astype(f32)
        k_ref[:, columns] = both[:, :HS]
        v_ref[:, columns] = both[:, HS:]

    def row_sum(weight_ref, grad_ref):
        return jnp.sum(weight_ref[...].astype(f32) * grad_ref[...], axis=1, keepdims=True)

    gain_ref[...] = row_sum(qw_ref, q_ref) + row_sum(kw_ref, k_ref) + row_sum(vw_ref, v_ref)


def attention_final(member, query_weight, key_weight, value_weight, qkv, out):
    rows, width = query_weight.shape
    whole = pl.BlockSpec(memory_space=pltpu.VMEM)
    shapes = [width, width // 2, width // 2, width, 1]
    return pl.pallas_call(
        attention_final_kernel,
        in_specs=[pl.BlockSpec(memory_space=pltpu.SMEM)] + [whole] * 11,
        out_specs=[whole] * 5,
        out_shape=[jax.ShapeDtypeStruct((rows, n), f32) for n in shapes],
        cost_estimate=pl.CostEstimate(
            flops=4 * rows * width, bytes_accessed=24 * rows * width, transcendentals=0
        ),
        compiler_params=pltpu.CompilerParams(vmem_limit_bytes=VMEM_LIMIT),
        name="attention_final",
    )(member, query_weight, key_weight, value_weight, *qkv, *out)


def rms_inverse(values):
    return lax.rsqrt(jnp.mean(values * values, axis=-1, keepdims=True) + epsilon)


def rope_tables(positions):
    half_size = HS // 2
    indices = jnp.arange(half_size, dtype=f32)
    inverse = theta_base ** (-2.0 * indices / HS)
    angles = positions.astype(f32)[:, None] * inverse[None, :]
    return jnp.cos(angles), jnp.sin(angles)


def rotate(vectors, cos, sin):
    front, back = vectors[:, : HS // 2], vectors[:, HS // 2 :]
    return jnp.concatenate([front * cos - back * sin, back * cos + front * sin], axis=-1)


def unrotate(grads, cos, sin):
    front, back = grads[:, : HS // 2], grads[:, HS // 2 :]
    return jnp.concatenate([front * cos + back * sin, back * cos - front * sin], axis=-1)


def mlp_tile(width, normed, cot, weight_ref):
    both = product(normed, weight_ref[:, : 2 * width])
    d_inner = product(cot, weight_ref[:, 2 * width :])
    gate, upward = both[:, :width], both[:, width:]
    sig = 1.0 / (1.0 + jnp.exp(-gate))
    silu = gate * sig
    d_gate = d_inner * upward * sig * (1.0 + gate * (1.0 - sig))
    return (
        (silu * upward).astype(bf16),
        jnp.concatenate([d_gate, d_inner * silu], axis=1).astype(bf16),
    )


def mlp_kernel(width, normed_ref, cot_ref, weight_ref, inner_ref, grads_ref):
    inner_ref[...], grads_ref[...] = mlp_tile(
        width, normed_ref[...], cot_ref[...], weight_ref
    )


def tail_kernel(width, normed_ref, cot_ref, weight_ref, base_ref, *refs):
    inner_ref, grads_ref, front_ref, back_ref = refs[-4:]
    inner, grads = mlp_tile(width, normed_ref[...], cot_ref[...], weight_ref)
    inner_ref[...], grads_ref[...] = inner, grads
    total = times_transposed(grads, weight_ref[:, : 2 * width]) + base_ref[...]
    half = total.shape[1] // 2
    front_ref[...] = total[:, :half].astype(front_ref.dtype)
    back_ref[...] = total[:, half:].astype(back_ref.dtype)


def mlp_tail(normed, cot, weight, base, part, dtype, chained=()):
    tokens, features = normed.shape
    width = weight.shape[1] // 3
    tile, rows = 256, tokens // 2
    steps = rows // tile
    count = len(chained)
    return pl.pallas_call(
        functools.partial(tail_kernel, width),
        grid=(steps,),
        in_specs=[
            pl.BlockSpec((tile, features), lambda i: (part * steps + i, 0)),
            pl.BlockSpec((tile, features), lambda i: (part * steps + i, 0)),
            pl.BlockSpec((features, 3 * width), lambda i: (0, 0)),
            pl.BlockSpec((tile, features), lambda i: (i, 0)),
        ]
        + [pl.BlockSpec(memory_space=pl.ANY)] * count,
        out_specs=[
            pl.BlockSpec((tile, width), lambda i: (part * steps + i, 0)),
            pl.BlockSpec((tile, 2 * width), lambda i: (part * steps + i, 0)),
            pl.BlockSpec((tile, features // 2), lambda i: (i, 0)),
            pl.BlockSpec((tile, features // 2), lambda i: (i, 0)),
        ],
        out_shape=[
            jax.ShapeDtypeStruct((tokens, width), bf16),
            jax.ShapeDtypeStruct((tokens, 2 * width), bf16),
            jax.ShapeDtypeStruct((rows, features // 2), dtype),
            jax.ShapeDtypeStruct((rows, features // 2), dtype),
        ],
        input_output_aliases={4 + i: i for i in range(count)},
        cost_estimate=pl.CostEstimate(
            flops=10 * rows * features * width,
            bytes_accessed=2 * features * (5 * rows + 3 * width),
            transcendentals=rows * width,
        ),
        compiler_params=pltpu.CompilerParams(vmem_limit_bytes=VMEM_LIMIT),
        name="mlp_tail",
    )(normed, cot, weight, base, *chained)


def mlp_chunk(normed, cot, weight):
    tokens, features = normed.shape
    width = weight.shape[1] // 3
    tile = 256
    return pl.pallas_call(
        functools.partial(mlp_kernel, width),
        grid=(tokens // tile,),
        in_specs=[
            pl.BlockSpec((tile, features), lambda i: (i, 0)),
            pl.BlockSpec((tile, features), lambda i: (i, 0)),
            pl.BlockSpec((features, 3 * width), lambda i: (0, 0)),
        ],
        out_specs=[
            pl.BlockSpec((tile, width), lambda i: (i, 0)),
            pl.BlockSpec((tile, 2 * width), lambda i: (i, 0)),
        ],
        out_shape=[
            jax.ShapeDtypeStruct((tokens, width), bf16),
            jax.ShapeDtypeStruct((tokens, 2 * width), bf16),
        ],
        cost_estimate=pl.CostEstimate(
            flops=6 * tokens * features * width,
            bytes_accessed=2 * features * (2 * tokens + 3 * width),
            transcendentals=tokens * width,
        ),
        compiler_params=pltpu.CompilerParams(vmem_limit_bytes=VMEM_LIMIT),
        name="mlp_chunk",
    )(normed, cot, weight)


def sum_kernel(count, *refs):
    lefts, rights, out_ref = refs[:count], refs[count : 2 * count], refs[-1]
    total = times_transposed(lefts[0][...], rights[0][...])
    for left, right in zip(lefts[1:], rights[1:]):
        total += times_transposed(left[...], right[...])
    for base in refs[2 * count : -1]:
        total += base[...].astype(f32)
    out_ref[...] = total.astype(out_ref.dtype)


def chunk_sum(lefts, rights, column, part, half, dtype):
    count = len(lefts)
    tokens, features = lefts[0].shape[0], rights[0].shape[0]
    widths = [left.shape[1] for left in lefts]
    rows = tokens // 2
    tile = 256
    if half is not None:
        features, tile = features // 2, 512
    steps = rows // tile
    block = half or 0
    return pl.pallas_call(
        functools.partial(sum_kernel, count),
        grid=(steps,),
        in_specs=[pl.BlockSpec((tile, w), lambda i: (part * steps + i, 0)) for w in widths]
        + [pl.BlockSpec((features, w), lambda i: (block, column)) for w in widths],
        out_specs=pl.BlockSpec((tile, features), lambda i: (i, 0)),
        out_shape=jax.ShapeDtypeStruct((rows, features), dtype),
        cost_estimate=pl.CostEstimate(
            flops=2 * rows * features * sum(widths),
            bytes_accessed=2 * sum(widths) * (rows + features) + 4 * rows * features,
            transcendentals=0,
        ),
        compiler_params=pltpu.CompilerParams(vmem_limit_bytes=VMEM_LIMIT),
        name="chunk_sum",
    )(*lefts, *rights)


def grads_kernel(count, *refs):
    column = 0
    for left, right in zip(refs[:count], refs[count : 2 * count]):
        width = right.shape[1]
        refs[-1][:, column : column + width] = outer_sum(left[...], right[...]).astype(bf16)
        column += width


def weight_grads(*pairs):
    lefts, rights = [left for left, _ in pairs], [right for _, right in pairs]
    count = len(pairs)
    tokens, features = lefts[0].shape
    widths = [right.shape[1] for right in rights]
    tile = 256
    return pl.pallas_call(
        functools.partial(grads_kernel, count),
        grid=(features // tile,),
        in_specs=[pl.BlockSpec((tokens, tile), lambda i: (0, i))] * count
        + [pl.BlockSpec((tokens, w), lambda i: (0, 0)) for w in widths],
        out_specs=pl.BlockSpec((tile, sum(widths)), lambda i: (i, 0)),
        out_shape=jax.ShapeDtypeStruct((features, sum(widths)), bf16),
        cost_estimate=pl.CostEstimate(
            flops=2 * tokens * features * sum(widths),
            bytes_accessed=2 * (count * tokens * features + sum(widths) * (tokens + features)),
            transcendentals=0,
        ),
        compiler_params=pltpu.CompilerParams(vmem_limit_bytes=VMEM_LIMIT),
        name="weight_grads",
    )(*lefts, *rights)


def project_kernel(place_ref, normed_ref, weight_ref, cos_ref, sin_ref, q_ref, k_ref, v_ref):
    step = pl.program_id(0)
    cos, sin = cos_ref[...], sin_ref[...]
    qkv = product(normed_ref[...], weight_ref[...])
    query = rotate(qkv[:, :HS], cos, sin).astype(bf16) * HS ** (-0.5)
    keys = rotate(qkv[:, HS : 2 * HS], cos, sin).astype(bf16)
    vals = qkv[:, 2 * HS :].astype(bf16)
    blocks = normed_ref.shape[0] // BLOCK
    for b in range(blocks):
        rows = pl.ds(pl.multiple_of(place_ref[step * blocks + b] * BLOCK, BLOCK), BLOCK)
        part = slice(b * BLOCK, (b + 1) * BLOCK)
        q_ref[rows, :] = query[part]
        k_ref[rows, :] = keys[part]
        v_ref[rows, :] = vals[part]


def project(place, normed, weight, cos, sin):
    tokens, features = normed.shape
    tile = 256
    whole = pl.BlockSpec((tokens, HS), lambda i, place: (0, 0))
    return pl.pallas_call(
        project_kernel,
        grid_spec=pltpu.PrefetchScalarGridSpec(
            num_scalar_prefetch=1,
            grid=(tokens // tile,),
            in_specs=[
                pl.BlockSpec((tile, features), lambda i, place: (i, 0)),
                pl.BlockSpec((features, 3 * HS), lambda i, place: (0, 0)),
                pl.BlockSpec((tile, HS // 2), lambda i, place: (i, 0)),
                pl.BlockSpec((tile, HS // 2), lambda i, place: (i, 0)),
            ],
            out_specs=[whole] * 3,
        ),
        out_shape=[jax.ShapeDtypeStruct((tokens, HS), bf16)] * 3,
        cost_estimate=pl.CostEstimate(
            flops=6 * tokens * features * HS,
            bytes_accessed=2 * features * (tokens + 3 * HS) + 10 * tokens * HS,
            transcendentals=0,
        ),
        compiler_params=pltpu.CompilerParams(vmem_limit_bytes=VMEM_LIMIT),
        name="project",
    )(place, normed, weight, cos, sin)


TILE = 256


def tile_masks():
    rows = lax.broadcasted_iota(jnp.int32, (TILE, TILE), 0)
    cols = lax.broadcasted_iota(jnp.int32, (TILE, TILE), 1)
    causal = rows >= cols
    return causal, causal & (rows // BLOCK == cols // BLOCK)


def block_rows(order_ref, index):
    return pl.ds(pl.multiple_of(order_ref[index] * BLOCK, BLOCK), BLOCK)


def forward_kernel(order_ref, q_ref, k_ref, v_ref, mixed_ref, lse_ref, peak_ref):
    causal, inside = tile_masks()
    prompt = GROUP // 2
    top = jnp.full((TILE, 1), masked_value, f32)
    for i in range(GROUP // TILE):
        rows = slice(i * TILE, (i + 1) * TILE)
        past = min(i * TILE, prompt)
        query = q_ref[rows, :]
        near = times_transposed(query, k_ref[rows, :])
        near = jnp.where(causal if i * TILE < prompt else inside, near, masked_value)
        peak = jnp.max(near, axis=1, keepdims=True)
        if past:
            far = times_transposed(query, k_ref[:past, :])
            peak = jnp.maximum(peak, jnp.max(far, axis=1, keepdims=True))
            far = jnp.exp(far - peak)
        near = jnp.exp(near - peak)
        total = jnp.sum(near, axis=1, keepdims=True)
        if past:
            total += jnp.sum(far, axis=1, keepdims=True)
        share = 1.0 / total
        mixed = product((near * share).astype(bf16), v_ref[rows, :])
        if past:
            mixed += product((far * share).astype(bf16), v_ref[:past, :])
        mixed = mixed.astype(bf16)
        for b in range(TILE // BLOCK):
            mixed_ref[block_rows(order_ref, i * (TILE // BLOCK) + b), :] = mixed[
                b * BLOCK : (b + 1) * BLOCK
            ]
        lse_ref[rows, :] = peak + jnp.log(total)
        top = jnp.maximum(top, peak)
    peak_ref[...] = jnp.full(peak_ref.shape, jnp.max(top), f32)


def attention_forward(order, query, keys, vals):
    whole = pl.BlockSpec(memory_space=pltpu.VMEM)
    return pl.pallas_call(
        forward_kernel,
        in_specs=[pl.BlockSpec(memory_space=pltpu.SMEM), whole, whole, whole],
        out_specs=[whole] * 3,
        out_shape=[
            jax.ShapeDtypeStruct((GROUP, HS), bf16),
            jax.ShapeDtypeStruct((GROUP, 1), f32),
            jax.ShapeDtypeStruct((8, 128), f32),
        ],
        cost_estimate=pl.CostEstimate(
            flops=2 * GROUP * GROUP * HS,
            bytes_accessed=8 * GROUP * HS,
            transcendentals=GROUP * GROUP // 2,
        ),
        compiler_params=pltpu.CompilerParams(vmem_limit_bytes=VMEM_LIMIT),
        name="attention_forward",
    )(order, query, keys, vals)


def backward_kernel(
    order_ref, q_ref, k_ref, v_ref, lse_ref, mixed_ref, cos_ref, sin_ref, out_ref, dk_ref, dv_ref
):
    causal, inside = tile_masks()
    prompt = GROUP // 2
    blocks = TILE // BLOCK

    def back(grad, index):
        rows = block_rows(order_ref, index)
        return rows, unrotate(grad, cos_ref[rows, :], sin_ref[rows, :]).astype(bf16)

    for i in range(GROUP // TILE):
        rows = slice(i * TILE, (i + 1) * TILE)
        past = min(i * TILE, prompt)
        query, lse = q_ref[rows, :], lse_ref[rows, :]
        d_mixed = jnp.concatenate(
            [mixed_ref[block_rows(order_ref, i * blocks + b), :] for b in range(blocks)], axis=0
        )
        near = times_transposed(query, k_ref[rows, :])
        near = jnp.where(causal if i * TILE < prompt else inside, near, masked_value)
        near = jnp.exp(near - lse)
        d_near = times_transposed(d_mixed, v_ref[rows, :])
        inner = jnp.sum(near * d_near, axis=1, keepdims=True)
        if past:
            far = jnp.exp(times_transposed(query, k_ref[:past, :]) - lse)
            d_far = times_transposed(d_mixed, v_ref[:past, :])
            inner += jnp.sum(far * d_far, axis=1, keepdims=True)
        d_near = (near * (d_near - inner)).astype(bf16)
        d_query = product(d_near, k_ref[rows, :])
        dk_ref[rows, :] = outer_sum(d_near, query)
        dv_ref[rows, :] = outer_sum(near.astype(bf16), d_mixed)
        if past:
            d_far = (far * (d_far - inner)).astype(bf16)
            d_query += product(d_far, k_ref[:past, :])
            dk_ref[:past, :] += outer_sum(d_far, query)
            dv_ref[:past, :] += outer_sum(far.astype(bf16), d_mixed)
        d_query = d_query * HS ** (-0.5)
        for b in range(blocks):
            where, grad = back(d_query[b * BLOCK : (b + 1) * BLOCK], i * blocks + b)
            out_ref[where, :HS] = grad
    for c in range(GROUP // BLOCK):
        part = slice(c * BLOCK, (c + 1) * BLOCK)
        where, grad = back(dk_ref[part, :], c)
        out_ref[where, HS : 2 * HS] = grad
        out_ref[where, 2 * HS :] = dv_ref[part, :].astype(bf16)


def attention_backward(order, query, keys, vals, lse, d_mixed, cos, sin):
    whole = pl.BlockSpec(memory_space=pltpu.VMEM)
    return pl.pallas_call(
        backward_kernel,
        in_specs=[pl.BlockSpec(memory_space=pltpu.SMEM)] + [whole] * 7,
        out_specs=whole,
        out_shape=jax.ShapeDtypeStruct((GROUP, 3 * HS), bf16),
        scratch_shapes=[pltpu.VMEM((GROUP, HS), f32), pltpu.VMEM((GROUP, HS), f32)],
        cost_estimate=pl.CostEstimate(
            flops=5 * GROUP * GROUP * HS,
            bytes_accessed=20 * GROUP * HS,
            transcendentals=GROUP * GROUP // 2,
        ),
        compiler_params=pltpu.CompilerParams(vmem_limit_bytes=VMEM_LIMIT),
        name="attention_backward",
    )(order, query, keys, vals, lse, d_mixed, cos, sin)


def local(
    tokens,
    cotangent,
    segment,
    position,
    clip_limit,
    attn_gain,
    query_weight,
    key_weight,
    value_weight,
    output_weight,
    mlp_gain,
    gate_weight,
    up_weight,
    down_weight,
):
    groups = lax.axis_size("group")
    group = lax.axis_index("group")
    core = lax.axis_index("tp")
    member = lax.axis_index(PLANE)
    token_rows = tokens.shape[0]
    own_rows, features = query_weight.shape[0], tokens.shape[1]
    hidden_own = gate_weight.shape[1] // 4
    chunks, offset = [], 0
    for part in SIXTEENTHS:
        chunks.append((offset, hidden_own * part // 16))
        offset += hidden_own * part // 16
    member_at = member.astype(jnp.int32).reshape(1)

    def own_order(array):
        parts = []
        for j in range(2):
            for k in range(4):
                start = group * GROUP + (member ^ k) * (2 * token_rows) + (core ^ j) * token_rows
                parts.append(lax.dynamic_slice_in_dim(array, start, token_rows))
        return jnp.concatenate(parts)

    def collect(blocks):
        return lax.all_gather(blocks, "group", axis=0, tiled=True)

    def mlp_blocks(chunk, waits):
        weights = [after(a, *waits) for a in (gate_weight, up_weight, down_weight)]
        spans = ((chunk[0], hidden_own, chunk[1], 0),) * 3
        return place_rows(member_at, swap_all(split(member_at, weights, spans)))

    index = lax.axis_index(FSDP)
    gains = jnp.stack([attn_gain, mlp_gain])[:, None, :]
    gains = jnp.where(jnp.arange(4 * groups)[None, :, None] == index, gains, 0)
    gains = combine_all(gains, groups, lambda a, b: a + b).reshape(2, features)
    head, pair = (0, HS, HS, 0), (0, HS, HS, 1)
    attn_pieces = swap_all(
        split(
            member_at,
            (query_weight, key_weight, value_weight, output_weight),
            (head, pair, pair, head),
        )
    )
    attn_weights = collect(place_rows(member_at, attn_pieces))
    late_tokens = after(tokens, *attn_pieces)
    neighbours = plane_neighbours(late_tokens)
    tokens_pieces = plane_pieces(late_tokens, neighbours, (gains,))
    tokens_all = pack(tokens_pieces)
    chunk_blocks = [mlp_blocks(chunks[0], tokens_pieces[3:5])]
    cot_pieces = plane_pieces(after(cotangent, chunk_blocks[0]))
    for chunk in chunks[1:]:
        chunk_blocks.append(mlp_blocks(chunk, cot_pieces[3:5]))
    mlp_weights = [collect(blocks) for blocks in chunk_blocks]
    gain_attn, gain_mlp = gains[0].astype(f32), gains[1].astype(f32)

    tokens_f = tokens.astype(f32)
    all_f = tokens_all.astype(f32)
    normed_all = (all_f * rms_inverse(all_f) * gain_attn).astype(bf16)
    inverse_attn = rms_inverse(tokens_f)
    unit_attn = tokens_f * inverse_attn
    seg, pos = own_order(segment), own_order(position)
    cos, sin = rope_tables(pos)
    seg_blocks, pos_blocks = seg[::BLOCK], pos[::BLOCK]
    half_blocks = GROUP // BLOCK // 2
    place = jnp.where(seg_blocks == 0, pos_blocks // BLOCK, half_blocks - 1 + seg_blocks)
    labels = jnp.arange(2 * half_blocks, dtype=jnp.int32)
    order = jnp.sum(jnp.where(place[None, :] == labels[:, None], labels[None, :], 0), axis=1)
    query, keys, vals = project(place, normed_all, attn_weights, cos, sin)
    mixed, logsum, peak = attention_forward(order, query, keys, vals)

    head_top = jnp.where(jnp.arange(4) == member, peak[0, :4], masked_value)
    head_top = combine_all(head_top, groups, jnp.maximum)

    def projected(left, column):
        return lambda j, h: chunk_sum([left], [attn_weights], column, j, h, bf16 if j else f32)

    attn_out, _ = plane_reduce(projected(mixed, 3))
    hidden = tokens_f + attn_out
    inverse_mlp = rms_inverse(hidden)
    unit_mlp = hidden * inverse_mlp
    cot_all = pack([after(cot_pieces[0], attn_out)] + cot_pieces[1:])
    normed_mlp = pack(plane_pieces((unit_mlp * gain_mlp).astype(bf16)))

    inners, d_boths = [], []
    for weights in mlp_weights[:-1]:
        inner, d_both = mlp_chunk(normed_mlp, cot_all, weights)
        inners.append(inner)
        d_boths.append(d_both)
    early = [chunk_sum(d_boths, mlp_weights[:-1], 0, j, None, f32) for j in range(2)]
    inner, d_both, front_1, back_1 = mlp_tail(
        normed_mlp, cot_all, mlp_weights[-1], early[1], 1, bf16
    )
    inner, d_both, front_0, back_0 = mlp_tail(
        normed_mlp, cot_all, mlp_weights[-1], early[0], 0, f32, (inner, d_both)
    )
    inners.append(inner)
    d_boths.append(d_both)
    sums = ((front_0, back_0), (front_1, back_1))
    d_normed, arrived = plane_reduce(lambda j, h: sums[j][h])
    cot_f = cotangent.astype(f32)
    scaled = d_normed * gain_mlp
    d_hidden = cot_f + inverse_mlp * (
        scaled - unit_mlp * jnp.mean(scaled * unit_mlp, axis=-1, keepdims=True)
    )
    d_attn_all = pack(plane_pieces(d_hidden.astype(bf16)))

    def line_sum(partial):
        return lax.psum_scatter(partial, "group", scatter_dimension=0, tiled=True)

    def send_grads(reduced, *waits):
        return swap_all(pick_rows(member_at, after(reduced, *waits)))

    chunk_grads = []
    for n in range(len(chunks)):
        grads = weight_grads((normed_mlp, d_boths[n]), (cot_all, inners[n]))
        if n == len(chunks) - 1:
            chunk_grads.append(line_sum(grads))
        else:
            blocks = grads.reshape(groups, 4 * own_rows, grads.shape[1])
            chunk_grads.append(line_reduce(blocks, groups, group))
    late_inners = [after(inner, *arrived) for inner in inners]
    mlp_out, _ = plane_reduce(
        lambda j, h: chunk_sum(late_inners, mlp_weights, 2, j, h, bf16 if j else f32),
        (d_attn_all,),
    )
    block_out = (hidden + mlp_out).astype(bf16)

    out_grads = weight_grads((d_attn_all, mixed))
    out_sum = line_sum(out_grads)
    d_mixed = product(
        after(d_attn_all, out_grads), attn_weights[:, 3 * HS :]
    ).astype(bf16)
    d_qkv = attention_backward(order, query, keys, vals, logsum, d_mixed, cos, sin)
    qkv_grads = weight_grads((normed_all, d_qkv))
    qkv_sum = line_sum(qkv_grads)
    d_normed, _ = plane_reduce(projected(after(d_qkv, qkv_grads), 0))
    scaled = d_normed * gain_attn
    tokens_grad = d_hidden + inverse_attn * (
        scaled - unit_attn * jnp.mean(scaled * unit_attn, axis=-1, keepdims=True)
    )

    mlp_parts = [send_grads(reduced, d_attn_all) for reduced in chunk_grads[:-1]]
    mlp_parts.append(send_grads(chunk_grads[-1], d_mixed))
    gate_grad, up_grad, down_grad, mlp_gain_row = mlp_final(
        member_at, gate_weight, up_weight, tuple(chunks), mlp_parts
    )
    query_grad, key_grad, value_grad, output_grad, attn_gain_row = attention_final(
        member_at,
        query_weight,
        key_weight,
        value_weight,
        send_grads(qkv_sum),
        send_grads(out_sum, d_qkv),
    )
    gain_grads = jnp.concatenate([attn_gain_row, mlp_gain_row], axis=1)
    gain_grads = gain_grads + swap(gain_grads, "tp")
    attn_gain_grad = gain_grads[:, 0] / attn_gain.astype(f32)
    mlp_gain_grad = gain_grads[:, 1] / mlp_gain.astype(f32)

    factor = clip_limit / jnp.maximum(head_top, clip_limit)
    query_scale = jnp.repeat(jnp.sqrt(factor), HS)
    key_factor = jnp.min(factor.reshape(2, 2), axis=1)
    key_scale = jnp.repeat(jnp.sqrt(key_factor), HS)
    query_clipped = (query_weight.astype(f32) * query_scale[None, :]).astype(bf16)
    key_clipped = (key_weight.astype(f32) * key_scale[None, :]).astype(bf16)
    return (
        block_out,
        tokens_grad,
        attn_gain_grad,
        query_grad,
        key_grad,
        value_grad,
        output_grad,
        mlp_gain_grad,
        gate_grad,
        up_grad,
        down_grad,
        head_top,
        query_clipped,
        key_clipped,
    )


def solution(mesh):
    shape = (mesh.shape["fsdp"] // 4, 2, 2, mesh.shape["tp"])
    fine = Mesh(mesh.devices.reshape(shape), ("group", "row", "col", "tp"))
    rows = P(("group", "row", "col", "tp"), None)
    weight = P(FSDP, "tp")
    gain = P(FSDP)
    heads = P("tp")
    return jax.shard_map(
        local,
        mesh=fine,
        in_specs=(
            rows, rows, P(), P(), heads, gain, weight, weight, weight, weight,
            gain, weight, weight, weight,
        ),
        out_specs=(
            rows, rows, gain, weight, weight, weight, weight, gain, weight, weight, weight,
            heads, weight, weight,
        ),
        check_vma=False,
    )
```

```python
import functools

import jax
import jax.numpy as jnp
from jax import lax
from jax.experimental import pallas as pl
from jax.experimental.pallas import tpu as pltpu
from jax.sharding import Mesh, PartitionSpec as P

HS = 256
GROUP = 2048
SIXTEENTHS = (10, 6)
BLOCK = 128

epsilon = 1e-05
theta_base = 1000042.0
masked_value = -1e30

bf16 = jnp.bfloat16
f32 = jnp.float32
PLANE = ("row", "col")
FSDP = ("group", "row", "col")
VMEM_LIMIT = 48 * 1024 * 1024


def product(left, right):
    return jnp.dot(left, right, preferred_element_type=f32)


def times_transposed(left, right):
    return lax.dot_general(left, right, (((1,), (1,)), ((), ())), preferred_element_type=f32)


def outer_sum(left, right):
    return lax.dot_general(left, right, (((0,), (0,)), ((), ())), preferred_element_type=f32)


def take(array, index, axis=0):
    return lax.dynamic_index_in_dim(array, index, axis, keepdims=False)


def swap(block, axis):
    return lax.ppermute(block, axis, [(0, 1), (1, 0)])


def swap_plane(block, distance):
    return lax.ppermute(block, PLANE, [(i, i ^ distance) for i in range(4)])


def after(value, *others):
    return lax.optimization_barrier((value,) + others)[0]


def combine_all(values, groups, combine):
    distance, count = 1, 4 * groups
    while distance < count:
        arrived = []
        for step in range(1, min(4, count // distance)):
            route = [(i, i ^ step * distance) for i in range(count)]
            arrived.append(lax.ppermute(values, FSDP, route))
        for other in arrived:
            values = combine(values, other)
        distance *= 4
    return values


def pack_kernel(count, *refs):
    out_ref, sems = refs[count], refs[count + 1]
    copies, start = [], 0
    for i in range(count):
        rows = refs[i].shape[0]
        copy = pltpu.make_async_copy(refs[i], out_ref.at[pl.ds(start, rows)], sems.at[i])
        copy.start()
        copies.append(copy)
        start += rows
    for copy in copies:
        copy.wait()


def pack(pieces):
    rows, width = sum(p.shape[0] for p in pieces), pieces[0].shape[1]
    count = len(pieces)
    return pl.pallas_call(
        functools.partial(pack_kernel, count),
        in_specs=[pl.BlockSpec(memory_space=pl.ANY)] * count,
        out_specs=pl.BlockSpec(memory_space=pltpu.VMEM),
        out_shape=jax.ShapeDtypeStruct((rows, width), pieces[0].dtype),
        scratch_shapes=[pltpu.SemaphoreType.DMA((count,))],
        cost_estimate=pl.CostEstimate(
            flops=0, bytes_accessed=4 * rows * width, transcendentals=0
        ),
        compiler_params=pltpu.CompilerParams(vmem_limit_bytes=VMEM_LIMIT),
        name="pack",
    )(*pieces)


def plane_neighbours(own):
    return swap(own, "col"), swap(own, "row")


def plane_far(neighbours, *waits):
    across, along = neighbours
    half = across.shape[0] // 2
    return (
        swap(after(across[:half], *waits), "row"),
        swap(after(along[half:], *waits), "col"),
    )


def with_partner(pieces):
    return pieces + [swap(piece, "tp") for piece in pieces]


def chip_sums(front, back):
    totals = []
    for own, other in (front, back):
        total = own.astype(f32) + swap(other, "tp").astype(f32)
        totals.append(total.reshape((4, total.shape[0] // 4, total.shape[1])))
    return totals


def first_operands(totals):
    first, second = totals
    return jnp.stack([first[1], first[3]]).astype(bf16), second[2:].astype(bf16)


def reduce_first(operands, *waits):
    front, back = operands
    return swap(after(front, *waits), "col"), swap(after(back, *waits), "row")


def reduce_operands(totals, arrived):
    first, second = totals
    got, got_second = arrived[0].astype(f32), arrived[1].astype(f32)
    return (
        (first[0] + got[0], (first[2] + got[1]).astype(bf16)),
        (second[0] + got_second[0], (second[1] + got_second[1]).astype(bf16)),
    )


def reduce_last(operands, *waits):
    (keep, send), (keep_back, send_back) = operands
    last = swap(after(send, *waits), "row")
    last_back = swap(after(send_back, *waits), "col")
    return jnp.concatenate([keep + last.astype(f32), keep_back + last_back.astype(f32)], axis=1)


def line_reduce(blocks, groups, index):
    up = down = None
    waits = yield
    for step in range(1, groups):
        out_up = take(blocks, jnp.minimum(index + groups - step, groups - 1))
        out_down = take(blocks, jnp.maximum(index - groups + step, 0))
        out_up, out_down = after(out_up, *waits), after(out_down, *waits)
        if up is not None:
            out_up = (out_up.astype(f32) + up.astype(f32)).astype(bf16)
            out_down = (out_down.astype(f32) + down.astype(f32)).astype(bf16)
        senders = range(min(step, groups - 1))
        up = lax.ppermute(out_up, "group", [(j, j + 1) for j in senders])
        down = lax.ppermute(
            out_down, "group", [(groups - 1 - j, groups - 2 - j) for j in senders]
        )
        waits = yield up, down
    total = take(blocks, index).astype(f32) + up.astype(f32) + down.astype(f32)
    yield total.astype(bf16)


def split_kernel(spans, member_ref, *refs):
    sources, outs = refs[: len(spans)], refs[len(spans) :]
    for k in range(4):
        target = member_ref[0] ^ k
        column = 0
        for source, (offset, stride, width, shift) in zip(sources, spans):
            start = pl.multiple_of((target >> shift) * stride + offset, 128)
            outs[k][:, column : column + width] = source[:, pl.ds(start, width)]
            column += width


def split(member, sources, spans):
    rows, width = sources[0].shape[0], sum(span[2] for span in spans)
    whole = pl.BlockSpec(memory_space=pltpu.VMEM)
    return pl.pallas_call(
        functools.partial(split_kernel, spans),
        in_specs=[pl.BlockSpec(memory_space=pltpu.SMEM)] + [whole] * len(sources),
        out_specs=[whole] * 4,
        out_shape=[jax.ShapeDtypeStruct((rows, width), bf16)] * 4,
        cost_estimate=pl.CostEstimate(
            flops=0, bytes_accessed=16 * rows * width, transcendentals=0
        ),
        compiler_params=pltpu.CompilerParams(vmem_limit_bytes=VMEM_LIMIT),
        name="split",
    )(member, *sources)


def place_kernel(member_ref, *refs):
    rows = refs[0].shape[0]
    for k in range(4):
        start = pl.multiple_of((member_ref[0] ^ k) * rows, rows)
        refs[4][pl.ds(start, rows), :] = refs[k][...]


def place_rows(member, pieces):
    rows, width = pieces[0].shape
    whole = pl.BlockSpec(memory_space=pltpu.VMEM)
    return pl.pallas_call(
        place_kernel,
        in_specs=[pl.BlockSpec(memory_space=pltpu.SMEM)] + [whole] * 4,
        out_specs=whole,
        out_shape=jax.ShapeDtypeStruct((4 * rows, width), bf16),
        cost_estimate=pl.CostEstimate(
            flops=0, bytes_accessed=16 * rows * width, transcendentals=0
        ),
        compiler_params=pltpu.CompilerParams(vmem_limit_bytes=VMEM_LIMIT),
        name="place_rows",
    )(member, *pieces)


def pick_kernel(member_ref, source_ref, *outs):
    rows = outs[0].shape[0]
    for k in range(4):
        start = pl.multiple_of((member_ref[0] ^ k) * rows, rows)
        outs[k][...] = source_ref[pl.ds(start, rows), :]


def pick_rows(member, source):
    rows, width = source.shape[0] // 4, source.shape[1]
    whole = pl.BlockSpec(memory_space=pltpu.VMEM)
    return pl.pallas_call(
        pick_kernel,
        in_specs=[pl.BlockSpec(memory_space=pltpu.SMEM), whole],
        out_specs=[whole] * 4,
        out_shape=[jax.ShapeDtypeStruct((rows, width), bf16)] * 4,
        cost_estimate=pl.CostEstimate(
            flops=0, bytes_accessed=16 * rows * width, transcendentals=0
        ),
        compiler_params=pltpu.CompilerParams(vmem_limit_bytes=VMEM_LIMIT),
        name="pick_rows",
    )(member, source)


def swap_all(pieces):
    return [pieces[0]] + [swap_plane(pieces[k], k) for k in (1, 2, 3)]


def mlp_final_kernel(chunks, stride, member_ref, gate_w_ref, up_w_ref, *refs):
    pieces, outs, gain_ref = refs[:-4], refs[-4:-1], refs[-1]
    for n, (offset, width) in enumerate(chunks):
        for k in range(4):
            column = pl.multiple_of((member_ref[0] ^ k) * stride + offset, 128)
            for i in range(3):
                part = pieces[4 * n + k][:, i * width : (i + 1) * width]
                outs[i][:, pl.ds(column, width)] = part.astype(f32)
    gain_ref[...] = jnp.sum(
        gate_w_ref[...].astype(f32) * outs[0][...] + up_w_ref[...].astype(f32) * outs[1][...],
        axis=1,
        keepdims=True,
    )


def mlp_final(member, gate_weight, up_weight, chunks, parts):
    rows, hidden = gate_weight.shape
    pieces = [piece for part in parts for piece in part]
    whole = pl.BlockSpec(memory_space=pltpu.VMEM)
    return pl.pallas_call(
        functools.partial(mlp_final_kernel, chunks, hidden // 4),
        in_specs=[pl.BlockSpec(memory_space=pltpu.SMEM)] + [whole] * (2 + len(pieces)),
        out_specs=[whole] * 4,
        out_shape=[jax.ShapeDtypeStruct((rows, hidden), f32)] * 3
        + [jax.ShapeDtypeStruct((rows, 1), f32)],
        cost_estimate=pl.CostEstimate(
            flops=4 * rows * hidden, bytes_accessed=22 * rows * hidden, transcendentals=0
        ),
        compiler_params=pltpu.CompilerParams(vmem_limit_bytes=VMEM_LIMIT),
        name="mlp_final",
    )(member, gate_weight, up_weight, *pieces)


def attention_final_kernel(member_ref, qw_ref, kw_ref, vw_ref, *refs):
    qkv, out = refs[:4], refs[4:8]
    q_ref, k_ref, v_ref, o_ref, gain_ref = refs[8:]
    member = member_ref[0]
    for k in range(4):
        columns = pl.ds(pl.multiple_of((member ^ k) * HS, HS), HS)
        q_ref[:, columns] = qkv[k][:, :HS].astype(f32)
        o_ref[:, columns] = out[k][...].astype(f32)
    for h in range(2):
        columns = pl.ds(pl.multiple_of(((member >> 1) ^ h) * HS, HS), HS)
        both = qkv[2 * h][:, HS:].astype(f32) + qkv[2 * h + 1][:, HS:].astype(f32)
        k_ref[:, columns] = both[:, :HS]
        v_ref[:, columns] = both[:, HS:]

    def row_sum(weight_ref, grad_ref):
        return jnp.sum(weight_ref[...].astype(f32) * grad_ref[...], axis=1, keepdims=True)

    gain_ref[...] = row_sum(qw_ref, q_ref) + row_sum(kw_ref, k_ref) + row_sum(vw_ref, v_ref)


def attention_final(member, query_weight, key_weight, value_weight, qkv, out):
    rows, width = query_weight.shape
    whole = pl.BlockSpec(memory_space=pltpu.VMEM)
    shapes = [width, width // 2, width // 2, width, 1]
    return pl.pallas_call(
        attention_final_kernel,
        in_specs=[pl.BlockSpec(memory_space=pltpu.SMEM)] + [whole] * 11,
        out_specs=[whole] * 5,
        out_shape=[jax.ShapeDtypeStruct((rows, n), f32) for n in shapes],
        cost_estimate=pl.CostEstimate(
            flops=4 * rows * width, bytes_accessed=24 * rows * width, transcendentals=0
        ),
        compiler_params=pltpu.CompilerParams(vmem_limit_bytes=VMEM_LIMIT),
        name="attention_final",
    )(member, query_weight, key_weight, value_weight, *qkv, *out)


def rms_inverse(values):
    return lax.rsqrt(jnp.mean(values * values, axis=-1, keepdims=True) + epsilon)


def rope_tables(positions):
    half_size = HS // 2
    indices = jnp.arange(half_size, dtype=f32)
    inverse = theta_base ** (-2.0 * indices / HS)
    angles = positions.astype(f32)[:, None] * inverse[None, :]
    return jnp.cos(angles), jnp.sin(angles)


def rotate(vectors, cos, sin):
    front, back = vectors[:, : HS // 2], vectors[:, HS // 2 :]
    return jnp.concatenate([front * cos - back * sin, back * cos + front * sin], axis=-1)


def unrotate(grads, cos, sin):
    front, back = grads[:, : HS // 2], grads[:, HS // 2 :]
    return jnp.concatenate([front * cos + back * sin, back * cos - front * sin], axis=-1)


def mlp_tile(width, normed, cot, weight_ref):
    both = product(normed, weight_ref[:, : 2 * width])
    d_inner = product(cot, weight_ref[:, 2 * width :])
    gate, upward = both[:, :width], both[:, width:]
    sig = 1.0 / (1.0 + jnp.exp(-gate))
    silu = gate * sig
    d_gate = d_inner * upward * sig * (1.0 + gate * (1.0 - sig))
    return (
        (silu * upward).astype(bf16),
        jnp.concatenate([d_gate, d_inner * silu], axis=1).astype(bf16),
    )


def mlp_kernel(width, normed_ref, cot_ref, weight_ref, inner_ref, grads_ref):
    inner_ref[...], grads_ref[...] = mlp_tile(
        width, normed_ref[...], cot_ref[...], weight_ref
    )


def tail_kernel(width, normed_ref, cot_ref, weight_ref, base_ref, *refs):
    inner_ref, grads_ref, front_ref, back_ref = refs[-4:]
    inner, grads = mlp_tile(width, normed_ref[...], cot_ref[...], weight_ref)
    inner_ref[...], grads_ref[...] = inner, grads
    total = times_transposed(grads, weight_ref[:, : 2 * width]) + base_ref[...]
    half = total.shape[1] // 2
    front_ref[...] = total[:, :half].astype(front_ref.dtype)
    back_ref[...] = total[:, half:].astype(back_ref.dtype)


def mlp_tail(normed, cot, weight, base, part, dtype, chained=()):
    tokens, features = normed.shape
    width = weight.shape[1] // 3
    tile, rows = 256, tokens // 2
    steps = rows // tile
    count = len(chained)
    return pl.pallas_call(
        functools.partial(tail_kernel, width),
        grid=(steps,),
        in_specs=[
            pl.BlockSpec((tile, features), lambda i: (part * steps + i, 0)),
            pl.BlockSpec((tile, features), lambda i: (part * steps + i, 0)),
            pl.BlockSpec((features, 3 * width), lambda i: (0, 0)),
            pl.BlockSpec((tile, features), lambda i: (i, 0)),
        ]
        + [pl.BlockSpec(memory_space=pl.ANY)] * count,
        out_specs=[
            pl.BlockSpec((tile, width), lambda i: (part * steps + i, 0)),
            pl.BlockSpec((tile, 2 * width), lambda i: (part * steps + i, 0)),
            pl.BlockSpec((tile, features // 2), lambda i: (i, 0)),
            pl.BlockSpec((tile, features // 2), lambda i: (i, 0)),
        ],
        out_shape=[
            jax.ShapeDtypeStruct((tokens, width), bf16),
            jax.ShapeDtypeStruct((tokens, 2 * width), bf16),
            jax.ShapeDtypeStruct((rows, features // 2), dtype),
            jax.ShapeDtypeStruct((rows, features // 2), dtype),
        ],
        input_output_aliases={4 + i: i for i in range(count)},
        cost_estimate=pl.CostEstimate(
            flops=10 * rows * features * width,
            bytes_accessed=2 * features * (5 * rows + 3 * width),
            transcendentals=rows * width,
        ),
        compiler_params=pltpu.CompilerParams(vmem_limit_bytes=VMEM_LIMIT),
        name="mlp_tail",
    )(normed, cot, weight, base, *chained)


def mlp_chunk(normed, cot, weight):
    tokens, features = normed.shape
    width = weight.shape[1] // 3
    tile = 256
    return pl.pallas_call(
        functools.partial(mlp_kernel, width),
        grid=(tokens // tile,),
        in_specs=[
            pl.BlockSpec((tile, features), lambda i: (i, 0)),
            pl.BlockSpec((tile, features), lambda i: (i, 0)),
            pl.BlockSpec((features, 3 * width), lambda i: (0, 0)),
        ],
        out_specs=[
            pl.BlockSpec((tile, width), lambda i: (i, 0)),
            pl.BlockSpec((tile, 2 * width), lambda i: (i, 0)),
        ],
        out_shape=[
            jax.ShapeDtypeStruct((tokens, width), bf16),
            jax.ShapeDtypeStruct((tokens, 2 * width), bf16),
        ],
        cost_estimate=pl.CostEstimate(
            flops=6 * tokens * features * width,
            bytes_accessed=2 * features * (2 * tokens + 3 * width),
            transcendentals=tokens * width,
        ),
        compiler_params=pltpu.CompilerParams(vmem_limit_bytes=VMEM_LIMIT),
        name="mlp_chunk",
    )(normed, cot, weight)


def sum_kernel(count, *refs):
    lefts, rights, out_ref = refs[:count], refs[count : 2 * count], refs[-1]
    total = times_transposed(lefts[0][...], rights[0][...])
    for left, right in zip(lefts[1:], rights[1:]):
        total += times_transposed(left[...], right[...])
    for base in refs[2 * count : -1]:
        total += base[...].astype(f32)
    out_ref[...] = total.astype(out_ref.dtype)


def chunk_sum(lefts, rights, column, part, half, dtype):
    count = len(lefts)
    tokens, features = lefts[0].shape[0], rights[0].shape[0]
    widths = [left.shape[1] for left in lefts]
    rows = tokens // 2
    tile = 256
    if half is not None:
        features, tile = features // 2, 512
    steps = rows // tile
    block = half or 0
    return pl.pallas_call(
        functools.partial(sum_kernel, count),
        grid=(steps,),
        in_specs=[pl.BlockSpec((tile, w), lambda i: (part * steps + i, 0)) for w in widths]
        + [pl.BlockSpec((features, w), lambda i: (block, column)) for w in widths],
        out_specs=pl.BlockSpec((tile, features), lambda i: (i, 0)),
        out_shape=jax.ShapeDtypeStruct((rows, features), dtype),
        cost_estimate=pl.CostEstimate(
            flops=2 * rows * features * sum(widths),
            bytes_accessed=2 * sum(widths) * (rows + features) + 4 * rows * features,
            transcendentals=0,
        ),
        compiler_params=pltpu.CompilerParams(vmem_limit_bytes=VMEM_LIMIT),
        name="chunk_sum",
    )(*lefts, *rights)


def grads_kernel(count, *refs):
    column = 0
    for left, right in zip(refs[:count], refs[count : 2 * count]):
        width = right.shape[1]
        refs[-1][:, column : column + width] = outer_sum(left[...], right[...]).astype(bf16)
        column += width


def weight_grads(*pairs):
    lefts, rights = [left for left, _ in pairs], [right for _, right in pairs]
    count = len(pairs)
    tokens, features = lefts[0].shape
    widths = [right.shape[1] for right in rights]
    tile = 256
    return pl.pallas_call(
        functools.partial(grads_kernel, count),
        grid=(features // tile,),
        in_specs=[pl.BlockSpec((tokens, tile), lambda i: (0, i))] * count
        + [pl.BlockSpec((tokens, w), lambda i: (0, 0)) for w in widths],
        out_specs=pl.BlockSpec((tile, sum(widths)), lambda i: (i, 0)),
        out_shape=jax.ShapeDtypeStruct((features, sum(widths)), bf16),
        cost_estimate=pl.CostEstimate(
            flops=2 * tokens * features * sum(widths),
            bytes_accessed=2 * (count * tokens * features + sum(widths) * (tokens + features)),
            transcendentals=0,
        ),
        compiler_params=pltpu.CompilerParams(vmem_limit_bytes=VMEM_LIMIT),
        name="weight_grads",
    )(*lefts, *rights)


def project_kernel(place_ref, normed_ref, weight_ref, cos_ref, sin_ref, q_ref, k_ref, v_ref):
    step = pl.program_id(0)
    cos, sin = cos_ref[...], sin_ref[...]
    qkv = product(normed_ref[...], weight_ref[...])
    query = rotate(qkv[:, :HS], cos, sin).astype(bf16) * HS ** (-0.5)
    keys = rotate(qkv[:, HS : 2 * HS], cos, sin).astype(bf16)
    vals = qkv[:, 2 * HS :].astype(bf16)
    blocks = normed_ref.shape[0] // BLOCK
    for b in range(blocks):
        rows = pl.ds(pl.multiple_of(place_ref[step * blocks + b] * BLOCK, BLOCK), BLOCK)
        part = slice(b * BLOCK, (b + 1) * BLOCK)
        q_ref[rows, :] = query[part]
        k_ref[rows, :] = keys[part]
        v_ref[rows, :] = vals[part]


def project(place, normed, weight, cos, sin):
    tokens, features = normed.shape
    tile = 256
    whole = pl.BlockSpec((tokens, HS), lambda i, place: (0, 0))
    return pl.pallas_call(
        project_kernel,
        grid_spec=pltpu.PrefetchScalarGridSpec(
            num_scalar_prefetch=1,
            grid=(tokens // tile,),
            in_specs=[
                pl.BlockSpec((tile, features), lambda i, place: (i, 0)),
                pl.BlockSpec((features, 3 * HS), lambda i, place: (0, 0)),
                pl.BlockSpec((tile, HS // 2), lambda i, place: (i, 0)),
                pl.BlockSpec((tile, HS // 2), lambda i, place: (i, 0)),
            ],
            out_specs=[whole] * 3,
        ),
        out_shape=[jax.ShapeDtypeStruct((tokens, HS), bf16)] * 3,
        cost_estimate=pl.CostEstimate(
            flops=6 * tokens * features * HS,
            bytes_accessed=2 * features * (tokens + 3 * HS) + 10 * tokens * HS,
            transcendentals=0,
        ),
        compiler_params=pltpu.CompilerParams(vmem_limit_bytes=VMEM_LIMIT),
        name="project",
    )(place, normed, weight, cos, sin)


TILE = 256


def tile_masks():
    rows = lax.broadcasted_iota(jnp.int32, (TILE, TILE), 0)
    cols = lax.broadcasted_iota(jnp.int32, (TILE, TILE), 1)
    causal = rows >= cols
    return causal, causal & (rows // BLOCK == cols // BLOCK)


def block_rows(order_ref, index):
    return pl.ds(pl.multiple_of(order_ref[index] * BLOCK, BLOCK), BLOCK)


def forward_kernel(order_ref, q_ref, k_ref, v_ref, mixed_ref, lse_ref, peak_ref):
    causal, inside = tile_masks()
    prompt = GROUP // 2
    top = jnp.full((TILE, 1), masked_value, f32)
    for i in range(GROUP // TILE):
        rows = slice(i * TILE, (i + 1) * TILE)
        past = min(i * TILE, prompt)
        query = q_ref[rows, :]
        near = times_transposed(query, k_ref[rows, :])
        near = jnp.where(causal if i * TILE < prompt else inside, near, masked_value)
        peak = jnp.max(near, axis=1, keepdims=True)
        if past:
            far = times_transposed(query, k_ref[:past, :])
            peak = jnp.maximum(peak, jnp.max(far, axis=1, keepdims=True))
            far = jnp.exp(far - peak)
        near = jnp.exp(near - peak)
        total = jnp.sum(near, axis=1, keepdims=True)
        if past:
            total += jnp.sum(far, axis=1, keepdims=True)
        share = 1.0 / total
        mixed = product((near * share).astype(bf16), v_ref[rows, :])
        if past:
            mixed += product((far * share).astype(bf16), v_ref[:past, :])
        mixed = mixed.astype(bf16)
        for b in range(TILE // BLOCK):
            mixed_ref[block_rows(order_ref, i * (TILE // BLOCK) + b), :] = mixed[
                b * BLOCK : (b + 1) * BLOCK
            ]
        lse_ref[rows, :] = peak + jnp.log(total)
        top = jnp.maximum(top, peak)
    peak_ref[...] = jnp.full(peak_ref.shape, jnp.max(top), f32)


def attention_forward(order, query, keys, vals):
    whole = pl.BlockSpec(memory_space=pltpu.VMEM)
    return pl.pallas_call(
        forward_kernel,
        in_specs=[pl.BlockSpec(memory_space=pltpu.SMEM), whole, whole, whole],
        out_specs=[whole] * 3,
        out_shape=[
            jax.ShapeDtypeStruct((GROUP, HS), bf16),
            jax.ShapeDtypeStruct((GROUP, 1), f32),
            jax.ShapeDtypeStruct((8, 128), f32),
        ],
        cost_estimate=pl.CostEstimate(
            flops=2 * GROUP * GROUP * HS,
            bytes_accessed=8 * GROUP * HS,
            transcendentals=GROUP * GROUP // 2,
        ),
        compiler_params=pltpu.CompilerParams(vmem_limit_bytes=VMEM_LIMIT),
        name="attention_forward",
    )(order, query, keys, vals)


def backward_kernel(
    order_ref, q_ref, k_ref, v_ref, lse_ref, mixed_ref, cos_ref, sin_ref, out_ref, dk_ref, dv_ref
):
    causal, inside = tile_masks()
    prompt = GROUP // 2
    blocks = TILE // BLOCK

    def back(grad, index):
        rows = block_rows(order_ref, index)
        return rows, unrotate(grad, cos_ref[rows, :], sin_ref[rows, :]).astype(bf16)

    for i in range(GROUP // TILE):
        rows = slice(i * TILE, (i + 1) * TILE)
        past = min(i * TILE, prompt)
        query, lse = q_ref[rows, :], lse_ref[rows, :]
        d_mixed = jnp.concatenate(
            [mixed_ref[block_rows(order_ref, i * blocks + b), :] for b in range(blocks)], axis=0
        )
        near = times_transposed(query, k_ref[rows, :])
        near = jnp.where(causal if i * TILE < prompt else inside, near, masked_value)
        near = jnp.exp(near - lse)
        d_near = times_transposed(d_mixed, v_ref[rows, :])
        inner = jnp.sum(near * d_near, axis=1, keepdims=True)
        if past:
            far = jnp.exp(times_transposed(query, k_ref[:past, :]) - lse)
            d_far = times_transposed(d_mixed, v_ref[:past, :])
            inner += jnp.sum(far * d_far, axis=1, keepdims=True)
        d_near = (near * (d_near - inner)).astype(bf16)
        d_query = product(d_near, k_ref[rows, :])
        dk_ref[rows, :] = outer_sum(d_near, query)
        dv_ref[rows, :] = outer_sum(near.astype(bf16), d_mixed)
        if past:
            d_far = (far * (d_far - inner)).astype(bf16)
            d_query += product(d_far, k_ref[:past, :])
            dk_ref[:past, :] += outer_sum(d_far, query)
            dv_ref[:past, :] += outer_sum(far.astype(bf16), d_mixed)
        d_query = d_query * HS ** (-0.5)
        for b in range(blocks):
            where, grad = back(d_query[b * BLOCK : (b + 1) * BLOCK], i * blocks + b)
            out_ref[where, :HS] = grad
    for c in range(GROUP // BLOCK):
        part = slice(c * BLOCK, (c + 1) * BLOCK)
        where, grad = back(dk_ref[part, :], c)
        out_ref[where, HS : 2 * HS] = grad
        out_ref[where, 2 * HS :] = dv_ref[part, :].astype(bf16)


def attention_backward(order, query, keys, vals, lse, d_mixed, cos, sin):
    whole = pl.BlockSpec(memory_space=pltpu.VMEM)
    return pl.pallas_call(
        backward_kernel,
        in_specs=[pl.BlockSpec(memory_space=pltpu.SMEM)] + [whole] * 7,
        out_specs=whole,
        out_shape=jax.ShapeDtypeStruct((GROUP, 3 * HS), bf16),
        scratch_shapes=[pltpu.VMEM((GROUP, HS), f32), pltpu.VMEM((GROUP, HS), f32)],
        cost_estimate=pl.CostEstimate(
            flops=5 * GROUP * GROUP * HS,
            bytes_accessed=20 * GROUP * HS,
            transcendentals=GROUP * GROUP // 2,
        ),
        compiler_params=pltpu.CompilerParams(vmem_limit_bytes=VMEM_LIMIT),
        name="attention_backward",
    )(order, query, keys, vals, lse, d_mixed, cos, sin)


def local(
    tokens,
    cotangent,
    segment,
    position,
    clip_limit,
    attn_gain,
    query_weight,
    key_weight,
    value_weight,
    output_weight,
    mlp_gain,
    gate_weight,
    up_weight,
    down_weight,
):
    groups = lax.axis_size("group")
    group = lax.axis_index("group")
    core = lax.axis_index("tp")
    member = lax.axis_index(PLANE)
    token_rows = tokens.shape[0]
    own_rows, features = query_weight.shape[0], tokens.shape[1]
    hidden_own = gate_weight.shape[1] // 4
    chunks, offset = [], 0
    for part in SIXTEENTHS:
        chunks.append((offset, hidden_own * part // 16))
        offset += hidden_own * part // 16
    member_at = member.astype(jnp.int32).reshape(1)

    def own_order(array):
        parts = []
        for j in range(2):
            for k in range(4):
                start = group * GROUP + (member ^ k) * (2 * token_rows) + (core ^ j) * token_rows
                parts.append(lax.dynamic_slice_in_dim(array, start, token_rows))
        return jnp.concatenate(parts)

    def collect(blocks):
        return lax.all_gather(blocks, "group", axis=0, tiled=True)

    def mlp_blocks(chunk, waits):
        weights = [after(a, *waits) for a in (gate_weight, up_weight, down_weight)]
        spans = ((chunk[0], hidden_own, chunk[1], 0),) * 3
        return place_rows(member_at, swap_all(split(member_at, weights, spans)))

    index = lax.axis_index(FSDP)
    gains = jnp.stack([attn_gain, mlp_gain])[:, None, :]
    gains = jnp.where(jnp.arange(4 * groups)[None, :, None] == index, gains, 0)
    gains = combine_all(gains, groups, lambda a, b: a + b).reshape(2, features)
    head, pair = (0, HS, HS, 0), (0, HS, HS, 1)
    attn_pieces = swap_all(
        split(
            member_at,
            (query_weight, key_weight, value_weight, output_weight),
            (head, pair, pair, head),
        )
    )
    attn_weights = collect(
        place_rows(member_at, [after(attn_pieces[0], gains)] + attn_pieces[1:])
    )
    late_tokens = after(tokens, *attn_pieces)
    neighbours = plane_neighbours(late_tokens)
    tokens_far = plane_far(neighbours)
    tokens_all = pack(with_partner([late_tokens, *neighbours, *tokens_far]))
    chunk_blocks = [mlp_blocks(chunks[0], tokens_far)]
    late_cot = after(cotangent, chunk_blocks[0])
    cot_near = [swap_plane(late_cot, k) for k in (1, 2)]
    cot_far = swap_plane(after(late_cot, *cot_near), 3)
    cot_pieces = with_partner([late_cot] + cot_near + [cot_far])
    gain_attn, gain_mlp = gains[0].astype(f32), gains[1].astype(f32)

    tokens_f = tokens.astype(f32)
    all_f = tokens_all.astype(f32)
    normed_all = (all_f * rms_inverse(all_f) * gain_attn).astype(bf16)
    inverse_attn = rms_inverse(tokens_f)
    unit_attn = tokens_f * inverse_attn
    seg, pos = own_order(segment), own_order(position)
    cos, sin = rope_tables(pos)
    seg_blocks, pos_blocks = seg[::BLOCK], pos[::BLOCK]
    half_blocks = GROUP // BLOCK // 2
    place = jnp.where(seg_blocks == 0, pos_blocks // BLOCK, half_blocks - 1 + seg_blocks)
    labels = jnp.arange(2 * half_blocks, dtype=jnp.int32)
    order = jnp.sum(jnp.where(place[None, :] == labels[:, None], labels[None, :], 0), axis=1)
    query, keys, vals = project(
        place, after(normed_all, chunk_blocks[0]), attn_weights, cos, sin
    )
    mixed, logsum, peak = attention_forward(order, after(query, *cot_near), keys, vals)

    head_top = jnp.where(jnp.arange(4) == member, peak[0, :4], masked_value)
    head_top = combine_all(head_top, groups, jnp.maximum)

    def projected(left, column, *waits):
        lefts = (after(left, *waits), left)
        return [
            [
                chunk_sum([lefts[j]], [attn_weights], column, j, h, bf16 if j else f32)
                for j in (0, 1)
            ]
            for h in range(2)
        ]

    attn_sums = chip_sums(*projected(mixed, 3, cot_far))
    arrived = reduce_first(first_operands(attn_sums))
    attn_operands = reduce_operands(attn_sums, arrived)
    cot_all = pack(cot_pieces)
    hidden = tokens_f + reduce_last(attn_operands, cot_all)
    inverse_mlp = rms_inverse(hidden)
    unit_mlp = hidden * inverse_mlp
    own_normed = (unit_mlp * gain_mlp).astype(bf16)
    neighbours = plane_neighbours(own_normed)
    normed_far = plane_far(neighbours)
    normed_mlp = pack(with_partner([own_normed, *neighbours, *normed_far]))
    for chunk in chunks[1:]:
        chunk_blocks.append(mlp_blocks(chunk, normed_far))
    mlp_weights = [collect(blocks) for blocks in chunk_blocks]

    inner_0, both_0 = mlp_chunk(normed_mlp, cot_all, mlp_weights[0])
    grads_0 = weight_grads((normed_mlp, both_0), (cot_all, inner_0))
    blocks_0 = grads_0.reshape(groups, 4 * own_rows, grads_0.shape[1])
    late_both = after(both_0, grads_0)
    early = [chunk_sum([late_both], mlp_weights[:1], 0, j, None, f32) for j in range(2)]
    inner_1, both_1, front_1, back_1 = mlp_tail(
        after(normed_mlp, *early), cot_all, mlp_weights[1], early[1], 1, bf16
    )
    line_0 = line_reduce(blocks_0, groups, group)
    next(line_0)
    line_0.send(())
    second_0 = line_0.send((front_1,))
    inner_1, both_1, front_0, back_0 = mlp_tail(
        normed_mlp, cot_all, mlp_weights[1], early[0], 0, f32, (inner_1, both_1)
    )

    def line_sum(partial):
        return lax.psum_scatter(partial, "group", scatter_dimension=0, tiled=True)

    mlp_sums = chip_sums((front_0, front_1), (back_0, back_1))
    operands = first_operands(mlp_sums)
    arrived = reduce_first(operands, *second_0)
    late_both = after(both_1, *operands)
    grads_1 = weight_grads((normed_mlp, late_both), (cot_all, inner_1))
    sum_1 = line_sum(after(grads_1, *arrived))
    mlp_operands = reduce_operands(mlp_sums, arrived)
    d_normed = reduce_last(mlp_operands, grads_1)
    cot_f = cotangent.astype(f32)
    scaled = d_normed * gain_mlp
    d_hidden = cot_f + inverse_mlp * (
        scaled - unit_mlp * jnp.mean(scaled * unit_mlp, axis=-1, keepdims=True)
    )
    own_d = d_hidden.astype(bf16)
    for _ in range(groups - 3):
        third_0 = line_0.send((own_d,))
    sum_0 = line_0.send(())
    inners = [after(inner, own_d) for inner in (inner_0, inner_1)]
    out_parts = [
        [chunk_sum(inners, mlp_weights, 2, j, h, bf16 if j else f32) for j in (0, 1)]
        for h in range(2)
    ]
    neighbours = plane_neighbours(own_d)
    d_far = plane_far(neighbours, *out_parts[0], *out_parts[1])
    d_attn_all = pack(with_partner([own_d, *neighbours, *d_far]))
    out_parts = [[part[0], after(part[1], *d_far)] for part in out_parts]
    out_sums = chip_sums(*out_parts)
    out_operands = reduce_operands(out_sums, reduce_first(first_operands(out_sums)))

    def send_grads(reduced, *waits):
        return swap_all(pick_rows(member_at, after(reduced, *waits)))

    final_0 = send_grads(sum_0, *d_far)
    out_grads = weight_grads((d_attn_all, mixed))
    out_sum = line_sum(out_grads)
    d_mixed = product(
        after(d_attn_all, out_grads), attn_weights[:, 3 * HS :]
    ).astype(bf16)
    d_qkv = attention_backward(order, query, keys, vals, logsum, d_mixed, cos, sin)
    qkv_grads = weight_grads((normed_all, d_qkv))
    qkv_sum = line_sum(after(qkv_grads, sum_1))
    late_qkv = after(d_qkv, qkv_grads, *third_0, out_operands[0][1], out_operands[1][1])
    qkv_sums = chip_sums(*projected(late_qkv, 0))
    arrived = reduce_first(first_operands(qkv_sums))
    d_normed = reduce_last(reduce_operands(qkv_sums, arrived))
    block_out = (hidden + reduce_last(out_operands)).astype(bf16)
    scaled = d_normed * gain_attn
    tokens_grad = d_hidden + inverse_attn * (
        scaled - unit_attn * jnp.mean(scaled * unit_attn, axis=-1, keepdims=True)
    )

    final_1 = send_grads(sum_1, *arrived)
    gate_grad, up_grad, down_grad, mlp_gain_row = mlp_final(
        member_at, gate_weight, up_weight, tuple(chunks), [final_0, final_1]
    )
    query_grad, key_grad, value_grad, output_grad, attn_gain_row = attention_final(
        member_at,
        query_weight,
        key_weight,
        value_weight,
        send_grads(qkv_sum),
        send_grads(out_sum, *arrived),
    )
    gain_grads = jnp.concatenate([attn_gain_row, mlp_gain_row], axis=1)
    gain_grads = gain_grads + swap(gain_grads, "tp")
    attn_gain_grad = gain_grads[:, 0] / attn_gain.astype(f32)
    mlp_gain_grad = gain_grads[:, 1] / mlp_gain.astype(f32)

    factor = clip_limit / jnp.maximum(head_top, clip_limit)
    query_scale = jnp.repeat(jnp.sqrt(factor), HS)
    key_factor = jnp.min(factor.reshape(2, 2), axis=1)
    key_scale = jnp.repeat(jnp.sqrt(key_factor), HS)
    query_clipped = (query_weight.astype(f32) * query_scale[None, :]).astype(bf16)
    key_clipped = (key_weight.astype(f32) * key_scale[None, :]).astype(bf16)
    return (
        block_out,
        tokens_grad,
        attn_gain_grad,
        query_grad,
        key_grad,
        value_grad,
        output_grad,
        mlp_gain_grad,
        gate_grad,
        up_grad,
        down_grad,
        head_top,
        query_clipped,
        key_clipped,
    )


def solution(mesh):
    shape = (mesh.shape["fsdp"] // 4, 2, 2, mesh.shape["tp"])
    fine = Mesh(mesh.devices.reshape(shape), ("group", "row", "col", "tp"))
    rows = P(("group", "row", "col", "tp"), None)
    weight = P(FSDP, "tp")
    gain = P(FSDP)
    heads = P("tp")
    return jax.shard_map(
        local,
        mesh=fine,
        in_specs=(
            rows, rows, P(), P(), heads, gain, weight, weight, weight, weight,
            gain, weight, weight, weight,
        ),
        out_specs=(
            rows, rows, gain, weight, weight, weight, weight, gain, weight, weight, weight,
            heads, weight, weight,
        ),
        check_vma=False,
    )
```

```python
import functools

import jax
import jax.numpy as jnp
from jax import lax
from jax.experimental import pallas as pl
from jax.experimental.pallas import tpu as pltpu
from jax.sharding import Mesh, PartitionSpec as P

HS = 256
GROUP = 2048
SIXTEENTHS = (10, 6)
BLOCK = 128

epsilon = 1e-05
theta_base = 1000042.0
masked_value = -1e30

bf16 = jnp.bfloat16
f32 = jnp.float32
PLANE = ("row", "col")
FSDP = ("group", "row", "col")
VMEM_LIMIT = 48 * 1024 * 1024


def product(left, right):
    return jnp.dot(left, right, preferred_element_type=f32)


def times_transposed(left, right):
    return lax.dot_general(left, right, (((1,), (1,)), ((), ())), preferred_element_type=f32)


def outer_sum(left, right):
    return lax.dot_general(left, right, (((0,), (0,)), ((), ())), preferred_element_type=f32)


def take(array, index, axis=0):
    return lax.dynamic_index_in_dim(array, index, axis, keepdims=False)


def swap(block, axis):
    return lax.ppermute(block, axis, [(0, 1), (1, 0)])


def swap_plane(block, distance):
    return lax.ppermute(block, PLANE, [(i, i ^ distance) for i in range(4)])


def after(value, *others):
    return lax.optimization_barrier((value,) + others)[0]


def combine_all(values, groups, combine):
    distance, count = 1, 4 * groups
    rounds = []
    while distance < count:
        arrived = []
        for step in range(1, min(4, count // distance)):
            route = [(i, i ^ step * distance) for i in range(count)]
            arrived.append(lax.ppermute(values, FSDP, route))
        for other in arrived:
            values = combine(values, other)
        rounds.append(arrived)
        distance *= 4
    return values, rounds


def pack_kernel(count, *refs):
    out_ref, sems = refs[count], refs[count + 1]
    copies, start = [], 0
    for i in range(count):
        rows = refs[i].shape[0]
        copy = pltpu.make_async_copy(refs[i], out_ref.at[pl.ds(start, rows)], sems.at[i])
        copy.start()
        copies.append(copy)
        start += rows
    for copy in copies:
        copy.wait()


def pack(pieces):
    rows, width = sum(p.shape[0] for p in pieces), pieces[0].shape[1]
    count = len(pieces)
    return pl.pallas_call(
        functools.partial(pack_kernel, count),
        in_specs=[pl.BlockSpec(memory_space=pl.ANY)] * count,
        out_specs=pl.BlockSpec(memory_space=pltpu.VMEM),
        out_shape=jax.ShapeDtypeStruct((rows, width), pieces[0].dtype),
        scratch_shapes=[pltpu.SemaphoreType.DMA((count,))],
        cost_estimate=pl.CostEstimate(
            flops=0, bytes_accessed=4 * rows * width, transcendentals=0
        ),
        compiler_params=pltpu.CompilerParams(vmem_limit_bytes=VMEM_LIMIT),
        name="pack",
    )(*pieces)


def norm_kernel(count, *refs):
    gain_ref, out_ref = refs[count], refs[count + 1]
    pack_kernel(count, *refs[:count], *refs[count + 1 :])
    tile = 256

    @pl.loop(0, out_ref.shape[0] // tile)
    def _(i):
        rows = pl.ds(pl.multiple_of(i * tile, tile), tile)
        values = out_ref[rows, :].astype(f32)
        out_ref[rows, :] = (values * rms_inverse(values) * gain_ref[...]).astype(bf16)


def pack_normed(pieces, gain):
    rows, width = sum(p.shape[0] for p in pieces), pieces[0].shape[1]
    count = len(pieces)
    return pl.pallas_call(
        functools.partial(norm_kernel, count),
        in_specs=[pl.BlockSpec(memory_space=pl.ANY)] * count
        + [pl.BlockSpec(memory_space=pltpu.VMEM)],
        out_specs=pl.BlockSpec(memory_space=pltpu.VMEM),
        out_shape=jax.ShapeDtypeStruct((rows, width), bf16),
        scratch_shapes=[pltpu.SemaphoreType.DMA((count,))],
        cost_estimate=pl.CostEstimate(
            flops=8 * rows * width, bytes_accessed=4 * rows * width, transcendentals=0
        ),
        compiler_params=pltpu.CompilerParams(vmem_limit_bytes=VMEM_LIMIT),
        name="pack_normed",
    )(*pieces, gain)


def plane_neighbours(own):
    return swap(own, "col"), swap(own, "row")


def plane_far(neighbours, *waits):
    across, along = neighbours
    half = across.shape[0] // 2
    return (
        swap(after(across[:half], *waits), "row"),
        swap(after(along[half:], *waits), "col"),
    )


def with_partner(pieces, swapped=()):
    return pieces + list(swapped) + [swap(piece, "tp") for piece in pieces[len(swapped) :]]


def chip_sums(front, back):
    totals = []
    for own, other in (front, back):
        total = own.astype(f32) + swap(other, "tp").astype(f32)
        totals.append(total.reshape((4, total.shape[0] // 4, total.shape[1])))
    return totals


def first_operands(totals):
    first, second = totals
    return jnp.stack([first[1], first[3]]).astype(bf16), second[2:].astype(bf16)


def reduce_first(operands, *waits):
    front, back = operands
    return swap(after(front, *waits), "col"), swap(after(back, *waits), "row")


def reduce_operands(totals, arrived):
    first, second = totals
    got, got_second = arrived[0].astype(f32), arrived[1].astype(f32)
    return (
        (first[0] + got[0], (first[2] + got[1]).astype(bf16)),
        (second[0] + got_second[0], (second[1] + got_second[1]).astype(bf16)),
    )


def last_swaps(operands, *waits):
    return (
        swap(after(operands[0][1], *waits), "row"),
        swap(after(operands[1][1], *waits), "col"),
    )


def reduce_last(operands, *waits, swapped=None):
    swapped = swapped or last_swaps(operands, *waits)
    return jnp.concatenate(
        [keep + last.astype(f32) for (keep, _), last in zip(operands, swapped)], axis=1
    )


def line_reduce(blocks, groups, index):
    up = down = None
    waits = yield
    for step in range(1, groups):
        out_up = take(blocks, jnp.minimum(index + groups - step, groups - 1))
        out_down = take(blocks, jnp.maximum(index - groups + step, 0))
        out_up, out_down = after(out_up, *waits), after(out_down, *waits)
        if up is not None:
            out_up = (out_up.astype(f32) + up.astype(f32)).astype(bf16)
            out_down = (out_down.astype(f32) + down.astype(f32)).astype(bf16)
        senders = range(min(step, groups - 1))
        up = lax.ppermute(out_up, "group", [(j, j + 1) for j in senders])
        down = lax.ppermute(
            out_down, "group", [(groups - 1 - j, groups - 2 - j) for j in senders]
        )
        waits = yield up, down
    total = take(blocks, index).astype(f32) + up.astype(f32) + down.astype(f32)
    yield total.astype(bf16)


def split_kernel(spans, member_ref, *refs):
    sources, outs = refs[: len(spans)], refs[len(spans) :]
    for k in range(4):
        target = member_ref[0] ^ k
        column = 0
        for source, (offset, stride, width, shift) in zip(sources, spans):
            start = pl.multiple_of((target >> shift) * stride + offset, 128)
            outs[k][:, column : column + width] = source[:, pl.ds(start, width)]
            column += width


def split(member, sources, spans):
    rows, width = sources[0].shape[0], sum(span[2] for span in spans)
    whole = pl.BlockSpec(memory_space=pltpu.VMEM)
    return pl.pallas_call(
        functools.partial(split_kernel, spans),
        in_specs=[pl.BlockSpec(memory_space=pltpu.SMEM)] + [whole] * len(sources),
        out_specs=[whole] * 4,
        out_shape=[jax.ShapeDtypeStruct((rows, width), bf16)] * 4,
        cost_estimate=pl.CostEstimate(
            flops=0, bytes_accessed=16 * rows * width, transcendentals=0
        ),
        compiler_params=pltpu.CompilerParams(vmem_limit_bytes=VMEM_LIMIT),
        name="split",
    )(member, *sources)


def place_kernel(member_ref, *refs):
    rows = refs[0].shape[0]
    for k in range(4):
        start = pl.multiple_of((member_ref[0] ^ k) * rows, rows)
        refs[4][pl.ds(start, rows), :] = refs[k][...]


def place_rows(member, pieces):
    rows, width = pieces[0].shape
    whole = pl.BlockSpec(memory_space=pltpu.VMEM)
    return pl.pallas_call(
        place_kernel,
        in_specs=[pl.BlockSpec(memory_space=pltpu.SMEM)] + [whole] * 4,
        out_specs=whole,
        out_shape=jax.ShapeDtypeStruct((4 * rows, width), bf16),
        cost_estimate=pl.CostEstimate(
            flops=0, bytes_accessed=16 * rows * width, transcendentals=0
        ),
        compiler_params=pltpu.CompilerParams(vmem_limit_bytes=VMEM_LIMIT),
        name="place_rows",
    )(member, *pieces)


def pick_kernel(member_ref, source_ref, *outs):
    rows = outs[0].shape[0]
    for k in range(4):
        start = pl.multiple_of((member_ref[0] ^ k) * rows, rows)
        outs[k][...] = source_ref[pl.ds(start, rows), :]


def pick_rows(member, source):
    rows, width = source.shape[0] // 4, source.shape[1]
    whole = pl.BlockSpec(memory_space=pltpu.VMEM)
    return pl.pallas_call(
        pick_kernel,
        in_specs=[pl.BlockSpec(memory_space=pltpu.SMEM), whole],
        out_specs=[whole] * 4,
        out_shape=[jax.ShapeDtypeStruct((rows, width), bf16)] * 4,
        cost_estimate=pl.CostEstimate(
            flops=0, bytes_accessed=16 * rows * width, transcendentals=0
        ),
        compiler_params=pltpu.CompilerParams(vmem_limit_bytes=VMEM_LIMIT),
        name="pick_rows",
    )(member, source)


def swap_all(pieces):
    return [pieces[0]] + [swap_plane(pieces[k], k) for k in (1, 2, 3)]


def mlp_final_kernel(chunks, stride, member_ref, gate_w_ref, up_w_ref, *refs):
    pieces, outs, gain_ref = refs[:-4], refs[-4:-1], refs[-1]
    for n, (offset, width) in enumerate(chunks):
        for k in range(4):
            column = pl.multiple_of((member_ref[0] ^ k) * stride + offset, 128)
            for i in range(3):
                part = pieces[4 * n + k][:, i * width : (i + 1) * width]
                outs[i][:, pl.ds(column, width)] = part.astype(f32)
    gain_ref[...] = jnp.sum(
        gate_w_ref[...].astype(f32) * outs[0][...] + up_w_ref[...].astype(f32) * outs[1][...],
        axis=1,
        keepdims=True,
    )


def mlp_final(member, gate_weight, up_weight, chunks, parts):
    rows, hidden = gate_weight.shape
    pieces = [piece for part in parts for piece in part]
    whole = pl.BlockSpec(memory_space=pltpu.VMEM)
    return pl.pallas_call(
        functools.partial(mlp_final_kernel, chunks, hidden // 4),
        in_specs=[pl.BlockSpec(memory_space=pltpu.SMEM)] + [whole] * (2 + len(pieces)),
        out_specs=[whole] * 4,
        out_shape=[jax.ShapeDtypeStruct((rows, hidden), f32)] * 3
        + [jax.ShapeDtypeStruct((rows, 1), f32)],
        cost_estimate=pl.CostEstimate(
            flops=4 * rows * hidden, bytes_accessed=22 * rows * hidden, transcendentals=0
        ),
        compiler_params=pltpu.CompilerParams(vmem_limit_bytes=VMEM_LIMIT),
        name="mlp_final",
    )(member, gate_weight, up_weight, *pieces)


def attention_final_kernel(member_ref, qw_ref, kw_ref, vw_ref, *refs):
    qkv, out = refs[:4], refs[4:8]
    q_ref, k_ref, v_ref, o_ref, gain_ref = refs[8:]
    member = member_ref[0]
    for k in range(4):
        columns = pl.ds(pl.multiple_of((member ^ k) * HS, HS), HS)
        q_ref[:, columns] = qkv[k][:, :HS].astype(f32)
        o_ref[:, columns] = out[k][...].astype(f32)
    for h in range(2):
        columns = pl.ds(pl.multiple_of(((member >> 1) ^ h) * HS, HS), HS)
        both = qkv[2 * h][:, HS:].astype(f32) + qkv[2 * h + 1][:, HS:].astype(f32)
        k_ref[:, columns] = both[:, :HS]
        v_ref[:, columns] = both[:, HS:]

    def row_sum(weight_ref, grad_ref):
        return jnp.sum(weight_ref[...].astype(f32) * grad_ref[...], axis=1, keepdims=True)

    gain_ref[...] = row_sum(qw_ref, q_ref) + row_sum(kw_ref, k_ref) + row_sum(vw_ref, v_ref)


def attention_final(member, query_weight, key_weight, value_weight, qkv, out):
    rows, width = query_weight.shape
    whole = pl.BlockSpec(memory_space=pltpu.VMEM)
    shapes = [width, width // 2, width // 2, width, 1]
    return pl.pallas_call(
        attention_final_kernel,
        in_specs=[pl.BlockSpec(memory_space=pltpu.SMEM)] + [whole] * 11,
        out_specs=[whole] * 5,
        out_shape=[jax.ShapeDtypeStruct((rows, n), f32) for n in shapes],
        cost_estimate=pl.CostEstimate(
            flops=4 * rows * width, bytes_accessed=24 * rows * width, transcendentals=0
        ),
        compiler_params=pltpu.CompilerParams(vmem_limit_bytes=VMEM_LIMIT),
        name="attention_final",
    )(member, query_weight, key_weight, value_weight, *qkv, *out)


def rms_inverse(values):
    return lax.rsqrt(jnp.mean(values * values, axis=-1, keepdims=True) + epsilon)


def rope_tables(positions):
    half_size = HS // 2
    indices = jnp.arange(half_size, dtype=f32)
    inverse = theta_base ** (-2.0 * indices / HS)
    angles = positions.astype(f32)[:, None] * inverse[None, :]
    return jnp.cos(angles), jnp.sin(angles)


def rotate(vectors, cos, sin):
    front, back = vectors[:, : HS // 2], vectors[:, HS // 2 :]
    return jnp.concatenate([front * cos - back * sin, back * cos + front * sin], axis=-1)


def unrotate(grads, cos, sin):
    front, back = grads[:, : HS // 2], grads[:, HS // 2 :]
    return jnp.concatenate([front * cos + back * sin, back * cos - front * sin], axis=-1)


def mlp_tile(width, normed, cot, weight_ref):
    both = product(normed, weight_ref[:, : 2 * width])
    d_inner = product(cot, weight_ref[:, 2 * width :])
    gate, upward = both[:, :width], both[:, width:]
    sig = 1.0 / (1.0 + jnp.exp(-gate))
    silu = gate * sig
    d_gate = d_inner * upward * sig * (1.0 + gate * (1.0 - sig))
    return (
        (silu * upward).astype(bf16),
        jnp.concatenate([d_gate, d_inner * silu], axis=1).astype(bf16),
    )


def mlp_kernel(width, normed_ref, cot_ref, weight_ref, inner_ref, grads_ref):
    inner_ref[...], grads_ref[...] = mlp_tile(
        width, normed_ref[...], cot_ref[...], weight_ref
    )


def tail_kernel(width, normed_ref, cot_ref, weight_ref, base_ref, *refs):
    inner_ref, grads_ref, front_ref, back_ref = refs[-4:]
    inner, grads = mlp_tile(width, normed_ref[...], cot_ref[...], weight_ref)
    inner_ref[...], grads_ref[...] = inner, grads
    total = times_transposed(grads, weight_ref[:, : 2 * width]) + base_ref[...]
    half = total.shape[1] // 2
    front_ref[...] = total[:, :half].astype(front_ref.dtype)
    back_ref[...] = total[:, half:].astype(back_ref.dtype)


def mlp_tail(normed, cot, weight, base, part, dtype, chained=()):
    tokens, features = normed.shape
    width = weight.shape[1] // 3
    tile, rows = 256, tokens // 2
    steps = rows // tile
    count = len(chained)
    return pl.pallas_call(
        functools.partial(tail_kernel, width),
        grid=(steps,),
        in_specs=[
            pl.BlockSpec((tile, features), lambda i: (part * steps + i, 0)),
            pl.BlockSpec((tile, features), lambda i: (part * steps + i, 0)),
            pl.BlockSpec((features, 3 * width), lambda i: (0, 0)),
            pl.BlockSpec((tile, features), lambda i: (i, 0)),
        ]
        + [pl.BlockSpec(memory_space=pl.ANY)] * count,
        out_specs=[
            pl.BlockSpec((tile, width), lambda i: (part * steps + i, 0)),
            pl.BlockSpec((tile, 2 * width), lambda i: (part * steps + i, 0)),
            pl.BlockSpec((tile, features // 2), lambda i: (i, 0)),
            pl.BlockSpec((tile, features // 2), lambda i: (i, 0)),
        ],
        out_shape=[
            jax.ShapeDtypeStruct((tokens, width), bf16),
            jax.ShapeDtypeStruct((tokens, 2 * width), bf16),
            jax.ShapeDtypeStruct((rows, features // 2), dtype),
            jax.ShapeDtypeStruct((rows, features // 2), dtype),
        ],
        input_output_aliases={4 + i: i for i in range(count)},
        cost_estimate=pl.CostEstimate(
            flops=10 * rows * features * width,
            bytes_accessed=2 * features * (5 * rows + 3 * width),
            transcendentals=rows * width,
        ),
        compiler_params=pltpu.CompilerParams(vmem_limit_bytes=VMEM_LIMIT),
        name="mlp_tail",
    )(normed, cot, weight, base, *chained)


def mlp_chunk(normed, cot, weight):
    tokens, features = normed.shape
    width = weight.shape[1] // 3
    tile = 256
    return pl.pallas_call(
        functools.partial(mlp_kernel, width),
        grid=(tokens // tile,),
        in_specs=[
            pl.BlockSpec((tile, features), lambda i: (i, 0)),
            pl.BlockSpec((tile, features), lambda i: (i, 0)),
            pl.BlockSpec((features, 3 * width), lambda i: (0, 0)),
        ],
        out_specs=[
            pl.BlockSpec((tile, width), lambda i: (i, 0)),
            pl.BlockSpec((tile, 2 * width), lambda i: (i, 0)),
        ],
        out_shape=[
            jax.ShapeDtypeStruct((tokens, width), bf16),
            jax.ShapeDtypeStruct((tokens, 2 * width), bf16),
        ],
        cost_estimate=pl.CostEstimate(
            flops=6 * tokens * features * width,
            bytes_accessed=2 * features * (2 * tokens + 3 * width),
            transcendentals=tokens * width,
        ),
        compiler_params=pltpu.CompilerParams(vmem_limit_bytes=VMEM_LIMIT),
        name="mlp_chunk",
    )(normed, cot, weight)


def sum_kernel(count, *refs):
    lefts, rights, out_ref = refs[:count], refs[count : 2 * count], refs[-1]
    total = times_transposed(lefts[0][...], rights[0][...])
    for left, right in zip(lefts[1:], rights[1:]):
        total += times_transposed(left[...], right[...])
    for base in refs[2 * count : -1]:
        total += base[...].astype(f32)
    out_ref[...] = total.astype(out_ref.dtype)


def chunk_sum(lefts, rights, column, part, half, dtype):
    count = len(lefts)
    tokens, features = lefts[0].shape[0], rights[0].shape[0]
    widths = [left.shape[1] for left in lefts]
    rows = tokens // 2
    tile = 256
    if half is not None:
        features, tile = features // 2, 512
    steps = rows // tile
    block = half or 0
    return pl.pallas_call(
        functools.partial(sum_kernel, count),
        grid=(steps,),
        in_specs=[pl.BlockSpec((tile, w), lambda i: (part * steps + i, 0)) for w in widths]
        + [pl.BlockSpec((features, w), lambda i: (block, column)) for w in widths],
        out_specs=pl.BlockSpec((tile, features), lambda i: (i, 0)),
        out_shape=jax.ShapeDtypeStruct((rows, features), dtype),
        cost_estimate=pl.CostEstimate(
            flops=2 * rows * features * sum(widths),
            bytes_accessed=2 * sum(widths) * (rows + features) + 4 * rows * features,
            transcendentals=0,
        ),
        compiler_params=pltpu.CompilerParams(vmem_limit_bytes=VMEM_LIMIT),
        name="chunk_sum",
    )(*lefts, *rights)


def grads_kernel(count, *refs):
    column = 0
    for left, right in zip(refs[:count], refs[count : 2 * count]):
        width = right.shape[1]
        refs[-1][:, column : column + width] = outer_sum(left[...], right[...]).astype(bf16)
        column += width


def weight_grads(*pairs):
    lefts, rights = [left for left, _ in pairs], [right for _, right in pairs]
    count = len(pairs)
    tokens, features = lefts[0].shape
    widths = [right.shape[1] for right in rights]
    tile = 256
    return pl.pallas_call(
        functools.partial(grads_kernel, count),
        grid=(features // tile,),
        in_specs=[pl.BlockSpec((tokens, tile), lambda i: (0, i))] * count
        + [pl.BlockSpec((tokens, w), lambda i: (0, 0)) for w in widths],
        out_specs=pl.BlockSpec((tile, sum(widths)), lambda i: (i, 0)),
        out_shape=jax.ShapeDtypeStruct((features, sum(widths)), bf16),
        cost_estimate=pl.CostEstimate(
            flops=2 * tokens * features * sum(widths),
            bytes_accessed=2 * (count * tokens * features + sum(widths) * (tokens + features)),
            transcendentals=0,
        ),
        compiler_params=pltpu.CompilerParams(vmem_limit_bytes=VMEM_LIMIT),
        name="weight_grads",
    )(*lefts, *rights)


def project_kernel(place_ref, normed_ref, weight_ref, cos_ref, sin_ref, q_ref, k_ref, v_ref):
    step = pl.program_id(0)
    cos, sin = cos_ref[...], sin_ref[...]
    qkv = product(normed_ref[...], weight_ref[...])
    query = rotate(qkv[:, :HS], cos, sin).astype(bf16) * HS ** (-0.5)
    keys = rotate(qkv[:, HS : 2 * HS], cos, sin).astype(bf16)
    vals = qkv[:, 2 * HS :].astype(bf16)
    blocks = normed_ref.shape[0] // BLOCK
    for b in range(blocks):
        rows = pl.ds(pl.multiple_of(place_ref[step * blocks + b] * BLOCK, BLOCK), BLOCK)
        part = slice(b * BLOCK, (b + 1) * BLOCK)
        q_ref[rows, :] = query[part]
        k_ref[rows, :] = keys[part]
        v_ref[rows, :] = vals[part]


def project(place, normed, weight, cos, sin):
    tokens, features = normed.shape
    tile = 256
    whole = pl.BlockSpec((tokens, HS), lambda i, place: (0, 0))
    return pl.pallas_call(
        project_kernel,
        grid_spec=pltpu.PrefetchScalarGridSpec(
            num_scalar_prefetch=1,
            grid=(tokens // tile,),
            in_specs=[
                pl.BlockSpec((tile, features), lambda i, place: (i, 0)),
                pl.BlockSpec((features, 3 * HS), lambda i, place: (0, 0)),
                pl.BlockSpec((tile, HS // 2), lambda i, place: (i, 0)),
                pl.BlockSpec((tile, HS // 2), lambda i, place: (i, 0)),
            ],
            out_specs=[whole] * 3,
        ),
        out_shape=[jax.ShapeDtypeStruct((tokens, HS), bf16)] * 3,
        cost_estimate=pl.CostEstimate(
            flops=6 * tokens * features * HS,
            bytes_accessed=2 * features * (tokens + 3 * HS) + 10 * tokens * HS,
            transcendentals=0,
        ),
        compiler_params=pltpu.CompilerParams(vmem_limit_bytes=VMEM_LIMIT),
        name="project",
    )(place, normed, weight, cos, sin)


TILE = 256


def tile_masks():
    rows = lax.broadcasted_iota(jnp.int32, (TILE, TILE), 0)
    cols = lax.broadcasted_iota(jnp.int32, (TILE, TILE), 1)
    causal = rows >= cols
    return causal, causal & (rows // BLOCK == cols // BLOCK)


def block_rows(order_ref, index):
    return pl.ds(pl.multiple_of(order_ref[index] * BLOCK, BLOCK), BLOCK)


def forward_kernel(order_ref, q_ref, k_ref, v_ref, mixed_ref, lse_ref, peak_ref):
    causal, inside = tile_masks()
    prompt = GROUP // 2
    top = jnp.full((TILE, 1), masked_value, f32)
    for i in range(GROUP // TILE):
        rows = slice(i * TILE, (i + 1) * TILE)
        past = min(i * TILE, prompt)
        query = q_ref[rows, :]
        near = times_transposed(query, k_ref[rows, :])
        near = jnp.where(causal if i * TILE < prompt else inside, near, masked_value)
        peak = jnp.max(near, axis=1, keepdims=True)
        if past:
            far = times_transposed(query, k_ref[:past, :])
            peak = jnp.maximum(peak, jnp.max(far, axis=1, keepdims=True))
            far = jnp.exp(far - peak)
        near = jnp.exp(near - peak)
        total = jnp.sum(near, axis=1, keepdims=True)
        if past:
            total += jnp.sum(far, axis=1, keepdims=True)
        share = 1.0 / total
        mixed = product((near * share).astype(bf16), v_ref[rows, :])
        if past:
            mixed += product((far * share).astype(bf16), v_ref[:past, :])
        mixed = mixed.astype(bf16)
        for b in range(TILE // BLOCK):
            mixed_ref[block_rows(order_ref, i * (TILE // BLOCK) + b), :] = mixed[
                b * BLOCK : (b + 1) * BLOCK
            ]
        lse_ref[rows, :] = peak + jnp.log(total)
        top = jnp.maximum(top, peak)
    peak_ref[...] = jnp.full(peak_ref.shape, jnp.max(top), f32)


def attention_forward(order, query, keys, vals):
    whole = pl.BlockSpec(memory_space=pltpu.VMEM)
    return pl.pallas_call(
        forward_kernel,
        in_specs=[pl.BlockSpec(memory_space=pltpu.SMEM), whole, whole, whole],
        out_specs=[whole] * 3,
        out_shape=[
            jax.ShapeDtypeStruct((GROUP, HS), bf16),
            jax.ShapeDtypeStruct((GROUP, 1), f32),
            jax.ShapeDtypeStruct((8, 128), f32),
        ],
        cost_estimate=pl.CostEstimate(
            flops=2 * GROUP * GROUP * HS,
            bytes_accessed=8 * GROUP * HS,
            transcendentals=GROUP * GROUP // 2,
        ),
        compiler_params=pltpu.CompilerParams(vmem_limit_bytes=VMEM_LIMIT),
        name="attention_forward",
    )(order, query, keys, vals)


def backward_kernel(
    order_ref, q_ref, k_ref, v_ref, lse_ref, mixed_ref, cos_ref, sin_ref, out_ref, dk_ref, dv_ref
):
    causal, inside = tile_masks()
    prompt = GROUP // 2
    blocks = TILE // BLOCK

    def back(grad, index):
        rows = block_rows(order_ref, index)
        return rows, unrotate(grad, cos_ref[rows, :], sin_ref[rows, :]).astype(bf16)

    for i in range(GROUP // TILE):
        rows = slice(i * TILE, (i + 1) * TILE)
        past = min(i * TILE, prompt)
        query, lse = q_ref[rows, :], lse_ref[rows, :]
        d_mixed = jnp.concatenate(
            [mixed_ref[block_rows(order_ref, i * blocks + b), :] for b in range(blocks)], axis=0
        )
        near = times_transposed(query, k_ref[rows, :])
        near = jnp.where(causal if i * TILE < prompt else inside, near, masked_value)
        near = jnp.exp(near - lse)
        d_near = times_transposed(d_mixed, v_ref[rows, :])
        inner = jnp.sum(near * d_near, axis=1, keepdims=True)
        if past:
            far = jnp.exp(times_transposed(query, k_ref[:past, :]) - lse)
            d_far = times_transposed(d_mixed, v_ref[:past, :])
            inner += jnp.sum(far * d_far, axis=1, keepdims=True)
        d_near = (near * (d_near - inner)).astype(bf16)
        d_query = product(d_near, k_ref[rows, :])
        dk_ref[rows, :] = outer_sum(d_near, query)
        dv_ref[rows, :] = outer_sum(near.astype(bf16), d_mixed)
        if past:
            d_far = (far * (d_far - inner)).astype(bf16)
            d_query += product(d_far, k_ref[:past, :])
            dk_ref[:past, :] += outer_sum(d_far, query)
            dv_ref[:past, :] += outer_sum(far.astype(bf16), d_mixed)
        d_query = d_query * HS ** (-0.5)
        for b in range(blocks):
            where, grad = back(d_query[b * BLOCK : (b + 1) * BLOCK], i * blocks + b)
            out_ref[where, :HS] = grad
    for c in range(GROUP // BLOCK):
        part = slice(c * BLOCK, (c + 1) * BLOCK)
        where, grad = back(dk_ref[part, :], c)
        out_ref[where, HS : 2 * HS] = grad
        out_ref[where, 2 * HS :] = dv_ref[part, :].astype(bf16)


def attention_backward(order, query, keys, vals, lse, d_mixed, cos, sin):
    whole = pl.BlockSpec(memory_space=pltpu.VMEM)
    return pl.pallas_call(
        backward_kernel,
        in_specs=[pl.BlockSpec(memory_space=pltpu.SMEM)] + [whole] * 7,
        out_specs=whole,
        out_shape=jax.ShapeDtypeStruct((GROUP, 3 * HS), bf16),
        scratch_shapes=[pltpu.VMEM((GROUP, HS), f32), pltpu.VMEM((GROUP, HS), f32)],
        cost_estimate=pl.CostEstimate(
            flops=5 * GROUP * GROUP * HS,
            bytes_accessed=20 * GROUP * HS,
            transcendentals=GROUP * GROUP // 2,
        ),
        compiler_params=pltpu.CompilerParams(vmem_limit_bytes=VMEM_LIMIT),
        name="attention_backward",
    )(order, query, keys, vals, lse, d_mixed, cos, sin)


def local(
    tokens,
    cotangent,
    segment,
    position,
    clip_limit,
    attn_gain,
    query_weight,
    key_weight,
    value_weight,
    output_weight,
    mlp_gain,
    gate_weight,
    up_weight,
    down_weight,
):
    groups = lax.axis_size("group")
    group = lax.axis_index("group")
    core = lax.axis_index("tp")
    member = lax.axis_index(PLANE)
    token_rows = tokens.shape[0]
    own_rows, features = query_weight.shape[0], tokens.shape[1]
    hidden_own = gate_weight.shape[1] // 4
    chunks, offset = [], 0
    for part in SIXTEENTHS:
        chunks.append((offset, hidden_own * part // 16))
        offset += hidden_own * part // 16
    member_at = member.astype(jnp.int32).reshape(1)

    def own_order(array):
        parts = []
        for j in range(2):
            for k in range(4):
                start = group * GROUP + (member ^ k) * (2 * token_rows) + (core ^ j) * token_rows
                parts.append(lax.dynamic_slice_in_dim(array, start, token_rows))
        return jnp.concatenate(parts)

    def collect(blocks):
        return lax.all_gather(blocks, "group", axis=0, tiled=True)

    def mlp_exchange(chunk, waits):
        weights = [after(a, *waits) for a in (gate_weight, up_weight, down_weight)]
        spans = ((chunk[0], hidden_own, chunk[1], 0),) * 3
        return swap_all(split(member_at, weights, spans))

    index = lax.axis_index(FSDP)
    gains = jnp.stack([attn_gain, mlp_gain])[:, None, :]
    gains = jnp.where(jnp.arange(4 * groups)[None, :, None] == index, gains, 0)
    gains, gain_rounds = combine_all(gains, groups, lambda a, b: a + b)
    gains = gains.reshape(2, features).astype(f32)
    head, pair = (0, HS, HS, 0), (0, HS, HS, 1)
    attn_pieces = swap_all(
        split(
            member_at,
            (query_weight, key_weight, value_weight, output_weight),
            (head, pair, pair, head),
        )
    )
    attn_weights = collect(
        place_rows(member_at, [after(attn_pieces[0], *gain_rounds[0])] + attn_pieces[1:])
    )
    late_tokens = after(tokens, *attn_pieces[1:], *gain_rounds[-1])
    neighbours = plane_neighbours(late_tokens)
    tokens_far = plane_far(neighbours)
    tokens_mine = [late_tokens, *neighbours, *tokens_far]
    tokens_near = [swap(piece, "tp") for piece in tokens_mine[:3]]
    normed_all = pack_normed(with_partner(tokens_mine, tokens_near), gains[:1])
    pieces_0 = mlp_exchange(chunks[0], (*tokens_far, *tokens_near))
    late_cot = after(cotangent, *pieces_0[1:])
    cot_near = [swap_plane(late_cot, k) for k in (1, 2)]
    gain_attn, gain_mlp = gains[0], gains[1]

    tokens_f = tokens.astype(f32)
    inverse_attn = rms_inverse(tokens_f)
    unit_attn = tokens_f * inverse_attn
    seg, pos = own_order(segment), own_order(position)
    cos, sin = rope_tables(pos)
    seg_blocks, pos_blocks = seg[::BLOCK], pos[::BLOCK]
    half_blocks = GROUP // BLOCK // 2
    place = jnp.where(seg_blocks == 0, pos_blocks // BLOCK, half_blocks - 1 + seg_blocks)
    labels = jnp.arange(2 * half_blocks, dtype=jnp.int32)
    order = jnp.sum(jnp.where(place[None, :] == labels[:, None], labels[None, :], 0), axis=1)
    query, keys, vals = project(
        place, after(normed_all, *pieces_0[1:]), attn_weights, cos, sin
    )
    mixed, logsum, peak = attention_forward(order, after(query, *cot_near), keys, vals)

    head_top = jnp.where(jnp.arange(4) == member, peak[0, :4], masked_value)
    head_top, _ = combine_all(head_top, groups, jnp.maximum)

    def projected(left, column, *waits):
        lefts = (after(left, *waits), left)
        return [
            [
                chunk_sum([lefts[j]], [attn_weights], column, j, h, bf16 if j else f32)
                for j in (0, 1)
            ]
            for h in range(2)
        ]

    attn_sums = chip_sums(*projected(mixed, 3))
    arrived = reduce_first(first_operands(attn_sums))
    attn_operands = reduce_operands(attn_sums, arrived)
    hidden = tokens_f + reduce_last(attn_operands)
    inverse_mlp = rms_inverse(hidden)
    unit_mlp = hidden * inverse_mlp
    own_normed = (unit_mlp * gain_mlp).astype(bf16)
    neighbours = plane_neighbours(own_normed)
    normed_far = plane_far(neighbours)
    pieces_1 = mlp_exchange(chunks[1], normed_far)
    mlp_weights = [
        collect(place_rows(member_at, pieces)) for pieces in (pieces_0, pieces_1)
    ]
    cot_far = swap_plane(after(late_cot, *normed_far), 3)
    normed_mlp = pack(with_partner([own_normed, *neighbours, *normed_far]))
    cot_all = pack(with_partner([late_cot, *cot_near, cot_far]))

    inner_0, both_0 = mlp_chunk(normed_mlp, cot_all, mlp_weights[0])
    grads_0 = weight_grads((normed_mlp, both_0), (cot_all, inner_0))
    blocks_0 = grads_0.reshape(groups, 4 * own_rows, grads_0.shape[1])
    late_both = after(both_0, grads_0)
    early = [chunk_sum([late_both], mlp_weights[:1], 0, j, None, f32) for j in range(2)]
    inner_1, both_1, front_1, back_1 = mlp_tail(
        after(normed_mlp, *early), cot_all, mlp_weights[1], early[1], 1, bf16
    )
    line_0 = line_reduce(blocks_0, groups, group)
    next(line_0)
    line_0.send(())
    second_0 = line_0.send((front_1,))
    inner_1, both_1, front_0, back_0 = mlp_tail(
        normed_mlp, cot_all, mlp_weights[1], early[0], 0, f32, (inner_1, both_1)
    )

    def line_sum(partial):
        return lax.psum_scatter(partial, "group", scatter_dimension=0, tiled=True)

    mlp_sums = chip_sums((front_0, front_1), (back_0, back_1))
    operands = first_operands(mlp_sums)
    arrived = reduce_first(operands)
    late_both = after(both_1, *arrived, *second_0)
    grads_1 = weight_grads((normed_mlp, late_both), (cot_all, inner_1))
    sum_1 = line_sum(grads_1)
    mlp_operands = reduce_operands(mlp_sums, arrived)
    d_normed = reduce_last(mlp_operands)
    cot_f = cotangent.astype(f32)
    scaled = d_normed * gain_mlp
    d_hidden = cot_f + inverse_mlp * (
        scaled - unit_mlp * jnp.mean(scaled * unit_mlp, axis=-1, keepdims=True)
    )
    own_d = d_hidden.astype(bf16)
    for _ in range(groups - 3):
        third_0 = line_0.send((own_d,))
    sum_0 = line_0.send(())
    inners = [after(inner, own_d, grads_1) for inner in (inner_0, inner_1)]
    out_parts = [
        [chunk_sum(inners, mlp_weights, 2, j, h, bf16 if j else f32) for j in (0, 1)]
        for h in range(2)
    ]
    neighbours = plane_neighbours(own_d)
    d_far = plane_far(neighbours, *out_parts[0], *out_parts[1])
    d_attn_all = pack(with_partner([own_d, *neighbours, *d_far]))
    out_parts = [[part[0], after(part[1], *d_far)] for part in out_parts]
    out_sums = chip_sums(*out_parts)
    out_operands = reduce_operands(out_sums, reduce_first(first_operands(out_sums)))

    def send_grads(reduced, *waits):
        return swap_all(pick_rows(member_at, after(reduced, *waits)))


    out_grads = weight_grads((d_attn_all, mixed))
    out_sum = line_sum(out_grads)
    d_mixed = product(
        after(d_attn_all, out_grads), attn_weights[:, 3 * HS :]
    ).astype(bf16)
    d_qkv = attention_backward(order, query, keys, vals, logsum, d_mixed, cos, sin)
    qkv_grads = weight_grads((normed_all, d_qkv))
    qkv_sum = line_sum(after(qkv_grads, sum_1))
    out_last = last_swaps(out_operands)
    late_qkv = after(d_qkv, qkv_grads, *third_0, *out_last)
    qkv_sums = chip_sums(*projected(late_qkv, 0))
    arrived = reduce_first(first_operands(qkv_sums))
    d_normed = reduce_last(reduce_operands(qkv_sums, arrived))
    block_out = (hidden + reduce_last(out_operands, swapped=out_last)).astype(bf16)
    scaled = d_normed * gain_attn
    tokens_grad = d_hidden + inverse_attn * (
        scaled - unit_attn * jnp.mean(scaled * unit_attn, axis=-1, keepdims=True)
    )

    final_0 = send_grads(sum_0, *arrived)
    final_1 = send_grads(sum_1, *arrived)
    gate_grad, up_grad, down_grad, mlp_gain_row = mlp_final(
        member_at, gate_weight, up_weight, tuple(chunks), [final_0, final_1]
    )
    query_grad, key_grad, value_grad, output_grad, attn_gain_row = attention_final(
        member_at,
        query_weight,
        key_weight,
        value_weight,
        send_grads(qkv_sum),
        send_grads(out_sum, *arrived),
    )
    gain_grads = jnp.concatenate([attn_gain_row, mlp_gain_row], axis=1)
    gain_grads = gain_grads + swap(gain_grads, "tp")
    attn_gain_grad = gain_grads[:, 0] / attn_gain.astype(f32)
    mlp_gain_grad = gain_grads[:, 1] / mlp_gain.astype(f32)

    factor = clip_limit / jnp.maximum(head_top, clip_limit)
    query_scale = jnp.repeat(jnp.sqrt(factor), HS)
    key_factor = jnp.min(factor.reshape(2, 2), axis=1)
    key_scale = jnp.repeat(jnp.sqrt(key_factor), HS)
    query_clipped = (query_weight.astype(f32) * query_scale[None, :]).astype(bf16)
    key_clipped = (key_weight.astype(f32) * key_scale[None, :]).astype(bf16)
    return (
        block_out,
        tokens_grad,
        attn_gain_grad,
        query_grad,
        key_grad,
        value_grad,
        output_grad,
        mlp_gain_grad,
        gate_grad,
        up_grad,
        down_grad,
        head_top,
        query_clipped,
        key_clipped,
    )


def solution(mesh):
    shape = (mesh.shape["fsdp"] // 4, 2, 2, mesh.shape["tp"])
    fine = Mesh(mesh.devices.reshape(shape), ("group", "row", "col", "tp"))
    rows = P(("group", "row", "col", "tp"), None)
    weight = P(FSDP, "tp")
    gain = P(FSDP)
    heads = P("tp")
    return jax.shard_map(
        local,
        mesh=fine,
        in_specs=(
            rows, rows, P(), P(), heads, gain, weight, weight, weight, weight,
            gain, weight, weight, weight,
        ),
        out_specs=(
            rows, rows, gain, weight, weight, weight, weight, gain, weight, weight, weight,
            heads, weight, weight,
        ),
        check_vma=False,
    )
```

```python
import functools

import jax
import jax.numpy as jnp
from jax import lax
from jax.experimental import pallas as pl
from jax.experimental.pallas import tpu as pltpu
from jax.sharding import Mesh, PartitionSpec as P

HS = 256
GROUP = 2048
SIXTEENTHS = (6, 6, 4)
BLOCK = 128

epsilon = 1e-05
theta_base = 1000042.0
masked_value = -1e30

bf16 = jnp.bfloat16
f32 = jnp.float32
PLANE = ("row", "col")
FSDP = ("group", "row", "col")
VMEM_LIMIT = 48 * 1024 * 1024


def product(left, right):
    return jnp.dot(left, right, preferred_element_type=f32)


def times_transposed(left, right):
    return lax.dot_general(left, right, (((1,), (1,)), ((), ())), preferred_element_type=f32)


def outer_sum(left, right):
    return lax.dot_general(left, right, (((0,), (0,)), ((), ())), preferred_element_type=f32)


def take(array, index, axis=0):
    return lax.dynamic_index_in_dim(array, index, axis, keepdims=False)


def swap(block, axis):
    return lax.ppermute(block, axis, [(0, 1), (1, 0)])


def swap_plane(block, distance):
    return lax.ppermute(block, PLANE, [(i, i ^ distance) for i in range(4)])


def after(value, *others):
    return lax.optimization_barrier((value,) + others)[0]


def combine_all(values, groups, combine):
    distance, count = 1, 4 * groups
    rounds = []
    while distance < count:
        arrived = []
        for step in range(1, min(4, count // distance)):
            route = [(i, i ^ step * distance) for i in range(count)]
            arrived.append(lax.ppermute(values, FSDP, route))
        for other in arrived:
            values = combine(values, other)
        rounds.append(arrived)
        distance *= 4
    return values, rounds


def pack_kernel(count, *refs):
    out_ref, sems = refs[count], refs[count + 1]
    copies, start = [], 0
    for i in range(count):
        rows = refs[i].shape[0]
        copy = pltpu.make_async_copy(refs[i], out_ref.at[pl.ds(start, rows)], sems.at[i])
        copy.start()
        copies.append(copy)
        start += rows
    for copy in copies:
        copy.wait()


def pack(pieces):
    rows, width = sum(p.shape[0] for p in pieces), pieces[0].shape[1]
    count = len(pieces)
    return pl.pallas_call(
        functools.partial(pack_kernel, count),
        in_specs=[pl.BlockSpec(memory_space=pl.ANY)] * count,
        out_specs=pl.BlockSpec(memory_space=pltpu.VMEM),
        out_shape=jax.ShapeDtypeStruct((rows, width), pieces[0].dtype),
        scratch_shapes=[pltpu.SemaphoreType.DMA((count,))],
        cost_estimate=pl.CostEstimate(
            flops=0, bytes_accessed=4 * rows * width, transcendentals=0
        ),
        compiler_params=pltpu.CompilerParams(vmem_limit_bytes=VMEM_LIMIT),
        name="pack",
    )(*pieces)


def norm_kernel(count, *refs):
    gain_ref, out_ref = refs[count], refs[-2]
    pack_kernel(count, *refs[:count], *refs[-2:])
    tile = 256

    @pl.loop(0, out_ref.shape[0] // tile)
    def _(i):
        rows = pl.ds(pl.multiple_of(i * tile, tile), tile)
        values = out_ref[rows, :].astype(f32)
        out_ref[rows, :] = (values * rms_inverse(values) * gain_ref[...]).astype(bf16)


def pack_normed(pieces, gain, early):
    rows, width = sum(p.shape[0] for p in pieces), pieces[0].shape[1]
    count = len(pieces)
    return pl.pallas_call(
        functools.partial(norm_kernel, count),
        in_specs=[pl.BlockSpec(memory_space=pl.ANY)] * count
        + [pl.BlockSpec(memory_space=pltpu.VMEM)]
        + [pl.BlockSpec(memory_space=pl.ANY)] * len(early),
        out_specs=pl.BlockSpec(memory_space=pltpu.VMEM),
        out_shape=jax.ShapeDtypeStruct((rows, width), bf16),
        scratch_shapes=[pltpu.SemaphoreType.DMA((count,))],
        cost_estimate=pl.CostEstimate(
            flops=8 * rows * width, bytes_accessed=4 * rows * width, transcendentals=0
        ),
        compiler_params=pltpu.CompilerParams(vmem_limit_bytes=VMEM_LIMIT),
        name="pack_normed",
    )(*pieces, gain, *early)


def plane_neighbours(own):
    return swap(own, "col"), swap(own, "row")


def plane_far(neighbours, *waits):
    across, along = neighbours
    half = across.shape[0] // 2
    return (
        swap(after(across[:half], *waits), "row"),
        swap(after(along[half:], *waits), "col"),
    )


def with_partner(pieces, swapped=()):
    return pieces + list(swapped) + [swap(piece, "tp") for piece in pieces[len(swapped) :]]


def chip_sums(front, back):
    pairs = []
    for own, other in (front, back):
        shape = (4, own.shape[0] // 4, own.shape[1])
        pairs.append((own.reshape(shape), swap(other, "tp").reshape(shape)))
    return pairs


def quarter(pair, k):
    return pair[0][k].astype(f32) + pair[1][k].astype(f32)


def first_operands(sums):
    front, back = sums
    return (
        jnp.concatenate([quarter(front, 1), quarter(front, 3)]).astype(bf16),
        (back[0][2:].astype(f32) + back[1][2:].astype(f32)).astype(bf16),
    )


def reduce_first(operands, *waits):
    front, back = operands
    rows = front.shape[0] // 2
    return (
        swap(after(front, *waits), "col").reshape(2, rows, -1),
        swap(after(back, *waits), "row"),
    )


def reduce_operands(sums, arrived):
    front, back = sums
    got, got_back = arrived[0].astype(f32), arrived[1].astype(f32)
    return (
        (quarter(front, 0) + got[0], (quarter(front, 2) + got[1]).astype(bf16)),
        (quarter(back, 0) + got_back[0], (quarter(back, 1) + got_back[1]).astype(bf16)),
    )


def last_swaps(operands, *waits):
    return (
        swap(after(operands[0][1], *waits), "row"),
        swap(after(operands[1][1], *waits), "col"),
    )


def reduce_last(operands, *waits, swapped=None):
    swapped = swapped or last_swaps(operands, *waits)
    return jnp.concatenate(
        [keep + last.astype(f32) for (keep, _), last in zip(operands, swapped)], axis=1
    )


def line_reduce(blocks, groups, index):
    up = down = None
    waits = yield
    for step in range(1, groups):
        source = after(blocks, *waits) if waits else blocks
        out_up = take(source, jnp.minimum(index + groups - step, groups - 1))
        out_down = take(source, jnp.maximum(index - groups + step, 0))
        if up is not None:
            out_up = (out_up.astype(f32) + up.astype(f32)).astype(bf16)
            out_down = (out_down.astype(f32) + down.astype(f32)).astype(bf16)
        senders = range(min(step, groups - 1))
        up = lax.ppermute(out_up, "group", [(j, j + 1) for j in senders])
        down = lax.ppermute(
            out_down, "group", [(groups - 1 - j, groups - 2 - j) for j in senders]
        )
        waits = yield up, down
    total = take(after(blocks, up, down), index).astype(f32) + up.astype(f32) + down.astype(f32)
    yield total.astype(bf16)


def split_kernel(spans, member_ref, *refs):
    sources, outs = refs[: len(spans)], refs[len(spans) :]
    for k in range(4):
        target = member_ref[0] ^ k
        column = 0
        for source, (offset, stride, width, shift) in zip(sources, spans):
            start = pl.multiple_of((target >> shift) * stride + offset, 128)
            outs[k][:, column : column + width] = source[:, pl.ds(start, width)]
            column += width


def split(member, sources, spans):
    rows, width = sources[0].shape[0], sum(span[2] for span in spans)
    whole = pl.BlockSpec(memory_space=pltpu.VMEM)
    return pl.pallas_call(
        functools.partial(split_kernel, spans),
        in_specs=[pl.BlockSpec(memory_space=pltpu.SMEM)] + [whole] * len(sources),
        out_specs=[whole] * 4,
        out_shape=[jax.ShapeDtypeStruct((rows, width), bf16)] * 4,
        cost_estimate=pl.CostEstimate(
            flops=0, bytes_accessed=16 * rows * width, transcendentals=0
        ),
        compiler_params=pltpu.CompilerParams(vmem_limit_bytes=VMEM_LIMIT),
        name="split",
    )(member, *sources)


def place_kernel(member_ref, *refs):
    rows = refs[0].shape[0]
    for k in range(4):
        start = pl.multiple_of((member_ref[0] ^ k) * rows, rows)
        column = 0
        for out_ref in refs[4:]:
            width = out_ref.shape[1]
            out_ref[pl.ds(start, rows), :] = refs[k][:, column : column + width]
            column += width


def place_rows(member, pieces, *widths):
    rows, width = pieces[0].shape
    whole = pl.BlockSpec(memory_space=pltpu.VMEM)
    return pl.pallas_call(
        place_kernel,
        in_specs=[pl.BlockSpec(memory_space=pltpu.SMEM)] + [whole] * 4,
        out_specs=[whole] * len(widths or (width,)),
        out_shape=[
            jax.ShapeDtypeStruct((4 * rows, w), bf16) for w in widths or (width,)
        ],
        cost_estimate=pl.CostEstimate(
            flops=0, bytes_accessed=16 * rows * width, transcendentals=0
        ),
        compiler_params=pltpu.CompilerParams(vmem_limit_bytes=VMEM_LIMIT),
        name="place_rows",
    )(member, *pieces)


def pick_kernel(member_ref, *refs):
    sources, outs = refs[:-4], refs[-4:]
    rows = outs[0].shape[0]
    for k in range(4):
        start = pl.multiple_of((member_ref[0] ^ k) * rows, rows)
        column = 0
        for source in sources:
            width = source.shape[1]
            outs[k][:, column : column + width] = source[pl.ds(start, rows), :]
            column += width


def pick_rows(member, *sources):
    rows, width = sources[0].shape[0] // 4, sum(source.shape[1] for source in sources)
    whole = pl.BlockSpec(memory_space=pltpu.VMEM)
    return pl.pallas_call(
        pick_kernel,
        in_specs=[pl.BlockSpec(memory_space=pltpu.SMEM)] + [whole] * len(sources),
        out_specs=[whole] * 4,
        out_shape=[jax.ShapeDtypeStruct((rows, width), bf16)] * 4,
        cost_estimate=pl.CostEstimate(
            flops=0, bytes_accessed=16 * rows * width, transcendentals=0
        ),
        compiler_params=pltpu.CompilerParams(vmem_limit_bytes=VMEM_LIMIT),
        name="pick_rows",
    )(member, *sources)


def swap_all(pieces):
    return [pieces[0]] + [swap_plane(pieces[k], k) for k in (1, 2, 3)]


def mlp_final_kernel(parts, stride, member_ref, gate_w_ref, up_w_ref, *refs):
    pieces, outs, gain_ref = refs[:-4], refs[-4:-1], refs[-1]
    for n, chunks in enumerate(parts):
        for k in range(4):
            start = 0
            for offset, width in chunks:
                column = pl.multiple_of((member_ref[0] ^ k) * stride + offset, 128)
                for i in range(3):
                    part = pieces[4 * n + k][:, start : start + width]
                    outs[i][:, pl.ds(column, width)] = part.astype(f32)
                    start += width
    gain_ref[...] = jnp.sum(
        gate_w_ref[...].astype(f32) * outs[0][...] + up_w_ref[...].astype(f32) * outs[1][...],
        axis=1,
        keepdims=True,
    )


def mlp_final(member, gate_weight, up_weight, chunks, parts):
    rows, hidden = gate_weight.shape
    pieces = [piece for part in parts for piece in part]
    whole = pl.BlockSpec(memory_space=pltpu.VMEM)
    return pl.pallas_call(
        functools.partial(mlp_final_kernel, chunks, hidden // 4),
        in_specs=[pl.BlockSpec(memory_space=pltpu.SMEM)] + [whole] * (2 + len(pieces)),
        out_specs=[whole] * 4,
        out_shape=[jax.ShapeDtypeStruct((rows, hidden), f32)] * 3
        + [jax.ShapeDtypeStruct((rows, 1), f32)],
        cost_estimate=pl.CostEstimate(
            flops=4 * rows * hidden, bytes_accessed=22 * rows * hidden, transcendentals=0
        ),
        compiler_params=pltpu.CompilerParams(vmem_limit_bytes=VMEM_LIMIT),
        name="mlp_final",
    )(member, gate_weight, up_weight, *pieces)


def attention_final_kernel(member_ref, qw_ref, kw_ref, vw_ref, *refs):
    pieces = refs[:4]
    q_ref, k_ref, v_ref, o_ref, gain_ref = refs[4:]
    member = member_ref[0]
    for k in range(4):
        columns = pl.ds(pl.multiple_of((member ^ k) * HS, HS), HS)
        q_ref[:, columns] = pieces[k][:, :HS].astype(f32)
        o_ref[:, columns] = pieces[k][:, 3 * HS :].astype(f32)
    for h in range(2):
        columns = pl.ds(pl.multiple_of(((member >> 1) ^ h) * HS, HS), HS)
        both = sum(pieces[2 * h + i][:, HS : 3 * HS].astype(f32) for i in range(2))
        k_ref[:, columns] = both[:, :HS]
        v_ref[:, columns] = both[:, HS:]

    def row_sum(weight_ref, grad_ref):
        return jnp.sum(weight_ref[...].astype(f32) * grad_ref[...], axis=1, keepdims=True)

    gain_ref[...] = row_sum(qw_ref, q_ref) + row_sum(kw_ref, k_ref) + row_sum(vw_ref, v_ref)


def attention_final(member, query_weight, key_weight, value_weight, pieces):
    rows, width = query_weight.shape
    whole = pl.BlockSpec(memory_space=pltpu.VMEM)
    shapes = [width, width // 2, width // 2, width, 1]
    return pl.pallas_call(
        attention_final_kernel,
        in_specs=[pl.BlockSpec(memory_space=pltpu.SMEM)] + [whole] * 7,
        out_specs=[whole] * 5,
        out_shape=[jax.ShapeDtypeStruct((rows, n), f32) for n in shapes],
        cost_estimate=pl.CostEstimate(
            flops=4 * rows * width, bytes_accessed=24 * rows * width, transcendentals=0
        ),
        compiler_params=pltpu.CompilerParams(vmem_limit_bytes=VMEM_LIMIT),
        name="attention_final",
    )(member, query_weight, key_weight, value_weight, *pieces)


def rms_inverse(values):
    return lax.rsqrt(jnp.mean(values * values, axis=-1, keepdims=True) + epsilon)


def rope_tables(positions):
    half_size = HS // 2
    indices = jnp.arange(half_size, dtype=f32)
    inverse = theta_base ** (-2.0 * indices / HS)
    angles = positions.astype(f32)[:, None] * inverse[None, :]
    return jnp.cos(angles), jnp.sin(angles)


def rotate(vectors, cos, sin):
    front, back = vectors[:, : HS // 2], vectors[:, HS // 2 :]
    return jnp.concatenate([front * cos - back * sin, back * cos + front * sin], axis=-1)


def unrotate(grads, cos, sin):
    front, back = grads[:, : HS // 2], grads[:, HS // 2 :]
    return jnp.concatenate([front * cos + back * sin, back * cos - front * sin], axis=-1)


def mlp_tile(width, normed, cot, weight_ref):
    both = product(normed, weight_ref[:, : 2 * width])
    d_inner = product(cot, weight_ref[:, 2 * width :])
    gate, upward = both[:, :width], both[:, width:]
    sig = 1.0 / (1.0 + jnp.exp(-gate))
    silu = gate * sig
    d_gate = d_inner * upward * sig * (1.0 + gate * (1.0 - sig))
    return (
        (silu * upward).astype(bf16),
        jnp.concatenate([d_gate, d_inner * silu], axis=1).astype(bf16),
    )


def mlp_kernel(width, normed_ref, cot_ref, weight_ref, inner_ref, grads_ref):
    inner_ref[...], grads_ref[...] = mlp_tile(
        width, normed_ref[...], cot_ref[...], weight_ref
    )


def tail_kernel(width, normed_ref, cot_ref, weight_ref, base_ref, *refs):
    inner_ref, grads_ref, front_ref, back_ref = refs[-4:]
    inner, grads = mlp_tile(width, normed_ref[...], cot_ref[...], weight_ref)
    inner_ref[...], grads_ref[...] = inner, grads
    total = times_transposed(grads, weight_ref[:, : 2 * width]) + base_ref[...]
    half = total.shape[1] // 2
    front_ref[...] = total[:, :half].astype(front_ref.dtype)
    back_ref[...] = total[:, half:].astype(back_ref.dtype)


def mlp_tail(normed, cot, weight, base, part, dtype, chained=()):
    tokens, features = normed.shape
    width = weight.shape[1] // 3
    tile, rows = 256, tokens // 2
    steps = rows // tile
    count = len(chained)
    return pl.pallas_call(
        functools.partial(tail_kernel, width),
        grid=(steps,),
        in_specs=[
            pl.BlockSpec((tile, features), lambda i: (part * steps + i, 0)),
            pl.BlockSpec((tile, features), lambda i: (part * steps + i, 0)),
            pl.BlockSpec((features, 3 * width), lambda i: (0, 0)),
            pl.BlockSpec((tile, features), lambda i: (i, 0)),
        ]
        + [pl.BlockSpec(memory_space=pl.ANY)] * count,
        out_specs=[
            pl.BlockSpec((tile, width), lambda i: (part * steps + i, 0)),
            pl.BlockSpec((tile, 2 * width), lambda i: (part * steps + i, 0)),
            pl.BlockSpec((tile, features // 2), lambda i: (i, 0)),
            pl.BlockSpec((tile, features // 2), lambda i: (i, 0)),
        ],
        out_shape=[
            jax.ShapeDtypeStruct((tokens, width), bf16),
            jax.ShapeDtypeStruct((tokens, 2 * width), bf16),
            jax.ShapeDtypeStruct((rows, features // 2), dtype),
            jax.ShapeDtypeStruct((rows, features // 2), dtype),
        ],
        input_output_aliases={4 + i: i for i in range(count)},
        cost_estimate=pl.CostEstimate(
            flops=10 * rows * features * width,
            bytes_accessed=2 * features * (5 * rows + 3 * width),
            transcendentals=rows * width,
        ),
        compiler_params=pltpu.CompilerParams(vmem_limit_bytes=VMEM_LIMIT),
        name="mlp_tail",
    )(normed, cot, weight, base, *chained)


def mlp_chunk(normed, cot, weight):
    tokens, features = normed.shape
    width = weight.shape[1] // 3
    tile = 256
    return pl.pallas_call(
        functools.partial(mlp_kernel, width),
        grid=(tokens // tile,),
        in_specs=[
            pl.BlockSpec((tile, features), lambda i: (i, 0)),
            pl.BlockSpec((tile, features), lambda i: (i, 0)),
            pl.BlockSpec((features, 3 * width), lambda i: (0, 0)),
        ],
        out_specs=[
            pl.BlockSpec((tile, width), lambda i: (i, 0)),
            pl.BlockSpec((tile, 2 * width), lambda i: (i, 0)),
        ],
        out_shape=[
            jax.ShapeDtypeStruct((tokens, width), bf16),
            jax.ShapeDtypeStruct((tokens, 2 * width), bf16),
        ],
        cost_estimate=pl.CostEstimate(
            flops=6 * tokens * features * width,
            bytes_accessed=2 * features * (2 * tokens + 3 * width),
            transcendentals=tokens * width,
        ),
        compiler_params=pltpu.CompilerParams(vmem_limit_bytes=VMEM_LIMIT),
        name="mlp_chunk",
    )(normed, cot, weight)


def sum_kernel(count, *refs):
    lefts, rights, out_ref = refs[:count], refs[count : 2 * count], refs[-1]
    total = times_transposed(lefts[0][...], rights[0][...])
    for left, right in zip(lefts[1:], rights[1:]):
        total += times_transposed(left[...], right[...])
    for base in refs[2 * count : -1]:
        total += base[...].astype(f32)
    out_ref[...] = total.astype(out_ref.dtype)


def chunk_sum(lefts, rights, column, part, half, dtype):
    count = len(lefts)
    tokens, features = lefts[0].shape[0], rights[0].shape[0]
    widths = [left.shape[1] for left in lefts]
    rows = tokens // 2
    tile = 256
    if half is not None:
        features, tile = features // 2, 512
    steps = rows // tile
    block = half or 0
    return pl.pallas_call(
        functools.partial(sum_kernel, count),
        grid=(steps,),
        in_specs=[pl.BlockSpec((tile, w), lambda i: (part * steps + i, 0)) for w in widths]
        + [pl.BlockSpec((features, w), lambda i: (block, column)) for w in widths],
        out_specs=pl.BlockSpec((tile, features), lambda i: (i, 0)),
        out_shape=jax.ShapeDtypeStruct((rows, features), dtype),
        cost_estimate=pl.CostEstimate(
            flops=2 * rows * features * sum(widths),
            bytes_accessed=2 * sum(widths) * (rows + features) + 4 * rows * features,
            transcendentals=0,
        ),
        compiler_params=pltpu.CompilerParams(vmem_limit_bytes=VMEM_LIMIT),
        name="chunk_sum",
    )(*lefts, *rights)


def grads_kernel(count, *refs):
    column = 0
    for left, right in zip(refs[:count], refs[count : 2 * count]):
        width = right.shape[1]
        refs[-1][:, column : column + width] = outer_sum(left[...], right[...]).astype(bf16)
        column += width


def weight_grads(*pairs):
    lefts, rights = [left for left, _ in pairs], [right for _, right in pairs]
    count = len(pairs)
    tokens, features = lefts[0].shape
    widths = [right.shape[1] for right in rights]
    tile = 256
    return pl.pallas_call(
        functools.partial(grads_kernel, count),
        grid=(features // tile,),
        in_specs=[pl.BlockSpec((tokens, tile), lambda i: (0, i))] * count
        + [pl.BlockSpec((tokens, w), lambda i: (0, 0)) for w in widths],
        out_specs=pl.BlockSpec((tile, sum(widths)), lambda i: (i, 0)),
        out_shape=jax.ShapeDtypeStruct((features, sum(widths)), bf16),
        cost_estimate=pl.CostEstimate(
            flops=2 * tokens * features * sum(widths),
            bytes_accessed=2 * (count * tokens * features + sum(widths) * (tokens + features)),
            transcendentals=0,
        ),
        compiler_params=pltpu.CompilerParams(vmem_limit_bytes=VMEM_LIMIT),
        name="weight_grads",
    )(*lefts, *rights)


def project_kernel(place_ref, normed_ref, weight_ref, cos_ref, sin_ref, q_ref, k_ref, v_ref):
    step = pl.program_id(0)
    cos, sin = cos_ref[...], sin_ref[...]
    qkv = product(normed_ref[...], weight_ref[...])
    query = rotate(qkv[:, :HS], cos, sin).astype(bf16) * HS ** (-0.5)
    keys = rotate(qkv[:, HS : 2 * HS], cos, sin).astype(bf16)
    vals = qkv[:, 2 * HS :].astype(bf16)
    blocks = normed_ref.shape[0] // BLOCK
    for b in range(blocks):
        rows = pl.ds(pl.multiple_of(place_ref[step * blocks + b] * BLOCK, BLOCK), BLOCK)
        part = slice(b * BLOCK, (b + 1) * BLOCK)
        q_ref[rows, :] = query[part]
        k_ref[rows, :] = keys[part]
        v_ref[rows, :] = vals[part]


def project(place, normed, weight, cos, sin):
    tokens, features = normed.shape
    tile = 256
    whole = pl.BlockSpec((tokens, HS), lambda i, place: (0, 0))
    return pl.pallas_call(
        project_kernel,
        grid_spec=pltpu.PrefetchScalarGridSpec(
            num_scalar_prefetch=1,
            grid=(tokens // tile,),
            in_specs=[
                pl.BlockSpec((tile, features), lambda i, place: (i, 0)),
                pl.BlockSpec((features, 3 * HS), lambda i, place: (0, 0)),
                pl.BlockSpec((tile, HS // 2), lambda i, place: (i, 0)),
                pl.BlockSpec((tile, HS // 2), lambda i, place: (i, 0)),
            ],
            out_specs=[whole] * 3,
        ),
        out_shape=[jax.ShapeDtypeStruct((tokens, HS), bf16)] * 3,
        cost_estimate=pl.CostEstimate(
            flops=6 * tokens * features * HS,
            bytes_accessed=2 * features * (tokens + 3 * HS) + 10 * tokens * HS,
            transcendentals=0,
        ),
        compiler_params=pltpu.CompilerParams(vmem_limit_bytes=VMEM_LIMIT),
        name="project",
    )(place, normed, weight, cos, sin)


TILE = 256


def tile_masks():
    rows = lax.broadcasted_iota(jnp.int32, (TILE, TILE), 0)
    cols = lax.broadcasted_iota(jnp.int32, (TILE, TILE), 1)
    causal = rows >= cols
    return causal, causal & (rows // BLOCK == cols // BLOCK)


def block_rows(order_ref, index):
    return pl.ds(pl.multiple_of(order_ref[index] * BLOCK, BLOCK), BLOCK)


def forward_kernel(order_ref, q_ref, k_ref, v_ref, mixed_ref, lse_ref, peak_ref):
    causal, inside = tile_masks()
    prompt = GROUP // 2
    top = jnp.full((TILE, 1), masked_value, f32)
    for i in range(GROUP // TILE):
        rows = slice(i * TILE, (i + 1) * TILE)
        past = min(i * TILE, prompt)
        query = q_ref[rows, :]
        near = times_transposed(query, k_ref[rows, :])
        near = jnp.where(causal if i * TILE < prompt else inside, near, masked_value)
        peak = jnp.max(near, axis=1, keepdims=True)
        if past:
            far = times_transposed(query, k_ref[:past, :])
            peak = jnp.maximum(peak, jnp.max(far, axis=1, keepdims=True))
            far = jnp.exp(far - peak)
        near = jnp.exp(near - peak)
        total = jnp.sum(near, axis=1, keepdims=True)
        if past:
            total += jnp.sum(far, axis=1, keepdims=True)
        share = 1.0 / total
        mixed = product((near * share).astype(bf16), v_ref[rows, :])
        if past:
            mixed += product((far * share).astype(bf16), v_ref[:past, :])
        mixed = mixed.astype(bf16)
        for b in range(TILE // BLOCK):
            mixed_ref[block_rows(order_ref, i * (TILE // BLOCK) + b), :] = mixed[
                b * BLOCK : (b + 1) * BLOCK
            ]
        lse_ref[rows, :] = peak + jnp.log(total)
        top = jnp.maximum(top, peak)
    peak_ref[...] = jnp.full(peak_ref.shape, jnp.max(top), f32)


def attention_forward(order, query, keys, vals):
    whole = pl.BlockSpec(memory_space=pltpu.VMEM)
    return pl.pallas_call(
        forward_kernel,
        in_specs=[pl.BlockSpec(memory_space=pltpu.SMEM), whole, whole, whole],
        out_specs=[whole] * 3,
        out_shape=[
            jax.ShapeDtypeStruct((GROUP, HS), bf16),
            jax.ShapeDtypeStruct((GROUP, 1), f32),
            jax.ShapeDtypeStruct((8, 128), f32),
        ],
        cost_estimate=pl.CostEstimate(
            flops=2 * GROUP * GROUP * HS,
            bytes_accessed=8 * GROUP * HS,
            transcendentals=GROUP * GROUP // 2,
        ),
        compiler_params=pltpu.CompilerParams(vmem_limit_bytes=VMEM_LIMIT),
        name="attention_forward",
    )(order, query, keys, vals)


def backward_kernel(
    order_ref, q_ref, k_ref, v_ref, lse_ref, mixed_ref, cos_ref, sin_ref, out_ref, dk_ref, dv_ref
):
    causal, inside = tile_masks()
    prompt = GROUP // 2
    blocks = TILE // BLOCK

    def back(grad, index):
        rows = block_rows(order_ref, index)
        return rows, unrotate(grad, cos_ref[rows, :], sin_ref[rows, :]).astype(bf16)

    for i in range(GROUP // TILE):
        rows = slice(i * TILE, (i + 1) * TILE)
        past = min(i * TILE, prompt)
        query, lse = q_ref[rows, :], lse_ref[rows, :]
        d_mixed = jnp.concatenate(
            [mixed_ref[block_rows(order_ref, i * blocks + b), :] for b in range(blocks)], axis=0
        )
        near = times_transposed(query, k_ref[rows, :])
        near = jnp.where(causal if i * TILE < prompt else inside, near, masked_value)
        near = jnp.exp(near - lse)
        d_near = times_transposed(d_mixed, v_ref[rows, :])
        inner = jnp.sum(near * d_near, axis=1, keepdims=True)
        if past:
            far = jnp.exp(times_transposed(query, k_ref[:past, :]) - lse)
            d_far = times_transposed(d_mixed, v_ref[:past, :])
            inner += jnp.sum(far * d_far, axis=1, keepdims=True)
        d_near = (near * (d_near - inner)).astype(bf16)
        d_query = product(d_near, k_ref[rows, :])
        dk_ref[rows, :] = outer_sum(d_near, query)
        dv_ref[rows, :] = outer_sum(near.astype(bf16), d_mixed)
        if past:
            d_far = (far * (d_far - inner)).astype(bf16)
            d_query += product(d_far, k_ref[:past, :])
            dk_ref[:past, :] += outer_sum(d_far, query)
            dv_ref[:past, :] += outer_sum(far.astype(bf16), d_mixed)
        d_query = d_query * HS ** (-0.5)
        for b in range(blocks):
            where, grad = back(d_query[b * BLOCK : (b + 1) * BLOCK], i * blocks + b)
            out_ref[where, :HS] = grad
    for c in range(GROUP // BLOCK):
        part = slice(c * BLOCK, (c + 1) * BLOCK)
        where, grad = back(dk_ref[part, :], c)
        out_ref[where, HS : 2 * HS] = grad
        out_ref[where, 2 * HS :] = dv_ref[part, :].astype(bf16)


def attention_backward(order, query, keys, vals, lse, d_mixed, cos, sin):
    whole = pl.BlockSpec(memory_space=pltpu.VMEM)
    return pl.pallas_call(
        backward_kernel,
        in_specs=[pl.BlockSpec(memory_space=pltpu.SMEM)] + [whole] * 7,
        out_specs=whole,
        out_shape=jax.ShapeDtypeStruct((GROUP, 3 * HS), bf16),
        scratch_shapes=[pltpu.VMEM((GROUP, HS), f32), pltpu.VMEM((GROUP, HS), f32)],
        cost_estimate=pl.CostEstimate(
            flops=5 * GROUP * GROUP * HS,
            bytes_accessed=20 * GROUP * HS,
            transcendentals=GROUP * GROUP // 2,
        ),
        compiler_params=pltpu.CompilerParams(vmem_limit_bytes=VMEM_LIMIT),
        name="attention_backward",
    )(order, query, keys, vals, lse, d_mixed, cos, sin)


def local(
    tokens,
    cotangent,
    segment,
    position,
    clip_limit,
    attn_gain,
    query_weight,
    key_weight,
    value_weight,
    output_weight,
    mlp_gain,
    gate_weight,
    up_weight,
    down_weight,
):
    groups = lax.axis_size("group")
    group = lax.axis_index("group")
    core = lax.axis_index("tp")
    member = lax.axis_index(PLANE)
    token_rows = tokens.shape[0]
    own_rows, features = query_weight.shape[0], tokens.shape[1]
    hidden_own = gate_weight.shape[1] // 4
    chunks, offset = [], 0
    for part in SIXTEENTHS:
        chunks.append((offset, hidden_own * part // 16))
        offset += hidden_own * part // 16
    member_at = member.astype(jnp.int32).reshape(1)

    def own_order(array):
        parts = []
        for j in range(2):
            for k in range(4):
                start = group * GROUP + (member ^ k) * (2 * token_rows) + (core ^ j) * token_rows
                parts.append(lax.dynamic_slice_in_dim(array, start, token_rows))
        return jnp.concatenate(parts)

    def collect(blocks):
        return lax.all_gather(blocks, "group", axis=0, tiled=True)

    def mlp_exchange(some, waits):
        weights = [after(a, *waits) for a in (gate_weight, up_weight, down_weight)]
        spans = tuple((start, hidden_own, count, 0) for start, count in some for _ in range(3))
        return swap_all(split(member_at, weights * len(some), spans))

    seg, pos = own_order(segment), own_order(position)
    cos, sin = rope_tables(pos)
    seg_blocks, pos_blocks = seg[::BLOCK], pos[::BLOCK]
    half_blocks = GROUP // BLOCK // 2
    place = jnp.where(seg_blocks == 0, pos_blocks // BLOCK, half_blocks - 1 + seg_blocks)
    labels = jnp.arange(2 * half_blocks, dtype=jnp.int32)
    order = jnp.sum(jnp.where(place[None, :] == labels[:, None], labels[None, :], 0), axis=1)
    index = lax.axis_index(FSDP)
    gains = jnp.stack([attn_gain, mlp_gain])[:, None, :]
    gains = jnp.where(jnp.arange(4 * groups)[None, :, None] == index, gains, 0)
    gains, gain_rounds = combine_all(gains, groups, lambda a, b: a + b)
    gains = gains.reshape(2, features).astype(f32)
    head, pair = (0, HS, HS, 0), (0, HS, HS, 1)
    attn_pieces = swap_all(
        split(
            member_at,
            (query_weight, key_weight, value_weight, output_weight),
            (head, pair, pair, head),
        )
    )
    attn_weights = collect(
        *place_rows(member_at, [after(attn_pieces[0], *gain_rounds[0])] + attn_pieces[1:])
    )
    late_tokens = after(tokens, *attn_pieces[1:], *gain_rounds[-1])
    neighbours = plane_neighbours(late_tokens)
    tokens_far = plane_far(neighbours)
    tokens_mine = [late_tokens, *neighbours, *tokens_far]
    tokens_near = [swap(piece, "tp") for piece in tokens_mine[:3]]
    normed_all = pack_normed(
        with_partner(tokens_mine, tokens_near), gains[:1], (cos, sin, place, order)
    )
    pieces_0 = mlp_exchange(chunks[:2], (*tokens_far, *tokens_near))
    blocks_0, blocks_1 = place_rows(
        member_at,
        [after(pieces_0[0], normed_all)] + pieces_0[1:],
        *(3 * count for _, count in chunks[:2]),
    )
    late_cot = after(cotangent, *pieces_0[1:])
    cot_near = [swap_plane(late_cot, k) for k in (1, 2)]
    gain_attn, gain_mlp = gains[0], gains[1]

    tokens_f = tokens.astype(f32)
    inverse_attn = rms_inverse(tokens_f)
    unit_attn = tokens_f * inverse_attn
    query, keys, vals = project(
        place, normed_all, attn_weights, cos, sin
    )
    mixed, logsum, peak = attention_forward(order, query, keys, vals)

    head_top = jnp.where(jnp.arange(4) == member, peak[0, :4], masked_value)
    head_top, head_rounds = combine_all(head_top, groups, jnp.maximum)

    def projected(left, column, *waits):
        lefts = (left, after(left, *waits))
        return [
            [
                chunk_sum([lefts[j]], [attn_weights], column, j, h, bf16 if j else f32)
                for j in (0, 1)
            ]
            for h in range(2)
        ]

    attn_sums = chip_sums(*projected(mixed, 3, *cot_near))
    arrived = reduce_first(first_operands(attn_sums))
    attn_operands = reduce_operands(attn_sums, arrived)
    hidden = tokens_f + reduce_last(attn_operands, *head_rounds[0])
    inverse_mlp = rms_inverse(hidden)
    unit_mlp = hidden * inverse_mlp
    own_normed = (unit_mlp * gain_mlp).astype(bf16)
    neighbours = plane_neighbours(own_normed)
    normed_far = plane_far(neighbours, *head_rounds[-1])
    pieces_2 = mlp_exchange(chunks[2:], normed_far)
    mlp_weights = [
        collect(blocks) for blocks in (blocks_0, blocks_1, *place_rows(member_at, pieces_2))
    ]
    cot_far = swap_plane(after(late_cot, *normed_far), 3)
    normed_mlp = pack(with_partner([own_normed, *neighbours, *normed_far]))
    cot_all = pack(with_partner([late_cot, *cot_near, cot_far]))

    def line_sum(partial):
        return lax.psum_scatter(partial, "group", scatter_dimension=0, tiled=True)

    inner_0, both_0 = mlp_chunk(normed_mlp, cot_all, mlp_weights[0])
    grads_0 = weight_grads((normed_mlp, both_0), (cot_all, inner_0))
    line_0 = line_reduce(grads_0.reshape(groups, 4 * own_rows, -1), groups, group)
    next(line_0)
    first_0 = line_0.send(())
    inner_1, both_1 = mlp_chunk(after(normed_mlp, grads_0), cot_all, mlp_weights[1])
    grads_1 = weight_grads((normed_mlp, both_1), (cot_all, inner_1))
    sum_1 = line_sum(grads_1)
    d_boths = [after(both_0, grads_1, *first_0), both_1]
    early = [chunk_sum(d_boths, mlp_weights[:2], 0, j, None, f32) for j in range(2)]
    second_0 = line_0.send(())
    inner_2, both_2, front_1, back_1 = mlp_tail(
        after(normed_mlp, *early, *second_0), cot_all, mlp_weights[2], early[1], 1, bf16
    )
    inner_2, both_2, front_0, back_0 = mlp_tail(
        normed_mlp, cot_all, mlp_weights[2], early[0], 0, f32, (inner_2, both_2)
    )
    for _ in range(groups - 3):
        third_0 = line_0.send(())
    sum_0 = line_0.send(())

    mlp_sums = chip_sums((front_0, front_1), (back_0, back_1))
    operands = first_operands(mlp_sums)
    arrived = reduce_first(operands)
    inners = [after(inner, *operands) for inner in (inner_0, inner_1, inner_2)]
    out_parts = [[chunk_sum(inners, mlp_weights, 2, j, 0, bf16 if j else f32) for j in (0, 1)]]
    late_inners = [after(inners[0], *third_0, *out_parts[0])] + inners[1:]
    out_parts.append(
        [chunk_sum(late_inners, mlp_weights, 2, j, 1, bf16 if j else f32) for j in (0, 1)]
    )
    mlp_last = last_swaps(
        reduce_operands(mlp_sums, arrived), *out_parts[0], *out_parts[1]
    )
    d_normed = reduce_last(reduce_operands(mlp_sums, arrived), swapped=mlp_last)
    cot_f = cotangent.astype(f32)
    scaled = d_normed * gain_mlp
    d_hidden = cot_f + inverse_mlp * (
        scaled - unit_mlp * jnp.mean(scaled * unit_mlp, axis=-1, keepdims=True)
    )
    own_d = d_hidden.astype(bf16)
    neighbours = plane_neighbours(own_d)
    late_both = after(both_2, *mlp_last)
    grads_2 = weight_grads((normed_mlp, late_both), (cot_all, inner_2))
    sum_2 = line_sum(after(grads_2, *neighbours))
    d_far = plane_far(neighbours, grads_2)
    d_attn_all = pack(with_partner([own_d, *neighbours, *d_far]))
    out_parts = [[part[0], after(part[1], *d_far)] for part in out_parts]
    out_sums = chip_sums(*out_parts)
    out_operands = reduce_operands(out_sums, reduce_first(first_operands(out_sums)))

    def send_grads(sources, *waits):
        first = after(sources[0], *waits) if waits else sources[0]
        return swap_all(pick_rows(member_at, first, *sources[1:]))


    final_0 = send_grads([sum_0, sum_1], *d_far)
    d_mixed = product(d_attn_all, attn_weights[:, 3 * HS :]).astype(bf16)
    d_qkv = attention_backward(order, query, keys, vals, logsum, d_mixed, cos, sin)
    late_qkv = after(d_qkv, *final_0[1:])
    attn_grads = weight_grads((normed_all, late_qkv), (d_attn_all, mixed))
    attn_sum = line_sum(after(attn_grads, sum_2))
    out_last = last_swaps(out_operands)
    late_qkv = after(d_qkv, attn_grads)
    qkv_sums = chip_sums(*projected(late_qkv, 0))
    arrived = reduce_first(first_operands(qkv_sums))
    d_normed = reduce_last(reduce_operands(qkv_sums, arrived))
    block_out = (hidden + reduce_last(out_operands, swapped=out_last)).astype(bf16)
    scaled = d_normed * gain_attn
    tokens_grad = d_hidden + inverse_attn * (
        scaled - unit_attn * jnp.mean(scaled * unit_attn, axis=-1, keepdims=True)
    )

    final_1 = send_grads([sum_2], *arrived)
    gate_grad, up_grad, down_grad, mlp_gain_row = mlp_final(
        member_at, gate_weight, up_weight, (chunks[:2], chunks[2:]), [final_0, final_1]
    )
    query_grad, key_grad, value_grad, output_grad, attn_gain_row = attention_final(
        member_at,
        query_weight,
        key_weight,
        value_weight,
        send_grads([attn_sum]),
    )
    gain_grads = jnp.concatenate([attn_gain_row, mlp_gain_row], axis=1)
    gain_grads = gain_grads + swap(gain_grads, "tp")
    attn_gain_grad = gain_grads[:, 0] / attn_gain.astype(f32)
    mlp_gain_grad = gain_grads[:, 1] / mlp_gain.astype(f32)

    factor = clip_limit / jnp.maximum(head_top, clip_limit)
    query_scale = jnp.repeat(jnp.sqrt(factor), HS)
    key_factor = jnp.min(factor.reshape(2, 2), axis=1)
    key_scale = jnp.repeat(jnp.sqrt(key_factor), HS)
    query_clipped = (query_weight.astype(f32) * query_scale[None, :]).astype(bf16)
    key_clipped = (key_weight.astype(f32) * key_scale[None, :]).astype(bf16)
    return (
        block_out,
        tokens_grad,
        attn_gain_grad,
        query_grad,
        key_grad,
        value_grad,
        output_grad,
        mlp_gain_grad,
        gate_grad,
        up_grad,
        down_grad,
        head_top,
        query_clipped,
        key_clipped,
    )


def solution(mesh):
    shape = (mesh.shape["fsdp"] // 4, 2, 2, mesh.shape["tp"])
    fine = Mesh(mesh.devices.reshape(shape), ("group", "row", "col", "tp"))
    rows = P(("group", "row", "col", "tp"), None)
    weight = P(FSDP, "tp")
    gain = P(FSDP)
    heads = P("tp")
    return jax.shard_map(
        local,
        mesh=fine,
        in_specs=(
            rows, rows, P(), P(), heads, gain, weight, weight, weight, weight,
            gain, weight, weight, weight,
        ),
        out_specs=(
            rows, rows, gain, weight, weight, weight, weight, gain, weight, weight, weight,
            heads, weight, weight,
        ),
        check_vma=False,
    )
```

```python
import functools

import jax
import jax.numpy as jnp
from jax import lax
from jax.experimental import pallas as pl
from jax.experimental.pallas import tpu as pltpu
from jax.sharding import Mesh, PartitionSpec as P

HS = 256
GROUP = 2048
SIXTEENTHS = (10, 6)
BLOCK = 128

epsilon = 1e-05
theta_base = 1000042.0
masked_value = -1e30

bf16 = jnp.bfloat16
f32 = jnp.float32
PLANE = ("row", "col")
FSDP = ("group", "row", "col")
VMEM_LIMIT = 48 * 1024 * 1024


def product(left, right):
    return jnp.dot(left, right, preferred_element_type=f32)


def times_transposed(left, right):
    return lax.dot_general(left, right, (((1,), (1,)), ((), ())), preferred_element_type=f32)


def outer_sum(left, right):
    return lax.dot_general(left, right, (((0,), (0,)), ((), ())), preferred_element_type=f32)


def take(array, index, axis=0):
    return lax.dynamic_index_in_dim(array, index, axis, keepdims=False)


def swap(block, axis):
    return lax.ppermute(block, axis, [(0, 1), (1, 0)])


def swap_plane(block, distance):
    return lax.ppermute(block, PLANE, [(i, i ^ distance) for i in range(4)])


def after(value, *others):
    return lax.optimization_barrier((value,) + others)[0]


def combine_all(values, groups, combine):
    distance, count = 1, 4 * groups
    rounds = []
    while distance < count:
        arrived = []
        for step in range(1, min(4, count // distance)):
            route = [(i, i ^ step * distance) for i in range(count)]
            arrived.append(lax.ppermute(values, FSDP, route))
        for other in arrived:
            values = combine(values, other)
        rounds.append(arrived)
        distance *= 4
    return values, rounds


def pack_kernel(count, *refs):
    out_ref, sems = refs[count], refs[count + 1]
    copies, start = [], 0
    for i in range(count):
        rows = refs[i].shape[0]
        copy = pltpu.make_async_copy(refs[i], out_ref.at[pl.ds(start, rows)], sems.at[i])
        copy.start()
        copies.append(copy)
        start += rows
    for copy in copies:
        copy.wait()


def pack(pieces):
    rows, width = sum(p.shape[0] for p in pieces), pieces[0].shape[1]
    count = len(pieces)
    return pl.pallas_call(
        functools.partial(pack_kernel, count),
        in_specs=[pl.BlockSpec(memory_space=pl.ANY)] * count,
        out_specs=pl.BlockSpec(memory_space=pltpu.VMEM),
        out_shape=jax.ShapeDtypeStruct((rows, width), pieces[0].dtype),
        scratch_shapes=[pltpu.SemaphoreType.DMA((count,))],
        cost_estimate=pl.CostEstimate(
            flops=0, bytes_accessed=4 * rows * width, transcendentals=0
        ),
        compiler_params=pltpu.CompilerParams(vmem_limit_bytes=VMEM_LIMIT),
        name="pack",
    )(*pieces)


def norm_kernel(count, *refs):
    gain_ref, out_ref = refs[count], refs[-2]
    pack_kernel(count, *refs[:count], *refs[-2:])
    tile = 256

    @pl.loop(0, out_ref.shape[0] // tile)
    def _(i):
        rows = pl.ds(pl.multiple_of(i * tile, tile), tile)
        values = out_ref[rows, :].astype(f32)
        out_ref[rows, :] = (values * rms_inverse(values) * gain_ref[...]).astype(bf16)


def pack_normed(pieces, gain, early):
    rows, width = sum(p.shape[0] for p in pieces), pieces[0].shape[1]
    count = len(pieces)
    return pl.pallas_call(
        functools.partial(norm_kernel, count),
        in_specs=[pl.BlockSpec(memory_space=pl.ANY)] * count
        + [pl.BlockSpec(memory_space=pltpu.VMEM)]
        + [pl.BlockSpec(memory_space=pl.ANY)] * len(early),
        out_specs=pl.BlockSpec(memory_space=pltpu.VMEM),
        out_shape=jax.ShapeDtypeStruct((rows, width), bf16),
        scratch_shapes=[pltpu.SemaphoreType.DMA((count,))],
        cost_estimate=pl.CostEstimate(
            flops=8 * rows * width, bytes_accessed=4 * rows * width, transcendentals=0
        ),
        compiler_params=pltpu.CompilerParams(vmem_limit_bytes=VMEM_LIMIT),
        name="pack_normed",
    )(*pieces, gain, *early)


def plane_neighbours(own):
    return swap(own, "col"), swap(own, "row")


def plane_far(neighbours, *waits):
    across, along = neighbours
    half = across.shape[0] // 2
    return (
        swap(after(across[:half], *waits), "row"),
        swap(after(along[half:], *waits), "col"),
    )


def with_partner(pieces, swapped=()):
    return pieces + list(swapped) + [swap(piece, "tp") for piece in pieces[len(swapped) :]]


def chip_sums(front, back):
    pairs = []
    for own, other in (front, back):
        shape = (4, own.shape[0] // 4, own.shape[1])
        pairs.append((own.reshape(shape), swap(other, "tp").reshape(shape)))
    return pairs


def quarter(pair, k):
    return pair[0][k].astype(f32) + pair[1][k].astype(f32)


def first_operands(sums):
    front, back = sums
    return (
        jnp.concatenate([quarter(front, 1), quarter(front, 3)]).astype(bf16),
        (back[0][2:].astype(f32) + back[1][2:].astype(f32)).astype(bf16),
    )


def reduce_first(operands, *waits):
    front, back = operands
    rows = front.shape[0] // 2
    return (
        swap(after(front, *waits), "col").reshape(2, rows, -1),
        swap(after(back, *waits), "row"),
    )


def reduce_operands(sums, arrived):
    front, back = sums
    got, got_back = arrived[0].astype(f32), arrived[1].astype(f32)
    return (
        (quarter(front, 0) + got[0], (quarter(front, 2) + got[1]).astype(bf16)),
        (quarter(back, 0) + got_back[0], (quarter(back, 1) + got_back[1]).astype(bf16)),
    )


def last_swaps(operands, *waits):
    return (
        swap(after(operands[0][1], *waits), "row"),
        swap(after(operands[1][1], *waits), "col"),
    )


def reduce_last(operands, swapped):
    return jnp.concatenate(
        [keep + last.astype(f32) for (keep, _), last in zip(operands, swapped)], axis=1
    )


def joined(front_ref, front_last_ref, back_ref, back_last_ref):
    return jnp.concatenate(
        [
            front_ref[...] + front_last_ref[...].astype(f32),
            back_ref[...] + back_last_ref[...].astype(f32),
        ],
        axis=1,
    )


def hidden_kernel(front, front_last, back, back_last, tokens_ref, gain_ref, hidden_ref, normed_ref):
    hidden = tokens_ref[...].astype(f32) + joined(front, front_last, back, back_last)
    hidden_ref[...] = hidden
    normed_ref[...] = (hidden * rms_inverse(hidden) * gain_ref[...]).astype(bf16)


def add_and_norm(operands, last, tokens, gain):
    halves = [part for (keep, _), got in zip(operands, last) for part in (keep, got)]
    return pl.pallas_call(
        hidden_kernel,
        in_specs=[pl.BlockSpec(memory_space=pltpu.VMEM)] * 6,
        out_specs=[pl.BlockSpec(memory_space=pltpu.VMEM)] * 2,
        out_shape=[
            jax.ShapeDtypeStruct(tokens.shape, f32),
            jax.ShapeDtypeStruct(tokens.shape, bf16),
        ],
        cost_estimate=pl.CostEstimate(
            flops=10 * tokens.size, bytes_accessed=14 * tokens.size, transcendentals=0
        ),
        compiler_params=pltpu.CompilerParams(vmem_limit_bytes=VMEM_LIMIT),
        name="add_and_norm",
    )(*halves, tokens, gain)


def back_kernel(front, front_last, back, back_last, values_ref, base_ref, gain_ref, *outs):
    values = values_ref[...].astype(f32)
    inverse = rms_inverse(values)
    unit = values * inverse
    scaled = joined(front, front_last, back, back_last) * gain_ref[...]
    grad = base_ref[...].astype(f32) + inverse * (
        scaled - unit * jnp.mean(scaled * unit, axis=-1, keepdims=True)
    )
    for out in outs:
        out[...] = grad.astype(out.dtype)


def norm_back(operands, last, values, base, gain, dtypes):
    halves = [part for (keep, _), got in zip(operands, last) for part in (keep, got)]
    return pl.pallas_call(
        back_kernel,
        in_specs=[pl.BlockSpec(memory_space=pltpu.VMEM)] * 7,
        out_specs=[pl.BlockSpec(memory_space=pltpu.VMEM)] * len(dtypes),
        out_shape=[jax.ShapeDtypeStruct(values.shape, dtype) for dtype in dtypes],
        cost_estimate=pl.CostEstimate(
            flops=16 * values.size, bytes_accessed=18 * values.size, transcendentals=0
        ),
        compiler_params=pltpu.CompilerParams(vmem_limit_bytes=VMEM_LIMIT),
        name="norm_back",
    )(*halves, values, base, gain)


def split_kernel(spans, member_ref, *refs):
    sources, outs = refs[: len(spans)], refs[len(spans) :]
    for k in range(4):
        target = member_ref[0] ^ k
        column = 0
        for source, (offset, stride, width, shift) in zip(sources, spans):
            start = pl.multiple_of((target >> shift) * stride + offset, 128)
            outs[k][:, column : column + width] = source[:, pl.ds(start, width)]
            column += width


def split(member, sources, spans):
    rows, width = sources[0].shape[0], sum(span[2] for span in spans)
    whole = pl.BlockSpec(memory_space=pltpu.VMEM)
    return pl.pallas_call(
        functools.partial(split_kernel, spans),
        in_specs=[pl.BlockSpec(memory_space=pltpu.SMEM)] + [whole] * len(sources),
        out_specs=[whole] * 4,
        out_shape=[jax.ShapeDtypeStruct((rows, width), bf16)] * 4,
        cost_estimate=pl.CostEstimate(
            flops=0, bytes_accessed=16 * rows * width, transcendentals=0
        ),
        compiler_params=pltpu.CompilerParams(vmem_limit_bytes=VMEM_LIMIT),
        name="split",
    )(member, *sources)


def place_kernel(member_ref, *refs):
    rows = refs[0].shape[0]
    for k in range(4):
        start = pl.multiple_of((member_ref[0] ^ k) * rows, rows)
        column = 0
        for out_ref in refs[4:]:
            width = out_ref.shape[1]
            out_ref[pl.ds(start, rows), :] = refs[k][:, column : column + width]
            column += width


def place_rows(member, pieces, *widths):
    rows, width = pieces[0].shape
    whole = pl.BlockSpec(memory_space=pltpu.VMEM)
    return pl.pallas_call(
        place_kernel,
        in_specs=[pl.BlockSpec(memory_space=pltpu.SMEM)] + [whole] * 4,
        out_specs=[whole] * len(widths or (width,)),
        out_shape=[
            jax.ShapeDtypeStruct((4 * rows, w), bf16) for w in widths or (width,)
        ],
        cost_estimate=pl.CostEstimate(
            flops=0, bytes_accessed=16 * rows * width, transcendentals=0
        ),
        compiler_params=pltpu.CompilerParams(vmem_limit_bytes=VMEM_LIMIT),
        name="place_rows",
    )(member, *pieces)


def pick_kernel(member_ref, *refs):
    sources, outs = refs[:-4], refs[-4:]
    rows = outs[0].shape[0]
    for k in range(4):
        start = pl.multiple_of((member_ref[0] ^ k) * rows, rows)
        column = 0
        for source in sources:
            width = source.shape[1]
            outs[k][:, column : column + width] = source[pl.ds(start, rows), :]
            column += width


def pick_rows(member, *sources):
    rows, width = sources[0].shape[0] // 4, sum(source.shape[1] for source in sources)
    whole = pl.BlockSpec(memory_space=pltpu.VMEM)
    return pl.pallas_call(
        pick_kernel,
        in_specs=[pl.BlockSpec(memory_space=pltpu.SMEM)] + [whole] * len(sources),
        out_specs=[whole] * 4,
        out_shape=[jax.ShapeDtypeStruct((rows, width), bf16)] * 4,
        cost_estimate=pl.CostEstimate(
            flops=0, bytes_accessed=16 * rows * width, transcendentals=0
        ),
        compiler_params=pltpu.CompilerParams(vmem_limit_bytes=VMEM_LIMIT),
        name="pick_rows",
    )(member, *sources)


def swap_all(pieces):
    return [pieces[0]] + [swap_plane(pieces[k], k) for k in (1, 2, 3)]


def mlp_final_kernel(parts, stride, member_ref, gate_w_ref, up_w_ref, *refs):
    pieces, outs, gain_ref = refs[:-4], refs[-4:-1], refs[-1]
    for n, chunks in enumerate(parts):
        for k in range(4):
            start = 0
            for offset, width in chunks:
                column = pl.multiple_of((member_ref[0] ^ k) * stride + offset, 128)
                for i in range(3):
                    part = pieces[4 * n + k][:, start : start + width]
                    outs[i][:, pl.ds(column, width)] = part.astype(f32)
                    start += width
    gain_ref[...] = jnp.sum(
        gate_w_ref[...].astype(f32) * outs[0][...] + up_w_ref[...].astype(f32) * outs[1][...],
        axis=1,
        keepdims=True,
    )


def mlp_final(member, gate_weight, up_weight, chunks, parts):
    rows, hidden = gate_weight.shape
    pieces = [piece for part in parts for piece in part]
    whole = pl.BlockSpec(memory_space=pltpu.VMEM)
    return pl.pallas_call(
        functools.partial(mlp_final_kernel, chunks, hidden // 4),
        in_specs=[pl.BlockSpec(memory_space=pltpu.SMEM)] + [whole] * (2 + len(pieces)),
        out_specs=[whole] * 4,
        out_shape=[jax.ShapeDtypeStruct((rows, hidden), f32)] * 3
        + [jax.ShapeDtypeStruct((rows, 1), f32)],
        cost_estimate=pl.CostEstimate(
            flops=4 * rows * hidden, bytes_accessed=22 * rows * hidden, transcendentals=0
        ),
        compiler_params=pltpu.CompilerParams(vmem_limit_bytes=VMEM_LIMIT),
        name="mlp_final",
    )(member, gate_weight, up_weight, *pieces)


def attention_final_kernel(member_ref, qw_ref, kw_ref, vw_ref, *refs):
    pieces = refs[:4]
    q_ref, k_ref, v_ref, o_ref, gain_ref = refs[4:]
    member = member_ref[0]
    for k in range(4):
        columns = pl.ds(pl.multiple_of((member ^ k) * HS, HS), HS)
        q_ref[:, columns] = pieces[k][:, :HS].astype(f32)
        o_ref[:, columns] = pieces[k][:, 3 * HS :].astype(f32)
    for h in range(2):
        columns = pl.ds(pl.multiple_of(((member >> 1) ^ h) * HS, HS), HS)
        both = sum(pieces[2 * h + i][:, HS : 3 * HS].astype(f32) for i in range(2))
        k_ref[:, columns] = both[:, :HS]
        v_ref[:, columns] = both[:, HS:]

    def row_sum(weight_ref, grad_ref):
        return jnp.sum(weight_ref[...].astype(f32) * grad_ref[...], axis=1, keepdims=True)

    gain_ref[...] = row_sum(qw_ref, q_ref) + row_sum(kw_ref, k_ref) + row_sum(vw_ref, v_ref)


def attention_final(member, query_weight, key_weight, value_weight, pieces):
    rows, width = query_weight.shape
    whole = pl.BlockSpec(memory_space=pltpu.VMEM)
    shapes = [width, width // 2, width // 2, width, 1]
    return pl.pallas_call(
        attention_final_kernel,
        in_specs=[pl.BlockSpec(memory_space=pltpu.SMEM)] + [whole] * 7,
        out_specs=[whole] * 5,
        out_shape=[jax.ShapeDtypeStruct((rows, n), f32) for n in shapes],
        cost_estimate=pl.CostEstimate(
            flops=4 * rows * width, bytes_accessed=24 * rows * width, transcendentals=0
        ),
        compiler_params=pltpu.CompilerParams(vmem_limit_bytes=VMEM_LIMIT),
        name="attention_final",
    )(member, query_weight, key_weight, value_weight, *pieces)


def rms_inverse(values):
    return lax.rsqrt(jnp.mean(values * values, axis=-1, keepdims=True) + epsilon)


def rope_tables(positions):
    half_size = HS // 2
    indices = jnp.arange(half_size, dtype=f32)
    inverse = theta_base ** (-2.0 * indices / HS)
    angles = positions.astype(f32)[:, None] * inverse[None, :]
    return jnp.cos(angles), jnp.sin(angles)


def rotate(vectors, cos, sin):
    front, back = vectors[:, : HS // 2], vectors[:, HS // 2 :]
    return jnp.concatenate([front * cos - back * sin, back * cos + front * sin], axis=-1)


def unrotate(grads, cos, sin):
    front, back = grads[:, : HS // 2], grads[:, HS // 2 :]
    return jnp.concatenate([front * cos + back * sin, back * cos - front * sin], axis=-1)


def mlp_tile(width, normed, cot, weight_ref):
    both = product(normed, weight_ref[:, : 2 * width])
    d_inner = product(cot, weight_ref[:, 2 * width :])
    gate, upward = both[:, :width], both[:, width:]
    sig = 1.0 / (1.0 + jnp.exp(-gate))
    silu = gate * sig
    d_gate = d_inner * upward * sig * (1.0 + gate * (1.0 - sig))
    return (
        (silu * upward).astype(bf16),
        jnp.concatenate([d_gate, d_inner * silu], axis=1).astype(bf16),
    )


def mlp_kernel(width, normed_ref, cot_ref, weight_ref, inner_ref, grads_ref):
    inner_ref[...], grads_ref[...] = mlp_tile(
        width, normed_ref[...], cot_ref[...], weight_ref
    )


def tail_kernel(width, normed_ref, cot_ref, weight_ref, base_ref, *refs):
    inner_ref, grads_ref, front_ref, back_ref = refs[-4:]
    inner, grads = mlp_tile(width, normed_ref[...], cot_ref[...], weight_ref)
    inner_ref[...], grads_ref[...] = inner, grads
    total = times_transposed(grads, weight_ref[:, : 2 * width]) + base_ref[...]
    half = total.shape[1] // 2
    front_ref[...] = total[:, :half].astype(front_ref.dtype)
    back_ref[...] = total[:, half:].astype(back_ref.dtype)


def mlp_tail(normed, cot, weight, base, part, dtype, chained=()):
    tokens, features = normed.shape
    width = weight.shape[1] // 3
    tile, rows = 256, tokens // 2
    steps = rows // tile
    count = len(chained)
    return pl.pallas_call(
        functools.partial(tail_kernel, width),
        grid=(steps,),
        in_specs=[
            pl.BlockSpec((tile, features), lambda i: (part * steps + i, 0)),
            pl.BlockSpec((tile, features), lambda i: (part * steps + i, 0)),
            pl.BlockSpec((features, 3 * width), lambda i: (0, 0)),
            pl.BlockSpec((tile, features), lambda i: (i, 0)),
        ]
        + [pl.BlockSpec(memory_space=pl.ANY)] * count,
        out_specs=[
            pl.BlockSpec((tile, width), lambda i: (part * steps + i, 0)),
            pl.BlockSpec((tile, 2 * width), lambda i: (part * steps + i, 0)),
            pl.BlockSpec((tile, features // 2), lambda i: (i, 0)),
            pl.BlockSpec((tile, features // 2), lambda i: (i, 0)),
        ],
        out_shape=[
            jax.ShapeDtypeStruct((tokens, width), bf16),
            jax.ShapeDtypeStruct((tokens, 2 * width), bf16),
            jax.ShapeDtypeStruct((rows, features // 2), dtype),
            jax.ShapeDtypeStruct((rows, features // 2), dtype),
        ],
        input_output_aliases={4 + i: i for i in range(count)},
        cost_estimate=pl.CostEstimate(
            flops=10 * rows * features * width,
            bytes_accessed=2 * features * (5 * rows + 3 * width),
            transcendentals=rows * width,
        ),
        compiler_params=pltpu.CompilerParams(vmem_limit_bytes=VMEM_LIMIT),
        name="mlp_tail",
    )(normed, cot, weight, base, *chained)


def mlp_chunk(normed, cot, weight):
    tokens, features = normed.shape
    width = weight.shape[1] // 3
    tile = 256
    return pl.pallas_call(
        functools.partial(mlp_kernel, width),
        grid=(tokens // tile,),
        in_specs=[
            pl.BlockSpec((tile, features), lambda i: (i, 0)),
            pl.BlockSpec((tile, features), lambda i: (i, 0)),
            pl.BlockSpec((features, 3 * width), lambda i: (0, 0)),
        ],
        out_specs=[
            pl.BlockSpec((tile, width), lambda i: (i, 0)),
            pl.BlockSpec((tile, 2 * width), lambda i: (i, 0)),
        ],
        out_shape=[
            jax.ShapeDtypeStruct((tokens, width), bf16),
            jax.ShapeDtypeStruct((tokens, 2 * width), bf16),
        ],
        cost_estimate=pl.CostEstimate(
            flops=6 * tokens * features * width,
            bytes_accessed=2 * features * (2 * tokens + 3 * width),
            transcendentals=tokens * width,
        ),
        compiler_params=pltpu.CompilerParams(vmem_limit_bytes=VMEM_LIMIT),
        name="mlp_chunk",
    )(normed, cot, weight)


def sum_kernel(count, *refs):
    lefts, rights, out_ref = refs[:count], refs[count : 2 * count], refs[-1]
    total = times_transposed(lefts[0][...], rights[0][...])
    for left, right in zip(lefts[1:], rights[1:]):
        total += times_transposed(left[...], right[...])
    for base in refs[2 * count : -1]:
        total += base[...].astype(f32)
    out_ref[...] = total.astype(out_ref.dtype)


def chunk_sum(lefts, rights, column, part, half, dtype):
    count = len(lefts)
    tokens, features = lefts[0].shape[0], rights[0].shape[0]
    widths = [left.shape[1] for left in lefts]
    rows = tokens // 2
    tile = 256
    if half is not None:
        features, tile = features // 2, 512
    steps = rows // tile
    block = half or 0
    return pl.pallas_call(
        functools.partial(sum_kernel, count),
        grid=(steps,),
        in_specs=[pl.BlockSpec((tile, w), lambda i: (part * steps + i, 0)) for w in widths]
        + [pl.BlockSpec((features, w), lambda i: (block, column)) for w in widths],
        out_specs=pl.BlockSpec((tile, features), lambda i: (i, 0)),
        out_shape=jax.ShapeDtypeStruct((rows, features), dtype),
        cost_estimate=pl.CostEstimate(
            flops=2 * rows * features * sum(widths),
            bytes_accessed=2 * sum(widths) * (rows + features) + 4 * rows * features,
            transcendentals=0,
        ),
        compiler_params=pltpu.CompilerParams(vmem_limit_bytes=VMEM_LIMIT),
        name="chunk_sum",
    )(*lefts, *rights)


def grads_kernel(count, *refs):
    column = 0
    for left, right in zip(refs[:count], refs[count : 2 * count]):
        width = right.shape[1]
        refs[-1][:, column : column + width] = outer_sum(left[...], right[...]).astype(bf16)
        column += width


def weight_grads(*pairs):
    lefts, rights = [left for left, _ in pairs], [right for _, right in pairs]
    count = len(pairs)
    tokens, features = lefts[0].shape
    widths = [right.shape[1] for right in rights]
    tile = 256
    return pl.pallas_call(
        functools.partial(grads_kernel, count),
        grid=(features // tile,),
        in_specs=[pl.BlockSpec((tokens, tile), lambda i: (0, i))] * count
        + [pl.BlockSpec((tokens, w), lambda i: (0, 0)) for w in widths],
        out_specs=pl.BlockSpec((tile, sum(widths)), lambda i: (i, 0)),
        out_shape=jax.ShapeDtypeStruct((features, sum(widths)), bf16),
        cost_estimate=pl.CostEstimate(
            flops=2 * tokens * features * sum(widths),
            bytes_accessed=2 * (count * tokens * features + sum(widths) * (tokens + features)),
            transcendentals=0,
        ),
        compiler_params=pltpu.CompilerParams(vmem_limit_bytes=VMEM_LIMIT),
        name="weight_grads",
    )(*lefts, *rights)


def project_kernel(place_ref, normed_ref, weight_ref, cos_ref, sin_ref, q_ref, k_ref, v_ref):
    step = pl.program_id(0)
    cos, sin = cos_ref[...], sin_ref[...]
    qkv = product(normed_ref[...], weight_ref[...])
    query = rotate(qkv[:, :HS], cos, sin).astype(bf16) * HS ** (-0.5)
    keys = rotate(qkv[:, HS : 2 * HS], cos, sin).astype(bf16)
    vals = qkv[:, 2 * HS :].astype(bf16)
    blocks = normed_ref.shape[0] // BLOCK
    for b in range(blocks):
        rows = pl.ds(pl.multiple_of(place_ref[step * blocks + b] * BLOCK, BLOCK), BLOCK)
        part = slice(b * BLOCK, (b + 1) * BLOCK)
        q_ref[rows, :] = query[part]
        k_ref[rows, :] = keys[part]
        v_ref[rows, :] = vals[part]


def project(place, normed, weight, cos, sin):
    tokens, features = normed.shape
    tile = 256
    whole = pl.BlockSpec((tokens, HS), lambda i, place: (0, 0))
    return pl.pallas_call(
        project_kernel,
        grid_spec=pltpu.PrefetchScalarGridSpec(
            num_scalar_prefetch=1,
            grid=(tokens // tile,),
            in_specs=[
                pl.BlockSpec((tile, features), lambda i, place: (i, 0)),
                pl.BlockSpec((features, 3 * HS), lambda i, place: (0, 0)),
                pl.BlockSpec((tile, HS // 2), lambda i, place: (i, 0)),
                pl.BlockSpec((tile, HS // 2), lambda i, place: (i, 0)),
            ],
            out_specs=[whole] * 3,
        ),
        out_shape=[jax.ShapeDtypeStruct((tokens, HS), bf16)] * 3,
        cost_estimate=pl.CostEstimate(
            flops=6 * tokens * features * HS,
            bytes_accessed=2 * features * (tokens + 3 * HS) + 10 * tokens * HS,
            transcendentals=0,
        ),
        compiler_params=pltpu.CompilerParams(vmem_limit_bytes=VMEM_LIMIT),
        name="project",
    )(place, normed, weight, cos, sin)


TILE = 256


def tile_masks():
    rows = lax.broadcasted_iota(jnp.int32, (TILE, TILE), 0)
    cols = lax.broadcasted_iota(jnp.int32, (TILE, TILE), 1)
    causal = rows >= cols
    return causal, causal & (rows // BLOCK == cols // BLOCK)


def block_rows(order_ref, index):
    return pl.ds(pl.multiple_of(order_ref[index] * BLOCK, BLOCK), BLOCK)


def forward_kernel(order_ref, q_ref, k_ref, v_ref, mixed_ref, lse_ref, peak_ref):
    causal, inside = tile_masks()
    prompt = GROUP // 2
    top = jnp.full((TILE, 1), masked_value, f32)
    for i in range(GROUP // TILE):
        rows = slice(i * TILE, (i + 1) * TILE)
        past = min(i * TILE, prompt)
        query = q_ref[rows, :]
        near = times_transposed(query, k_ref[rows, :])
        near = jnp.where(causal if i * TILE < prompt else inside, near, masked_value)
        peak = jnp.max(near, axis=1, keepdims=True)
        if past:
            far = times_transposed(query, k_ref[:past, :])
            peak = jnp.maximum(peak, jnp.max(far, axis=1, keepdims=True))
            far = jnp.exp(far - peak)
        near = jnp.exp(near - peak)
        total = jnp.sum(near, axis=1, keepdims=True)
        if past:
            total += jnp.sum(far, axis=1, keepdims=True)
        share = 1.0 / total
        mixed = product((near * share).astype(bf16), v_ref[rows, :])
        if past:
            mixed += product((far * share).astype(bf16), v_ref[:past, :])
        mixed = mixed.astype(bf16)
        for b in range(TILE // BLOCK):
            mixed_ref[block_rows(order_ref, i * (TILE // BLOCK) + b), :] = mixed[
                b * BLOCK : (b + 1) * BLOCK
            ]
        lse_ref[rows, :] = peak + jnp.log(total)
        top = jnp.maximum(top, peak)
    peak_ref[...] = jnp.full(peak_ref.shape, jnp.max(top), f32)


def attention_forward(order, query, keys, vals):
    whole = pl.BlockSpec(memory_space=pltpu.VMEM)
    return pl.pallas_call(
        forward_kernel,
        in_specs=[pl.BlockSpec(memory_space=pltpu.SMEM), whole, whole, whole],
        out_specs=[whole] * 3,
        out_shape=[
            jax.ShapeDtypeStruct((GROUP, HS), bf16),
            jax.ShapeDtypeStruct((GROUP, 1), f32),
            jax.ShapeDtypeStruct((8, 128), f32),
        ],
        cost_estimate=pl.CostEstimate(
            flops=2 * GROUP * GROUP * HS,
            bytes_accessed=8 * GROUP * HS,
            transcendentals=GROUP * GROUP // 2,
        ),
        compiler_params=pltpu.CompilerParams(vmem_limit_bytes=VMEM_LIMIT),
        name="attention_forward",
    )(order, query, keys, vals)


def backward_kernel(
    order_ref, q_ref, k_ref, v_ref, lse_ref, mixed_ref, cos_ref, sin_ref, out_ref, dk_ref, dv_ref
):
    causal, inside = tile_masks()
    prompt = GROUP // 2
    blocks = TILE // BLOCK

    def back(grad, index):
        rows = block_rows(order_ref, index)
        return rows, unrotate(grad, cos_ref[rows, :], sin_ref[rows, :]).astype(bf16)

    for i in range(GROUP // TILE):
        rows = slice(i * TILE, (i + 1) * TILE)
        past = min(i * TILE, prompt)
        query, lse = q_ref[rows, :], lse_ref[rows, :]
        d_mixed = jnp.concatenate(
            [mixed_ref[block_rows(order_ref, i * blocks + b), :] for b in range(blocks)], axis=0
        )
        near = times_transposed(query, k_ref[rows, :])
        near = jnp.where(causal if i * TILE < prompt else inside, near, masked_value)
        near = jnp.exp(near - lse)
        d_near = times_transposed(d_mixed, v_ref[rows, :])
        inner = jnp.sum(near * d_near, axis=1, keepdims=True)
        if past:
            far = jnp.exp(times_transposed(query, k_ref[:past, :]) - lse)
            d_far = times_transposed(d_mixed, v_ref[:past, :])
            inner += jnp.sum(far * d_far, axis=1, keepdims=True)
        d_near = (near * (d_near - inner)).astype(bf16)
        d_query = product(d_near, k_ref[rows, :])
        dk_ref[rows, :] = outer_sum(d_near, query)
        dv_ref[rows, :] = outer_sum(near.astype(bf16), d_mixed)
        if past:
            d_far = (far * (d_far - inner)).astype(bf16)
            d_query += product(d_far, k_ref[:past, :])
            dk_ref[:past, :] += outer_sum(d_far, query)
            dv_ref[:past, :] += outer_sum(far.astype(bf16), d_mixed)
        d_query = d_query * HS ** (-0.5)
        for b in range(blocks):
            where, grad = back(d_query[b * BLOCK : (b + 1) * BLOCK], i * blocks + b)
            out_ref[where, :HS] = grad
    for c in range(GROUP // BLOCK):
        part = slice(c * BLOCK, (c + 1) * BLOCK)
        where, grad = back(dk_ref[part, :], c)
        out_ref[where, HS : 2 * HS] = grad
        out_ref[where, 2 * HS :] = dv_ref[part, :].astype(bf16)


def attention_backward(order, query, keys, vals, lse, d_mixed, cos, sin):
    whole = pl.BlockSpec(memory_space=pltpu.VMEM)
    return pl.pallas_call(
        backward_kernel,
        in_specs=[pl.BlockSpec(memory_space=pltpu.SMEM)] + [whole] * 7,
        out_specs=whole,
        out_shape=jax.ShapeDtypeStruct((GROUP, 3 * HS), bf16),
        scratch_shapes=[pltpu.VMEM((GROUP, HS), f32), pltpu.VMEM((GROUP, HS), f32)],
        cost_estimate=pl.CostEstimate(
            flops=5 * GROUP * GROUP * HS,
            bytes_accessed=20 * GROUP * HS,
            transcendentals=GROUP * GROUP // 2,
        ),
        compiler_params=pltpu.CompilerParams(vmem_limit_bytes=VMEM_LIMIT),
        name="attention_backward",
    )(order, query, keys, vals, lse, d_mixed, cos, sin)


def local(
    tokens,
    cotangent,
    segment,
    position,
    clip_limit,
    attn_gain,
    query_weight,
    key_weight,
    value_weight,
    output_weight,
    mlp_gain,
    gate_weight,
    up_weight,
    down_weight,
):
    groups = lax.axis_size("group")
    group = lax.axis_index("group")
    core = lax.axis_index("tp")
    member = lax.axis_index(PLANE)
    token_rows = tokens.shape[0]
    own_rows, features = query_weight.shape[0], tokens.shape[1]
    hidden_own = gate_weight.shape[1] // 4
    chunks, offset = [], 0
    for part in SIXTEENTHS:
        chunks.append((offset, hidden_own * part // 16))
        offset += hidden_own * part // 16
    member_at = member.astype(jnp.int32).reshape(1)

    def own_order(array):
        parts = []
        for j in range(2):
            for k in range(4):
                start = group * GROUP + (member ^ k) * (2 * token_rows) + (core ^ j) * token_rows
                parts.append(lax.dynamic_slice_in_dim(array, start, token_rows))
        return jnp.concatenate(parts)

    def collect(blocks):
        return lax.all_gather(blocks, "group", axis=0, tiled=True)

    def mlp_exchange(some, waits):
        weights = [after(a, *waits) for a in (gate_weight, up_weight, down_weight)]
        spans = tuple((start, hidden_own, count, 0) for start, count in some for _ in range(3))
        return swap_all(split(member_at, weights * len(some), spans))

    seg, pos = own_order(segment), own_order(position)
    cos, sin = rope_tables(pos)
    seg_blocks, pos_blocks = seg[::BLOCK], pos[::BLOCK]
    half_blocks = GROUP // BLOCK // 2
    place = jnp.where(seg_blocks == 0, pos_blocks // BLOCK, half_blocks - 1 + seg_blocks)
    labels = jnp.arange(2 * half_blocks, dtype=jnp.int32)
    order = jnp.sum(jnp.where(place[None, :] == labels[:, None], labels[None, :], 0), axis=1)
    index = lax.axis_index(FSDP)
    gains = jnp.stack([attn_gain, mlp_gain])[:, None, :]
    gains = jnp.where(jnp.arange(4 * groups)[None, :, None] == index, gains, 0)
    gains, gain_rounds = combine_all(gains, groups, lambda a, b: a + b)
    gains = gains.reshape(2, features).astype(f32)
    head, pair = (0, HS, HS, 0), (0, HS, HS, 1)
    attn_pieces = swap_all(
        split(
            member_at,
            (query_weight, key_weight, value_weight, output_weight),
            (head, pair, pair, head),
        )
    )
    attn_weights = collect(
        *place_rows(member_at, [after(attn_pieces[0], *gain_rounds[0])] + attn_pieces[1:])
    )
    late_tokens = after(tokens, *attn_pieces[1:], *gain_rounds[-1])
    neighbours = plane_neighbours(late_tokens)
    tokens_far = plane_far(neighbours)
    tokens_mine = [late_tokens, *neighbours, *tokens_far]
    tokens_near = [swap(piece, "tp") for piece in tokens_mine[:3]]
    normed_all = pack_normed(
        with_partner(tokens_mine, tokens_near), gains[:1], (cos, sin, place, order)
    )
    pieces_0 = mlp_exchange(chunks[:1], (*tokens_far, *tokens_near))
    (blocks_0,) = place_rows(member_at, [after(pieces_0[0], normed_all)] + pieces_0[1:])
    late_cot = after(cotangent, *pieces_0[1:])
    cot_near = [swap_plane(late_cot, k) for k in (1, 2)]
    query, keys, vals = project(
        place, normed_all, attn_weights, cos, sin
    )
    mixed, logsum, peak = attention_forward(order, query, keys, vals)

    head_top = jnp.where(jnp.arange(4) == member, peak[0, :4], masked_value)
    head_top, head_rounds = combine_all(head_top, groups, jnp.maximum)

    def projected(left, column, *waits):
        lefts = (left, after(left, *waits))
        return [
            [
                chunk_sum([lefts[j]], [attn_weights], column, j, h, bf16 if j else f32)
                for j in (0, 1)
            ]
            for h in range(2)
        ]

    attn_sums = chip_sums(*projected(mixed, 3, *cot_near))
    arrived = reduce_first(first_operands(attn_sums))
    attn_operands = reduce_operands(attn_sums, arrived)
    attn_last = last_swaps(attn_operands, *head_rounds[0])
    hidden, own_normed = add_and_norm(attn_operands, attn_last, tokens, gains[1:])
    neighbours = plane_neighbours(own_normed)
    normed_far = plane_far(neighbours, *head_rounds[-1])
    pieces_1 = mlp_exchange(chunks[1:], normed_far)
    mlp_weights = [collect(blocks_0), collect(*place_rows(member_at, pieces_1))]
    cot_far = swap_plane(after(late_cot, *normed_far), 3)
    normed_mlp = pack(with_partner([own_normed, *neighbours, *normed_far]))
    cot_all = pack(with_partner([late_cot, *cot_near, cot_far]))

    def line_sum(partial):
        return lax.psum_scatter(partial, "group", scatter_dimension=0, tiled=True)

    inner_0, both_0 = mlp_chunk(normed_mlp, cot_all, mlp_weights[0])
    grads_0 = weight_grads((normed_mlp, both_0), (cot_all, inner_0))
    sum_0 = line_sum(grads_0)
    late_both = after(both_0, grads_0)
    early = [chunk_sum([late_both], mlp_weights[:1], 0, j, None, f32) for j in range(2)]
    inner_1, both_1, front_1, back_1 = mlp_tail(
        after(normed_mlp, *early), cot_all, mlp_weights[1], early[1], 1, bf16
    )
    inner_1, both_1, front_0, back_0 = mlp_tail(
        normed_mlp, cot_all, mlp_weights[1], early[0], 0, f32, (inner_1, both_1)
    )

    mlp_sums = chip_sums((front_0, front_1), (back_0, back_1))
    operands = first_operands(mlp_sums)
    arrived = reduce_first(operands)
    inners = [after(inner, *operands) for inner in (inner_0, inner_1)]
    out_parts = [
        [chunk_sum(inners, mlp_weights, 2, j, h, bf16 if j else f32) for j in (0, 1)]
        for h in range(2)
    ]
    mlp_operands = reduce_operands(mlp_sums, arrived)
    mlp_last = last_swaps(mlp_operands, *out_parts[0], *out_parts[1])
    d_hidden, own_d = norm_back(
        mlp_operands, mlp_last, hidden, cotangent, gains[1:], (f32, bf16)
    )
    neighbours = plane_neighbours(own_d)
    late_both = after(both_1, own_d)
    grads_1 = weight_grads((normed_mlp, late_both), (cot_all, inner_1))
    sum_1 = line_sum(after(grads_1, *neighbours))
    d_far = plane_far(neighbours, grads_1)
    d_attn_all = pack(with_partner([own_d, *neighbours, *d_far]))
    out_parts = [[part[0], after(part[1], *d_far)] for part in out_parts]
    out_sums = chip_sums(*out_parts)
    out_operands = reduce_operands(out_sums, reduce_first(first_operands(out_sums)))

    def send_grads(sources, *waits):
        first = after(sources[0], *waits) if waits else sources[0]
        return swap_all(pick_rows(member_at, first, *sources[1:]))


    d_mixed = product(d_attn_all, attn_weights[:, 3 * HS :]).astype(bf16)
    d_qkv = attention_backward(order, query, keys, vals, logsum, d_mixed, cos, sin)
    attn_grads = weight_grads((normed_all, d_qkv), (d_attn_all, mixed))
    attn_sum = line_sum(attn_grads)
    out_last = last_swaps(out_operands)
    late_qkv = after(d_qkv, attn_grads)
    qkv_sums = chip_sums(*projected(late_qkv, 0))
    arrived = reduce_first(first_operands(qkv_sums))
    qkv_operands = reduce_operands(qkv_sums, arrived)
    qkv_last = last_swaps(qkv_operands)
    (tokens_grad,) = norm_back(qkv_operands, qkv_last, tokens, d_hidden, gains[:1], (f32,))
    block_out = (hidden + reduce_last(out_operands, out_last)).astype(bf16)

    final_0 = send_grads([sum_0], *arrived)
    final_1 = send_grads([sum_1], *arrived)
    gate_grad, up_grad, down_grad, mlp_gain_row = mlp_final(
        member_at, gate_weight, up_weight, (chunks[:1], chunks[1:]), [final_0, final_1]
    )
    query_grad, key_grad, value_grad, output_grad, attn_gain_row = attention_final(
        member_at,
        query_weight,
        key_weight,
        value_weight,
        send_grads([attn_sum], mlp_gain_row, tokens_grad, *out_last),
    )
    gain_grads = jnp.concatenate([attn_gain_row, mlp_gain_row], axis=1)
    gain_grads = gain_grads + swap(gain_grads, "tp")
    attn_gain_grad = gain_grads[:, 0] / attn_gain.astype(f32)
    mlp_gain_grad = gain_grads[:, 1] / mlp_gain.astype(f32)

    factor = clip_limit / jnp.maximum(head_top, clip_limit)
    query_scale = jnp.repeat(jnp.sqrt(factor), HS)
    key_factor = jnp.min(factor.reshape(2, 2), axis=1)
    key_scale = jnp.repeat(jnp.sqrt(key_factor), HS)
    query_clipped = (query_weight.astype(f32) * query_scale[None, :]).astype(bf16)
    key_clipped = (key_weight.astype(f32) * key_scale[None, :]).astype(bf16)
    return (
        block_out,
        tokens_grad,
        attn_gain_grad,
        query_grad,
        key_grad,
        value_grad,
        output_grad,
        mlp_gain_grad,
        gate_grad,
        up_grad,
        down_grad,
        head_top,
        query_clipped,
        key_clipped,
    )


def solution(mesh):
    shape = (mesh.shape["fsdp"] // 4, 2, 2, mesh.shape["tp"])
    fine = Mesh(mesh.devices.reshape(shape), ("group", "row", "col", "tp"))
    rows = P(("group", "row", "col", "tp"), None)
    weight = P(FSDP, "tp")
    gain = P(FSDP)
    heads = P("tp")
    return jax.shard_map(
        local,
        mesh=fine,
        in_specs=(
            rows, rows, P(), P(), heads, gain, weight, weight, weight, weight,
            gain, weight, weight, weight,
        ),
        out_specs=(
            rows, rows, gain, weight, weight, weight, weight, gain, weight, weight, weight,
            heads, weight, weight,
        ),
        check_vma=False,
    )
```

```python
import functools

import jax
import jax.numpy as jnp
from jax import lax
from jax.experimental import pallas as pl
from jax.experimental.pallas import tpu as pltpu
from jax.sharding import Mesh, PartitionSpec as P

HS = 256
GROUP = 2048
SIXTEENTHS = (10, 6)
BLOCK = 128

epsilon = 1e-05
theta_base = 1000042.0
masked_value = -1e30

bf16 = jnp.bfloat16
f32 = jnp.float32
PLANE = ("row", "col")
FSDP = ("group", "row", "col")
VMEM_LIMIT = 48 * 1024 * 1024


def product(left, right):
    return jnp.dot(left, right, preferred_element_type=f32)


def times_transposed(left, right):
    return lax.dot_general(left, right, (((1,), (1,)), ((), ())), preferred_element_type=f32)


def outer_sum(left, right):
    return lax.dot_general(left, right, (((0,), (0,)), ((), ())), preferred_element_type=f32)


def take(array, index, axis=0):
    return lax.dynamic_index_in_dim(array, index, axis, keepdims=False)


def swap(block, axis):
    return lax.ppermute(block, axis, [(0, 1), (1, 0)])


def swap_plane(block, distance):
    return lax.ppermute(block, PLANE, [(i, i ^ distance) for i in range(4)])


def after(value, *others):
    return lax.optimization_barrier((value,) + others)[0]


def combine_all(values, groups, combine):
    distance, count = 1, 4 * groups
    rounds = []
    while distance < count:
        arrived = []
        for step in range(1, min(4, count // distance)):
            route = [(i, i ^ step * distance) for i in range(count)]
            arrived.append(lax.ppermute(values, FSDP, route))
        for other in arrived:
            values = combine(values, other)
        rounds.append(arrived)
        distance *= 4
    return values, rounds


def pack_kernel(count, *refs):
    out_ref, sems = refs[count], refs[count + 1]
    copies, start = [], 0
    for i in range(count):
        rows = refs[i].shape[0]
        copy = pltpu.make_async_copy(refs[i], out_ref.at[pl.ds(start, rows)], sems.at[i])
        copy.start()
        copies.append(copy)
        start += rows
    for copy in copies:
        copy.wait()


def pack(pieces):
    rows, width = sum(p.shape[0] for p in pieces), pieces[0].shape[1]
    count = len(pieces)
    return pl.pallas_call(
        functools.partial(pack_kernel, count),
        in_specs=[pl.BlockSpec(memory_space=pl.ANY)] * count,
        out_specs=pl.BlockSpec(memory_space=pltpu.VMEM),
        out_shape=jax.ShapeDtypeStruct((rows, width), pieces[0].dtype),
        scratch_shapes=[pltpu.SemaphoreType.DMA((count,))],
        cost_estimate=pl.CostEstimate(
            flops=0, bytes_accessed=4 * rows * width, transcendentals=0
        ),
        compiler_params=pltpu.CompilerParams(vmem_limit_bytes=VMEM_LIMIT),
        name="pack",
    )(*pieces)


def norm_kernel(count, *refs):
    gain_ref, out_ref = refs[count], refs[-2]
    pack_kernel(count, *refs[:count], *refs[-2:])
    tile = 256

    @pl.loop(0, out_ref.shape[0] // tile)
    def _(i):
        rows = pl.ds(pl.multiple_of(i * tile, tile), tile)
        values = out_ref[rows, :].astype(f32)
        out_ref[rows, :] = (values * rms_inverse(values) * gain_ref[...]).astype(bf16)


def pack_normed(pieces, gain, early):
    rows, width = sum(p.shape[0] for p in pieces), pieces[0].shape[1]
    count = len(pieces)
    return pl.pallas_call(
        functools.partial(norm_kernel, count),
        in_specs=[pl.BlockSpec(memory_space=pl.ANY)] * count
        + [pl.BlockSpec(memory_space=pltpu.VMEM)]
        + [pl.BlockSpec(memory_space=pl.ANY)] * len(early),
        out_specs=pl.BlockSpec(memory_space=pltpu.VMEM),
        out_shape=jax.ShapeDtypeStruct((rows, width), bf16),
        scratch_shapes=[pltpu.SemaphoreType.DMA((count,))],
        cost_estimate=pl.CostEstimate(
            flops=8 * rows * width, bytes_accessed=4 * rows * width, transcendentals=0
        ),
        compiler_params=pltpu.CompilerParams(vmem_limit_bytes=VMEM_LIMIT),
        name="pack_normed",
    )(*pieces, gain, *early)


def plane_neighbours(own):
    return swap(own, "col"), swap(own, "row")


def plane_far(neighbours, *waits):
    across, along = neighbours
    half = across.shape[0] // 2
    return (
        swap(after(across[:half], *waits), "row"),
        swap(after(along[half:], *waits), "col"),
    )


def with_partner(pieces, swapped=()):
    return pieces + list(swapped) + [swap(piece, "tp") for piece in pieces[len(swapped) :]]


def chip_sums(front, back):
    pairs = []
    for own, other in (front, back):
        shape = (4, own.shape[0] // 4, own.shape[1])
        pairs.append((own.reshape(shape), swap(other, "tp").reshape(shape)))
    return pairs


def quarter(pair, k):
    return pair[0][k].astype(f32) + pair[1][k].astype(f32)


def first_operands(sums):
    front, back = sums
    return (
        jnp.concatenate([quarter(front, 1), quarter(front, 3)]).astype(bf16),
        (back[0][2:].astype(f32) + back[1][2:].astype(f32)).astype(bf16),
    )


def reduce_first(operands, *waits):
    front, back = operands
    rows = front.shape[0] // 2
    return (
        swap(after(front, *waits), "col").reshape(2, rows, -1),
        swap(after(back, *waits), "row"),
    )


def reduce_operands(sums, arrived):
    front, back = sums
    got, got_back = arrived[0].astype(f32), arrived[1].astype(f32)
    return (
        (quarter(front, 0) + got[0], (quarter(front, 2) + got[1]).astype(bf16)),
        (quarter(back, 0) + got_back[0], (quarter(back, 1) + got_back[1]).astype(bf16)),
    )


def last_swaps(operands, *waits):
    return (
        swap(after(operands[0][1], *waits), "row"),
        swap(after(operands[1][1], *waits), "col"),
    )


def reduce_last(operands, swapped):
    return jnp.concatenate(
        [keep + last.astype(f32) for (keep, _), last in zip(operands, swapped)], axis=1
    )


def joined(front_ref, front_last_ref, back_ref, back_last_ref):
    return jnp.concatenate(
        [
            front_ref[...] + front_last_ref[...].astype(f32),
            back_ref[...] + back_last_ref[...].astype(f32),
        ],
        axis=1,
    )


def hidden_kernel(front, front_last, back, back_last, tokens_ref, gain_ref, hidden_ref, normed_ref):
    hidden = tokens_ref[...].astype(f32) + joined(front, front_last, back, back_last)
    hidden_ref[...] = hidden
    normed_ref[...] = (hidden * rms_inverse(hidden) * gain_ref[...]).astype(bf16)


def add_and_norm(operands, last, tokens, gain):
    halves = [part for (keep, _), got in zip(operands, last) for part in (keep, got)]
    return pl.pallas_call(
        hidden_kernel,
        in_specs=[pl.BlockSpec(memory_space=pltpu.VMEM)] * 6,
        out_specs=[pl.BlockSpec(memory_space=pltpu.VMEM)] * 2,
        out_shape=[
            jax.ShapeDtypeStruct(tokens.shape, f32),
            jax.ShapeDtypeStruct(tokens.shape, bf16),
        ],
        cost_estimate=pl.CostEstimate(
            flops=10 * tokens.size, bytes_accessed=14 * tokens.size, transcendentals=0
        ),
        compiler_params=pltpu.CompilerParams(vmem_limit_bytes=VMEM_LIMIT),
        name="add_and_norm",
    )(*halves, tokens, gain)


def back_kernel(front, front_last, back, back_last, values_ref, base_ref, gain_ref, *outs):
    values = values_ref[...].astype(f32)
    inverse = rms_inverse(values)
    unit = values * inverse
    scaled = joined(front, front_last, back, back_last) * gain_ref[...]
    grad = base_ref[...].astype(f32) + inverse * (
        scaled - unit * jnp.mean(scaled * unit, axis=-1, keepdims=True)
    )
    for out in outs:
        out[...] = grad.astype(out.dtype)


def norm_back(operands, last, values, base, gain, dtypes):
    halves = [part for (keep, _), got in zip(operands, last) for part in (keep, got)]
    return pl.pallas_call(
        back_kernel,
        in_specs=[pl.BlockSpec(memory_space=pltpu.VMEM)] * 7,
        out_specs=[pl.BlockSpec(memory_space=pltpu.VMEM)] * len(dtypes),
        out_shape=[jax.ShapeDtypeStruct(values.shape, dtype) for dtype in dtypes],
        cost_estimate=pl.CostEstimate(
            flops=16 * values.size, bytes_accessed=18 * values.size, transcendentals=0
        ),
        compiler_params=pltpu.CompilerParams(vmem_limit_bytes=VMEM_LIMIT),
        name="norm_back",
    )(*halves, values, base, gain)


def split_kernel(spans, member_ref, *refs):
    sources, outs = refs[: len(spans)], refs[len(spans) :]
    for k in range(4):
        target = member_ref[0] ^ k
        column = 0
        for source, (offset, stride, width, shift) in zip(sources, spans):
            start = pl.multiple_of((target >> shift) * stride + offset, 128)
            outs[k][:, column : column + width] = source[:, pl.ds(start, width)]
            column += width


def split(member, sources, spans):
    rows, width = sources[0].shape[0], sum(span[2] for span in spans)
    whole = pl.BlockSpec(memory_space=pltpu.VMEM)
    return pl.pallas_call(
        functools.partial(split_kernel, spans),
        in_specs=[pl.BlockSpec(memory_space=pltpu.SMEM)] + [whole] * len(sources),
        out_specs=[whole] * 4,
        out_shape=[jax.ShapeDtypeStruct((rows, width), bf16)] * 4,
        cost_estimate=pl.CostEstimate(
            flops=0, bytes_accessed=16 * rows * width, transcendentals=0
        ),
        compiler_params=pltpu.CompilerParams(vmem_limit_bytes=VMEM_LIMIT),
        name="split",
    )(member, *sources)


def place_kernel(member_ref, *refs):
    rows = refs[0].shape[0]
    for k in range(4):
        start = pl.multiple_of((member_ref[0] ^ k) * rows, rows)
        column = 0
        for out_ref in refs[4:]:
            width = out_ref.shape[1]
            out_ref[pl.ds(start, rows), :] = refs[k][:, column : column + width]
            column += width


def place_rows(member, pieces, *widths):
    rows, width = pieces[0].shape
    whole = pl.BlockSpec(memory_space=pltpu.VMEM)
    return pl.pallas_call(
        place_kernel,
        in_specs=[pl.BlockSpec(memory_space=pltpu.SMEM)] + [whole] * 4,
        out_specs=[whole] * len(widths or (width,)),
        out_shape=[
            jax.ShapeDtypeStruct((4 * rows, w), bf16) for w in widths or (width,)
        ],
        cost_estimate=pl.CostEstimate(
            flops=0, bytes_accessed=16 * rows * width, transcendentals=0
        ),
        compiler_params=pltpu.CompilerParams(vmem_limit_bytes=VMEM_LIMIT),
        name="place_rows",
    )(member, *pieces)


def pick_kernel(member_ref, *refs):
    sources, outs = refs[:-4], refs[-4:]
    rows = outs[0].shape[0]
    for k in range(4):
        start = pl.multiple_of((member_ref[0] ^ k) * rows, rows)
        column = 0
        for source in sources:
            width = source.shape[1]
            outs[k][:, column : column + width] = source[pl.ds(start, rows), :]
            column += width


def pick_rows(member, *sources):
    rows, width = sources[0].shape[0] // 4, sum(source.shape[1] for source in sources)
    whole = pl.BlockSpec(memory_space=pltpu.VMEM)
    return pl.pallas_call(
        pick_kernel,
        in_specs=[pl.BlockSpec(memory_space=pltpu.SMEM)] + [whole] * len(sources),
        out_specs=[whole] * 4,
        out_shape=[jax.ShapeDtypeStruct((rows, width), bf16)] * 4,
        cost_estimate=pl.CostEstimate(
            flops=0, bytes_accessed=16 * rows * width, transcendentals=0
        ),
        compiler_params=pltpu.CompilerParams(vmem_limit_bytes=VMEM_LIMIT),
        name="pick_rows",
    )(member, *sources)


def swap_all(pieces):
    return [pieces[0]] + [swap_plane(pieces[k], k) for k in (1, 2, 3)]


def mlp_final_kernel(parts, stride, member_ref, gate_w_ref, up_w_ref, *refs):
    pieces, outs, gain_ref = refs[:-4], refs[-4:-1], refs[-1]
    for n, chunks in enumerate(parts):
        for k in range(4):
            start = 0
            for offset, width in chunks:
                column = pl.multiple_of((member_ref[0] ^ k) * stride + offset, 128)
                for i in range(3):
                    part = pieces[4 * n + k][:, start : start + width]
                    outs[i][:, pl.ds(column, width)] = part.astype(f32)
                    start += width
    gain_ref[...] = jnp.sum(
        gate_w_ref[...].astype(f32) * outs[0][...] + up_w_ref[...].astype(f32) * outs[1][...],
        axis=1,
        keepdims=True,
    )


def mlp_final(member, gate_weight, up_weight, chunks, parts):
    rows, hidden = gate_weight.shape
    pieces = [piece for part in parts for piece in part]
    whole = pl.BlockSpec(memory_space=pltpu.VMEM)
    return pl.pallas_call(
        functools.partial(mlp_final_kernel, chunks, hidden // 4),
        in_specs=[pl.BlockSpec(memory_space=pltpu.SMEM)] + [whole] * (2 + len(pieces)),
        out_specs=[whole] * 4,
        out_shape=[jax.ShapeDtypeStruct((rows, hidden), f32)] * 3
        + [jax.ShapeDtypeStruct((rows, 1), f32)],
        cost_estimate=pl.CostEstimate(
            flops=4 * rows * hidden, bytes_accessed=22 * rows * hidden, transcendentals=0
        ),
        compiler_params=pltpu.CompilerParams(vmem_limit_bytes=VMEM_LIMIT),
        name="mlp_final",
    )(member, gate_weight, up_weight, *pieces)


TURN = [(0, 0), (1, 2), (2, 1), (3, 3)]
CROSS = [(0, 2), (1, 0), (2, 3), (3, 1)]
CROSS_BACK = [(2, 0), (0, 1), (3, 2), (1, 3)]


def vmem_call(kernel, name, out_shape, *operands):
    whole = pl.BlockSpec(memory_space=pltpu.VMEM)
    moved = sum(a.size * a.dtype.itemsize for a in operands)
    moved += sum(a.size * a.dtype.itemsize for a in out_shape)
    return pl.pallas_call(
        kernel,
        in_specs=[pl.BlockSpec(memory_space=pltpu.SMEM)] + [whole] * (len(operands) - 1),
        out_specs=[whole] * len(out_shape),
        out_shape=out_shape,
        cost_estimate=pl.CostEstimate(flops=0, bytes_accessed=moved, transcendentals=0),
        compiler_params=pltpu.CompilerParams(vmem_limit_bytes=VMEM_LIMIT),
        name=name,
    )(*operands)


def head_columns(index):
    return pl.ds(pl.multiple_of(index * HS, HS), HS)


def attention_split_kernel(member_ref, q_ref, k_ref, v_ref, o_ref, *outs):
    member = member_ref[0]
    for k in range(4):
        columns = head_columns(member ^ k)
        outs[k][:, :HS] = q_ref[:, columns]
        outs[k][:, HS:] = o_ref[:, columns]
    for h in range(2):
        columns = head_columns((member & 1) ^ h)
        outs[4 + h][:, :HS] = k_ref[:, columns]
        outs[4 + h][:, HS:] = v_ref[:, columns]


def attention_exchange(member, query_weight, key_weight, value_weight, output_weight):
    rows = query_weight.shape[0]
    *both, turned, crossed = vmem_call(
        attention_split_kernel,
        "attention_split",
        [jax.ShapeDtypeStruct((rows, 2 * HS), bf16)] * 6,
        member,
        query_weight,
        key_weight,
        value_weight,
        output_weight,
    )
    return swap_all(both) + [
        lax.ppermute(turned, PLANE, TURN),
        lax.ppermute(crossed, PLANE, CROSS),
    ]


def attention_place_kernel(member_ref, *refs):
    member = member_ref[0]
    out_ref, rows = refs[6], refs[0].shape[0]
    for k in range(4):
        out_ref[pl.ds(pl.multiple_of((member ^ k) * rows, rows), rows), : 2 * HS] = refs[k][...]
    for h in range(2):
        start = ((member >> 1) ^ h) * rows
        at = pl.ds(pl.multiple_of(start, rows), rows)
        out_ref[at, 2 * HS :] = refs[4 + h][:, :HS]
        at = pl.ds(pl.multiple_of(start + 2 * rows, rows), rows)
        out_ref[at, 2 * HS :] = refs[4 + h][:, HS:]


def attention_merge_kernel(rows, member_ref, mine_ref, other_ref, out_ref):
    out_ref[:, 2 * HS : 3 * HS] = mine_ref[:, :HS]
    out_ref[:, 3 * HS :] = mine_ref[:, HS : 2 * HS]
    half = (member_ref[0] & 1) * 2 * rows
    for base in range(0, out_ref.shape[0], 4 * rows):
        mine = pl.ds(pl.multiple_of(base + half, 2 * rows), 2 * rows)
        other = pl.ds(pl.multiple_of(base + 2 * rows - half, 2 * rows), 2 * rows)
        for i in range(2):
            part = slice(base + i * 2 * rows, base + (i + 1) * 2 * rows)
            out_ref[mine, i * HS : (i + 1) * HS] = mine_ref[part, 2 * HS :]
            out_ref[other, i * HS : (i + 1) * HS] = other_ref[part, :]


def halves_kernel(rows, member_ref, grads_ref, keep_ref, send_ref):
    half = (member_ref[0] & 1) * 2 * rows
    for i, base in enumerate(range(0, grads_ref.shape[0], 4 * rows)):
        part = slice(i * 2 * rows, (i + 1) * 2 * rows)
        mine = pl.ds(pl.multiple_of(base + half, 2 * rows), 2 * rows)
        other = pl.ds(pl.multiple_of(base + 2 * rows - half, 2 * rows), 2 * rows)
        keep_ref[part, :] = grads_ref[mine, :]
        send_ref[part, :] = grads_ref[other, :]


def join_kernel(rows, member_ref, keep_ref, got_ref, both_ref, out_ref):
    out_ref[:, : 2 * HS] = both_ref[...]
    for i, base in enumerate(range(0, out_ref.shape[0], 4 * rows)):
        part = slice(i * 2 * rows, (i + 1) * 2 * rows)
        total = (keep_ref[part, :].astype(f32) + got_ref[part, :].astype(f32)).astype(bf16)
        out_ref[base : base + 2 * rows, 2 * HS :] = total[:, :HS]
        out_ref[base + 2 * rows : base + 4 * rows, 2 * HS :] = total[:, HS:]


def attention_pick_kernel(member_ref, source_ref, *outs):
    member, rows = member_ref[0], outs[0].shape[0]
    for k in range(4):
        at = pl.ds(pl.multiple_of((member ^ k) * rows, rows), rows)
        outs[k][...] = source_ref[at, : 2 * HS]
    for h in range(2):
        start = ((member >> 1) ^ h) * rows
        at = pl.ds(pl.multiple_of(start, rows), rows)
        outs[4 + h][:, :HS] = source_ref[at, 2 * HS :]
        at = pl.ds(pl.multiple_of(start + 2 * rows, rows), rows)
        outs[4 + h][:, HS:] = source_ref[at, 2 * HS :]


def attention_return(member, reduced):
    rows = reduced.shape[0] // 4
    *both, turned, crossed = vmem_call(
        attention_pick_kernel,
        "attention_pick",
        [jax.ShapeDtypeStruct((rows, 2 * HS), bf16)] * 6,
        member,
        reduced,
    )
    return swap_all(both) + [
        lax.ppermute(turned, PLANE, TURN),
        lax.ppermute(crossed, PLANE, CROSS_BACK),
    ]


def attention_final_kernel(member_ref, qw_ref, kw_ref, vw_ref, *refs):
    pieces = refs[:6]
    q_ref, k_ref, v_ref, o_ref, gain_ref = refs[6:]
    member = member_ref[0]
    for k in range(4):
        columns = head_columns(member ^ k)
        q_ref[:, columns] = pieces[k][:, :HS].astype(f32)
        o_ref[:, columns] = pieces[k][:, HS:].astype(f32)
    for h in range(2):
        columns = head_columns((member & 1) ^ h)
        k_ref[:, columns] = pieces[4 + h][:, :HS].astype(f32)
        v_ref[:, columns] = pieces[4 + h][:, HS:].astype(f32)

    def row_sum(weight_ref, grad_ref):
        return jnp.sum(weight_ref[...].astype(f32) * grad_ref[...], axis=1, keepdims=True)

    gain_ref[...] = row_sum(qw_ref, q_ref) + row_sum(kw_ref, k_ref) + row_sum(vw_ref, v_ref)


def attention_final(member, query_weight, key_weight, value_weight, pieces):
    rows, width = query_weight.shape
    shapes = [jax.ShapeDtypeStruct((rows, n), f32) for n in (width, width // 2, width // 2, width, 1)]
    return vmem_call(
        attention_final_kernel,
        "attention_final",
        shapes,
        member,
        query_weight,
        key_weight,
        value_weight,
        *pieces,
    )


def rms_inverse(values):
    return lax.rsqrt(jnp.mean(values * values, axis=-1, keepdims=True) + epsilon)


def rope_tables(positions):
    half_size = HS // 2
    indices = jnp.arange(half_size, dtype=f32)
    inverse = theta_base ** (-2.0 * indices / HS)
    angles = positions.astype(f32)[:, None] * inverse[None, :]
    return jnp.cos(angles), jnp.sin(angles)


def rotate(vectors, cos, sin):
    front, back = vectors[:, : HS // 2], vectors[:, HS // 2 :]
    return jnp.concatenate([front * cos - back * sin, back * cos + front * sin], axis=-1)


def unrotate(grads, cos, sin):
    front, back = grads[:, : HS // 2], grads[:, HS // 2 :]
    return jnp.concatenate([front * cos + back * sin, back * cos - front * sin], axis=-1)


def mlp_tile(width, normed, cot, weight_ref):
    both = product(normed, weight_ref[:, : 2 * width])
    d_inner = product(cot, weight_ref[:, 2 * width :])
    gate, upward = both[:, :width], both[:, width:]
    sig = 1.0 / (1.0 + jnp.exp(-gate))
    silu = gate * sig
    d_gate = d_inner * upward * sig * (1.0 + gate * (1.0 - sig))
    return (
        (silu * upward).astype(bf16),
        jnp.concatenate([d_gate, d_inner * silu], axis=1).astype(bf16),
    )


def mlp_kernel(width, normed_ref, cot_ref, weight_ref, inner_ref, grads_ref):
    inner_ref[...], grads_ref[...] = mlp_tile(
        width, normed_ref[...], cot_ref[...], weight_ref
    )


def tail_kernel(width, normed_ref, cot_ref, weight_ref, base_ref, *refs):
    inner_ref, grads_ref, front_ref, back_ref = refs[-4:]
    inner, grads = mlp_tile(width, normed_ref[...], cot_ref[...], weight_ref)
    inner_ref[...], grads_ref[...] = inner, grads
    total = times_transposed(grads, weight_ref[:, : 2 * width]) + base_ref[...]
    half = total.shape[1] // 2
    front_ref[...] = total[:, :half].astype(front_ref.dtype)
    back_ref[...] = total[:, half:].astype(back_ref.dtype)


def mlp_tail(normed, cot, weight, base, part, dtype, chained=()):
    tokens, features = normed.shape
    width = weight.shape[1] // 3
    tile, rows = 256, tokens // 2
    steps = rows // tile
    count = len(chained)
    return pl.pallas_call(
        functools.partial(tail_kernel, width),
        grid=(steps,),
        in_specs=[
            pl.BlockSpec((tile, features), lambda i: (part * steps + i, 0)),
            pl.BlockSpec((tile, features), lambda i: (part * steps + i, 0)),
            pl.BlockSpec((features, 3 * width), lambda i: (0, 0)),
            pl.BlockSpec((tile, features), lambda i: (i, 0)),
        ]
        + [pl.BlockSpec(memory_space=pl.ANY)] * count,
        out_specs=[
            pl.BlockSpec((tile, width), lambda i: (part * steps + i, 0)),
            pl.BlockSpec((tile, 2 * width), lambda i: (part * steps + i, 0)),
            pl.BlockSpec((tile, features // 2), lambda i: (i, 0)),
            pl.BlockSpec((tile, features // 2), lambda i: (i, 0)),
        ],
        out_shape=[
            jax.ShapeDtypeStruct((tokens, width), bf16),
            jax.ShapeDtypeStruct((tokens, 2 * width), bf16),
            jax.ShapeDtypeStruct((rows, features // 2), dtype),
            jax.ShapeDtypeStruct((rows, features // 2), dtype),
        ],
        input_output_aliases={4 + i: i for i in range(count)},
        cost_estimate=pl.CostEstimate(
            flops=10 * rows * features * width,
            bytes_accessed=2 * features * (5 * rows + 3 * width),
            transcendentals=rows * width,
        ),
        compiler_params=pltpu.CompilerParams(vmem_limit_bytes=VMEM_LIMIT),
        name="mlp_tail",
    )(normed, cot, weight, base, *chained)


def mlp_chunk(normed, cot, weight):
    tokens, features = normed.shape
    width = weight.shape[1] // 3
    tile = 256
    return pl.pallas_call(
        functools.partial(mlp_kernel, width),
        grid=(tokens // tile,),
        in_specs=[
            pl.BlockSpec((tile, features), lambda i: (i, 0)),
            pl.BlockSpec((tile, features), lambda i: (i, 0)),
            pl.BlockSpec((features, 3 * width), lambda i: (0, 0)),
        ],
        out_specs=[
            pl.BlockSpec((tile, width), lambda i: (i, 0)),
            pl.BlockSpec((tile, 2 * width), lambda i: (i, 0)),
        ],
        out_shape=[
            jax.ShapeDtypeStruct((tokens, width), bf16),
            jax.ShapeDtypeStruct((tokens, 2 * width), bf16),
        ],
        cost_estimate=pl.CostEstimate(
            flops=6 * tokens * features * width,
            bytes_accessed=2 * features * (2 * tokens + 3 * width),
            transcendentals=tokens * width,
        ),
        compiler_params=pltpu.CompilerParams(vmem_limit_bytes=VMEM_LIMIT),
        name="mlp_chunk",
    )(normed, cot, weight)


def sum_kernel(count, *refs):
    lefts, rights, out_ref = refs[:count], refs[count : 2 * count], refs[-1]
    total = times_transposed(lefts[0][...], rights[0][...])
    for left, right in zip(lefts[1:], rights[1:]):
        total += times_transposed(left[...], right[...])
    for base in refs[2 * count : -1]:
        total += base[...].astype(f32)
    out_ref[...] = total.astype(out_ref.dtype)


def chunk_sum(lefts, rights, column, part, half, dtype):
    count = len(lefts)
    tokens, features = lefts[0].shape[0], rights[0].shape[0]
    widths = [left.shape[1] for left in lefts]
    rows = tokens // 2
    tile = 256
    if half is not None:
        features, tile = features // 2, 512
    steps = rows // tile
    block = half or 0
    return pl.pallas_call(
        functools.partial(sum_kernel, count),
        grid=(steps,),
        in_specs=[pl.BlockSpec((tile, w), lambda i: (part * steps + i, 0)) for w in widths]
        + [pl.BlockSpec((features, w), lambda i: (block, column)) for w in widths],
        out_specs=pl.BlockSpec((tile, features), lambda i: (i, 0)),
        out_shape=jax.ShapeDtypeStruct((rows, features), dtype),
        cost_estimate=pl.CostEstimate(
            flops=2 * rows * features * sum(widths),
            bytes_accessed=2 * sum(widths) * (rows + features) + 4 * rows * features,
            transcendentals=0,
        ),
        compiler_params=pltpu.CompilerParams(vmem_limit_bytes=VMEM_LIMIT),
        name="chunk_sum",
    )(*lefts, *rights)


def grads_kernel(count, *refs):
    column = 0
    for left, right in zip(refs[:count], refs[count : 2 * count]):
        width = right.shape[1]
        refs[-1][:, column : column + width] = outer_sum(left[...], right[...]).astype(bf16)
        column += width


def weight_grads(*pairs):
    lefts = [left for left, _ in pairs]
    rights = [r if isinstance(r, tuple) else (r, r.shape[1], 0) for _, r in pairs]
    count = len(pairs)
    tokens, features = lefts[0].shape
    widths = [width for _, width, _ in rights]
    tile = 256

    def block(width, at):
        return pl.BlockSpec((tokens, width), lambda i: (0, at))

    return pl.pallas_call(
        functools.partial(grads_kernel, count),
        grid=(features // tile,),
        in_specs=[pl.BlockSpec((tokens, tile), lambda i: (0, i))] * count
        + [block(width, at) for _, width, at in rights],
        out_specs=pl.BlockSpec((tile, sum(widths)), lambda i: (i, 0)),
        out_shape=jax.ShapeDtypeStruct((features, sum(widths)), bf16),
        cost_estimate=pl.CostEstimate(
            flops=2 * tokens * features * sum(widths),
            bytes_accessed=2 * (count * tokens * features + sum(widths) * (tokens + features)),
            transcendentals=0,
        ),
        compiler_params=pltpu.CompilerParams(vmem_limit_bytes=VMEM_LIMIT),
        name="weight_grads",
    )(*lefts, *[array for array, _, _ in rights])


def project_kernel(place_ref, normed_ref, weight_ref, cos_ref, sin_ref, q_ref, k_ref, v_ref):
    step = pl.program_id(0)
    cos, sin = cos_ref[...], sin_ref[...]
    qkv = product(normed_ref[...], weight_ref[...])
    keys = rotate(qkv[:, :HS], cos, sin).astype(bf16)
    vals = qkv[:, HS : 2 * HS].astype(bf16)
    query = rotate(qkv[:, 2 * HS :], cos, sin).astype(bf16) * HS ** (-0.5)
    blocks = normed_ref.shape[0] // BLOCK
    for b in range(blocks):
        rows = pl.ds(pl.multiple_of(place_ref[step * blocks + b] * BLOCK, BLOCK), BLOCK)
        part = slice(b * BLOCK, (b + 1) * BLOCK)
        q_ref[rows, :] = query[part]
        k_ref[rows, :] = keys[part]
        v_ref[rows, :] = vals[part]


def project(place, normed, weight, cos, sin):
    tokens, features = normed.shape
    tile = 256
    whole = pl.BlockSpec((tokens, HS), lambda i, place: (0, 0))
    return pl.pallas_call(
        project_kernel,
        grid_spec=pltpu.PrefetchScalarGridSpec(
            num_scalar_prefetch=1,
            grid=(tokens // tile,),
            in_specs=[
                pl.BlockSpec((tile, features), lambda i, place: (i, 0)),
                pl.BlockSpec((features, 3 * HS), lambda i, place: (0, 0)),
                pl.BlockSpec((tile, HS // 2), lambda i, place: (i, 0)),
                pl.BlockSpec((tile, HS // 2), lambda i, place: (i, 0)),
            ],
            out_specs=[whole] * 3,
        ),
        out_shape=[jax.ShapeDtypeStruct((tokens, HS), bf16)] * 3,
        cost_estimate=pl.CostEstimate(
            flops=6 * tokens * features * HS,
            bytes_accessed=2 * features * (tokens + 3 * HS) + 10 * tokens * HS,
            transcendentals=0,
        ),
        compiler_params=pltpu.CompilerParams(vmem_limit_bytes=VMEM_LIMIT),
        name="project",
    )(place, normed, weight, cos, sin)


TILE = 256


def tile_masks():
    rows = lax.broadcasted_iota(jnp.int32, (TILE, TILE), 0)
    cols = lax.broadcasted_iota(jnp.int32, (TILE, TILE), 1)
    causal = rows >= cols
    return causal, causal & (rows // BLOCK == cols // BLOCK)


def block_rows(order_ref, index):
    return pl.ds(pl.multiple_of(order_ref[index] * BLOCK, BLOCK), BLOCK)


def forward_kernel(order_ref, q_ref, k_ref, v_ref, mixed_ref, lse_ref, peak_ref):
    causal, inside = tile_masks()
    prompt = GROUP // 2
    top = jnp.full((TILE, 1), masked_value, f32)
    for i in range(GROUP // TILE):
        rows = slice(i * TILE, (i + 1) * TILE)
        past = min(i * TILE, prompt)
        query = q_ref[rows, :]
        near = times_transposed(query, k_ref[rows, :])
        near = jnp.where(causal if i * TILE < prompt else inside, near, masked_value)
        peak = jnp.max(near, axis=1, keepdims=True)
        if past:
            far = times_transposed(query, k_ref[:past, :])
            peak = jnp.maximum(peak, jnp.max(far, axis=1, keepdims=True))
            far = jnp.exp(far - peak)
        near = jnp.exp(near - peak)
        total = jnp.sum(near, axis=1, keepdims=True)
        if past:
            total += jnp.sum(far, axis=1, keepdims=True)
        share = 1.0 / total
        mixed = product((near * share).astype(bf16), v_ref[rows, :])
        if past:
            mixed += product((far * share).astype(bf16), v_ref[:past, :])
        mixed = mixed.astype(bf16)
        for b in range(TILE // BLOCK):
            mixed_ref[block_rows(order_ref, i * (TILE // BLOCK) + b), :] = mixed[
                b * BLOCK : (b + 1) * BLOCK
            ]
        lse_ref[rows, :] = peak + jnp.log(total)
        top = jnp.maximum(top, peak)
    peak_ref[...] = jnp.full(peak_ref.shape, jnp.max(top), f32)


def attention_forward(order, query, keys, vals):
    whole = pl.BlockSpec(memory_space=pltpu.VMEM)
    return pl.pallas_call(
        forward_kernel,
        in_specs=[pl.BlockSpec(memory_space=pltpu.SMEM), whole, whole, whole],
        out_specs=[whole] * 3,
        out_shape=[
            jax.ShapeDtypeStruct((GROUP, HS), bf16),
            jax.ShapeDtypeStruct((GROUP, 1), f32),
            jax.ShapeDtypeStruct((8, 128), f32),
        ],
        cost_estimate=pl.CostEstimate(
            flops=2 * GROUP * GROUP * HS,
            bytes_accessed=8 * GROUP * HS,
            transcendentals=GROUP * GROUP // 2,
        ),
        compiler_params=pltpu.CompilerParams(vmem_limit_bytes=VMEM_LIMIT),
        name="attention_forward",
    )(order, query, keys, vals)


def backward_kernel(
    order_ref, q_ref, k_ref, v_ref, lse_ref, mixed_ref, cos_ref, sin_ref, out_ref, dk_ref, dv_ref
):
    causal, inside = tile_masks()
    prompt = GROUP // 2
    blocks = TILE // BLOCK

    def back(grad, index):
        rows = block_rows(order_ref, index)
        return rows, unrotate(grad, cos_ref[rows, :], sin_ref[rows, :]).astype(bf16)

    for i in range(GROUP // TILE):
        rows = slice(i * TILE, (i + 1) * TILE)
        past = min(i * TILE, prompt)
        query, lse = q_ref[rows, :], lse_ref[rows, :]
        d_mixed = jnp.concatenate(
            [mixed_ref[block_rows(order_ref, i * blocks + b), :] for b in range(blocks)], axis=0
        )
        near = times_transposed(query, k_ref[rows, :])
        near = jnp.where(causal if i * TILE < prompt else inside, near, masked_value)
        near = jnp.exp(near - lse)
        d_near = times_transposed(d_mixed, v_ref[rows, :])
        inner = jnp.sum(near * d_near, axis=1, keepdims=True)
        if past:
            far = jnp.exp(times_transposed(query, k_ref[:past, :]) - lse)
            d_far = times_transposed(d_mixed, v_ref[:past, :])
            inner += jnp.sum(far * d_far, axis=1, keepdims=True)
        d_near = (near * (d_near - inner)).astype(bf16)
        d_query = product(d_near, k_ref[rows, :])
        dk_ref[rows, :] = outer_sum(d_near, query)
        dv_ref[rows, :] = outer_sum(near.astype(bf16), d_mixed)
        if past:
            d_far = (far * (d_far - inner)).astype(bf16)
            d_query += product(d_far, k_ref[:past, :])
            dk_ref[:past, :] += outer_sum(d_far, query)
            dv_ref[:past, :] += outer_sum(far.astype(bf16), d_mixed)
        d_query = d_query * HS ** (-0.5)
        for b in range(blocks):
            where, grad = back(d_query[b * BLOCK : (b + 1) * BLOCK], i * blocks + b)
            out_ref[where, 2 * HS :] = grad
    for c in range(GROUP // BLOCK):
        part = slice(c * BLOCK, (c + 1) * BLOCK)
        where, grad = back(dk_ref[part, :], c)
        out_ref[where, :HS] = grad
        out_ref[where, HS : 2 * HS] = dv_ref[part, :].astype(bf16)


def attention_backward(order, query, keys, vals, lse, d_mixed, cos, sin):
    whole = pl.BlockSpec(memory_space=pltpu.VMEM)
    return pl.pallas_call(
        backward_kernel,
        in_specs=[pl.BlockSpec(memory_space=pltpu.SMEM)] + [whole] * 7,
        out_specs=whole,
        out_shape=jax.ShapeDtypeStruct((GROUP, 3 * HS), bf16),
        scratch_shapes=[pltpu.VMEM((GROUP, HS), f32), pltpu.VMEM((GROUP, HS), f32)],
        cost_estimate=pl.CostEstimate(
            flops=5 * GROUP * GROUP * HS,
            bytes_accessed=20 * GROUP * HS,
            transcendentals=GROUP * GROUP // 2,
        ),
        compiler_params=pltpu.CompilerParams(vmem_limit_bytes=VMEM_LIMIT),
        name="attention_backward",
    )(order, query, keys, vals, lse, d_mixed, cos, sin)


def local(
    tokens,
    cotangent,
    segment,
    position,
    clip_limit,
    attn_gain,
    query_weight,
    key_weight,
    value_weight,
    output_weight,
    mlp_gain,
    gate_weight,
    up_weight,
    down_weight,
):
    groups = lax.axis_size("group")
    group = lax.axis_index("group")
    core = lax.axis_index("tp")
    member = lax.axis_index(PLANE)
    token_rows = tokens.shape[0]
    own_rows, features = query_weight.shape[0], tokens.shape[1]
    hidden_own = gate_weight.shape[1] // 4
    chunks, offset = [], 0
    for part in SIXTEENTHS:
        chunks.append((offset, hidden_own * part // 16))
        offset += hidden_own * part // 16
    member_at = member.astype(jnp.int32).reshape(1)

    def own_order(array):
        parts = []
        for j in range(2):
            for k in range(4):
                start = group * GROUP + (member ^ k) * (2 * token_rows) + (core ^ j) * token_rows
                parts.append(lax.dynamic_slice_in_dim(array, start, token_rows))
        return jnp.concatenate(parts)

    def collect(blocks):
        return lax.all_gather(blocks, "group", axis=0, tiled=True)

    def mlp_exchange(some, waits):
        weights = [after(a, *waits) for a in (gate_weight, up_weight, down_weight)]
        spans = tuple((start, hidden_own, count, 0) for start, count in some for _ in range(3))
        return swap_all(split(member_at, weights * len(some), spans))

    seg, pos = own_order(segment), own_order(position)
    cos, sin = rope_tables(pos)
    seg_blocks, pos_blocks = seg[::BLOCK], pos[::BLOCK]
    half_blocks = GROUP // BLOCK // 2
    place = jnp.where(seg_blocks == 0, pos_blocks // BLOCK, half_blocks - 1 + seg_blocks)
    labels = jnp.arange(2 * half_blocks, dtype=jnp.int32)
    order = jnp.sum(jnp.where(place[None, :] == labels[:, None], labels[None, :], 0), axis=1)
    index = lax.axis_index(FSDP)
    gains = jnp.stack([attn_gain, mlp_gain])[:, None, :]
    gains = jnp.where(jnp.arange(4 * groups)[None, :, None] == index, gains, 0)
    gains, gain_rounds = combine_all(gains, groups, lambda a, b: a + b)
    gains = gains.reshape(2, features).astype(f32)
    attn_pieces = attention_exchange(
        member_at, query_weight, key_weight, value_weight, output_weight
    )
    (attn_blocks,) = vmem_call(
        attention_place_kernel,
        "attention_place",
        [jax.ShapeDtypeStruct((4 * own_rows, 3 * HS), bf16)],
        member_at,
        after(attn_pieces[0], *gain_rounds[0]),
        *attn_pieces[1:],
    )
    pieces_0 = mlp_exchange(chunks[:1], attn_pieces[1:])
    late_tokens = after(tokens, *pieces_0[1:], *gain_rounds[-1])
    neighbours = plane_neighbours(late_tokens)
    tokens_far = plane_far(neighbours)
    tokens_mine = [late_tokens, *neighbours, *tokens_far]
    tokens_swapped = [swap(piece, "tp") for piece in tokens_mine]
    normed_all = pack_normed(tokens_mine + tokens_swapped, gains[:1], (cos, sin, place, order))
    attn_halves = collect(attn_blocks)
    other_half = swap(after(attn_halves[:, 2 * HS :], *tokens_swapped), "col")
    (attn_weights,) = vmem_call(
        functools.partial(attention_merge_kernel, own_rows),
        "attention_merge",
        [jax.ShapeDtypeStruct((features, 4 * HS), bf16)],
        member_at,
        attn_halves,
        other_half,
    )
    (blocks_0,) = place_rows(member_at, pieces_0)
    cot_near = (
        swap(after(cotangent, other_half, normed_all), "col"),
        swap(after(cotangent, *tokens_far), "row"),
    )
    cot_far = plane_far(cot_near)
    query, keys, vals = project(
        place, normed_all, attn_weights, cos, sin
    )
    mixed, logsum, peak = attention_forward(order, after(query, *cot_near), keys, vals)

    head_top = jnp.where(jnp.arange(4) == member, peak[0, :4], masked_value)
    head_top, head_rounds = combine_all(head_top, groups, jnp.maximum)

    def projected(left, column, waits=(), others=()):
        lefts = (after(left, *others) if others else left, after(left, *waits) if waits else left)
        return [
            [
                chunk_sum([lefts[j]], [attn_weights], column, j, h, bf16 if j else f32)
                for j in (0, 1)
            ]
            for h in range(2)
        ]

    attn_sums = chip_sums(*projected(mixed, 3, (), cot_far))
    arrived = reduce_first(first_operands(attn_sums))
    attn_operands = reduce_operands(attn_sums, arrived)
    attn_last = last_swaps(attn_operands, *head_rounds[0])
    hidden, own_normed = add_and_norm(attn_operands, attn_last, tokens, gains[1:])
    neighbours = plane_neighbours(own_normed)
    normed_far = plane_far(neighbours, *head_rounds[-1])
    pieces_1 = mlp_exchange(chunks[1:], normed_far)
    mlp_weights = [collect(blocks_0), collect(*place_rows(member_at, pieces_1))]
    normed_mlp = pack(with_partner([own_normed, *neighbours, *normed_far]))
    cot_all = pack(with_partner([cotangent, *cot_near, *cot_far]))

    def line_sum(partial):
        return lax.psum_scatter(partial, "group", scatter_dimension=0, tiled=True)

    inner_0, both_0 = mlp_chunk(normed_mlp, cot_all, mlp_weights[0])
    grads_0 = weight_grads((normed_mlp, both_0), (cot_all, inner_0))
    sum_0 = line_sum(grads_0)
    late_both = after(both_0, grads_0)
    early = [chunk_sum([late_both], mlp_weights[:1], 0, j, None, f32) for j in range(2)]
    inner_1, both_1, front_1, back_1 = mlp_tail(
        after(normed_mlp, *early), cot_all, mlp_weights[1], early[1], 1, bf16
    )
    inner_1, both_1, front_0, back_0 = mlp_tail(
        normed_mlp, cot_all, mlp_weights[1], early[0], 0, f32, (inner_1, both_1)
    )

    mlp_sums = chip_sums((front_0, front_1), (back_0, back_1))
    operands = first_operands(mlp_sums)
    arrived = reduce_first(operands)
    inners = [after(inner, *operands) for inner in (inner_0, inner_1)]
    out_parts = [
        [chunk_sum(inners, mlp_weights, 2, j, h, bf16 if j else f32) for j in (0, 1)]
        for h in range(2)
    ]
    mlp_operands = reduce_operands(mlp_sums, arrived)
    mlp_last = last_swaps(mlp_operands, *out_parts[0], *out_parts[1])
    d_hidden, own_d = norm_back(
        mlp_operands, mlp_last, hidden, cotangent, gains[1:], (f32, bf16)
    )
    neighbours = plane_neighbours(own_d)
    late_both = after(both_1, own_d)
    grads_1 = weight_grads((normed_mlp, late_both), (cot_all, inner_1))
    sum_1 = line_sum(after(grads_1, *neighbours))
    d_far = plane_far(neighbours, grads_1)
    d_attn_all = pack(with_partner([own_d, *neighbours, *d_far]))
    out_parts = [[part[0], after(part[1], *d_far)] for part in out_parts]
    out_sums = chip_sums(*out_parts)
    out_operands = reduce_operands(out_sums, reduce_first(first_operands(out_sums)))

    def send_grads(sources, *waits):
        first = after(sources[0], *waits) if waits else sources[0]
        return swap_all(pick_rows(member_at, first, *sources[1:]))


    final_0 = send_grads([sum_0], *d_far)
    d_mixed = product(d_attn_all, attn_weights[:, 3 * HS :]).astype(bf16)
    d_qkv = attention_backward(order, query, keys, vals, logsum, d_mixed, cos, sin)
    pair_grads = weight_grads((normed_all, (after(d_qkv, *final_0[1:]), 2 * HS, 0)))
    half_shape = jax.ShapeDtypeStruct((features // 2, 2 * HS), bf16)
    keep, send = vmem_call(
        functools.partial(halves_kernel, own_rows),
        "halves",
        [half_shape] * 2,
        member_at,
        pair_grads,
    )
    got = swap(send, "col")
    both_grads = weight_grads(
        (normed_all, (after(d_qkv, keep), HS, 2)), (d_attn_all, mixed)
    )
    late_qkv = after(d_qkv, both_grads)
    qkv_parts = projected(late_qkv, 0)
    (attn_grads,) = vmem_call(
        functools.partial(join_kernel, own_rows),
        "join",
        [jax.ShapeDtypeStruct((features, 3 * HS), bf16)],
        member_at,
        after(keep, *qkv_parts[0], *qkv_parts[1]),
        got,
        both_grads,
    )
    attn_sum = line_sum(attn_grads)
    out_last = last_swaps(out_operands)
    qkv_sums = chip_sums(*qkv_parts)
    arrived = reduce_first(first_operands(qkv_sums))
    qkv_operands = reduce_operands(qkv_sums, arrived)
    qkv_last = last_swaps(qkv_operands)
    (tokens_grad,) = norm_back(qkv_operands, qkv_last, tokens, d_hidden, gains[:1], (f32,))
    block_out = (hidden + reduce_last(out_operands, out_last)).astype(bf16)

    final_1 = send_grads([sum_1], *arrived)
    gate_grad, up_grad, down_grad, mlp_gain_row = mlp_final(
        member_at, gate_weight, up_weight, (chunks[:1], chunks[1:]), [final_0, final_1]
    )
    query_grad, key_grad, value_grad, output_grad, attn_gain_row = attention_final(
        member_at,
        query_weight,
        key_weight,
        value_weight,
        attention_return(member_at, after(attn_sum, tokens_grad, *out_last)),
    )
    gain_grads = jnp.concatenate([attn_gain_row, mlp_gain_row], axis=1)
    gain_grads = gain_grads + swap(gain_grads, "tp")
    attn_gain_grad = gain_grads[:, 0] / attn_gain.astype(f32)
    mlp_gain_grad = gain_grads[:, 1] / mlp_gain.astype(f32)

    factor = clip_limit / jnp.maximum(head_top, clip_limit)
    query_scale = jnp.repeat(jnp.sqrt(factor), HS)
    key_factor = jnp.min(factor.reshape(2, 2), axis=1)
    key_scale = jnp.repeat(jnp.sqrt(key_factor), HS)
    query_clipped = (query_weight.astype(f32) * query_scale[None, :]).astype(bf16)
    key_clipped = (key_weight.astype(f32) * key_scale[None, :]).astype(bf16)
    return (
        block_out,
        tokens_grad,
        attn_gain_grad,
        query_grad,
        key_grad,
        value_grad,
        output_grad,
        mlp_gain_grad,
        gate_grad,
        up_grad,
        down_grad,
        head_top,
        query_clipped,
        key_clipped,
    )


def solution(mesh):
    shape = (mesh.shape["fsdp"] // 4, 2, 2, mesh.shape["tp"])
    fine = Mesh(mesh.devices.reshape(shape), ("group", "row", "col", "tp"))
    rows = P(("group", "row", "col", "tp"), None)
    weight = P(FSDP, "tp")
    gain = P(FSDP)
    heads = P("tp")
    return jax.shard_map(
        local,
        mesh=fine,
        in_specs=(
            rows, rows, P(), P(), heads, gain, weight, weight, weight, weight,
            gain, weight, weight, weight,
        ),
        out_specs=(
            rows, rows, gain, weight, weight, weight, weight, gain, weight, weight, weight,
            heads, weight, weight,
        ),
        check_vma=False,
    )
```

```python
import functools

import jax
import jax.numpy as jnp
from jax import lax
from jax.experimental import pallas as pl
from jax.experimental.pallas import tpu as pltpu
from jax.sharding import Mesh, PartitionSpec as P

HS = 256
GROUP = 2048
SIXTEENTHS = (10, 6)
BLOCK = 128

epsilon = 1e-05
theta_base = 1000042.0
masked_value = -1e30

bf16 = jnp.bfloat16
f32 = jnp.float32
PLANE = ("row", "col")
FSDP = ("group", "row", "col")
VMEM_LIMIT = 48 * 1024 * 1024


def product(left, right):
    return jnp.dot(left, right, preferred_element_type=f32)


def times_transposed(left, right):
    return lax.dot_general(left, right, (((1,), (1,)), ((), ())), preferred_element_type=f32)


def outer_sum(left, right):
    return lax.dot_general(left, right, (((0,), (0,)), ((), ())), preferred_element_type=f32)


def take(array, index, axis=0):
    return lax.dynamic_index_in_dim(array, index, axis, keepdims=False)


def swap(block, axis):
    return lax.ppermute(block, axis, [(0, 1), (1, 0)])


def swap_plane(block, distance):
    return lax.ppermute(block, PLANE, [(i, i ^ distance) for i in range(4)])


def after(value, *others):
    return lax.optimization_barrier((value,) + others)[0]


def combine_all(values, groups, combine):
    distance, count = 1, 4 * groups
    rounds = []
    while distance < count:
        arrived = []
        for step in range(1, min(4, count // distance)):
            route = [(i, i ^ step * distance) for i in range(count)]
            arrived.append(lax.ppermute(values, FSDP, route))
        for other in arrived:
            values = combine(values, other)
        rounds.append(arrived)
        distance *= 4
    return values, rounds


def pack_kernel(count, *refs):
    out_ref, sems = refs[count], refs[count + 1]
    copies, start = [], 0
    for i in range(count):
        rows = refs[i].shape[0]
        copy = pltpu.make_async_copy(refs[i], out_ref.at[pl.ds(start, rows)], sems.at[i])
        copy.start()
        copies.append(copy)
        start += rows
    for copy in copies:
        copy.wait()


def pack(pieces):
    rows, width = sum(p.shape[0] for p in pieces), pieces[0].shape[1]
    count = len(pieces)
    return pl.pallas_call(
        functools.partial(pack_kernel, count),
        in_specs=[pl.BlockSpec(memory_space=pl.ANY)] * count,
        out_specs=pl.BlockSpec(memory_space=pltpu.VMEM),
        out_shape=jax.ShapeDtypeStruct((rows, width), pieces[0].dtype),
        scratch_shapes=[pltpu.SemaphoreType.DMA((count,))],
        cost_estimate=pl.CostEstimate(
            flops=0, bytes_accessed=4 * rows * width, transcendentals=0
        ),
        compiler_params=pltpu.CompilerParams(vmem_limit_bytes=VMEM_LIMIT),
        name="pack",
    )(*pieces)


def norm_kernel(count, *refs):
    gain_ref, out_ref = refs[count], refs[-2]
    pack_kernel(count, *refs[:count], *refs[-2:])
    tile = 256

    @pl.loop(0, out_ref.shape[0] // tile)
    def _(i):
        rows = pl.ds(pl.multiple_of(i * tile, tile), tile)
        values = out_ref[rows, :].astype(f32)
        out_ref[rows, :] = (values * rms_inverse(values) * gain_ref[...]).astype(bf16)


def pack_normed(pieces, gain, early):
    rows, width = sum(p.shape[0] for p in pieces), pieces[0].shape[1]
    count = len(pieces)
    return pl.pallas_call(
        functools.partial(norm_kernel, count),
        in_specs=[pl.BlockSpec(memory_space=pl.ANY)] * count
        + [pl.BlockSpec(memory_space=pltpu.VMEM)]
        + [pl.BlockSpec(memory_space=pl.ANY)] * len(early),
        out_specs=pl.BlockSpec(memory_space=pltpu.VMEM),
        out_shape=jax.ShapeDtypeStruct((rows, width), bf16),
        scratch_shapes=[pltpu.SemaphoreType.DMA((count,))],
        cost_estimate=pl.CostEstimate(
            flops=8 * rows * width, bytes_accessed=4 * rows * width, transcendentals=0
        ),
        compiler_params=pltpu.CompilerParams(vmem_limit_bytes=VMEM_LIMIT),
        name="pack_normed",
    )(*pieces, gain, *early)


def plane_neighbours(own):
    return swap(own, "col"), swap(own, "row")


def plane_far(neighbours, *waits):
    across, along = neighbours
    half = across.shape[0] // 2
    return (
        swap(after(across[:half], *waits), "row"),
        swap(after(along[half:], *waits), "col"),
    )


def with_partner(pieces, swapped=()):
    return pieces + list(swapped) + [swap(piece, "tp") for piece in pieces[len(swapped) :]]


def chip_sums(front, back):
    pairs = []
    for own, other in (front, back):
        shape = (4, own.shape[0] // 4, own.shape[1])
        pairs.append((own.reshape(shape), swap(other, "tp").reshape(shape)))
    return pairs


def quarter(pair, k):
    return pair[0][k].astype(f32) + pair[1][k].astype(f32)


def first_operands(sums):
    front, back = sums
    return (
        jnp.concatenate([quarter(front, 1), quarter(front, 3)]).astype(bf16),
        (back[0][2:].astype(f32) + back[1][2:].astype(f32)).astype(bf16),
    )


def reduce_first(operands, *waits):
    front, back = operands
    rows = front.shape[0] // 2
    return (
        swap(after(front, *waits), "col").reshape(2, rows, -1),
        swap(after(back, *waits), "row"),
    )


def reduce_operands(sums, arrived):
    front, back = sums
    got, got_back = arrived[0].astype(f32), arrived[1].astype(f32)
    return (
        (quarter(front, 0) + got[0], (quarter(front, 2) + got[1]).astype(bf16)),
        (quarter(back, 0) + got_back[0], (quarter(back, 1) + got_back[1]).astype(bf16)),
    )


def last_swaps(operands, *waits):
    return (
        swap(after(operands[0][1], *waits), "row"),
        swap(after(operands[1][1], *waits), "col"),
    )


def reduce_last(operands, swapped):
    return jnp.concatenate(
        [keep + last.astype(f32) for (keep, _), last in zip(operands, swapped)], axis=1
    )


def joined(front_ref, front_last_ref, back_ref, back_last_ref):
    return jnp.concatenate(
        [
            front_ref[...] + front_last_ref[...].astype(f32),
            back_ref[...] + back_last_ref[...].astype(f32),
        ],
        axis=1,
    )


def hidden_kernel(front, front_last, back, back_last, tokens_ref, gain_ref, hidden_ref, normed_ref):
    hidden = tokens_ref[...].astype(f32) + joined(front, front_last, back, back_last)
    hidden_ref[...] = hidden
    normed_ref[...] = (hidden * rms_inverse(hidden) * gain_ref[...]).astype(bf16)


def add_and_norm(operands, last, tokens, gain):
    halves = [part for (keep, _), got in zip(operands, last) for part in (keep, got)]
    return pl.pallas_call(
        hidden_kernel,
        in_specs=[pl.BlockSpec(memory_space=pltpu.VMEM)] * 6,
        out_specs=[pl.BlockSpec(memory_space=pltpu.VMEM)] * 2,
        out_shape=[
            jax.ShapeDtypeStruct(tokens.shape, f32),
            jax.ShapeDtypeStruct(tokens.shape, bf16),
        ],
        cost_estimate=pl.CostEstimate(
            flops=10 * tokens.size, bytes_accessed=14 * tokens.size, transcendentals=0
        ),
        compiler_params=pltpu.CompilerParams(vmem_limit_bytes=VMEM_LIMIT),
        name="add_and_norm",
    )(*halves, tokens, gain)


def back_kernel(front, front_last, back, back_last, values_ref, base_ref, gain_ref, *outs):
    values = values_ref[...].astype(f32)
    inverse = rms_inverse(values)
    unit = values * inverse
    scaled = joined(front, front_last, back, back_last) * gain_ref[...]
    grad = base_ref[...].astype(f32) + inverse * (
        scaled - unit * jnp.mean(scaled * unit, axis=-1, keepdims=True)
    )
    for out in outs:
        out[...] = grad.astype(out.dtype)


def norm_back(operands, last, values, base, gain, dtypes):
    halves = [part for (keep, _), got in zip(operands, last) for part in (keep, got)]
    return pl.pallas_call(
        back_kernel,
        in_specs=[pl.BlockSpec(memory_space=pltpu.VMEM)] * 7,
        out_specs=[pl.BlockSpec(memory_space=pltpu.VMEM)] * len(dtypes),
        out_shape=[jax.ShapeDtypeStruct(values.shape, dtype) for dtype in dtypes],
        cost_estimate=pl.CostEstimate(
            flops=16 * values.size, bytes_accessed=18 * values.size, transcendentals=0
        ),
        compiler_params=pltpu.CompilerParams(vmem_limit_bytes=VMEM_LIMIT),
        name="norm_back",
    )(*halves, values, base, gain)


def split_kernel(spans, member_ref, *refs):
    sources, outs = refs[: len(spans)], refs[len(spans) :]
    for k in range(4):
        target = member_ref[0] ^ k
        column = 0
        for source, (offset, stride, width, shift) in zip(sources, spans):
            start = pl.multiple_of((target >> shift) * stride + offset, 128)
            outs[k][:, column : column + width] = source[:, pl.ds(start, width)]
            column += width


def split(member, sources, spans):
    rows, width = sources[0].shape[0], sum(span[2] for span in spans)
    whole = pl.BlockSpec(memory_space=pltpu.VMEM)
    return pl.pallas_call(
        functools.partial(split_kernel, spans),
        in_specs=[pl.BlockSpec(memory_space=pltpu.SMEM)] + [whole] * len(sources),
        out_specs=[whole] * 4,
        out_shape=[jax.ShapeDtypeStruct((rows, width), bf16)] * 4,
        cost_estimate=pl.CostEstimate(
            flops=0, bytes_accessed=16 * rows * width, transcendentals=0
        ),
        compiler_params=pltpu.CompilerParams(vmem_limit_bytes=VMEM_LIMIT),
        name="split",
    )(member, *sources)


def place_kernel(member_ref, *refs):
    rows = refs[0].shape[0]
    for k in range(4):
        start = pl.multiple_of((member_ref[0] ^ k) * rows, rows)
        column = 0
        for out_ref in refs[4:]:
            width = out_ref.shape[1]
            out_ref[pl.ds(start, rows), :] = refs[k][:, column : column + width]
            column += width


def place_rows(member, pieces, *widths):
    rows, width = pieces[0].shape
    whole = pl.BlockSpec(memory_space=pltpu.VMEM)
    return pl.pallas_call(
        place_kernel,
        in_specs=[pl.BlockSpec(memory_space=pltpu.SMEM)] + [whole] * 4,
        out_specs=[whole] * len(widths or (width,)),
        out_shape=[
            jax.ShapeDtypeStruct((4 * rows, w), bf16) for w in widths or (width,)
        ],
        cost_estimate=pl.CostEstimate(
            flops=0, bytes_accessed=16 * rows * width, transcendentals=0
        ),
        compiler_params=pltpu.CompilerParams(vmem_limit_bytes=VMEM_LIMIT),
        name="place_rows",
    )(member, *pieces)


def pick_kernel(member_ref, *refs):
    sources, outs = refs[:-4], refs[-4:]
    rows = outs[0].shape[0]
    for k in range(4):
        start = pl.multiple_of((member_ref[0] ^ k) * rows, rows)
        column = 0
        for source in sources:
            width = source.shape[1]
            outs[k][:, column : column + width] = source[pl.ds(start, rows), :]
            column += width


def pick_rows(member, *sources):
    rows, width = sources[0].shape[0] // 4, sum(source.shape[1] for source in sources)
    whole = pl.BlockSpec(memory_space=pltpu.VMEM)
    return pl.pallas_call(
        pick_kernel,
        in_specs=[pl.BlockSpec(memory_space=pltpu.SMEM)] + [whole] * len(sources),
        out_specs=[whole] * 4,
        out_shape=[jax.ShapeDtypeStruct((rows, width), bf16)] * 4,
        cost_estimate=pl.CostEstimate(
            flops=0, bytes_accessed=16 * rows * width, transcendentals=0
        ),
        compiler_params=pltpu.CompilerParams(vmem_limit_bytes=VMEM_LIMIT),
        name="pick_rows",
    )(member, *sources)


def swap_all(pieces):
    return [pieces[0]] + [swap_plane(pieces[k], k) for k in (1, 2, 3)]


def mlp_final_kernel(parts, stride, member_ref, gate_w_ref, up_w_ref, *refs):
    pieces, outs, gain_ref = refs[:-4], refs[-4:-1], refs[-1]
    for n, chunks in enumerate(parts):
        for k in range(4):
            start = 0
            for offset, width in chunks:
                column = pl.multiple_of((member_ref[0] ^ k) * stride + offset, 128)
                for i in range(3):
                    part = pieces[4 * n + k][:, start : start + width]
                    outs[i][:, pl.ds(column, width)] = part.astype(f32)
                    start += width
    gain_ref[...] = jnp.sum(
        gate_w_ref[...].astype(f32) * outs[0][...] + up_w_ref[...].astype(f32) * outs[1][...],
        axis=1,
        keepdims=True,
    )


def mlp_final(member, gate_weight, up_weight, chunks, parts):
    rows, hidden = gate_weight.shape
    pieces = [piece for part in parts for piece in part]
    whole = pl.BlockSpec(memory_space=pltpu.VMEM)
    return pl.pallas_call(
        functools.partial(mlp_final_kernel, chunks, hidden // 4),
        in_specs=[pl.BlockSpec(memory_space=pltpu.SMEM)] + [whole] * (2 + len(pieces)),
        out_specs=[whole] * 4,
        out_shape=[jax.ShapeDtypeStruct((rows, hidden), f32)] * 3
        + [jax.ShapeDtypeStruct((rows, 1), f32)],
        cost_estimate=pl.CostEstimate(
            flops=4 * rows * hidden, bytes_accessed=22 * rows * hidden, transcendentals=0
        ),
        compiler_params=pltpu.CompilerParams(vmem_limit_bytes=VMEM_LIMIT),
        name="mlp_final",
    )(member, gate_weight, up_weight, *pieces)


TURN = [(0, 0), (1, 2), (2, 1), (3, 3)]
CROSS = [(0, 2), (1, 0), (2, 3), (3, 1)]
CROSS_BACK = [(2, 0), (0, 1), (3, 2), (1, 3)]


def vmem_call(kernel, name, out_shape, *operands):
    whole = pl.BlockSpec(memory_space=pltpu.VMEM)
    moved = sum(a.size * a.dtype.itemsize for a in operands)
    moved += sum(a.size * a.dtype.itemsize for a in out_shape)
    return pl.pallas_call(
        kernel,
        in_specs=[pl.BlockSpec(memory_space=pltpu.SMEM)] + [whole] * (len(operands) - 1),
        out_specs=[whole] * len(out_shape),
        out_shape=out_shape,
        cost_estimate=pl.CostEstimate(flops=0, bytes_accessed=moved, transcendentals=0),
        compiler_params=pltpu.CompilerParams(vmem_limit_bytes=VMEM_LIMIT),
        name=name,
    )(*operands)


def head_columns(index):
    return pl.ds(pl.multiple_of(index * HS, HS), HS)


def attention_split_kernel(member_ref, q_ref, k_ref, v_ref, o_ref, *outs):
    member = member_ref[0]
    for k in range(4):
        columns = head_columns(member ^ k)
        outs[k][:, :HS] = q_ref[:, columns]
        outs[k][:, HS:] = o_ref[:, columns]
    for h in range(2):
        columns = head_columns((member & 1) ^ h)
        outs[4 + h][:, :HS] = k_ref[:, columns]
        outs[4 + h][:, HS:] = v_ref[:, columns]


def attention_exchange(member, query_weight, key_weight, value_weight, output_weight):
    rows = query_weight.shape[0]
    *both, turned, crossed = vmem_call(
        attention_split_kernel,
        "attention_split",
        [jax.ShapeDtypeStruct((rows, 2 * HS), bf16)] * 6,
        member,
        query_weight,
        key_weight,
        value_weight,
        output_weight,
    )
    return swap_all(both) + [
        lax.ppermute(turned, PLANE, TURN),
        lax.ppermute(crossed, PLANE, CROSS),
    ]


def attention_place_kernel(member_ref, *refs):
    member = member_ref[0]
    out_ref, rows = refs[6], refs[0].shape[0]
    for k in range(4):
        out_ref[pl.ds(pl.multiple_of((member ^ k) * rows, rows), rows), : 2 * HS] = refs[k][...]
    for h in range(2):
        start = ((member >> 1) ^ h) * rows
        at = pl.ds(pl.multiple_of(start, rows), rows)
        out_ref[at, 2 * HS :] = refs[4 + h][:, :HS]
        at = pl.ds(pl.multiple_of(start + 2 * rows, rows), rows)
        out_ref[at, 2 * HS :] = refs[4 + h][:, HS:]


def attention_merge_kernel(rows, member_ref, mine_ref, other_ref, out_ref):
    out_ref[:, 2 * HS : 3 * HS] = mine_ref[:, :HS]
    out_ref[:, 3 * HS :] = mine_ref[:, HS : 2 * HS]
    half = (member_ref[0] & 1) * 2 * rows
    for base in range(0, out_ref.shape[0], 4 * rows):
        mine = pl.ds(pl.multiple_of(base + half, 2 * rows), 2 * rows)
        other = pl.ds(pl.multiple_of(base + 2 * rows - half, 2 * rows), 2 * rows)
        for i in range(2):
            part = slice(base + i * 2 * rows, base + (i + 1) * 2 * rows)
            out_ref[mine, i * HS : (i + 1) * HS] = mine_ref[part, 2 * HS :]
            out_ref[other, i * HS : (i + 1) * HS] = other_ref[part, :]


def halves_kernel(rows, member_ref, grads_ref, keep_ref, send_ref):
    half = (member_ref[0] & 1) * 2 * rows
    for i, base in enumerate(range(0, grads_ref.shape[0], 4 * rows)):
        part = slice(i * 2 * rows, (i + 1) * 2 * rows)
        mine = pl.ds(pl.multiple_of(base + half, 2 * rows), 2 * rows)
        other = pl.ds(pl.multiple_of(base + 2 * rows - half, 2 * rows), 2 * rows)
        keep_ref[part, :] = grads_ref[mine, :]
        send_ref[part, :] = grads_ref[other, :]


def join_kernel(rows, member_ref, keep_ref, got_ref, both_ref, out_ref):
    out_ref[:, : 2 * HS] = both_ref[...]
    for i, base in enumerate(range(0, out_ref.shape[0], 4 * rows)):
        part = slice(i * 2 * rows, (i + 1) * 2 * rows)
        total = (keep_ref[part, :].astype(f32) + got_ref[part, :].astype(f32)).astype(bf16)
        out_ref[base : base + 2 * rows, 2 * HS :] = total[:, :HS]
        out_ref[base + 2 * rows : base + 4 * rows, 2 * HS :] = total[:, HS:]


def attention_pick_kernel(member_ref, source_ref, *outs):
    member, rows = member_ref[0], outs[0].shape[0]
    for k in range(4):
        at = pl.ds(pl.multiple_of((member ^ k) * rows, rows), rows)
        outs[k][...] = source_ref[at, : 2 * HS]
    for h in range(2):
        start = ((member >> 1) ^ h) * rows
        at = pl.ds(pl.multiple_of(start, rows), rows)
        outs[4 + h][:, :HS] = source_ref[at, 2 * HS :]
        at = pl.ds(pl.multiple_of(start + 2 * rows, rows), rows)
        outs[4 + h][:, HS:] = source_ref[at, 2 * HS :]


def attention_return(member, reduced):
    rows = reduced.shape[0] // 4
    *both, turned, crossed = vmem_call(
        attention_pick_kernel,
        "attention_pick",
        [jax.ShapeDtypeStruct((rows, 2 * HS), bf16)] * 6,
        member,
        reduced,
    )
    return swap_all(both) + [
        lax.ppermute(turned, PLANE, TURN),
        lax.ppermute(crossed, PLANE, CROSS_BACK),
    ]


def attention_final_kernel(member_ref, qw_ref, kw_ref, vw_ref, *refs):
    pieces = refs[:6]
    q_ref, k_ref, v_ref, o_ref, gain_ref = refs[6:]
    member = member_ref[0]
    for k in range(4):
        columns = head_columns(member ^ k)
        q_ref[:, columns] = pieces[k][:, :HS].astype(f32)
        o_ref[:, columns] = pieces[k][:, HS:].astype(f32)
    for h in range(2):
        columns = head_columns((member & 1) ^ h)
        k_ref[:, columns] = pieces[4 + h][:, :HS].astype(f32)
        v_ref[:, columns] = pieces[4 + h][:, HS:].astype(f32)

    def row_sum(weight_ref, grad_ref):
        return jnp.sum(weight_ref[...].astype(f32) * grad_ref[...], axis=1, keepdims=True)

    gain_ref[...] = row_sum(qw_ref, q_ref) + row_sum(kw_ref, k_ref) + row_sum(vw_ref, v_ref)


def attention_final(member, query_weight, key_weight, value_weight, pieces):
    rows, width = query_weight.shape
    shapes = [jax.ShapeDtypeStruct((rows, n), f32) for n in (width, width // 2, width // 2, width, 1)]
    return vmem_call(
        attention_final_kernel,
        "attention_final",
        shapes,
        member,
        query_weight,
        key_weight,
        value_weight,
        *pieces,
    )


def rms_inverse(values):
    return lax.rsqrt(jnp.mean(values * values, axis=-1, keepdims=True) + epsilon)


def rope_tables(positions):
    half_size = HS // 2
    indices = jnp.arange(half_size, dtype=f32)
    inverse = theta_base ** (-2.0 * indices / HS)
    angles = positions.astype(f32)[:, None] * inverse[None, :]
    return jnp.cos(angles), jnp.sin(angles)


def rotate(vectors, cos, sin):
    front, back = vectors[:, : HS // 2], vectors[:, HS // 2 :]
    return jnp.concatenate([front * cos - back * sin, back * cos + front * sin], axis=-1)


def unrotate(grads, cos, sin):
    front, back = grads[:, : HS // 2], grads[:, HS // 2 :]
    return jnp.concatenate([front * cos + back * sin, back * cos - front * sin], axis=-1)


def mlp_tile(width, normed, cot, weight_ref):
    both = product(normed, weight_ref[:, : 2 * width])
    d_inner = product(cot, weight_ref[:, 2 * width :])
    gate, upward = both[:, :width], both[:, width:]
    sig = 1.0 / (1.0 + jnp.exp(-gate))
    silu = gate * sig
    d_gate = d_inner * upward * sig * (1.0 + gate * (1.0 - sig))
    return (
        (silu * upward).astype(bf16),
        jnp.concatenate([d_gate, d_inner * silu], axis=1).astype(bf16),
    )


def mlp_kernel(width, normed_ref, cot_ref, weight_ref, inner_ref, grads_ref):
    inner_ref[...], grads_ref[...] = mlp_tile(
        width, normed_ref[...], cot_ref[...], weight_ref
    )


def tail_kernel(width, normed_ref, cot_ref, weight_ref, base_ref, *refs):
    inner_ref, grads_ref, front_ref, back_ref = refs[-4:]
    inner, grads = mlp_tile(width, normed_ref[...], cot_ref[...], weight_ref)
    inner_ref[...], grads_ref[...] = inner, grads
    total = times_transposed(grads, weight_ref[:, : 2 * width]) + base_ref[...]
    half = total.shape[1] // 2
    front_ref[...] = total[:, :half].astype(front_ref.dtype)
    back_ref[...] = total[:, half:].astype(back_ref.dtype)


def mlp_tail(normed, cot, weight, base, part, dtype, chained=()):
    tokens, features = normed.shape
    width = weight.shape[1] // 3
    tile, rows = 256, tokens // 2
    steps = rows // tile
    count = len(chained)
    return pl.pallas_call(
        functools.partial(tail_kernel, width),
        grid=(steps,),
        in_specs=[
            pl.BlockSpec((tile, features), lambda i: (part * steps + i, 0)),
            pl.BlockSpec((tile, features), lambda i: (part * steps + i, 0)),
            pl.BlockSpec((features, 3 * width), lambda i: (0, 0)),
            pl.BlockSpec((tile, features), lambda i: (i, 0)),
        ]
        + [pl.BlockSpec(memory_space=pl.ANY)] * count,
        out_specs=[
            pl.BlockSpec((tile, width), lambda i: (part * steps + i, 0)),
            pl.BlockSpec((tile, 2 * width), lambda i: (part * steps + i, 0)),
            pl.BlockSpec((tile, features // 2), lambda i: (i, 0)),
            pl.BlockSpec((tile, features // 2), lambda i: (i, 0)),
        ],
        out_shape=[
            jax.ShapeDtypeStruct((tokens, width), bf16),
            jax.ShapeDtypeStruct((tokens, 2 * width), bf16),
            jax.ShapeDtypeStruct((rows, features // 2), dtype),
            jax.ShapeDtypeStruct((rows, features // 2), dtype),
        ],
        input_output_aliases={4 + i: i for i in range(count)},
        cost_estimate=pl.CostEstimate(
            flops=10 * rows * features * width,
            bytes_accessed=2 * features * (5 * rows + 3 * width),
            transcendentals=rows * width,
        ),
        compiler_params=pltpu.CompilerParams(vmem_limit_bytes=VMEM_LIMIT),
        name="mlp_tail",
    )(normed, cot, weight, base, *chained)


def mlp_chunk(normed, cot, weight):
    tokens, features = normed.shape
    width = weight.shape[1] // 3
    tile = 256
    return pl.pallas_call(
        functools.partial(mlp_kernel, width),
        grid=(tokens // tile,),
        in_specs=[
            pl.BlockSpec((tile, features), lambda i: (i, 0)),
            pl.BlockSpec((tile, features), lambda i: (i, 0)),
            pl.BlockSpec((features, 3 * width), lambda i: (0, 0)),
        ],
        out_specs=[
            pl.BlockSpec((tile, width), lambda i: (i, 0)),
            pl.BlockSpec((tile, 2 * width), lambda i: (i, 0)),
        ],
        out_shape=[
            jax.ShapeDtypeStruct((tokens, width), bf16),
            jax.ShapeDtypeStruct((tokens, 2 * width), bf16),
        ],
        cost_estimate=pl.CostEstimate(
            flops=6 * tokens * features * width,
            bytes_accessed=2 * features * (2 * tokens + 3 * width),
            transcendentals=tokens * width,
        ),
        compiler_params=pltpu.CompilerParams(vmem_limit_bytes=VMEM_LIMIT),
        name="mlp_chunk",
    )(normed, cot, weight)


def sum_kernel(count, *refs):
    lefts, rights, out_ref = refs[:count], refs[count : 2 * count], refs[-1]
    total = times_transposed(lefts[0][...], rights[0][...])
    for left, right in zip(lefts[1:], rights[1:]):
        total += times_transposed(left[...], right[...])
    for base in refs[2 * count : -1]:
        total += base[...].astype(f32)
    out_ref[...] = total.astype(out_ref.dtype)


def chunk_sum(lefts, rights, column, part, half, dtype):
    count = len(lefts)
    tokens, features = lefts[0].shape[0], rights[0].shape[0]
    widths = [left.shape[1] for left in lefts]
    rows = tokens // 2
    tile = 256
    if half is not None:
        features, tile = features // 2, 512
    steps = rows // tile
    block = half or 0
    return pl.pallas_call(
        functools.partial(sum_kernel, count),
        grid=(steps,),
        in_specs=[pl.BlockSpec((tile, w), lambda i: (part * steps + i, 0)) for w in widths]
        + [pl.BlockSpec((features, w), lambda i: (block, column)) for w in widths],
        out_specs=pl.BlockSpec((tile, features), lambda i: (i, 0)),
        out_shape=jax.ShapeDtypeStruct((rows, features), dtype),
        cost_estimate=pl.CostEstimate(
            flops=2 * rows * features * sum(widths),
            bytes_accessed=2 * sum(widths) * (rows + features) + 4 * rows * features,
            transcendentals=0,
        ),
        compiler_params=pltpu.CompilerParams(vmem_limit_bytes=VMEM_LIMIT),
        name="chunk_sum",
    )(*lefts, *rights)


def grads_kernel(count, *refs):
    column = 0
    for left, right in zip(refs[:count], refs[count : 2 * count]):
        width = right.shape[1]
        refs[-1][:, column : column + width] = outer_sum(left[...], right[...]).astype(bf16)
        column += width


def weight_grads(*pairs):
    lefts = [left for left, _ in pairs]
    rights = [r if isinstance(r, tuple) else (r, r.shape[1], 0) for _, r in pairs]
    count = len(pairs)
    tokens, features = lefts[0].shape
    widths = [width for _, width, _ in rights]
    tile = 256

    def block(width, at):
        return pl.BlockSpec((tokens, width), lambda i: (0, at))

    return pl.pallas_call(
        functools.partial(grads_kernel, count),
        grid=(features // tile,),
        in_specs=[pl.BlockSpec((tokens, tile), lambda i: (0, i))] * count
        + [block(width, at) for _, width, at in rights],
        out_specs=pl.BlockSpec((tile, sum(widths)), lambda i: (i, 0)),
        out_shape=jax.ShapeDtypeStruct((features, sum(widths)), bf16),
        cost_estimate=pl.CostEstimate(
            flops=2 * tokens * features * sum(widths),
            bytes_accessed=2 * (count * tokens * features + sum(widths) * (tokens + features)),
            transcendentals=0,
        ),
        compiler_params=pltpu.CompilerParams(vmem_limit_bytes=VMEM_LIMIT),
        name="weight_grads",
    )(*lefts, *[array for array, _, _ in rights])


def project_kernel(place_ref, normed_ref, weight_ref, cos_ref, sin_ref, q_ref, k_ref, v_ref):
    step = pl.program_id(0)
    cos, sin = cos_ref[...], sin_ref[...]
    qkv = product(normed_ref[...], weight_ref[...])
    keys = rotate(qkv[:, :HS], cos, sin).astype(bf16)
    vals = qkv[:, HS : 2 * HS].astype(bf16)
    query = rotate(qkv[:, 2 * HS :], cos, sin).astype(bf16) * HS ** (-0.5)
    blocks = normed_ref.shape[0] // BLOCK
    for b in range(blocks):
        rows = pl.ds(pl.multiple_of(place_ref[step * blocks + b] * BLOCK, BLOCK), BLOCK)
        part = slice(b * BLOCK, (b + 1) * BLOCK)
        q_ref[rows, :] = query[part]
        k_ref[rows, :] = keys[part]
        v_ref[rows, :] = vals[part]


def project(place, normed, weight, cos, sin):
    tokens, features = normed.shape
    tile = 256
    whole = pl.BlockSpec((tokens, HS), lambda i, place: (0, 0))
    return pl.pallas_call(
        project_kernel,
        grid_spec=pltpu.PrefetchScalarGridSpec(
            num_scalar_prefetch=1,
            grid=(tokens // tile,),
            in_specs=[
                pl.BlockSpec((tile, features), lambda i, place: (i, 0)),
                pl.BlockSpec((features, 3 * HS), lambda i, place: (0, 0)),
                pl.BlockSpec((tile, HS // 2), lambda i, place: (i, 0)),
                pl.BlockSpec((tile, HS // 2), lambda i, place: (i, 0)),
            ],
            out_specs=[whole] * 3,
        ),
        out_shape=[jax.ShapeDtypeStruct((tokens, HS), bf16)] * 3,
        cost_estimate=pl.CostEstimate(
            flops=6 * tokens * features * HS,
            bytes_accessed=2 * features * (tokens + 3 * HS) + 10 * tokens * HS,
            transcendentals=0,
        ),
        compiler_params=pltpu.CompilerParams(vmem_limit_bytes=VMEM_LIMIT),
        name="project",
    )(place, normed, weight, cos, sin)


TILE = 256


def tile_masks():
    rows = lax.broadcasted_iota(jnp.int32, (TILE, TILE), 0)
    cols = lax.broadcasted_iota(jnp.int32, (TILE, TILE), 1)
    causal = rows >= cols
    return causal, causal & (rows // BLOCK == cols // BLOCK)


def block_rows(order_ref, index):
    return pl.ds(pl.multiple_of(order_ref[index] * BLOCK, BLOCK), BLOCK)


def forward_kernel(order_ref, q_ref, k_ref, v_ref, mixed_ref, lse_ref, peak_ref):
    causal, inside = tile_masks()
    prompt = GROUP // 2
    top = jnp.full((TILE, 1), masked_value, f32)
    for i in range(GROUP // TILE):
        rows = slice(i * TILE, (i + 1) * TILE)
        past = min(i * TILE, prompt)
        query = q_ref[rows, :]
        near = times_transposed(query, k_ref[rows, :])
        near = jnp.where(causal if i * TILE < prompt else inside, near, masked_value)
        peak = jnp.max(near, axis=1, keepdims=True)
        if past:
            far = times_transposed(query, k_ref[:past, :])
            peak = jnp.maximum(peak, jnp.max(far, axis=1, keepdims=True))
            far = jnp.exp(far - peak)
        near = jnp.exp(near - peak)
        total = jnp.sum(near, axis=1, keepdims=True)
        if past:
            total += jnp.sum(far, axis=1, keepdims=True)
        share = 1.0 / total
        mixed = product((near * share).astype(bf16), v_ref[rows, :])
        if past:
            mixed += product((far * share).astype(bf16), v_ref[:past, :])
        mixed = mixed.astype(bf16)
        for b in range(TILE // BLOCK):
            mixed_ref[block_rows(order_ref, i * (TILE // BLOCK) + b), :] = mixed[
                b * BLOCK : (b + 1) * BLOCK
            ]
        lse_ref[rows, :] = peak + jnp.log(total)
        top = jnp.maximum(top, peak)
    peak_ref[...] = jnp.full(peak_ref.shape, jnp.max(top), f32)


def attention_forward(order, query, keys, vals):
    whole = pl.BlockSpec(memory_space=pltpu.VMEM)
    return pl.pallas_call(
        forward_kernel,
        in_specs=[pl.BlockSpec(memory_space=pltpu.SMEM), whole, whole, whole],
        out_specs=[whole] * 3,
        out_shape=[
            jax.ShapeDtypeStruct((GROUP, HS), bf16),
            jax.ShapeDtypeStruct((GROUP, 1), f32),
            jax.ShapeDtypeStruct((8, 128), f32),
        ],
        cost_estimate=pl.CostEstimate(
            flops=2 * GROUP * GROUP * HS,
            bytes_accessed=8 * GROUP * HS,
            transcendentals=GROUP * GROUP // 2,
        ),
        compiler_params=pltpu.CompilerParams(vmem_limit_bytes=VMEM_LIMIT),
        name="attention_forward",
    )(order, query, keys, vals)


def backward_kernel(
    order_ref, q_ref, k_ref, v_ref, lse_ref, mixed_ref, cos_ref, sin_ref, out_ref, dk_ref, dv_ref
):
    causal, inside = tile_masks()
    prompt = GROUP // 2
    blocks = TILE // BLOCK

    def back(grad, index):
        rows = block_rows(order_ref, index)
        return rows, unrotate(grad, cos_ref[rows, :], sin_ref[rows, :]).astype(bf16)

    for i in range(GROUP // TILE):
        rows = slice(i * TILE, (i + 1) * TILE)
        past = min(i * TILE, prompt)
        query, lse = q_ref[rows, :], lse_ref[rows, :]
        d_mixed = jnp.concatenate(
            [mixed_ref[block_rows(order_ref, i * blocks + b), :] for b in range(blocks)], axis=0
        )
        near = times_transposed(query, k_ref[rows, :])
        near = jnp.where(causal if i * TILE < prompt else inside, near, masked_value)
        near = jnp.exp(near - lse)
        d_near = times_transposed(d_mixed, v_ref[rows, :])
        inner = jnp.sum(near * d_near, axis=1, keepdims=True)
        if past:
            far = jnp.exp(times_transposed(query, k_ref[:past, :]) - lse)
            d_far = times_transposed(d_mixed, v_ref[:past, :])
            inner += jnp.sum(far * d_far, axis=1, keepdims=True)
        d_near = (near * (d_near - inner)).astype(bf16)
        d_query = product(d_near, k_ref[rows, :])
        dk_ref[rows, :] = outer_sum(d_near, query)
        dv_ref[rows, :] = outer_sum(near.astype(bf16), d_mixed)
        if past:
            d_far = (far * (d_far - inner)).astype(bf16)
            d_query += product(d_far, k_ref[:past, :])
            dk_ref[:past, :] += outer_sum(d_far, query)
            dv_ref[:past, :] += outer_sum(far.astype(bf16), d_mixed)
        d_query = d_query * HS ** (-0.5)
        for b in range(blocks):
            where, grad = back(d_query[b * BLOCK : (b + 1) * BLOCK], i * blocks + b)
            out_ref[where, 2 * HS :] = grad
    for c in range(GROUP // BLOCK):
        part = slice(c * BLOCK, (c + 1) * BLOCK)
        where, grad = back(dk_ref[part, :], c)
        out_ref[where, :HS] = grad
        out_ref[where, HS : 2 * HS] = dv_ref[part, :].astype(bf16)


def attention_backward(order, query, keys, vals, lse, d_mixed, cos, sin):
    whole = pl.BlockSpec(memory_space=pltpu.VMEM)
    return pl.pallas_call(
        backward_kernel,
        in_specs=[pl.BlockSpec(memory_space=pltpu.SMEM)] + [whole] * 7,
        out_specs=whole,
        out_shape=jax.ShapeDtypeStruct((GROUP, 3 * HS), bf16),
        scratch_shapes=[pltpu.VMEM((GROUP, HS), f32), pltpu.VMEM((GROUP, HS), f32)],
        cost_estimate=pl.CostEstimate(
            flops=5 * GROUP * GROUP * HS,
            bytes_accessed=20 * GROUP * HS,
            transcendentals=GROUP * GROUP // 2,
        ),
        compiler_params=pltpu.CompilerParams(vmem_limit_bytes=VMEM_LIMIT),
        name="attention_backward",
    )(order, query, keys, vals, lse, d_mixed, cos, sin)


def local(
    tokens,
    cotangent,
    segment,
    position,
    clip_limit,
    attn_gain,
    query_weight,
    key_weight,
    value_weight,
    output_weight,
    mlp_gain,
    gate_weight,
    up_weight,
    down_weight,
):
    groups = lax.axis_size("group")
    group = lax.axis_index("group")
    core = lax.axis_index("tp")
    member = lax.axis_index(PLANE)
    token_rows = tokens.shape[0]
    own_rows, features = query_weight.shape[0], tokens.shape[1]
    hidden_own = gate_weight.shape[1] // 4
    chunks, offset = [], 0
    for part in SIXTEENTHS:
        chunks.append((offset, hidden_own * part // 16))
        offset += hidden_own * part // 16
    member_at = member.astype(jnp.int32).reshape(1)

    def own_order(array):
        parts = []
        for j in range(2):
            for k in range(4):
                start = group * GROUP + (member ^ k) * (2 * token_rows) + (core ^ j) * token_rows
                parts.append(lax.dynamic_slice_in_dim(array, start, token_rows))
        return jnp.concatenate(parts)

    def collect(blocks):
        return lax.all_gather(blocks, "group", axis=0, tiled=True)

    def mlp_exchange(some, waits):
        weights = [after(a, *waits) for a in (gate_weight, up_weight, down_weight)]
        spans = tuple((start, hidden_own, count, 0) for start, count in some for _ in range(3))
        return swap_all(split(member_at, weights * len(some), spans))

    seg, pos = own_order(segment), own_order(position)
    cos, sin = rope_tables(pos)
    seg_blocks, pos_blocks = seg[::BLOCK], pos[::BLOCK]
    half_blocks = GROUP // BLOCK // 2
    place = jnp.where(seg_blocks == 0, pos_blocks // BLOCK, half_blocks - 1 + seg_blocks)
    labels = jnp.arange(2 * half_blocks, dtype=jnp.int32)
    order = jnp.sum(jnp.where(place[None, :] == labels[:, None], labels[None, :], 0), axis=1)
    index = lax.axis_index(FSDP)
    gains = jnp.stack([attn_gain, mlp_gain])[:, None, :]
    gains = jnp.where(jnp.arange(4 * groups)[None, :, None] == index, gains, 0)
    gains, gain_rounds = combine_all(gains, groups, lambda a, b: a + b)
    gains = gains.reshape(2, features).astype(f32)
    attn_pieces = attention_exchange(
        member_at, query_weight, key_weight, value_weight, output_weight
    )
    (attn_blocks,) = vmem_call(
        attention_place_kernel,
        "attention_place",
        [jax.ShapeDtypeStruct((4 * own_rows, 3 * HS), bf16)],
        member_at,
        after(attn_pieces[0], *gain_rounds[0]),
        *attn_pieces[1:],
    )
    pieces_0 = mlp_exchange(chunks[:1], attn_pieces[1:])
    late_tokens = after(tokens, *attn_pieces[1:])
    neighbours = plane_neighbours(late_tokens)
    tokens_far = plane_far(neighbours)
    tokens_mine = [late_tokens, *neighbours, *tokens_far]
    tokens_swapped = [swap(piece, "tp") for piece in tokens_mine]
    normed_all = pack_normed(tokens_mine + tokens_swapped, gains[:1], (cos, sin, place, order))
    attn_halves = collect(attn_blocks)
    other_half = swap(after(attn_halves[:, 2 * HS :], *tokens_swapped), "col")
    (attn_weights,) = vmem_call(
        functools.partial(attention_merge_kernel, own_rows),
        "attention_merge",
        [jax.ShapeDtypeStruct((features, 4 * HS), bf16)],
        member_at,
        attn_halves,
        other_half,
    )
    (blocks_0,) = place_rows(
        member_at, [after(pieces_0[0], *tokens_far, *gain_rounds[-1])] + pieces_0[1:]
    )
    pieces_1 = mlp_exchange(chunks[1:], (other_half,))
    cot_along = swap(after(cotangent, *tokens_far), "row")
    query, keys, vals = project(
        place, normed_all, attn_weights, cos, sin
    )
    mixed, logsum, peak = attention_forward(
        order, after(query, *pieces_1[1:], cot_along), keys, vals
    )

    head_top = jnp.where(jnp.arange(4) == member, peak[0, :4], masked_value)
    head_top, head_rounds = combine_all(head_top, groups, jnp.maximum)

    def projected(left, column, waits=(), others=()):
        lefts = (after(left, *others) if others else left, after(left, *waits) if waits else left)
        return [
            [
                chunk_sum([lefts[j]], [attn_weights], column, j, h, bf16 if j else f32)
                for j in (0, 1)
            ]
            for h in range(2)
        ]

    attn_sums = chip_sums(*projected(mixed, 3))
    arrived = reduce_first(first_operands(attn_sums))
    attn_operands = reduce_operands(attn_sums, arrived)
    attn_last = last_swaps(attn_operands, *head_rounds[0])
    hidden, own_normed = add_and_norm(attn_operands, attn_last, tokens, gains[1:])
    neighbours = plane_neighbours(own_normed)
    normed_far = plane_far(neighbours, *head_rounds[-1])
    cot_near = (swap(after(cotangent, *normed_far), "col"), cot_along)
    cot_far = plane_far(cot_near, *normed_far)
    mlp_weights = [collect(blocks_0), collect(*place_rows(member_at, pieces_1))]
    normed_mlp = pack(with_partner([own_normed, *neighbours, *normed_far]))
    cot_all = pack(with_partner([cotangent, *cot_near, *cot_far]))

    def line_sum(partial):
        return lax.psum_scatter(partial, "group", scatter_dimension=0, tiled=True)

    inner_0, both_0 = mlp_chunk(normed_mlp, cot_all, mlp_weights[0])
    grads_0 = weight_grads((normed_mlp, both_0), (cot_all, inner_0))
    sum_0 = line_sum(grads_0)
    late_both = after(both_0, grads_0)
    early = [chunk_sum([late_both], mlp_weights[:1], 0, j, None, f32) for j in range(2)]
    inner_1, both_1, front_1, back_1 = mlp_tail(
        after(normed_mlp, *early), cot_all, mlp_weights[1], early[1], 1, bf16
    )
    inner_1, both_1, front_0, back_0 = mlp_tail(
        normed_mlp, cot_all, mlp_weights[1], early[0], 0, f32, (inner_1, both_1)
    )

    mlp_sums = chip_sums((front_0, front_1), (back_0, back_1))
    operands = first_operands(mlp_sums)
    arrived = reduce_first(operands)
    inners = [after(inner, *operands) for inner in (inner_0, inner_1)]
    out_parts = [
        [chunk_sum(inners, mlp_weights, 2, j, h, bf16 if j else f32) for j in (0, 1)]
        for h in range(2)
    ]
    mlp_operands = reduce_operands(mlp_sums, arrived)
    mlp_last = last_swaps(mlp_operands, *out_parts[0], *out_parts[1])
    d_hidden, own_d = norm_back(
        mlp_operands, mlp_last, hidden, cotangent, gains[1:], (f32, bf16)
    )
    neighbours = plane_neighbours(own_d)
    late_both = after(both_1, own_d)
    grads_1 = weight_grads((normed_mlp, late_both), (cot_all, inner_1))
    sum_1 = line_sum(after(grads_1, *neighbours))
    d_far = plane_far(neighbours, grads_1)
    d_attn_all = pack(with_partner([own_d, *neighbours, *d_far]))
    out_parts = [[part[0], after(part[1], *d_far)] for part in out_parts]
    out_sums = chip_sums(*out_parts)
    out_arrived = reduce_first(first_operands(out_sums))
    out_operands = reduce_operands(out_sums, out_arrived)
    out_last = last_swaps(out_operands)

    def send_grads(sources, *waits):
        first = after(sources[0], *waits) if waits else sources[0]
        return swap_all(pick_rows(member_at, first, *sources[1:]))


    final_0 = send_grads([sum_0], *d_far)
    d_mixed = product(d_attn_all, attn_weights[:, 3 * HS :]).astype(bf16)
    d_qkv = attention_backward(order, query, keys, vals, logsum, d_mixed, cos, sin)
    pair_grads = weight_grads((normed_all, (after(d_qkv, *out_arrived), 2 * HS, 0)))
    half_shape = jax.ShapeDtypeStruct((features // 2, 2 * HS), bf16)
    keep, send = vmem_call(
        functools.partial(halves_kernel, own_rows),
        "halves",
        [half_shape] * 2,
        member_at,
        pair_grads,
    )
    got = swap(send, "col")
    both_grads = weight_grads(
        (normed_all, (after(d_qkv, keep), HS, 2)), (d_attn_all, mixed)
    )
    late_qkv = after(d_qkv, both_grads, *out_last, *final_0[1:])
    qkv_parts = projected(late_qkv, 0)
    (attn_grads,) = vmem_call(
        functools.partial(join_kernel, own_rows),
        "join",
        [jax.ShapeDtypeStruct((features, 3 * HS), bf16)],
        member_at,
        after(keep, *qkv_parts[0], *qkv_parts[1]),
        got,
        both_grads,
    )
    attn_sum = line_sum(attn_grads)
    qkv_sums = chip_sums(*qkv_parts)
    arrived = reduce_first(first_operands(qkv_sums))
    qkv_operands = reduce_operands(qkv_sums, arrived)
    qkv_last = last_swaps(qkv_operands)
    (tokens_grad,) = norm_back(qkv_operands, qkv_last, tokens, d_hidden, gains[:1], (f32,))
    block_out = (hidden + reduce_last(out_operands, out_last)).astype(bf16)

    final_1 = send_grads([sum_1], *arrived)
    gate_grad, up_grad, down_grad, mlp_gain_row = mlp_final(
        member_at, gate_weight, up_weight, (chunks[:1], chunks[1:]), [final_0, final_1]
    )
    query_grad, key_grad, value_grad, output_grad, attn_gain_row = attention_final(
        member_at,
        query_weight,
        key_weight,
        value_weight,
        attention_return(member_at, after(attn_sum, *qkv_last)),
    )
    gain_grads = jnp.concatenate([attn_gain_row, mlp_gain_row], axis=1)
    gain_grads = gain_grads + swap(gain_grads, "tp")
    attn_gain_grad = gain_grads[:, 0] / attn_gain.astype(f32)
    mlp_gain_grad = gain_grads[:, 1] / mlp_gain.astype(f32)

    factor = clip_limit / jnp.maximum(head_top, clip_limit)
    query_scale = jnp.repeat(jnp.sqrt(factor), HS)
    key_factor = jnp.min(factor.reshape(2, 2), axis=1)
    key_scale = jnp.repeat(jnp.sqrt(key_factor), HS)
    query_clipped = (query_weight.astype(f32) * query_scale[None, :]).astype(bf16)
    key_clipped = (key_weight.astype(f32) * key_scale[None, :]).astype(bf16)
    return (
        block_out,
        tokens_grad,
        attn_gain_grad,
        query_grad,
        key_grad,
        value_grad,
        output_grad,
        mlp_gain_grad,
        gate_grad,
        up_grad,
        down_grad,
        head_top,
        query_clipped,
        key_clipped,
    )


def solution(mesh):
    shape = (mesh.shape["fsdp"] // 4, 2, 2, mesh.shape["tp"])
    fine = Mesh(mesh.devices.reshape(shape), ("group", "row", "col", "tp"))
    rows = P(("group", "row", "col", "tp"), None)
    weight = P(FSDP, "tp")
    gain = P(FSDP)
    heads = P("tp")
    return jax.shard_map(
        local,
        mesh=fine,
        in_specs=(
            rows, rows, P(), P(), heads, gain, weight, weight, weight, weight,
            gain, weight, weight, weight,
        ),
        out_specs=(
            rows, rows, gain, weight, weight, weight, weight, gain, weight, weight, weight,
            heads, weight, weight,
        ),
        check_vma=False,
    )
```

```python
import functools

import jax
import jax.numpy as jnp
from jax import lax
from jax.experimental import pallas as pl
from jax.experimental.pallas import tpu as pltpu
from jax.sharding import Mesh, PartitionSpec as P

HS = 256
GROUP = 2048
SIXTEENTHS = (10, 6)
BLOCK = 128

epsilon = 1e-05
theta_base = 1000042.0
masked_value = -1e30

bf16 = jnp.bfloat16
f32 = jnp.float32
PLANE = ("row", "col")
FSDP = ("group", "row", "col")
VMEM_LIMIT = 48 * 1024 * 1024


def product(left, right):
    return jnp.dot(left, right, preferred_element_type=f32)


def times_transposed(left, right):
    return lax.dot_general(left, right, (((1,), (1,)), ((), ())), preferred_element_type=f32)


def outer_sum(left, right):
    return lax.dot_general(left, right, (((0,), (0,)), ((), ())), preferred_element_type=f32)


def take(array, index, axis=0):
    return lax.dynamic_index_in_dim(array, index, axis, keepdims=False)


def swap(block, axis):
    return lax.ppermute(block, axis, [(0, 1), (1, 0)])


def swap_plane(block, distance):
    return lax.ppermute(block, PLANE, [(i, i ^ distance) for i in range(4)])


def after(value, *others):
    return lax.optimization_barrier((value,) + others)[0]


def combine_all(values, groups, combine):
    distance, count = 1, 4 * groups
    rounds = []
    while distance < count:
        arrived = []
        for step in range(1, min(4, count // distance)):
            route = [(i, i ^ step * distance) for i in range(count)]
            arrived.append(lax.ppermute(values, FSDP, route))
        for other in arrived:
            values = combine(values, other)
        rounds.append(arrived)
        distance *= 4
    return values, rounds


def pack_kernel(count, *refs):
    out_ref, sems = refs[count], refs[count + 1]
    copies, start = [], 0
    for i in range(count):
        rows = refs[i].shape[0]
        copy = pltpu.make_async_copy(refs[i], out_ref.at[pl.ds(start, rows)], sems.at[i])
        copy.start()
        copies.append(copy)
        start += rows
    for copy in copies:
        copy.wait()


def pack(pieces):
    rows, width = sum(p.shape[0] for p in pieces), pieces[0].shape[1]
    count = len(pieces)
    return pl.pallas_call(
        functools.partial(pack_kernel, count),
        in_specs=[pl.BlockSpec(memory_space=pl.ANY)] * count,
        out_specs=pl.BlockSpec(memory_space=pltpu.VMEM),
        out_shape=jax.ShapeDtypeStruct((rows, width), pieces[0].dtype),
        scratch_shapes=[pltpu.SemaphoreType.DMA((count,))],
        cost_estimate=pl.CostEstimate(
            flops=0, bytes_accessed=4 * rows * width, transcendentals=0
        ),
        compiler_params=pltpu.CompilerParams(vmem_limit_bytes=VMEM_LIMIT),
        name="pack",
    )(*pieces)


def norm_kernel(count, *refs):
    gain_ref, out_ref = refs[count], refs[-2]
    pack_kernel(count, *refs[:count], *refs[-2:])
    tile = 256

    @pl.loop(0, out_ref.shape[0] // tile)
    def _(i):
        rows = pl.ds(pl.multiple_of(i * tile, tile), tile)
        values = out_ref[rows, :].astype(f32)
        out_ref[rows, :] = (values * rms_inverse(values) * gain_ref[...]).astype(bf16)


def pack_normed(pieces, gain, early):
    rows, width = sum(p.shape[0] for p in pieces), pieces[0].shape[1]
    count = len(pieces)
    return pl.pallas_call(
        functools.partial(norm_kernel, count),
        in_specs=[pl.BlockSpec(memory_space=pl.ANY)] * count
        + [pl.BlockSpec(memory_space=pltpu.VMEM)]
        + [pl.BlockSpec(memory_space=pl.ANY)] * len(early),
        out_specs=pl.BlockSpec(memory_space=pltpu.VMEM),
        out_shape=jax.ShapeDtypeStruct((rows, width), bf16),
        scratch_shapes=[pltpu.SemaphoreType.DMA((count,))],
        cost_estimate=pl.CostEstimate(
            flops=8 * rows * width, bytes_accessed=4 * rows * width, transcendentals=0
        ),
        compiler_params=pltpu.CompilerParams(vmem_limit_bytes=VMEM_LIMIT),
        name="pack_normed",
    )(*pieces, gain, *early)


def plane_neighbours(own):
    return swap(own, "col"), swap(own, "row")


def plane_far(neighbours, *waits):
    across, along = neighbours
    half = across.shape[0] // 2
    return (
        swap(after(across[:half], *waits), "row"),
        swap(after(along[half:], *waits), "col"),
    )


def with_partner(pieces, swapped=()):
    return pieces + list(swapped) + [swap(piece, "tp") for piece in pieces[len(swapped) :]]


def chip_sums(front, back):
    pairs = []
    for own, other in (front, back):
        shape = (4, own.shape[0] // 4, own.shape[1])
        pairs.append((own.reshape(shape), swap(other, "tp").reshape(shape)))
    return pairs


def quarter(pair, k):
    return pair[0][k].astype(f32) + pair[1][k].astype(f32)


def first_operands(sums):
    front, back = sums
    return (
        jnp.concatenate([quarter(front, 1), quarter(front, 3)]).astype(bf16),
        (back[0][2:].astype(f32) + back[1][2:].astype(f32)).astype(bf16),
    )


def reduce_first(operands, *waits):
    front, back = operands
    rows = front.shape[0] // 2
    return (
        swap(after(front, *waits), "col").reshape(2, rows, -1),
        swap(after(back, *waits), "row"),
    )


def reduce_operands(sums, arrived):
    front, back = sums
    got, got_back = arrived[0].astype(f32), arrived[1].astype(f32)
    return (
        (quarter(front, 0) + got[0], (quarter(front, 2) + got[1]).astype(bf16)),
        (quarter(back, 0) + got_back[0], (quarter(back, 1) + got_back[1]).astype(bf16)),
    )


def last_swaps(operands, *waits):
    return (
        swap(after(operands[0][1], *waits), "row"),
        swap(after(operands[1][1], *waits), "col"),
    )


def reduce_last(operands, swapped):
    return jnp.concatenate(
        [keep + last.astype(f32) for (keep, _), last in zip(operands, swapped)], axis=1
    )


def joined(front_ref, front_last_ref, back_ref, back_last_ref):
    return jnp.concatenate(
        [
            front_ref[...] + front_last_ref[...].astype(f32),
            back_ref[...] + back_last_ref[...].astype(f32),
        ],
        axis=1,
    )


def hidden_kernel(front, front_last, back, back_last, tokens_ref, gain_ref, hidden_ref, normed_ref):
    hidden = tokens_ref[...].astype(f32) + joined(front, front_last, back, back_last)
    hidden_ref[...] = hidden
    normed_ref[...] = (hidden * rms_inverse(hidden) * gain_ref[...]).astype(bf16)


def add_and_norm(operands, last, tokens, gain):
    halves = [part for (keep, _), got in zip(operands, last) for part in (keep, got)]
    return pl.pallas_call(
        hidden_kernel,
        in_specs=[pl.BlockSpec(memory_space=pltpu.VMEM)] * 6,
        out_specs=[pl.BlockSpec(memory_space=pltpu.VMEM)] * 2,
        out_shape=[
            jax.ShapeDtypeStruct(tokens.shape, f32),
            jax.ShapeDtypeStruct(tokens.shape, bf16),
        ],
        cost_estimate=pl.CostEstimate(
            flops=10 * tokens.size, bytes_accessed=14 * tokens.size, transcendentals=0
        ),
        compiler_params=pltpu.CompilerParams(vmem_limit_bytes=VMEM_LIMIT),
        name="add_and_norm",
    )(*halves, tokens, gain)


def back_kernel(front, front_last, back, back_last, values_ref, base_ref, gain_ref, *outs):
    values = values_ref[...].astype(f32)
    inverse = rms_inverse(values)
    unit = values * inverse
    scaled = joined(front, front_last, back, back_last) * gain_ref[...]
    grad = base_ref[...].astype(f32) + inverse * (
        scaled - unit * jnp.mean(scaled * unit, axis=-1, keepdims=True)
    )
    for out in outs:
        out[...] = grad.astype(out.dtype)


def norm_back(operands, last, values, base, gain, dtypes):
    halves = [part for (keep, _), got in zip(operands, last) for part in (keep, got)]
    return pl.pallas_call(
        back_kernel,
        in_specs=[pl.BlockSpec(memory_space=pltpu.VMEM)] * 7,
        out_specs=[pl.BlockSpec(memory_space=pltpu.VMEM)] * len(dtypes),
        out_shape=[jax.ShapeDtypeStruct(values.shape, dtype) for dtype in dtypes],
        cost_estimate=pl.CostEstimate(
            flops=16 * values.size, bytes_accessed=18 * values.size, transcendentals=0
        ),
        compiler_params=pltpu.CompilerParams(vmem_limit_bytes=VMEM_LIMIT),
        name="norm_back",
    )(*halves, values, base, gain)


def split_kernel(spans, member_ref, *refs):
    sources, outs = refs[: len(spans)], refs[len(spans) :]
    for k in range(4):
        target = member_ref[0] ^ k
        column = 0
        for source, (offset, stride, width, shift) in zip(sources, spans):
            start = pl.multiple_of((target >> shift) * stride + offset, 128)
            outs[k][:, column : column + width] = source[:, pl.ds(start, width)]
            column += width


def split(member, sources, spans):
    rows, width = sources[0].shape[0], sum(span[2] for span in spans)
    whole = pl.BlockSpec(memory_space=pltpu.VMEM)
    return pl.pallas_call(
        functools.partial(split_kernel, spans),
        in_specs=[pl.BlockSpec(memory_space=pltpu.SMEM)] + [whole] * len(sources),
        out_specs=[whole] * 4,
        out_shape=[jax.ShapeDtypeStruct((rows, width), bf16)] * 4,
        cost_estimate=pl.CostEstimate(
            flops=0, bytes_accessed=16 * rows * width, transcendentals=0
        ),
        compiler_params=pltpu.CompilerParams(vmem_limit_bytes=VMEM_LIMIT),
        name="split",
    )(member, *sources)


def place_kernel(member_ref, *refs):
    rows = refs[0].shape[0]
    for k in range(4):
        start = pl.multiple_of((member_ref[0] ^ k) * rows, rows)
        column = 0
        for out_ref in refs[4:]:
            width = out_ref.shape[1]
            out_ref[pl.ds(start, rows), :] = refs[k][:, column : column + width]
            column += width


def place_rows(member, pieces, *widths):
    rows, width = pieces[0].shape
    whole = pl.BlockSpec(memory_space=pltpu.VMEM)
    return pl.pallas_call(
        place_kernel,
        in_specs=[pl.BlockSpec(memory_space=pltpu.SMEM)] + [whole] * 4,
        out_specs=[whole] * len(widths or (width,)),
        out_shape=[
            jax.ShapeDtypeStruct((4 * rows, w), bf16) for w in widths or (width,)
        ],
        cost_estimate=pl.CostEstimate(
            flops=0, bytes_accessed=16 * rows * width, transcendentals=0
        ),
        compiler_params=pltpu.CompilerParams(vmem_limit_bytes=VMEM_LIMIT),
        name="place_rows",
    )(member, *pieces)


def pick_kernel(member_ref, *refs):
    sources, outs = refs[:-4], refs[-4:]
    rows = outs[0].shape[0]
    for k in range(4):
        start = pl.multiple_of((member_ref[0] ^ k) * rows, rows)
        column = 0
        for source in sources:
            width = source.shape[1]
            outs[k][:, column : column + width] = source[pl.ds(start, rows), :]
            column += width


def pick_rows(member, *sources):
    rows, width = sources[0].shape[0] // 4, sum(source.shape[1] for source in sources)
    whole = pl.BlockSpec(memory_space=pltpu.VMEM)
    return pl.pallas_call(
        pick_kernel,
        in_specs=[pl.BlockSpec(memory_space=pltpu.SMEM)] + [whole] * len(sources),
        out_specs=[whole] * 4,
        out_shape=[jax.ShapeDtypeStruct((rows, width), bf16)] * 4,
        cost_estimate=pl.CostEstimate(
            flops=0, bytes_accessed=16 * rows * width, transcendentals=0
        ),
        compiler_params=pltpu.CompilerParams(vmem_limit_bytes=VMEM_LIMIT),
        name="pick_rows",
    )(member, *sources)


def swap_all(pieces):
    return [pieces[0]] + [swap_plane(pieces[k], k) for k in (1, 2, 3)]


def mlp_final_kernel(parts, stride, member_ref, gate_w_ref, up_w_ref, *refs):
    pieces, outs, gain_ref = refs[:-4], refs[-4:-1], refs[-1]
    for n, chunks in enumerate(parts):
        for k in range(4):
            start = 0
            for offset, width in chunks:
                column = pl.multiple_of((member_ref[0] ^ k) * stride + offset, 128)
                for i in range(3):
                    part = pieces[4 * n + k][:, start : start + width]
                    outs[i][:, pl.ds(column, width)] = part.astype(f32)
                    start += width
    gain_ref[...] = jnp.sum(
        gate_w_ref[...].astype(f32) * outs[0][...] + up_w_ref[...].astype(f32) * outs[1][...],
        axis=1,
        keepdims=True,
    )


def mlp_final(member, gate_weight, up_weight, chunks, parts):
    rows, hidden = gate_weight.shape
    pieces = [piece for part in parts for piece in part]
    whole = pl.BlockSpec(memory_space=pltpu.VMEM)
    return pl.pallas_call(
        functools.partial(mlp_final_kernel, chunks, hidden // 4),
        in_specs=[pl.BlockSpec(memory_space=pltpu.SMEM)] + [whole] * (2 + len(pieces)),
        out_specs=[whole] * 4,
        out_shape=[jax.ShapeDtypeStruct((rows, hidden), f32)] * 3
        + [jax.ShapeDtypeStruct((rows, 1), f32)],
        cost_estimate=pl.CostEstimate(
            flops=4 * rows * hidden, bytes_accessed=22 * rows * hidden, transcendentals=0
        ),
        compiler_params=pltpu.CompilerParams(vmem_limit_bytes=VMEM_LIMIT),
        name="mlp_final",
    )(member, gate_weight, up_weight, *pieces)


TURN = [(0, 0), (1, 2), (2, 1), (3, 3)]
CROSS = [(0, 2), (1, 0), (2, 3), (3, 1)]
CROSS_BACK = [(2, 0), (0, 1), (3, 2), (1, 3)]


def vmem_call(kernel, name, out_shape, *operands):
    whole = pl.BlockSpec(memory_space=pltpu.VMEM)
    moved = sum(a.size * a.dtype.itemsize for a in operands)
    moved += sum(a.size * a.dtype.itemsize for a in out_shape)
    return pl.pallas_call(
        kernel,
        in_specs=[pl.BlockSpec(memory_space=pltpu.SMEM)] + [whole] * (len(operands) - 1),
        out_specs=[whole] * len(out_shape),
        out_shape=out_shape,
        cost_estimate=pl.CostEstimate(flops=0, bytes_accessed=moved, transcendentals=0),
        compiler_params=pltpu.CompilerParams(vmem_limit_bytes=VMEM_LIMIT),
        name=name,
    )(*operands)


def head_columns(index):
    return pl.ds(pl.multiple_of(index * HS, HS), HS)


def halves_kernel(rows, member_ref, grads_ref, keep_ref, send_ref):
    half = (member_ref[0] & 1) * 2 * rows
    for i, base in enumerate(range(0, grads_ref.shape[0], 4 * rows)):
        part = slice(i * 2 * rows, (i + 1) * 2 * rows)
        mine = pl.ds(pl.multiple_of(base + half, 2 * rows), 2 * rows)
        other = pl.ds(pl.multiple_of(base + 2 * rows - half, 2 * rows), 2 * rows)
        keep_ref[part, :] = grads_ref[mine, :]
        send_ref[part, :] = grads_ref[other, :]


def join_kernel(rows, member_ref, keep_ref, got_ref, both_ref, out_ref):
    out_ref[:, : 2 * HS] = both_ref[...]
    for i, base in enumerate(range(0, out_ref.shape[0], 4 * rows)):
        part = slice(i * 2 * rows, (i + 1) * 2 * rows)
        total = (keep_ref[part, :].astype(f32) + got_ref[part, :].astype(f32)).astype(bf16)
        out_ref[base : base + 2 * rows, 2 * HS :] = total[:, :HS]
        out_ref[base + 2 * rows : base + 4 * rows, 2 * HS :] = total[:, HS:]


def attention_pick_kernel(member_ref, source_ref, *outs):
    member, rows = member_ref[0], outs[0].shape[0]
    for k in range(4):
        at = pl.ds(pl.multiple_of((member ^ k) * rows, rows), rows)
        outs[k][...] = source_ref[at, : 2 * HS]
    for h in range(2):
        start = ((member >> 1) ^ h) * rows
        at = pl.ds(pl.multiple_of(start, rows), rows)
        outs[4 + h][:, :HS] = source_ref[at, 2 * HS :]
        at = pl.ds(pl.multiple_of(start + 2 * rows, rows), rows)
        outs[4 + h][:, HS:] = source_ref[at, 2 * HS :]


def attention_return(member, reduced):
    rows = reduced.shape[0] // 4
    *both, turned, crossed = vmem_call(
        attention_pick_kernel,
        "attention_pick",
        [jax.ShapeDtypeStruct((rows, 2 * HS), bf16)] * 6,
        member,
        reduced,
    )
    return swap_all(both) + [
        lax.ppermute(turned, PLANE, TURN),
        lax.ppermute(crossed, PLANE, CROSS_BACK),
    ]


def attention_final_kernel(member_ref, qw_ref, kw_ref, vw_ref, *refs):
    pieces = refs[:6]
    q_ref, k_ref, v_ref, o_ref, gain_ref = refs[6:]
    member = member_ref[0]
    for k in range(4):
        columns = head_columns(member ^ k)
        q_ref[:, columns] = pieces[k][:, :HS].astype(f32)
        o_ref[:, columns] = pieces[k][:, HS:].astype(f32)
    for h in range(2):
        columns = head_columns((member & 1) ^ h)
        k_ref[:, columns] = pieces[4 + h][:, :HS].astype(f32)
        v_ref[:, columns] = pieces[4 + h][:, HS:].astype(f32)

    def row_sum(weight_ref, grad_ref):
        return jnp.sum(weight_ref[...].astype(f32) * grad_ref[...], axis=1, keepdims=True)

    gain_ref[...] = row_sum(qw_ref, q_ref) + row_sum(kw_ref, k_ref) + row_sum(vw_ref, v_ref)


def attention_final(member, query_weight, key_weight, value_weight, pieces):
    rows, width = query_weight.shape
    shapes = [jax.ShapeDtypeStruct((rows, n), f32) for n in (width, width // 2, width // 2, width, 1)]
    return vmem_call(
        attention_final_kernel,
        "attention_final",
        shapes,
        member,
        query_weight,
        key_weight,
        value_weight,
        *pieces,
    )


def rms_inverse(values):
    return lax.rsqrt(jnp.mean(values * values, axis=-1, keepdims=True) + epsilon)


def rope_tables(positions):
    half_size = HS // 2
    indices = jnp.arange(half_size, dtype=f32)
    inverse = theta_base ** (-2.0 * indices / HS)
    angles = positions.astype(f32)[:, None] * inverse[None, :]
    return jnp.cos(angles), jnp.sin(angles)


def rotate(vectors, cos, sin):
    front, back = vectors[:, : HS // 2], vectors[:, HS // 2 :]
    return jnp.concatenate([front * cos - back * sin, back * cos + front * sin], axis=-1)


def unrotate(grads, cos, sin):
    front, back = grads[:, : HS // 2], grads[:, HS // 2 :]
    return jnp.concatenate([front * cos + back * sin, back * cos - front * sin], axis=-1)


def mlp_tile(width, normed, cot, weight_ref):
    both = product(normed, weight_ref[:, : 2 * width])
    d_inner = product(cot, weight_ref[:, 2 * width :])
    gate, upward = both[:, :width], both[:, width:]
    sig = 1.0 / (1.0 + jnp.exp(-gate))
    silu = gate * sig
    d_gate = d_inner * upward * sig * (1.0 + gate * (1.0 - sig))
    return (
        (silu * upward).astype(bf16),
        jnp.concatenate([d_gate, d_inner * silu], axis=1).astype(bf16),
    )


def mlp_kernel(width, normed_ref, cot_ref, weight_ref, inner_ref, grads_ref):
    inner_ref[...], grads_ref[...] = mlp_tile(
        width, normed_ref[...], cot_ref[...], weight_ref
    )


def tail_kernel(width, normed_ref, cot_ref, weight_ref, base_ref, *refs):
    inner_ref, grads_ref, front_ref, back_ref = refs[-4:]
    inner, grads = mlp_tile(width, normed_ref[...], cot_ref[...], weight_ref)
    inner_ref[...], grads_ref[...] = inner, grads
    total = times_transposed(grads, weight_ref[:, : 2 * width]) + base_ref[...]
    half = total.shape[1] // 2
    front_ref[...] = total[:, :half].astype(front_ref.dtype)
    back_ref[...] = total[:, half:].astype(back_ref.dtype)


def mlp_tail(normed, cot, weight, base, part, dtype, chained=()):
    tokens, features = normed.shape
    width = weight.shape[1] // 3
    tile, rows = 256, tokens // 2
    steps = rows // tile
    count = len(chained)
    return pl.pallas_call(
        functools.partial(tail_kernel, width),
        grid=(steps,),
        in_specs=[
            pl.BlockSpec((tile, features), lambda i: (part * steps + i, 0)),
            pl.BlockSpec((tile, features), lambda i: (part * steps + i, 0)),
            pl.BlockSpec((features, 3 * width), lambda i: (0, 0)),
            pl.BlockSpec((tile, features), lambda i: (i, 0)),
        ]
        + [pl.BlockSpec(memory_space=pl.ANY)] * count,
        out_specs=[
            pl.BlockSpec((tile, width), lambda i: (part * steps + i, 0)),
            pl.BlockSpec((tile, 2 * width), lambda i: (part * steps + i, 0)),
            pl.BlockSpec((tile, features // 2), lambda i: (i, 0)),
            pl.BlockSpec((tile, features // 2), lambda i: (i, 0)),
        ],
        out_shape=[
            jax.ShapeDtypeStruct((tokens, width), bf16),
            jax.ShapeDtypeStruct((tokens, 2 * width), bf16),
            jax.ShapeDtypeStruct((rows, features // 2), dtype),
            jax.ShapeDtypeStruct((rows, features // 2), dtype),
        ],
        input_output_aliases={4 + i: i for i in range(count)},
        cost_estimate=pl.CostEstimate(
            flops=10 * rows * features * width,
            bytes_accessed=2 * features * (5 * rows + 3 * width),
            transcendentals=rows * width,
        ),
        compiler_params=pltpu.CompilerParams(vmem_limit_bytes=VMEM_LIMIT),
        name="mlp_tail",
    )(normed, cot, weight, base, *chained)


def mlp_chunk(normed, cot, weight):
    tokens, features = normed.shape
    width = weight.shape[1] // 3
    tile = 256
    return pl.pallas_call(
        functools.partial(mlp_kernel, width),
        grid=(tokens // tile,),
        in_specs=[
            pl.BlockSpec((tile, features), lambda i: (i, 0)),
            pl.BlockSpec((tile, features), lambda i: (i, 0)),
            pl.BlockSpec((features, 3 * width), lambda i: (0, 0)),
        ],
        out_specs=[
            pl.BlockSpec((tile, width), lambda i: (i, 0)),
            pl.BlockSpec((tile, 2 * width), lambda i: (i, 0)),
        ],
        out_shape=[
            jax.ShapeDtypeStruct((tokens, width), bf16),
            jax.ShapeDtypeStruct((tokens, 2 * width), bf16),
        ],
        cost_estimate=pl.CostEstimate(
            flops=6 * tokens * features * width,
            bytes_accessed=2 * features * (2 * tokens + 3 * width),
            transcendentals=tokens * width,
        ),
        compiler_params=pltpu.CompilerParams(vmem_limit_bytes=VMEM_LIMIT),
        name="mlp_chunk",
    )(normed, cot, weight)


def sum_kernel(count, *refs):
    lefts, rights, out_ref = refs[:count], refs[count : 2 * count], refs[-1]
    total = times_transposed(lefts[0][...], rights[0][...])
    for left, right in zip(lefts[1:], rights[1:]):
        total += times_transposed(left[...], right[...])
    for base in refs[2 * count : -1]:
        total += base[...].astype(f32)
    out_ref[...] = total.astype(out_ref.dtype)


def chunk_sum(lefts, rights, column, part, half, dtype):
    count = len(lefts)
    tokens, features = lefts[0].shape[0], rights[0].shape[0]
    widths = [left.shape[1] for left in lefts]
    rows = tokens // 2
    tile = 256
    if half is not None:
        features, tile = features // 2, 512
    steps = rows // tile
    block = half or 0
    return pl.pallas_call(
        functools.partial(sum_kernel, count),
        grid=(steps,),
        in_specs=[pl.BlockSpec((tile, w), lambda i: (part * steps + i, 0)) for w in widths]
        + [pl.BlockSpec((features, w), lambda i: (block, column)) for w in widths],
        out_specs=pl.BlockSpec((tile, features), lambda i: (i, 0)),
        out_shape=jax.ShapeDtypeStruct((rows, features), dtype),
        cost_estimate=pl.CostEstimate(
            flops=2 * rows * features * sum(widths),
            bytes_accessed=2 * sum(widths) * (rows + features) + 4 * rows * features,
            transcendentals=0,
        ),
        compiler_params=pltpu.CompilerParams(vmem_limit_bytes=VMEM_LIMIT),
        name="chunk_sum",
    )(*lefts, *rights)


def grads_kernel(count, *refs):
    column = 0
    for left, right in zip(refs[:count], refs[count : 2 * count]):
        width = right.shape[1]
        refs[-1][:, column : column + width] = outer_sum(left[...], right[...]).astype(bf16)
        column += width


def weight_grads(*pairs):
    lefts = [left for left, _ in pairs]
    rights = [r if isinstance(r, tuple) else (r, r.shape[1], 0) for _, r in pairs]
    count = len(pairs)
    tokens, features = lefts[0].shape
    widths = [width for _, width, _ in rights]
    tile = 256

    def block(width, at):
        return pl.BlockSpec((tokens, width), lambda i: (0, at))

    return pl.pallas_call(
        functools.partial(grads_kernel, count),
        grid=(features // tile,),
        in_specs=[pl.BlockSpec((tokens, tile), lambda i: (0, i))] * count
        + [block(width, at) for _, width, at in rights],
        out_specs=pl.BlockSpec((tile, sum(widths)), lambda i: (i, 0)),
        out_shape=jax.ShapeDtypeStruct((features, sum(widths)), bf16),
        cost_estimate=pl.CostEstimate(
            flops=2 * tokens * features * sum(widths),
            bytes_accessed=2 * (count * tokens * features + sum(widths) * (tokens + features)),
            transcendentals=0,
        ),
        compiler_params=pltpu.CompilerParams(vmem_limit_bytes=VMEM_LIMIT),
        name="weight_grads",
    )(*lefts, *[array for array, _, _ in rights])


def project_kernel(place_ref, normed_ref, weight_ref, cos_ref, sin_ref, q_ref, k_ref, v_ref):
    step = pl.program_id(0)
    cos, sin = cos_ref[...], sin_ref[...]
    qkv = product(normed_ref[...], weight_ref[...])
    keys = rotate(qkv[:, :HS], cos, sin).astype(bf16)
    vals = qkv[:, HS : 2 * HS].astype(bf16)
    query = rotate(qkv[:, 2 * HS :], cos, sin).astype(bf16) * HS ** (-0.5)
    blocks = normed_ref.shape[0] // BLOCK
    for b in range(blocks):
        rows = pl.ds(pl.multiple_of(place_ref[step * blocks + b] * BLOCK, BLOCK), BLOCK)
        part = slice(b * BLOCK, (b + 1) * BLOCK)
        q_ref[rows, :] = query[part]
        k_ref[rows, :] = keys[part]
        v_ref[rows, :] = vals[part]


def project(place, normed, weight, cos, sin):
    tokens, features = normed.shape
    tile = 256
    whole = pl.BlockSpec((tokens, HS), lambda i, place: (0, 0))
    return pl.pallas_call(
        project_kernel,
        grid_spec=pltpu.PrefetchScalarGridSpec(
            num_scalar_prefetch=1,
            grid=(tokens // tile,),
            in_specs=[
                pl.BlockSpec((tile, features), lambda i, place: (i, 0)),
                pl.BlockSpec((features, 3 * HS), lambda i, place: (0, 0)),
                pl.BlockSpec((tile, HS // 2), lambda i, place: (i, 0)),
                pl.BlockSpec((tile, HS // 2), lambda i, place: (i, 0)),
            ],
            out_specs=[whole] * 3,
        ),
        out_shape=[jax.ShapeDtypeStruct((tokens, HS), bf16)] * 3,
        cost_estimate=pl.CostEstimate(
            flops=6 * tokens * features * HS,
            bytes_accessed=2 * features * (tokens + 3 * HS) + 10 * tokens * HS,
            transcendentals=0,
        ),
        compiler_params=pltpu.CompilerParams(vmem_limit_bytes=VMEM_LIMIT),
        name="project",
    )(place, normed, weight, cos, sin)


TILE = 256


def tile_masks():
    rows = lax.broadcasted_iota(jnp.int32, (TILE, TILE), 0)
    cols = lax.broadcasted_iota(jnp.int32, (TILE, TILE), 1)
    causal = rows >= cols
    return causal, causal & (rows // BLOCK == cols // BLOCK)


def block_rows(order_ref, index):
    return pl.ds(pl.multiple_of(order_ref[index] * BLOCK, BLOCK), BLOCK)


def forward_kernel(order_ref, q_ref, k_ref, v_ref, mixed_ref, lse_ref, peak_ref):
    causal, inside = tile_masks()
    prompt = GROUP // 2
    top = jnp.full((TILE, 1), masked_value, f32)
    for i in range(GROUP // TILE):
        rows = slice(i * TILE, (i + 1) * TILE)
        past = min(i * TILE, prompt)
        query = q_ref[rows, :]
        near = times_transposed(query, k_ref[rows, :])
        near = jnp.where(causal if i * TILE < prompt else inside, near, masked_value)
        peak = jnp.max(near, axis=1, keepdims=True)
        if past:
            far = times_transposed(query, k_ref[:past, :])
            peak = jnp.maximum(peak, jnp.max(far, axis=1, keepdims=True))
            far = jnp.exp(far - peak)
        near = jnp.exp(near - peak)
        total = jnp.sum(near, axis=1, keepdims=True)
        if past:
            total += jnp.sum(far, axis=1, keepdims=True)
        share = 1.0 / total
        mixed = product((near * share).astype(bf16), v_ref[rows, :])
        if past:
            mixed += product((far * share).astype(bf16), v_ref[:past, :])
        mixed = mixed.astype(bf16)
        for b in range(TILE // BLOCK):
            mixed_ref[block_rows(order_ref, i * (TILE // BLOCK) + b), :] = mixed[
                b * BLOCK : (b + 1) * BLOCK
            ]
        lse_ref[rows, :] = peak + jnp.log(total)
        top = jnp.maximum(top, peak)
    peak_ref[...] = jnp.full(peak_ref.shape, jnp.max(top), f32)


def attention_forward(order, query, keys, vals):
    whole = pl.BlockSpec(memory_space=pltpu.VMEM)
    return pl.pallas_call(
        forward_kernel,
        in_specs=[pl.BlockSpec(memory_space=pltpu.SMEM), whole, whole, whole],
        out_specs=[whole] * 3,
        out_shape=[
            jax.ShapeDtypeStruct((GROUP, HS), bf16),
            jax.ShapeDtypeStruct((GROUP, 1), f32),
            jax.ShapeDtypeStruct((8, 128), f32),
        ],
        cost_estimate=pl.CostEstimate(
            flops=2 * GROUP * GROUP * HS,
            bytes_accessed=8 * GROUP * HS,
            transcendentals=GROUP * GROUP // 2,
        ),
        compiler_params=pltpu.CompilerParams(vmem_limit_bytes=VMEM_LIMIT),
        name="attention_forward",
    )(order, query, keys, vals)


def backward_kernel(
    order_ref, q_ref, k_ref, v_ref, lse_ref, mixed_ref, cos_ref, sin_ref, out_ref, dk_ref, dv_ref
):
    causal, inside = tile_masks()
    prompt = GROUP // 2
    blocks = TILE // BLOCK

    def back(grad, index):
        rows = block_rows(order_ref, index)
        return rows, unrotate(grad, cos_ref[rows, :], sin_ref[rows, :]).astype(bf16)

    for i in range(GROUP // TILE):
        rows = slice(i * TILE, (i + 1) * TILE)
        past = min(i * TILE, prompt)
        query, lse = q_ref[rows, :], lse_ref[rows, :]
        d_mixed = jnp.concatenate(
            [mixed_ref[block_rows(order_ref, i * blocks + b), :] for b in range(blocks)], axis=0
        )
        near = times_transposed(query, k_ref[rows, :])
        near = jnp.where(causal if i * TILE < prompt else inside, near, masked_value)
        near = jnp.exp(near - lse)
        d_near = times_transposed(d_mixed, v_ref[rows, :])
        inner = jnp.sum(near * d_near, axis=1, keepdims=True)
        if past:
            far = jnp.exp(times_transposed(query, k_ref[:past, :]) - lse)
            d_far = times_transposed(d_mixed, v_ref[:past, :])
            inner += jnp.sum(far * d_far, axis=1, keepdims=True)
        d_near = (near * (d_near - inner)).astype(bf16)
        d_query = product(d_near, k_ref[rows, :])
        dk_ref[rows, :] = outer_sum(d_near, query)
        dv_ref[rows, :] = outer_sum(near.astype(bf16), d_mixed)
        if past:
            d_far = (far * (d_far - inner)).astype(bf16)
            d_query += product(d_far, k_ref[:past, :])
            dk_ref[:past, :] += outer_sum(d_far, query)
            dv_ref[:past, :] += outer_sum(far.astype(bf16), d_mixed)
        d_query = d_query * HS ** (-0.5)
        for b in range(blocks):
            where, grad = back(d_query[b * BLOCK : (b + 1) * BLOCK], i * blocks + b)
            out_ref[where, 2 * HS :] = grad
    for c in range(GROUP // BLOCK):
        part = slice(c * BLOCK, (c + 1) * BLOCK)
        where, grad = back(dk_ref[part, :], c)
        out_ref[where, :HS] = grad
        out_ref[where, HS : 2 * HS] = dv_ref[part, :].astype(bf16)


def attention_backward(order, query, keys, vals, lse, d_mixed, cos, sin):
    whole = pl.BlockSpec(memory_space=pltpu.VMEM)
    return pl.pallas_call(
        backward_kernel,
        in_specs=[pl.BlockSpec(memory_space=pltpu.SMEM)] + [whole] * 7,
        out_specs=whole,
        out_shape=jax.ShapeDtypeStruct((GROUP, 3 * HS), bf16),
        scratch_shapes=[pltpu.VMEM((GROUP, HS), f32), pltpu.VMEM((GROUP, HS), f32)],
        cost_estimate=pl.CostEstimate(
            flops=5 * GROUP * GROUP * HS,
            bytes_accessed=20 * GROUP * HS,
            transcendentals=GROUP * GROUP // 2,
        ),
        compiler_params=pltpu.CompilerParams(vmem_limit_bytes=VMEM_LIMIT),
        name="attention_backward",
    )(order, query, keys, vals, lse, d_mixed, cos, sin)


def local(
    tokens,
    cotangent,
    segment,
    position,
    clip_limit,
    attn_gain,
    query_weight,
    key_weight,
    value_weight,
    output_weight,
    mlp_gain,
    gate_weight,
    up_weight,
    down_weight,
):
    groups = lax.axis_size("group")
    group = lax.axis_index("group")
    core = lax.axis_index("tp")
    member = lax.axis_index(PLANE)
    token_rows = tokens.shape[0]
    own_rows, features = query_weight.shape[0], tokens.shape[1]
    hidden_own = gate_weight.shape[1] // 4
    chunks, offset = [], 0
    for part in SIXTEENTHS:
        chunks.append((offset, hidden_own * part // 16))
        offset += hidden_own * part // 16
    member_at = member.astype(jnp.int32).reshape(1)

    def own_order(array):
        parts = []
        for j in range(2):
            for k in range(4):
                start = group * GROUP + (member ^ k) * (2 * token_rows) + (core ^ j) * token_rows
                parts.append(lax.dynamic_slice_in_dim(array, start, token_rows))
        return jnp.concatenate(parts)

    def collect(blocks):
        return lax.all_gather(blocks, "group", axis=0, tiled=True)

    def mlp_exchange(some, waits):
        weights = [after(a, *waits) for a in (gate_weight, up_weight, down_weight)]
        spans = tuple((start, hidden_own, count, 0) for start, count in some for _ in range(3))
        return swap_all(split(member_at, weights * len(some), spans))

    seg, pos = own_order(segment), own_order(position)
    cos, sin = rope_tables(pos)
    seg_blocks, pos_blocks = seg[::BLOCK], pos[::BLOCK]
    half_blocks = GROUP // BLOCK // 2
    place = jnp.where(seg_blocks == 0, pos_blocks // BLOCK, half_blocks - 1 + seg_blocks)
    labels = jnp.arange(2 * half_blocks, dtype=jnp.int32)
    order = jnp.sum(jnp.where(place[None, :] == labels[:, None], labels[None, :], 0), axis=1)
    index = lax.axis_index(FSDP)
    gains = jnp.stack([attn_gain, mlp_gain])[:, None, :]
    gains = jnp.where(jnp.arange(4 * groups)[None, :, None] == index, gains, 0)
    gains, gain_rounds = combine_all(gains, groups, lambda a, b: a + b)
    gains = gains.reshape(2, features).astype(f32)
    head, pair = (0, HS, HS, 0), (0, HS, HS, 1)
    attn_pieces = swap_all(
        split(
            member_at,
            (key_weight, value_weight, query_weight, output_weight),
            (pair, pair, head, head),
        )
    )
    (attn_blocks,) = place_rows(
        member_at, [after(attn_pieces[0], *gain_rounds[0])] + attn_pieces[1:]
    )
    attn_weights = collect(attn_blocks)
    late_tokens = after(tokens, *attn_pieces[1:])
    neighbours = plane_neighbours(late_tokens)
    tokens_far = plane_far(neighbours)
    tokens_mine = [late_tokens, *neighbours, *tokens_far]
    tokens_near = [swap(piece, "tp") for piece in tokens_mine[:3]]
    normed_all = pack_normed(
        with_partner(tokens_mine, tokens_near), gains[:1], (cos, sin, place, order)
    )
    pieces_0 = mlp_exchange(chunks[:1], (*tokens_far, *tokens_near))
    (blocks_0,) = place_rows(
        member_at, [after(pieces_0[0], normed_all)] + pieces_0[1:]
    )
    late_cot = after(cotangent, *pieces_0[1:])
    cot_near = plane_neighbours(late_cot)
    cot_far = plane_far(cot_near)
    query, keys, vals = project(
        place, after(normed_all, *cot_near), attn_weights, cos, sin
    )
    mixed, logsum, peak = attention_forward(
        order, after(query, *cot_far), keys, vals
    )

    head_top = jnp.where(jnp.arange(4) == member, peak[0, :4], masked_value)
    head_top, head_rounds = combine_all(head_top, groups, jnp.maximum)

    def projected(left, column, waits=(), others=()):
        lefts = (after(left, *others) if others else left, after(left, *waits) if waits else left)
        return [
            [
                chunk_sum([lefts[j]], [attn_weights], column, j, h, bf16 if j else f32)
                for j in (0, 1)
            ]
            for h in range(2)
        ]

    attn_sums = chip_sums(*projected(mixed, 3))
    arrived = reduce_first(first_operands(attn_sums))
    attn_operands = reduce_operands(attn_sums, arrived)
    attn_last = last_swaps(attn_operands, *head_rounds[0])
    hidden, own_normed = add_and_norm(attn_operands, attn_last, tokens, gains[1:])
    neighbours = plane_neighbours(own_normed)
    normed_far = plane_far(neighbours, *head_rounds[-1])
    pieces_1 = mlp_exchange(chunks[1:], normed_far)
    mlp_weights = [collect(blocks_0), collect(*place_rows(member_at, pieces_1))]
    normed_mlp = pack(with_partner([own_normed, *neighbours, *normed_far]))
    cot_all = pack(with_partner([late_cot, *cot_near, *cot_far]))

    def line_sum(partial):
        return lax.psum_scatter(partial, "group", scatter_dimension=0, tiled=True)

    inner_0, both_0 = mlp_chunk(normed_mlp, cot_all, mlp_weights[0])
    grads_0 = weight_grads((normed_mlp, both_0), (cot_all, inner_0))
    sum_0 = line_sum(grads_0)
    late_both = after(both_0, grads_0)
    early = [chunk_sum([late_both], mlp_weights[:1], 0, j, None, f32) for j in range(2)]
    inner_1, both_1, front_1, back_1 = mlp_tail(
        after(normed_mlp, *early), cot_all, mlp_weights[1], early[1], 1, bf16
    )
    inner_1, both_1, front_0, back_0 = mlp_tail(
        normed_mlp, cot_all, mlp_weights[1], early[0], 0, f32, (inner_1, both_1)
    )

    mlp_sums = chip_sums((front_0, front_1), (back_0, back_1))
    operands = first_operands(mlp_sums)
    arrived = reduce_first(operands)
    inners = [after(inner, *operands) for inner in (inner_0, inner_1)]
    out_parts = [
        [chunk_sum(inners, mlp_weights, 2, j, h, bf16 if j else f32) for j in (0, 1)]
        for h in range(2)
    ]
    mlp_operands = reduce_operands(mlp_sums, arrived)
    mlp_last = last_swaps(mlp_operands, *out_parts[0], *out_parts[1])
    d_hidden, own_d = norm_back(
        mlp_operands, mlp_last, hidden, cotangent, gains[1:], (f32, bf16)
    )
    neighbours = plane_neighbours(own_d)
    late_both = after(both_1, own_d)
    grads_1 = weight_grads((normed_mlp, late_both), (cot_all, inner_1))
    sum_1 = line_sum(after(grads_1, *neighbours))
    d_far = plane_far(neighbours, grads_1)
    d_attn_all = pack(with_partner([own_d, *neighbours, *d_far]))
    out_parts = [[part[0], after(part[1], *d_far)] for part in out_parts]
    out_sums = chip_sums(*out_parts)

    def send_grads(sources, *waits):
        first = after(sources[0], *waits) if waits else sources[0]
        return swap_all(pick_rows(member_at, first, *sources[1:]))


    final_0 = send_grads([sum_0], *d_far)
    d_mixed = product(d_attn_all, attn_weights[:, 3 * HS :]).astype(bf16)
    d_qkv = attention_backward(order, query, keys, vals, logsum, d_mixed, cos, sin)
    pair_grads = weight_grads((normed_all, (d_qkv, 2 * HS, 0)))
    half_shape = jax.ShapeDtypeStruct((features // 2, 2 * HS), bf16)
    keep, send = vmem_call(
        functools.partial(halves_kernel, own_rows),
        "halves",
        [half_shape] * 2,
        member_at,
        pair_grads,
    )
    got = swap(send, "col")
    both_grads = weight_grads(
        (normed_all, (after(d_qkv, keep, *final_0[1:]), HS, 2)), (d_attn_all, mixed)
    )
    late_qkv = after(d_qkv, both_grads)
    qkv_parts = projected(late_qkv, 0)
    (attn_grads,) = vmem_call(
        functools.partial(join_kernel, own_rows),
        "join",
        [jax.ShapeDtypeStruct((features, 3 * HS), bf16)],
        member_at,
        after(keep, *qkv_parts[0], *qkv_parts[1]),
        got,
        both_grads,
    )
    attn_sum = line_sum(attn_grads)
    qkv_sums = chip_sums(*qkv_parts)
    arrived = reduce_first(first_operands(qkv_sums))
    qkv_operands = reduce_operands(qkv_sums, arrived)
    qkv_last = last_swaps(qkv_operands)
    out_operands = reduce_operands(out_sums, reduce_first(first_operands(out_sums), *arrived))
    out_last = last_swaps(out_operands, *qkv_last)
    (tokens_grad,) = norm_back(qkv_operands, qkv_last, tokens, d_hidden, gains[:1], (f32,))
    block_out = (hidden + reduce_last(out_operands, out_last)).astype(bf16)

    final_1 = send_grads([sum_1], *arrived)
    gate_grad, up_grad, down_grad, mlp_gain_row = mlp_final(
        member_at, gate_weight, up_weight, (chunks[:1], chunks[1:]), [final_0, final_1]
    )
    query_grad, key_grad, value_grad, output_grad, attn_gain_row = attention_final(
        member_at,
        query_weight,
        key_weight,
        value_weight,
        attention_return(member_at, after(attn_sum, tokens_grad, mlp_gain_row)),
    )
    gain_grads = jnp.concatenate([attn_gain_row, mlp_gain_row], axis=1)
    gain_grads = gain_grads + swap(gain_grads, "tp")
    attn_gain_grad = gain_grads[:, 0] / attn_gain.astype(f32)
    mlp_gain_grad = gain_grads[:, 1] / mlp_gain.astype(f32)

    factor = clip_limit / jnp.maximum(head_top, clip_limit)
    query_scale = jnp.repeat(jnp.sqrt(factor), HS)
    key_factor = jnp.min(factor.reshape(2, 2), axis=1)
    key_scale = jnp.repeat(jnp.sqrt(key_factor), HS)
    query_clipped = (query_weight.astype(f32) * query_scale[None, :]).astype(bf16)
    key_clipped = (key_weight.astype(f32) * key_scale[None, :]).astype(bf16)
    return (
        block_out,
        tokens_grad,
        attn_gain_grad,
        query_grad,
        key_grad,
        value_grad,
        output_grad,
        mlp_gain_grad,
        gate_grad,
        up_grad,
        down_grad,
        head_top,
        query_clipped,
        key_clipped,
    )


def solution(mesh):
    shape = (mesh.shape["fsdp"] // 4, 2, 2, mesh.shape["tp"])
    fine = Mesh(mesh.devices.reshape(shape), ("group", "row", "col", "tp"))
    rows = P(("group", "row", "col", "tp"), None)
    weight = P(FSDP, "tp")
    gain = P(FSDP)
    heads = P("tp")
    return jax.shard_map(
        local,
        mesh=fine,
        in_specs=(
            rows, rows, P(), P(), heads, gain, weight, weight, weight, weight,
            gain, weight, weight, weight,
        ),
        out_specs=(
            rows, rows, gain, weight, weight, weight, weight, gain, weight, weight, weight,
            heads, weight, weight,
        ),
        check_vma=False,
    )
```

```python
import functools

import jax
import jax.numpy as jnp
from jax import lax
from jax.experimental import pallas as pl
from jax.experimental.pallas import tpu as pltpu
from jax.sharding import Mesh, PartitionSpec as P

HS = 256
GROUP = 2048
SIXTEENTHS = (10, 6)
BLOCK = 128

epsilon = 1e-05
theta_base = 1000042.0
masked_value = -1e30

bf16 = jnp.bfloat16
f32 = jnp.float32
PLANE = ("row", "col")
FSDP = ("group", "row", "col")
VMEM_LIMIT = 48 * 1024 * 1024


def product(left, right):
    return jnp.dot(left, right, preferred_element_type=f32)


def times_transposed(left, right):
    return lax.dot_general(left, right, (((1,), (1,)), ((), ())), preferred_element_type=f32)


def outer_sum(left, right):
    return lax.dot_general(left, right, (((0,), (0,)), ((), ())), preferred_element_type=f32)


def take(array, index, axis=0):
    return lax.dynamic_index_in_dim(array, index, axis, keepdims=False)


def swap(block, axis):
    return lax.ppermute(block, axis, [(0, 1), (1, 0)])


def swap_plane(block, distance):
    return lax.ppermute(block, PLANE, [(i, i ^ distance) for i in range(4)])


def after(value, *others):
    return lax.optimization_barrier((value,) + others)[0]


def combine_all(values, groups, combine):
    distance, count = 1, 4 * groups
    rounds = []
    while distance < count:
        arrived = []
        for step in range(1, min(4, count // distance)):
            route = [(i, i ^ step * distance) for i in range(count)]
            arrived.append(lax.ppermute(values, FSDP, route))
        for other in arrived:
            values = combine(values, other)
        rounds.append(arrived)
        distance *= 4
    return values, rounds


def pack_kernel(count, *refs):
    out_ref, sems = refs[count], refs[count + 1]
    copies, start = [], 0
    for i in range(count):
        rows = refs[i].shape[0]
        copy = pltpu.make_async_copy(refs[i], out_ref.at[pl.ds(start, rows)], sems.at[i])
        copy.start()
        copies.append(copy)
        start += rows
    for copy in copies:
        copy.wait()


def pack(pieces):
    rows, width = sum(p.shape[0] for p in pieces), pieces[0].shape[1]
    count = len(pieces)
    return pl.pallas_call(
        functools.partial(pack_kernel, count),
        in_specs=[pl.BlockSpec(memory_space=pl.ANY)] * count,
        out_specs=pl.BlockSpec(memory_space=pltpu.VMEM),
        out_shape=jax.ShapeDtypeStruct((rows, width), pieces[0].dtype),
        scratch_shapes=[pltpu.SemaphoreType.DMA((count,))],
        cost_estimate=pl.CostEstimate(
            flops=0, bytes_accessed=4 * rows * width, transcendentals=0
        ),
        compiler_params=pltpu.CompilerParams(vmem_limit_bytes=VMEM_LIMIT),
        name="pack",
    )(*pieces)


def norm_kernel(count, *refs):
    gain_ref, out_ref = refs[count], refs[-2]
    pack_kernel(count, *refs[:count], *refs[-2:])
    tile = 256

    @pl.loop(0, out_ref.shape[0] // tile)
    def _(i):
        rows = pl.ds(pl.multiple_of(i * tile, tile), tile)
        values = out_ref[rows, :].astype(f32)
        out_ref[rows, :] = (values * rms_inverse(values) * gain_ref[...]).astype(bf16)


def pack_normed(pieces, gain, early):
    rows, width = sum(p.shape[0] for p in pieces), pieces[0].shape[1]
    count = len(pieces)
    return pl.pallas_call(
        functools.partial(norm_kernel, count),
        in_specs=[pl.BlockSpec(memory_space=pl.ANY)] * count
        + [pl.BlockSpec(memory_space=pltpu.VMEM)]
        + [pl.BlockSpec(memory_space=pl.ANY)] * len(early),
        out_specs=pl.BlockSpec(memory_space=pltpu.VMEM),
        out_shape=jax.ShapeDtypeStruct((rows, width), bf16),
        scratch_shapes=[pltpu.SemaphoreType.DMA((count,))],
        cost_estimate=pl.CostEstimate(
            flops=8 * rows * width, bytes_accessed=4 * rows * width, transcendentals=0
        ),
        compiler_params=pltpu.CompilerParams(vmem_limit_bytes=VMEM_LIMIT),
        name="pack_normed",
    )(*pieces, gain, *early)


def plane_neighbours(own):
    return swap(own, "col"), swap(own, "row")


def plane_far(neighbours, *waits):
    across, along = neighbours
    half = across.shape[0] // 2
    return (
        swap(after(across[:half], *waits), "row"),
        swap(after(along[half:], *waits), "col"),
    )


def with_partner(pieces, swapped=()):
    return pieces + list(swapped) + [swap(piece, "tp") for piece in pieces[len(swapped) :]]


def chip_sums(front, back):
    pairs = []
    for own, other in (front, back):
        shape = (4, own.shape[0] // 4, own.shape[1])
        pairs.append((own.reshape(shape), swap(other, "tp").reshape(shape)))
    return pairs


def quarter(pair, k):
    return pair[0][k].astype(f32) + pair[1][k].astype(f32)


def first_operands(sums):
    front, back = sums
    return (
        jnp.concatenate([quarter(front, 1), quarter(front, 3)]).astype(bf16),
        (back[0][2:].astype(f32) + back[1][2:].astype(f32)).astype(bf16),
    )


def reduce_first(operands, *waits):
    front, back = operands
    rows = front.shape[0] // 2
    return (
        swap(after(front, *waits), "col").reshape(2, rows, -1),
        swap(after(back, *waits), "row"),
    )


def reduce_operands(sums, arrived):
    front, back = sums
    got, got_back = arrived[0].astype(f32), arrived[1].astype(f32)
    return (
        (quarter(front, 0) + got[0], (quarter(front, 2) + got[1]).astype(bf16)),
        (quarter(back, 0) + got_back[0], (quarter(back, 1) + got_back[1]).astype(bf16)),
    )


def last_swaps(operands, *waits):
    return (
        swap(after(operands[0][1], *waits), "row"),
        swap(after(operands[1][1], *waits), "col"),
    )


def reduce_last(operands, swapped):
    return jnp.concatenate(
        [keep + last.astype(f32) for (keep, _), last in zip(operands, swapped)], axis=1
    )


def joined(front_ref, front_last_ref, back_ref, back_last_ref):
    return jnp.concatenate(
        [
            front_ref[...] + front_last_ref[...].astype(f32),
            back_ref[...] + back_last_ref[...].astype(f32),
        ],
        axis=1,
    )


def hidden_kernel(front, front_last, back, back_last, tokens_ref, gain_ref, hidden_ref, normed_ref):
    hidden = tokens_ref[...].astype(f32) + joined(front, front_last, back, back_last)
    hidden_ref[...] = hidden
    normed_ref[...] = (hidden * rms_inverse(hidden) * gain_ref[...]).astype(bf16)


def add_and_norm(operands, last, tokens, gain):
    halves = [part for (keep, _), got in zip(operands, last) for part in (keep, got)]
    return pl.pallas_call(
        hidden_kernel,
        in_specs=[pl.BlockSpec(memory_space=pltpu.VMEM)] * 6,
        out_specs=[pl.BlockSpec(memory_space=pltpu.VMEM)] * 2,
        out_shape=[
            jax.ShapeDtypeStruct(tokens.shape, f32),
            jax.ShapeDtypeStruct(tokens.shape, bf16),
        ],
        cost_estimate=pl.CostEstimate(
            flops=10 * tokens.size, bytes_accessed=14 * tokens.size, transcendentals=0
        ),
        compiler_params=pltpu.CompilerParams(vmem_limit_bytes=VMEM_LIMIT),
        name="add_and_norm",
    )(*halves, tokens, gain)


def back_kernel(front, front_last, back, back_last, values_ref, base_ref, gain_ref, *outs):
    values = values_ref[...].astype(f32)
    inverse = rms_inverse(values)
    unit = values * inverse
    scaled = joined(front, front_last, back, back_last) * gain_ref[...]
    grad = base_ref[...].astype(f32) + inverse * (
        scaled - unit * jnp.mean(scaled * unit, axis=-1, keepdims=True)
    )
    for out in outs:
        out[...] = grad.astype(out.dtype)


def norm_back(operands, last, values, base, gain, dtypes):
    halves = [part for (keep, _), got in zip(operands, last) for part in (keep, got)]
    return pl.pallas_call(
        back_kernel,
        in_specs=[pl.BlockSpec(memory_space=pltpu.VMEM)] * 7,
        out_specs=[pl.BlockSpec(memory_space=pltpu.VMEM)] * len(dtypes),
        out_shape=[jax.ShapeDtypeStruct(values.shape, dtype) for dtype in dtypes],
        cost_estimate=pl.CostEstimate(
            flops=16 * values.size, bytes_accessed=18 * values.size, transcendentals=0
        ),
        compiler_params=pltpu.CompilerParams(vmem_limit_bytes=VMEM_LIMIT),
        name="norm_back",
    )(*halves, values, base, gain)


def split_kernel(spans, member_ref, *refs):
    sources, outs = refs[: len(spans)], refs[len(spans) :]
    for k in range(4):
        target = member_ref[0] ^ k
        column = 0
        for source, (offset, stride, width, shift) in zip(sources, spans):
            start = pl.multiple_of((target >> shift) * stride + offset, 128)
            outs[k][:, column : column + width] = source[:, pl.ds(start, width)]
            column += width


def split(member, sources, spans):
    rows, width = sources[0].shape[0], sum(span[2] for span in spans)
    whole = pl.BlockSpec(memory_space=pltpu.VMEM)
    return pl.pallas_call(
        functools.partial(split_kernel, spans),
        in_specs=[pl.BlockSpec(memory_space=pltpu.SMEM)] + [whole] * len(sources),
        out_specs=[whole] * 4,
        out_shape=[jax.ShapeDtypeStruct((rows, width), bf16)] * 4,
        cost_estimate=pl.CostEstimate(
            flops=0, bytes_accessed=16 * rows * width, transcendentals=0
        ),
        compiler_params=pltpu.CompilerParams(vmem_limit_bytes=VMEM_LIMIT),
        name="split",
    )(member, *sources)


def place_kernel(member_ref, *refs):
    rows = refs[0].shape[0]
    for k in range(4):
        start = pl.multiple_of((member_ref[0] ^ k) * rows, rows)
        column = 0
        for out_ref in refs[4:]:
            width = out_ref.shape[1]
            out_ref[pl.ds(start, rows), :] = refs[k][:, column : column + width]
            column += width


def place_rows(member, pieces, *widths):
    rows, width = pieces[0].shape
    whole = pl.BlockSpec(memory_space=pltpu.VMEM)
    return pl.pallas_call(
        place_kernel,
        in_specs=[pl.BlockSpec(memory_space=pltpu.SMEM)] + [whole] * 4,
        out_specs=[whole] * len(widths or (width,)),
        out_shape=[
            jax.ShapeDtypeStruct((4 * rows, w), bf16) for w in widths or (width,)
        ],
        cost_estimate=pl.CostEstimate(
            flops=0, bytes_accessed=16 * rows * width, transcendentals=0
        ),
        compiler_params=pltpu.CompilerParams(vmem_limit_bytes=VMEM_LIMIT),
        name="place_rows",
    )(member, *pieces)


def pick_kernel(member_ref, *refs):
    sources, outs = refs[:-4], refs[-4:]
    rows = outs[0].shape[0]
    for k in range(4):
        start = pl.multiple_of((member_ref[0] ^ k) * rows, rows)
        column = 0
        for source in sources:
            width = source.shape[1]
            outs[k][:, column : column + width] = source[pl.ds(start, rows), :]
            column += width


def pick_rows(member, *sources):
    rows, width = sources[0].shape[0] // 4, sum(source.shape[1] for source in sources)
    whole = pl.BlockSpec(memory_space=pltpu.VMEM)
    return pl.pallas_call(
        pick_kernel,
        in_specs=[pl.BlockSpec(memory_space=pltpu.SMEM)] + [whole] * len(sources),
        out_specs=[whole] * 4,
        out_shape=[jax.ShapeDtypeStruct((rows, width), bf16)] * 4,
        cost_estimate=pl.CostEstimate(
            flops=0, bytes_accessed=16 * rows * width, transcendentals=0
        ),
        compiler_params=pltpu.CompilerParams(vmem_limit_bytes=VMEM_LIMIT),
        name="pick_rows",
    )(member, *sources)


def swap_all(pieces):
    return [pieces[0]] + [swap_plane(pieces[k], k) for k in (1, 2, 3)]


def mlp_final_kernel(parts, stride, member_ref, gate_w_ref, up_w_ref, *refs):
    pieces, outs, gain_ref = refs[:-4], refs[-4:-1], refs[-1]
    for n, chunks in enumerate(parts):
        for k in range(4):
            start = 0
            for offset, width in chunks:
                column = pl.multiple_of((member_ref[0] ^ k) * stride + offset, 128)
                for i in range(3):
                    part = pieces[4 * n + k][:, start : start + width]
                    outs[i][:, pl.ds(column, width)] = part.astype(f32)
                    start += width
    gain_ref[...] = jnp.sum(
        gate_w_ref[...].astype(f32) * outs[0][...] + up_w_ref[...].astype(f32) * outs[1][...],
        axis=1,
        keepdims=True,
    )


def mlp_final(member, gate_weight, up_weight, chunks, parts):
    rows, hidden = gate_weight.shape
    pieces = [piece for part in parts for piece in part]
    whole = pl.BlockSpec(memory_space=pltpu.VMEM)
    return pl.pallas_call(
        functools.partial(mlp_final_kernel, chunks, hidden // 4),
        in_specs=[pl.BlockSpec(memory_space=pltpu.SMEM)] + [whole] * (2 + len(pieces)),
        out_specs=[whole] * 4,
        out_shape=[jax.ShapeDtypeStruct((rows, hidden), f32)] * 3
        + [jax.ShapeDtypeStruct((rows, 1), f32)],
        cost_estimate=pl.CostEstimate(
            flops=4 * rows * hidden, bytes_accessed=22 * rows * hidden, transcendentals=0
        ),
        compiler_params=pltpu.CompilerParams(vmem_limit_bytes=VMEM_LIMIT),
        name="mlp_final",
    )(member, gate_weight, up_weight, *pieces)


TURN = [(0, 0), (1, 2), (2, 1), (3, 3)]
CROSS = [(0, 2), (1, 0), (2, 3), (3, 1)]
CROSS_BACK = [(2, 0), (0, 1), (3, 2), (1, 3)]


def vmem_call(kernel, name, out_shape, *operands):
    whole = pl.BlockSpec(memory_space=pltpu.VMEM)
    moved = sum(a.size * a.dtype.itemsize for a in operands)
    moved += sum(a.size * a.dtype.itemsize for a in out_shape)
    return pl.pallas_call(
        kernel,
        in_specs=[pl.BlockSpec(memory_space=pltpu.SMEM)] + [whole] * (len(operands) - 1),
        out_specs=[whole] * len(out_shape),
        out_shape=out_shape,
        cost_estimate=pl.CostEstimate(flops=0, bytes_accessed=moved, transcendentals=0),
        compiler_params=pltpu.CompilerParams(vmem_limit_bytes=VMEM_LIMIT),
        name=name,
    )(*operands)


def head_columns(index):
    return pl.ds(pl.multiple_of(index * HS, HS), HS)


def halves_kernel(rows, member_ref, grads_ref, keep_ref, send_ref):
    half = (member_ref[0] & 1) * 2 * rows
    for i, base in enumerate(range(0, grads_ref.shape[0], 4 * rows)):
        part = slice(i * 2 * rows, (i + 1) * 2 * rows)
        mine = pl.ds(pl.multiple_of(base + half, 2 * rows), 2 * rows)
        other = pl.ds(pl.multiple_of(base + 2 * rows - half, 2 * rows), 2 * rows)
        keep_ref[part, :] = grads_ref[mine, :]
        send_ref[part, :] = grads_ref[other, :]


def join_kernel(rows, member_ref, keep_ref, got_ref, both_ref, out_ref):
    out_ref[:, : 2 * HS] = both_ref[...]
    for i, base in enumerate(range(0, out_ref.shape[0], 4 * rows)):
        part = slice(i * 2 * rows, (i + 1) * 2 * rows)
        total = (keep_ref[part, :].astype(f32) + got_ref[part, :].astype(f32)).astype(bf16)
        out_ref[base : base + 2 * rows, 2 * HS :] = total[:, :HS]
        out_ref[base + 2 * rows : base + 4 * rows, 2 * HS :] = total[:, HS:]


def attention_pick_kernel(member_ref, source_ref, *outs):
    member, rows = member_ref[0], outs[0].shape[0]
    for k in range(4):
        at = pl.ds(pl.multiple_of((member ^ k) * rows, rows), rows)
        outs[k][...] = source_ref[at, : 2 * HS]
    for h in range(2):
        start = ((member >> 1) ^ h) * rows
        at = pl.ds(pl.multiple_of(start, rows), rows)
        outs[4 + h][:, :HS] = source_ref[at, 2 * HS :]
        at = pl.ds(pl.multiple_of(start + 2 * rows, rows), rows)
        outs[4 + h][:, HS:] = source_ref[at, 2 * HS :]


def attention_return(member, reduced):
    rows = reduced.shape[0] // 4
    *both, turned, crossed = vmem_call(
        attention_pick_kernel,
        "attention_pick",
        [jax.ShapeDtypeStruct((rows, 2 * HS), bf16)] * 6,
        member,
        reduced,
    )
    return swap_all(both) + [
        lax.ppermute(turned, PLANE, TURN),
        lax.ppermute(crossed, PLANE, CROSS_BACK),
    ]


def attention_final_kernel(member_ref, qw_ref, kw_ref, vw_ref, *refs):
    pieces = refs[:6]
    q_ref, k_ref, v_ref, o_ref, gain_ref = refs[6:]
    member = member_ref[0]
    for k in range(4):
        columns = head_columns(member ^ k)
        q_ref[:, columns] = pieces[k][:, :HS].astype(f32)
        o_ref[:, columns] = pieces[k][:, HS:].astype(f32)
    for h in range(2):
        columns = head_columns((member & 1) ^ h)
        k_ref[:, columns] = pieces[4 + h][:, :HS].astype(f32)
        v_ref[:, columns] = pieces[4 + h][:, HS:].astype(f32)

    def row_sum(weight_ref, grad_ref):
        return jnp.sum(weight_ref[...].astype(f32) * grad_ref[...], axis=1, keepdims=True)

    gain_ref[...] = row_sum(qw_ref, q_ref) + row_sum(kw_ref, k_ref) + row_sum(vw_ref, v_ref)


def attention_final(member, query_weight, key_weight, value_weight, pieces):
    rows, width = query_weight.shape
    shapes = [jax.ShapeDtypeStruct((rows, n), f32) for n in (width, width // 2, width // 2, width, 1)]
    return vmem_call(
        attention_final_kernel,
        "attention_final",
        shapes,
        member,
        query_weight,
        key_weight,
        value_weight,
        *pieces,
    )


def rms_inverse(values):
    return lax.rsqrt(jnp.mean(values * values, axis=-1, keepdims=True) + epsilon)


def rope_tables(positions):
    half_size = HS // 2
    indices = jnp.arange(half_size, dtype=f32)
    inverse = theta_base ** (-2.0 * indices / HS)
    angles = positions.astype(f32)[:, None] * inverse[None, :]
    return jnp.cos(angles), jnp.sin(angles)


def rotate(vectors, cos, sin):
    front, back = vectors[:, : HS // 2], vectors[:, HS // 2 :]
    return jnp.concatenate([front * cos - back * sin, back * cos + front * sin], axis=-1)


def unrotate(grads, cos, sin):
    front, back = grads[:, : HS // 2], grads[:, HS // 2 :]
    return jnp.concatenate([front * cos + back * sin, back * cos - front * sin], axis=-1)


def mlp_tile(width, normed, cot, weight_ref):
    both = product(normed, weight_ref[:, : 2 * width])
    d_inner = product(cot, weight_ref[:, 2 * width :])
    gate, upward = both[:, :width], both[:, width:]
    sig = 1.0 / (1.0 + jnp.exp(-gate))
    silu = gate * sig
    d_gate = d_inner * upward * sig * (1.0 + gate * (1.0 - sig))
    return (
        (silu * upward).astype(bf16),
        jnp.concatenate([d_gate, d_inner * silu], axis=1).astype(bf16),
    )


def mlp_kernel(width, normed_ref, cot_ref, weight_ref, inner_ref, grads_ref):
    inner_ref[...], grads_ref[...] = mlp_tile(
        width, normed_ref[...], cot_ref[...], weight_ref
    )


def tail_kernel(width, normed_ref, cot_ref, weight_ref, base_ref, *refs):
    inner_ref, grads_ref, front_ref, back_ref = refs[-4:]
    inner, grads = mlp_tile(width, normed_ref[...], cot_ref[...], weight_ref)
    inner_ref[...], grads_ref[...] = inner, grads
    total = times_transposed(grads, weight_ref[:, : 2 * width]) + base_ref[...]
    half = total.shape[1] // 2
    front_ref[...] = total[:, :half].astype(front_ref.dtype)
    back_ref[...] = total[:, half:].astype(back_ref.dtype)


def mlp_tail(normed, cot, weight, base, part, dtype, chained=()):
    tokens, features = normed.shape
    width = weight.shape[1] // 3
    tile, rows = 256, tokens // 2
    steps = rows // tile
    count = len(chained)
    return pl.pallas_call(
        functools.partial(tail_kernel, width),
        grid=(steps,),
        in_specs=[
            pl.BlockSpec((tile, features), lambda i: (part * steps + i, 0)),
            pl.BlockSpec((tile, features), lambda i: (part * steps + i, 0)),
            pl.BlockSpec((features, 3 * width), lambda i: (0, 0)),
            pl.BlockSpec((tile, features), lambda i: (i, 0)),
        ]
        + [pl.BlockSpec(memory_space=pl.ANY)] * count,
        out_specs=[
            pl.BlockSpec((tile, width), lambda i: (part * steps + i, 0)),
            pl.BlockSpec((tile, 2 * width), lambda i: (part * steps + i, 0)),
            pl.BlockSpec((tile, features // 2), lambda i: (i, 0)),
            pl.BlockSpec((tile, features // 2), lambda i: (i, 0)),
        ],
        out_shape=[
            jax.ShapeDtypeStruct((tokens, width), bf16),
            jax.ShapeDtypeStruct((tokens, 2 * width), bf16),
            jax.ShapeDtypeStruct((rows, features // 2), dtype),
            jax.ShapeDtypeStruct((rows, features // 2), dtype),
        ],
        input_output_aliases={4 + i: i for i in range(count)},
        cost_estimate=pl.CostEstimate(
            flops=10 * rows * features * width,
            bytes_accessed=2 * features * (5 * rows + 3 * width),
            transcendentals=rows * width,
        ),
        compiler_params=pltpu.CompilerParams(vmem_limit_bytes=VMEM_LIMIT),
        name="mlp_tail",
    )(normed, cot, weight, base, *chained)


def mlp_chunk(normed, cot, weight):
    tokens, features = normed.shape
    width = weight.shape[1] // 3
    tile = 256
    return pl.pallas_call(
        functools.partial(mlp_kernel, width),
        grid=(tokens // tile,),
        in_specs=[
            pl.BlockSpec((tile, features), lambda i: (i, 0)),
            pl.BlockSpec((tile, features), lambda i: (i, 0)),
            pl.BlockSpec((features, 3 * width), lambda i: (0, 0)),
        ],
        out_specs=[
            pl.BlockSpec((tile, width), lambda i: (i, 0)),
            pl.BlockSpec((tile, 2 * width), lambda i: (i, 0)),
        ],
        out_shape=[
            jax.ShapeDtypeStruct((tokens, width), bf16),
            jax.ShapeDtypeStruct((tokens, 2 * width), bf16),
        ],
        cost_estimate=pl.CostEstimate(
            flops=6 * tokens * features * width,
            bytes_accessed=2 * features * (2 * tokens + 3 * width),
            transcendentals=tokens * width,
        ),
        compiler_params=pltpu.CompilerParams(vmem_limit_bytes=VMEM_LIMIT),
        name="mlp_chunk",
    )(normed, cot, weight)


def sum_kernel(count, *refs):
    lefts, rights, out_ref = refs[:count], refs[count : 2 * count], refs[-1]
    total = times_transposed(lefts[0][...], rights[0][...])
    for left, right in zip(lefts[1:], rights[1:]):
        total += times_transposed(left[...], right[...])
    for base in refs[2 * count : -1]:
        total += base[...].astype(f32)
    out_ref[...] = total.astype(out_ref.dtype)


def chunk_sum(lefts, rights, column, part, half, dtype):
    count = len(lefts)
    tokens, features = lefts[0].shape[0], rights[0].shape[0]
    widths = [left.shape[1] for left in lefts]
    rows = tokens // 2
    tile = 256
    if half is not None:
        features, tile = features // 2, 512
    steps = rows // tile
    block = half or 0
    return pl.pallas_call(
        functools.partial(sum_kernel, count),
        grid=(steps,),
        in_specs=[pl.BlockSpec((tile, w), lambda i: (part * steps + i, 0)) for w in widths]
        + [pl.BlockSpec((features, w), lambda i: (block, column)) for w in widths],
        out_specs=pl.BlockSpec((tile, features), lambda i: (i, 0)),
        out_shape=jax.ShapeDtypeStruct((rows, features), dtype),
        cost_estimate=pl.CostEstimate(
            flops=2 * rows * features * sum(widths),
            bytes_accessed=2 * sum(widths) * (rows + features) + 4 * rows * features,
            transcendentals=0,
        ),
        compiler_params=pltpu.CompilerParams(vmem_limit_bytes=VMEM_LIMIT),
        name="chunk_sum",
    )(*lefts, *rights)


def grads_kernel(count, *refs):
    column = 0
    for left, right in zip(refs[:count], refs[count : 2 * count]):
        width = right.shape[1]
        refs[-1][:, column : column + width] = outer_sum(left[...], right[...]).astype(bf16)
        column += width


def weight_grads(*pairs):
    lefts = [left for left, _ in pairs]
    rights = [r if isinstance(r, tuple) else (r, r.shape[1], 0) for _, r in pairs]
    count = len(pairs)
    tokens, features = lefts[0].shape
    widths = [width for _, width, _ in rights]
    tile = 256

    def block(width, at):
        return pl.BlockSpec((tokens, width), lambda i: (0, at))

    return pl.pallas_call(
        functools.partial(grads_kernel, count),
        grid=(features // tile,),
        in_specs=[pl.BlockSpec((tokens, tile), lambda i: (0, i))] * count
        + [block(width, at) for _, width, at in rights],
        out_specs=pl.BlockSpec((tile, sum(widths)), lambda i: (i, 0)),
        out_shape=jax.ShapeDtypeStruct((features, sum(widths)), bf16),
        cost_estimate=pl.CostEstimate(
            flops=2 * tokens * features * sum(widths),
            bytes_accessed=2 * (count * tokens * features + sum(widths) * (tokens + features)),
            transcendentals=0,
        ),
        compiler_params=pltpu.CompilerParams(vmem_limit_bytes=VMEM_LIMIT),
        name="weight_grads",
    )(*lefts, *[array for array, _, _ in rights])


def project_kernel(place_ref, normed_ref, weight_ref, cos_ref, sin_ref, q_ref, k_ref, v_ref):
    step = pl.program_id(0)
    cos, sin = cos_ref[...], sin_ref[...]
    qkv = product(normed_ref[...], weight_ref[...])
    keys = rotate(qkv[:, :HS], cos, sin).astype(bf16)
    vals = qkv[:, HS : 2 * HS].astype(bf16)
    query = rotate(qkv[:, 2 * HS :], cos, sin).astype(bf16) * HS ** (-0.5)
    blocks = normed_ref.shape[0] // BLOCK
    for b in range(blocks):
        rows = pl.ds(pl.multiple_of(place_ref[step * blocks + b] * BLOCK, BLOCK), BLOCK)
        part = slice(b * BLOCK, (b + 1) * BLOCK)
        q_ref[rows, :] = query[part]
        k_ref[rows, :] = keys[part]
        v_ref[rows, :] = vals[part]


def project(place, normed, weight, cos, sin):
    tokens, features = normed.shape
    tile = 256
    whole = pl.BlockSpec((tokens, HS), lambda i, place: (0, 0))
    return pl.pallas_call(
        project_kernel,
        grid_spec=pltpu.PrefetchScalarGridSpec(
            num_scalar_prefetch=1,
            grid=(tokens // tile,),
            in_specs=[
                pl.BlockSpec((tile, features), lambda i, place: (i, 0)),
                pl.BlockSpec((features, 3 * HS), lambda i, place: (0, 0)),
                pl.BlockSpec((tile, HS // 2), lambda i, place: (i, 0)),
                pl.BlockSpec((tile, HS // 2), lambda i, place: (i, 0)),
            ],
            out_specs=[whole] * 3,
        ),
        out_shape=[jax.ShapeDtypeStruct((tokens, HS), bf16)] * 3,
        cost_estimate=pl.CostEstimate(
            flops=6 * tokens * features * HS,
            bytes_accessed=2 * features * (tokens + 3 * HS) + 10 * tokens * HS,
            transcendentals=0,
        ),
        compiler_params=pltpu.CompilerParams(vmem_limit_bytes=VMEM_LIMIT),
        name="project",
    )(place, normed, weight, cos, sin)


TILE = 256


def tile_masks():
    rows = lax.broadcasted_iota(jnp.int32, (TILE, TILE), 0)
    cols = lax.broadcasted_iota(jnp.int32, (TILE, TILE), 1)
    causal = rows >= cols
    return causal, causal & (rows // BLOCK == cols // BLOCK)


def block_rows(order_ref, index):
    return pl.ds(pl.multiple_of(order_ref[index] * BLOCK, BLOCK), BLOCK)


def forward_kernel(order_ref, q_ref, k_ref, v_ref, mixed_ref, lse_ref, peak_ref):
    causal, inside = tile_masks()
    prompt = GROUP // 2
    top = jnp.full((TILE, 1), masked_value, f32)
    for i in range(GROUP // TILE):
        rows = slice(i * TILE, (i + 1) * TILE)
        past = min(i * TILE, prompt)
        query = q_ref[rows, :]
        near = times_transposed(query, k_ref[rows, :])
        near = jnp.where(causal if i * TILE < prompt else inside, near, masked_value)
        peak = jnp.max(near, axis=1, keepdims=True)
        if past:
            far = times_transposed(query, k_ref[:past, :])
            peak = jnp.maximum(peak, jnp.max(far, axis=1, keepdims=True))
            far = jnp.exp(far - peak)
        near = jnp.exp(near - peak)
        total = jnp.sum(near, axis=1, keepdims=True)
        if past:
            total += jnp.sum(far, axis=1, keepdims=True)
        share = 1.0 / total
        mixed = product((near * share).astype(bf16), v_ref[rows, :])
        if past:
            mixed += product((far * share).astype(bf16), v_ref[:past, :])
        mixed = mixed.astype(bf16)
        for b in range(TILE // BLOCK):
            mixed_ref[block_rows(order_ref, i * (TILE // BLOCK) + b), :] = mixed[
                b * BLOCK : (b + 1) * BLOCK
            ]
        lse_ref[rows, :] = peak + jnp.log(total)
        top = jnp.maximum(top, peak)
    peak_ref[...] = jnp.full(peak_ref.shape, jnp.max(top), f32)


def attention_forward(order, query, keys, vals):
    whole = pl.BlockSpec(memory_space=pltpu.VMEM)
    return pl.pallas_call(
        forward_kernel,
        in_specs=[pl.BlockSpec(memory_space=pltpu.SMEM), whole, whole, whole],
        out_specs=[whole] * 3,
        out_shape=[
            jax.ShapeDtypeStruct((GROUP, HS), bf16),
            jax.ShapeDtypeStruct((GROUP, 1), f32),
            jax.ShapeDtypeStruct((8, 128), f32),
        ],
        cost_estimate=pl.CostEstimate(
            flops=2 * GROUP * GROUP * HS,
            bytes_accessed=8 * GROUP * HS,
            transcendentals=GROUP * GROUP // 2,
        ),
        compiler_params=pltpu.CompilerParams(vmem_limit_bytes=VMEM_LIMIT),
        name="attention_forward",
    )(order, query, keys, vals)


def backward_kernel(
    order_ref, q_ref, k_ref, v_ref, lse_ref, mixed_ref, cos_ref, sin_ref, out_ref, dk_ref, dv_ref
):
    causal, inside = tile_masks()
    prompt = GROUP // 2
    blocks = TILE // BLOCK

    def back(grad, index):
        rows = block_rows(order_ref, index)
        return rows, unrotate(grad, cos_ref[rows, :], sin_ref[rows, :]).astype(bf16)

    for i in range(GROUP // TILE):
        rows = slice(i * TILE, (i + 1) * TILE)
        past = min(i * TILE, prompt)
        query, lse = q_ref[rows, :], lse_ref[rows, :]
        d_mixed = jnp.concatenate(
            [mixed_ref[block_rows(order_ref, i * blocks + b), :] for b in range(blocks)], axis=0
        )
        near = times_transposed(query, k_ref[rows, :])
        near = jnp.where(causal if i * TILE < prompt else inside, near, masked_value)
        near = jnp.exp(near - lse)
        d_near = times_transposed(d_mixed, v_ref[rows, :])
        inner = jnp.sum(near * d_near, axis=1, keepdims=True)
        if past:
            far = jnp.exp(times_transposed(query, k_ref[:past, :]) - lse)
            d_far = times_transposed(d_mixed, v_ref[:past, :])
            inner += jnp.sum(far * d_far, axis=1, keepdims=True)
        d_near = (near * (d_near - inner)).astype(bf16)
        d_query = product(d_near, k_ref[rows, :])
        dk_ref[rows, :] = outer_sum(d_near, query)
        dv_ref[rows, :] = outer_sum(near.astype(bf16), d_mixed)
        if past:
            d_far = (far * (d_far - inner)).astype(bf16)
            d_query += product(d_far, k_ref[:past, :])
            dk_ref[:past, :] += outer_sum(d_far, query)
            dv_ref[:past, :] += outer_sum(far.astype(bf16), d_mixed)
        d_query = d_query * HS ** (-0.5)
        for b in range(blocks):
            where, grad = back(d_query[b * BLOCK : (b + 1) * BLOCK], i * blocks + b)
            out_ref[where, 2 * HS :] = grad
    for c in range(GROUP // BLOCK):
        part = slice(c * BLOCK, (c + 1) * BLOCK)
        where, grad = back(dk_ref[part, :], c)
        out_ref[where, :HS] = grad
        out_ref[where, HS : 2 * HS] = dv_ref[part, :].astype(bf16)


def attention_backward(order, query, keys, vals, lse, d_mixed, cos, sin):
    whole = pl.BlockSpec(memory_space=pltpu.VMEM)
    return pl.pallas_call(
        backward_kernel,
        in_specs=[pl.BlockSpec(memory_space=pltpu.SMEM)] + [whole] * 7,
        out_specs=whole,
        out_shape=jax.ShapeDtypeStruct((GROUP, 3 * HS), bf16),
        scratch_shapes=[pltpu.VMEM((GROUP, HS), f32), pltpu.VMEM((GROUP, HS), f32)],
        cost_estimate=pl.CostEstimate(
            flops=5 * GROUP * GROUP * HS,
            bytes_accessed=20 * GROUP * HS,
            transcendentals=GROUP * GROUP // 2,
        ),
        compiler_params=pltpu.CompilerParams(vmem_limit_bytes=VMEM_LIMIT),
        name="attention_backward",
    )(order, query, keys, vals, lse, d_mixed, cos, sin)


def local(
    tokens,
    cotangent,
    segment,
    position,
    clip_limit,
    attn_gain,
    query_weight,
    key_weight,
    value_weight,
    output_weight,
    mlp_gain,
    gate_weight,
    up_weight,
    down_weight,
):
    groups = lax.axis_size("group")
    group = lax.axis_index("group")
    core = lax.axis_index("tp")
    member = lax.axis_index(PLANE)
    token_rows = tokens.shape[0]
    own_rows, features = query_weight.shape[0], tokens.shape[1]
    hidden_own = gate_weight.shape[1] // 4
    chunks, offset = [], 0
    for part in SIXTEENTHS:
        chunks.append((offset, hidden_own * part // 16))
        offset += hidden_own * part // 16
    member_at = member.astype(jnp.int32).reshape(1)

    def own_order(array):
        parts = []
        for j in range(2):
            for k in range(4):
                start = group * GROUP + (member ^ k) * (2 * token_rows) + (core ^ j) * token_rows
                parts.append(lax.dynamic_slice_in_dim(array, start, token_rows))
        return jnp.concatenate(parts)

    def collect(blocks):
        return lax.all_gather(blocks, "group", axis=0, tiled=True)

    def mlp_exchange(some, waits):
        weights = [after(a, *waits) for a in (gate_weight, up_weight, down_weight)]
        spans = tuple((start, hidden_own, count, 0) for start, count in some for _ in range(3))
        return swap_all(split(member_at, weights * len(some), spans))

    seg, pos = own_order(segment), own_order(position)
    cos, sin = rope_tables(pos)
    seg_blocks, pos_blocks = seg[::BLOCK], pos[::BLOCK]
    half_blocks = GROUP // BLOCK // 2
    place = jnp.where(seg_blocks == 0, pos_blocks // BLOCK, half_blocks - 1 + seg_blocks)
    labels = jnp.arange(2 * half_blocks, dtype=jnp.int32)
    order = jnp.sum(jnp.where(place[None, :] == labels[:, None], labels[None, :], 0), axis=1)
    index = lax.axis_index(FSDP)
    gains = jnp.stack([attn_gain, mlp_gain])[:, None, :]
    gains = jnp.where(jnp.arange(4 * groups)[None, :, None] == index, gains, 0)
    gains, gain_rounds = combine_all(gains, groups, lambda a, b: a + b)
    gains = gains.reshape(2, features).astype(f32)
    head, pair = (0, HS, HS, 0), (0, HS, HS, 1)
    attn_pieces = swap_all(
        split(
            member_at,
            (key_weight, value_weight, query_weight, output_weight),
            (pair, pair, head, head),
        )
    )
    (attn_blocks,) = place_rows(
        member_at, [after(attn_pieces[0], *gain_rounds[0])] + attn_pieces[1:]
    )
    attn_weights = collect(attn_blocks)
    late_tokens = after(tokens, *attn_pieces[1:])
    neighbours = plane_neighbours(late_tokens)
    tokens_far = plane_far(neighbours)
    tokens_mine = [late_tokens, *neighbours, *tokens_far]
    tokens_near = [swap(piece, "tp") for piece in tokens_mine[:3]]
    normed_all = pack_normed(
        with_partner(tokens_mine, tokens_near), gains[:1], (cos, sin, place, order)
    )
    pieces_0 = mlp_exchange(chunks[:1], (*tokens_far, *tokens_near))
    (blocks_0,) = place_rows(
        member_at, [after(pieces_0[0], normed_all)] + pieces_0[1:]
    )
    late_cot = after(cotangent, *pieces_0[1:])
    cot_near = plane_neighbours(late_cot)
    cot_far = plane_far(cot_near)
    query, keys, vals = project(
        place, normed_all, attn_weights, cos, sin
    )
    mixed, logsum, peak = attention_forward(
        order, after(query, *cot_near), keys, vals
    )

    head_top = jnp.where(jnp.arange(4) == member, peak[0, :4], masked_value)
    head_top, head_rounds = combine_all(head_top, groups, jnp.maximum)

    def projected(left, column, waits=(), others=()):
        lefts = (after(left, *others) if others else left, after(left, *waits) if waits else left)
        return [
            [
                chunk_sum([lefts[j]], [attn_weights], column, j, h, bf16 if j else f32)
                for j in (0, 1)
            ]
            for h in range(2)
        ]

    attn_sums = chip_sums(*projected(mixed, 3, (), cot_far))
    arrived = reduce_first(first_operands(attn_sums))
    attn_operands = reduce_operands(attn_sums, arrived)
    attn_last = last_swaps(attn_operands, *head_rounds[0])
    hidden, own_normed = add_and_norm(attn_operands, attn_last, tokens, gains[1:])
    neighbours = plane_neighbours(own_normed)
    normed_far = plane_far(neighbours, *head_rounds[-1])
    pieces_1 = mlp_exchange(chunks[1:], normed_far)
    mlp_weights = [collect(blocks_0), collect(*place_rows(member_at, pieces_1))]
    normed_mlp = pack(with_partner([own_normed, *neighbours, *normed_far]))
    cot_all = pack(with_partner([late_cot, *cot_near, *cot_far]))

    def line_sum(partial):
        return lax.psum_scatter(partial, "group", scatter_dimension=0, tiled=True)

    inner_0, both_0 = mlp_chunk(normed_mlp, cot_all, mlp_weights[0])
    grads_0 = weight_grads((normed_mlp, both_0), (cot_all, inner_0))
    sum_0 = line_sum(grads_0)
    late_both = after(both_0, grads_0)
    early = [chunk_sum([late_both], mlp_weights[:1], 0, j, None, f32) for j in range(2)]
    inner_1, both_1, front_1, back_1 = mlp_tail(
        after(normed_mlp, *early), cot_all, mlp_weights[1], early[1], 1, bf16
    )
    inner_1, both_1, front_0, back_0 = mlp_tail(
        normed_mlp, cot_all, mlp_weights[1], early[0], 0, f32, (inner_1, both_1)
    )

    mlp_sums = chip_sums((front_0, front_1), (back_0, back_1))
    operands = first_operands(mlp_sums)
    arrived = reduce_first(operands)
    inners = [after(inner, *operands) for inner in (inner_0, inner_1)]
    out_parts = [
        [chunk_sum(inners, mlp_weights, 2, j, h, bf16 if j else f32) for j in (0, 1)]
        for h in range(2)
    ]
    mlp_operands = reduce_operands(mlp_sums, arrived)
    mlp_last = last_swaps(mlp_operands, *out_parts[0], *out_parts[1])
    d_hidden, own_d = norm_back(
        mlp_operands, mlp_last, hidden, cotangent, gains[1:], (f32, bf16)
    )
    neighbours = plane_neighbours(own_d)
    late_both = after(both_1, own_d)
    grads_1 = weight_grads((normed_mlp, late_both), (cot_all, inner_1))
    sum_1 = line_sum(after(grads_1, *neighbours))
    d_far = plane_far(neighbours, grads_1)
    d_attn_all = pack(with_partner([own_d, *neighbours, *d_far]))
    out_sums = chip_sums(*out_parts)
    out_arrived = reduce_first(first_operands(out_sums), *d_far)
    out_operands = reduce_operands(out_sums, out_arrived)
    out_last = last_swaps(out_operands)

    def send_grads(sources, *waits):
        first = after(sources[0], *waits) if waits else sources[0]
        return swap_all(pick_rows(member_at, first, *sources[1:]))


    final_0 = send_grads([sum_0], *out_arrived)
    d_mixed = product(d_attn_all, attn_weights[:, 3 * HS :]).astype(bf16)
    d_qkv = attention_backward(
        order, after(query, *out_arrived), keys, vals, logsum, d_mixed, cos, sin
    )
    pair_grads = weight_grads((normed_all, (d_qkv, 2 * HS, 0)))
    half_shape = jax.ShapeDtypeStruct((features // 2, 2 * HS), bf16)
    keep, send = vmem_call(
        functools.partial(halves_kernel, own_rows),
        "halves",
        [half_shape] * 2,
        member_at,
        pair_grads,
    )
    got = swap(send, "col")
    both_grads = weight_grads(
        (normed_all, (after(d_qkv, keep), HS, 2)), (d_attn_all, mixed)
    )
    late_qkv = after(d_qkv, both_grads, *out_last, *final_0[1:])
    qkv_parts = projected(late_qkv, 0)
    (attn_grads,) = vmem_call(
        functools.partial(join_kernel, own_rows),
        "join",
        [jax.ShapeDtypeStruct((features, 3 * HS), bf16)],
        member_at,
        after(keep, *qkv_parts[0], *qkv_parts[1]),
        got,
        both_grads,
    )
    attn_sum = line_sum(attn_grads)
    qkv_sums = chip_sums(*qkv_parts)
    arrived = reduce_first(first_operands(qkv_sums))
    qkv_operands = reduce_operands(qkv_sums, arrived)
    qkv_last = last_swaps(qkv_operands)
    (tokens_grad,) = norm_back(qkv_operands, qkv_last, tokens, d_hidden, gains[:1], (f32,))
    block_out = (hidden + reduce_last(out_operands, out_last)).astype(bf16)

    final_1 = send_grads([sum_1], *arrived)
    gate_grad, up_grad, down_grad, mlp_gain_row = mlp_final(
        member_at, gate_weight, up_weight, (chunks[:1], chunks[1:]), [final_0, final_1]
    )
    query_grad, key_grad, value_grad, output_grad, attn_gain_row = attention_final(
        member_at,
        query_weight,
        key_weight,
        value_weight,
        attention_return(member_at, after(attn_sum, *qkv_last)),
    )
    gain_grads = jnp.concatenate([attn_gain_row, mlp_gain_row], axis=1)
    gain_grads = gain_grads + swap(gain_grads, "tp")
    attn_gain_grad = gain_grads[:, 0] / attn_gain.astype(f32)
    mlp_gain_grad = gain_grads[:, 1] / mlp_gain.astype(f32)

    factor = clip_limit / jnp.maximum(head_top, clip_limit)
    query_scale = jnp.repeat(jnp.sqrt(factor), HS)
    key_factor = jnp.min(factor.reshape(2, 2), axis=1)
    key_scale = jnp.repeat(jnp.sqrt(key_factor), HS)
    query_clipped = (query_weight.astype(f32) * query_scale[None, :]).astype(bf16)
    key_clipped = (key_weight.astype(f32) * key_scale[None, :]).astype(bf16)
    return (
        block_out,
        tokens_grad,
        attn_gain_grad,
        query_grad,
        key_grad,
        value_grad,
        output_grad,
        mlp_gain_grad,
        gate_grad,
        up_grad,
        down_grad,
        head_top,
        query_clipped,
        key_clipped,
    )


def solution(mesh):
    shape = (mesh.shape["fsdp"] // 4, 2, 2, mesh.shape["tp"])
    fine = Mesh(mesh.devices.reshape(shape), ("group", "row", "col", "tp"))
    rows = P(("group", "row", "col", "tp"), None)
    weight = P(FSDP, "tp")
    gain = P(FSDP)
    heads = P("tp")
    return jax.shard_map(
        local,
        mesh=fine,
        in_specs=(
            rows, rows, P(), P(), heads, gain, weight, weight, weight, weight,
            gain, weight, weight, weight,
        ),
        out_specs=(
            rows, rows, gain, weight, weight, weight, weight, gain, weight, weight, weight,
            heads, weight, weight,
        ),
        check_vma=False,
    )
```

```python
import functools

import jax
import jax.numpy as jnp
from jax import lax
from jax.experimental import pallas as pl
from jax.experimental.pallas import tpu as pltpu
from jax.sharding import Mesh, PartitionSpec as P

HS = 256
GROUP = 2048
SIXTEENTHS = (10, 6)
BLOCK = 128

epsilon = 1e-05
theta_base = 1000042.0
masked_value = -1e30

bf16 = jnp.bfloat16
f32 = jnp.float32
PLANE = ("row", "col")
FSDP = ("group", "row", "col")
VMEM_LIMIT = 48 * 1024 * 1024


def product(left, right):
    return jnp.dot(left, right, preferred_element_type=f32)


def times_transposed(left, right):
    return lax.dot_general(left, right, (((1,), (1,)), ((), ())), preferred_element_type=f32)


def outer_sum(left, right):
    return lax.dot_general(left, right, (((0,), (0,)), ((), ())), preferred_element_type=f32)


def take(array, index, axis=0):
    return lax.dynamic_index_in_dim(array, index, axis, keepdims=False)


def swap(block, axis):
    return lax.ppermute(block, axis, [(0, 1), (1, 0)])


def swap_plane(block, distance):
    return lax.ppermute(block, PLANE, [(i, i ^ distance) for i in range(4)])


def after(value, *others):
    return lax.optimization_barrier((value,) + others)[0]


def combine_all(values, groups, combine):
    distance, count = 1, 4 * groups
    rounds = []
    while distance < count:
        arrived = []
        for step in range(1, min(4, count // distance)):
            route = [(i, i ^ step * distance) for i in range(count)]
            arrived.append(lax.ppermute(values, FSDP, route))
        for other in arrived:
            values = combine(values, other)
        rounds.append(arrived)
        distance *= 4
    return values, rounds


def pack_kernel(count, *refs):
    out_ref, sems = refs[count], refs[count + 1]
    copies, start = [], 0
    for i in range(count):
        rows = refs[i].shape[0]
        copy = pltpu.make_async_copy(refs[i], out_ref.at[pl.ds(start, rows)], sems.at[i])
        copy.start()
        copies.append(copy)
        start += rows
    for copy in copies:
        copy.wait()


def pack(pieces):
    rows, width = sum(p.shape[0] for p in pieces), pieces[0].shape[1]
    count = len(pieces)
    return pl.pallas_call(
        functools.partial(pack_kernel, count),
        in_specs=[pl.BlockSpec(memory_space=pl.ANY)] * count,
        out_specs=pl.BlockSpec(memory_space=pltpu.VMEM),
        out_shape=jax.ShapeDtypeStruct((rows, width), pieces[0].dtype),
        scratch_shapes=[pltpu.SemaphoreType.DMA((count,))],
        cost_estimate=pl.CostEstimate(
            flops=0, bytes_accessed=4 * rows * width, transcendentals=0
        ),
        compiler_params=pltpu.CompilerParams(vmem_limit_bytes=VMEM_LIMIT),
        name="pack",
    )(*pieces)


def norm_kernel(count, *refs):
    gain_ref, out_ref = refs[count], refs[-2]
    pack_kernel(count, *refs[:count], *refs[-2:])
    tile = 256

    @pl.loop(0, out_ref.shape[0] // tile)
    def _(i):
        rows = pl.ds(pl.multiple_of(i * tile, tile), tile)
        values = out_ref[rows, :].astype(f32)
        out_ref[rows, :] = (values * rms_inverse(values) * gain_ref[...]).astype(bf16)


def pack_normed(pieces, gain, early):
    rows, width = sum(p.shape[0] for p in pieces), pieces[0].shape[1]
    count = len(pieces)
    return pl.pallas_call(
        functools.partial(norm_kernel, count),
        in_specs=[pl.BlockSpec(memory_space=pl.ANY)] * count
        + [pl.BlockSpec(memory_space=pltpu.VMEM)]
        + [pl.BlockSpec(memory_space=pl.ANY)] * len(early),
        out_specs=pl.BlockSpec(memory_space=pltpu.VMEM),
        out_shape=jax.ShapeDtypeStruct((rows, width), bf16),
        scratch_shapes=[pltpu.SemaphoreType.DMA((count,))],
        cost_estimate=pl.CostEstimate(
            flops=8 * rows * width, bytes_accessed=4 * rows * width, transcendentals=0
        ),
        compiler_params=pltpu.CompilerParams(vmem_limit_bytes=VMEM_LIMIT),
        name="pack_normed",
    )(*pieces, gain, *early)


def plane_neighbours(own):
    return swap(own, "col"), swap(own, "row")


def plane_far(neighbours, *waits):
    across, along = neighbours
    half = across.shape[0] // 2
    return (
        swap(after(across[:half], *waits), "row"),
        swap(after(along[half:], *waits), "col"),
    )


def with_partner(pieces, swapped=()):
    return pieces + list(swapped) + [swap(piece, "tp") for piece in pieces[len(swapped) :]]


def chip_sums(front, back):
    pairs = []
    for own, other in (front, back):
        shape = (4, own.shape[0] // 4, own.shape[1])
        pairs.append((own.reshape(shape), swap(other, "tp").reshape(shape)))
    return pairs


def quarter(pair, k):
    return pair[0][k].astype(f32) + pair[1][k].astype(f32)


def first_operands(sums):
    front, back = sums
    return (
        jnp.concatenate([quarter(front, 1), quarter(front, 3)]).astype(bf16),
        (back[0][2:].astype(f32) + back[1][2:].astype(f32)).astype(bf16),
    )


def reduce_first(operands, *waits):
    front, back = operands
    rows = front.shape[0] // 2
    return (
        swap(after(front, *waits), "col").reshape(2, rows, -1),
        swap(after(back, *waits), "row"),
    )


def reduce_operands(sums, arrived):
    front, back = sums
    got, got_back = arrived[0].astype(f32), arrived[1].astype(f32)
    return (
        (quarter(front, 0) + got[0], (quarter(front, 2) + got[1]).astype(bf16)),
        (quarter(back, 0) + got_back[0], (quarter(back, 1) + got_back[1]).astype(bf16)),
    )


def last_swaps(operands, *waits):
    return (
        swap(after(operands[0][1], *waits), "row"),
        swap(after(operands[1][1], *waits), "col"),
    )


def joined(front_ref, front_last_ref, back_ref, back_last_ref):
    return jnp.concatenate(
        [
            front_ref[...] + front_last_ref[...].astype(f32),
            back_ref[...] + back_last_ref[...].astype(f32),
        ],
        axis=1,
    )


def hidden_kernel(front, front_last, back, back_last, tokens_ref, gain_ref, hidden_ref, normed_ref):
    hidden = tokens_ref[...].astype(f32) + joined(front, front_last, back, back_last)
    hidden_ref[...] = hidden
    normed_ref[...] = (hidden * rms_inverse(hidden) * gain_ref[...]).astype(bf16)


def add_and_norm(operands, last, tokens, gain):
    halves = [part for (keep, _), got in zip(operands, last) for part in (keep, got)]
    return pl.pallas_call(
        hidden_kernel,
        in_specs=[pl.BlockSpec(memory_space=pltpu.VMEM)] * 6,
        out_specs=[pl.BlockSpec(memory_space=pltpu.VMEM)] * 2,
        out_shape=[
            jax.ShapeDtypeStruct(tokens.shape, f32),
            jax.ShapeDtypeStruct(tokens.shape, bf16),
        ],
        cost_estimate=pl.CostEstimate(
            flops=10 * tokens.size, bytes_accessed=14 * tokens.size, transcendentals=0
        ),
        compiler_params=pltpu.CompilerParams(vmem_limit_bytes=VMEM_LIMIT),
        name="add_and_norm",
    )(*halves, tokens, gain)


def out_kernel(front, front_last, back, back_last, hidden_ref, out_ref):
    out_ref[...] = (hidden_ref[...] + joined(front, front_last, back, back_last)).astype(bf16)


def add_sum(operands, last, hidden):
    halves = [part for (keep, _), got in zip(operands, last) for part in (keep, got)]
    return pl.pallas_call(
        out_kernel,
        in_specs=[pl.BlockSpec(memory_space=pltpu.VMEM)] * 5,
        out_specs=pl.BlockSpec(memory_space=pltpu.VMEM),
        out_shape=jax.ShapeDtypeStruct(hidden.shape, bf16),
        cost_estimate=pl.CostEstimate(
            flops=2 * hidden.size, bytes_accessed=12 * hidden.size, transcendentals=0
        ),
        compiler_params=pltpu.CompilerParams(vmem_limit_bytes=VMEM_LIMIT),
        name="add_sum",
    )(*halves, hidden)


def back_kernel(front, front_last, back, back_last, values_ref, base_ref, gain_ref, *outs):
    values = values_ref[...].astype(f32)
    inverse = rms_inverse(values)
    unit = values * inverse
    scaled = joined(front, front_last, back, back_last) * gain_ref[...]
    grad = base_ref[...].astype(f32) + inverse * (
        scaled - unit * jnp.mean(scaled * unit, axis=-1, keepdims=True)
    )
    for out in outs:
        out[...] = grad.astype(out.dtype)


def norm_back(operands, last, values, base, gain, dtypes):
    halves = [part for (keep, _), got in zip(operands, last) for part in (keep, got)]
    return pl.pallas_call(
        back_kernel,
        in_specs=[pl.BlockSpec(memory_space=pltpu.VMEM)] * 7,
        out_specs=[pl.BlockSpec(memory_space=pltpu.VMEM)] * len(dtypes),
        out_shape=[jax.ShapeDtypeStruct(values.shape, dtype) for dtype in dtypes],
        cost_estimate=pl.CostEstimate(
            flops=16 * values.size, bytes_accessed=18 * values.size, transcendentals=0
        ),
        compiler_params=pltpu.CompilerParams(vmem_limit_bytes=VMEM_LIMIT),
        name="norm_back",
    )(*halves, values, base, gain)


def split_kernel(spans, member_ref, *refs):
    sources, outs = refs[: len(spans)], refs[len(spans) :]
    for k in range(4):
        target = member_ref[0] ^ k
        column = 0
        for source, (offset, stride, width, shift) in zip(sources, spans):
            start = pl.multiple_of((target >> shift) * stride + offset, 128)
            outs[k][:, column : column + width] = source[:, pl.ds(start, width)]
            column += width


def split(member, sources, spans):
    rows, width = sources[0].shape[0], sum(span[2] for span in spans)
    whole = pl.BlockSpec(memory_space=pltpu.VMEM)
    return pl.pallas_call(
        functools.partial(split_kernel, spans),
        in_specs=[pl.BlockSpec(memory_space=pltpu.SMEM)] + [whole] * len(sources),
        out_specs=[whole] * 4,
        out_shape=[jax.ShapeDtypeStruct((rows, width), bf16)] * 4,
        cost_estimate=pl.CostEstimate(
            flops=0, bytes_accessed=16 * rows * width, transcendentals=0
        ),
        compiler_params=pltpu.CompilerParams(vmem_limit_bytes=VMEM_LIMIT),
        name="split",
    )(member, *sources)


def place_kernel(member_ref, *refs):
    rows = refs[0].shape[0]
    for k in range(4):
        start = pl.multiple_of((member_ref[0] ^ k) * rows, rows)
        column = 0
        for out_ref in refs[4:]:
            width = out_ref.shape[1]
            out_ref[pl.ds(start, rows), :] = refs[k][:, column : column + width]
            column += width


def place_rows(member, pieces, *widths):
    rows, width = pieces[0].shape
    whole = pl.BlockSpec(memory_space=pltpu.VMEM)
    return pl.pallas_call(
        place_kernel,
        in_specs=[pl.BlockSpec(memory_space=pltpu.SMEM)] + [whole] * 4,
        out_specs=[whole] * len(widths or (width,)),
        out_shape=[
            jax.ShapeDtypeStruct((4 * rows, w), bf16) for w in widths or (width,)
        ],
        cost_estimate=pl.CostEstimate(
            flops=0, bytes_accessed=16 * rows * width, transcendentals=0
        ),
        compiler_params=pltpu.CompilerParams(vmem_limit_bytes=VMEM_LIMIT),
        name="place_rows",
    )(member, *pieces)


def pick_kernel(member_ref, *refs):
    sources, outs = refs[:-4], refs[-4:]
    rows = outs[0].shape[0]
    for k in range(4):
        start = pl.multiple_of((member_ref[0] ^ k) * rows, rows)
        column = 0
        for source in sources:
            width = source.shape[1]
            outs[k][:, column : column + width] = source[pl.ds(start, rows), :]
            column += width


def pick_rows(member, *sources):
    rows, width = sources[0].shape[0] // 4, sum(source.shape[1] for source in sources)
    whole = pl.BlockSpec(memory_space=pltpu.VMEM)
    return pl.pallas_call(
        pick_kernel,
        in_specs=[pl.BlockSpec(memory_space=pltpu.SMEM)] + [whole] * len(sources),
        out_specs=[whole] * 4,
        out_shape=[jax.ShapeDtypeStruct((rows, width), bf16)] * 4,
        cost_estimate=pl.CostEstimate(
            flops=0, bytes_accessed=16 * rows * width, transcendentals=0
        ),
        compiler_params=pltpu.CompilerParams(vmem_limit_bytes=VMEM_LIMIT),
        name="pick_rows",
    )(member, *sources)


def swap_all(pieces):
    return [pieces[0]] + [swap_plane(pieces[k], k) for k in (1, 2, 3)]


def mlp_final_kernel(parts, stride, member_ref, gate_w_ref, up_w_ref, *refs):
    pieces, outs, gain_ref = refs[:-4], refs[-4:-1], refs[-1]
    for n, chunks in enumerate(parts):
        for k in range(4):
            start = 0
            for offset, width in chunks:
                column = pl.multiple_of((member_ref[0] ^ k) * stride + offset, 128)
                for i in range(3):
                    part = pieces[4 * n + k][:, start : start + width]
                    outs[i][:, pl.ds(column, width)] = part.astype(f32)
                    start += width
    gain_ref[...] = jnp.sum(
        gate_w_ref[...].astype(f32) * outs[0][...] + up_w_ref[...].astype(f32) * outs[1][...],
        axis=1,
        keepdims=True,
    )


def mlp_final(member, gate_weight, up_weight, chunks, parts):
    rows, hidden = gate_weight.shape
    pieces = [piece for part in parts for piece in part]
    whole = pl.BlockSpec(memory_space=pltpu.VMEM)
    return pl.pallas_call(
        functools.partial(mlp_final_kernel, chunks, hidden // 4),
        in_specs=[pl.BlockSpec(memory_space=pltpu.SMEM)] + [whole] * (2 + len(pieces)),
        out_specs=[whole] * 4,
        out_shape=[jax.ShapeDtypeStruct((rows, hidden), f32)] * 3
        + [jax.ShapeDtypeStruct((rows, 1), f32)],
        cost_estimate=pl.CostEstimate(
            flops=4 * rows * hidden, bytes_accessed=22 * rows * hidden, transcendentals=0
        ),
        compiler_params=pltpu.CompilerParams(vmem_limit_bytes=VMEM_LIMIT),
        name="mlp_final",
    )(member, gate_weight, up_weight, *pieces)


TURN = [(0, 0), (1, 2), (2, 1), (3, 3)]
CROSS = [(0, 2), (1, 0), (2, 3), (3, 1)]
CROSS_BACK = [(2, 0), (0, 1), (3, 2), (1, 3)]


def vmem_call(kernel, name, out_shape, *operands):
    whole = pl.BlockSpec(memory_space=pltpu.VMEM)
    moved = sum(a.size * a.dtype.itemsize for a in operands)
    moved += sum(a.size * a.dtype.itemsize for a in out_shape)
    return pl.pallas_call(
        kernel,
        in_specs=[pl.BlockSpec(memory_space=pltpu.SMEM)] + [whole] * (len(operands) - 1),
        out_specs=[whole] * len(out_shape),
        out_shape=out_shape,
        cost_estimate=pl.CostEstimate(flops=0, bytes_accessed=moved, transcendentals=0),
        compiler_params=pltpu.CompilerParams(vmem_limit_bytes=VMEM_LIMIT),
        name=name,
    )(*operands)


def head_columns(index):
    return pl.ds(pl.multiple_of(index * HS, HS), HS)


def halves_kernel(rows, member_ref, grads_ref, keep_ref, send_ref):
    half = (member_ref[0] & 1) * 2 * rows
    for i, base in enumerate(range(0, grads_ref.shape[0], 4 * rows)):
        part = slice(i * 2 * rows, (i + 1) * 2 * rows)
        mine = pl.ds(pl.multiple_of(base + half, 2 * rows), 2 * rows)
        other = pl.ds(pl.multiple_of(base + 2 * rows - half, 2 * rows), 2 * rows)
        keep_ref[part, :] = grads_ref[mine, :]
        send_ref[part, :] = grads_ref[other, :]


def join_kernel(rows, member_ref, keep_ref, got_ref, both_ref, out_ref):
    out_ref[:, : 2 * HS] = both_ref[...]
    for i, base in enumerate(range(0, out_ref.shape[0], 4 * rows)):
        part = slice(i * 2 * rows, (i + 1) * 2 * rows)
        total = (keep_ref[part, :].astype(f32) + got_ref[part, :].astype(f32)).astype(bf16)
        out_ref[base : base + 2 * rows, 2 * HS :] = total[:, :HS]
        out_ref[base + 2 * rows : base + 4 * rows, 2 * HS :] = total[:, HS:]


def attention_pick_kernel(member_ref, source_ref, *outs):
    member, rows = member_ref[0], outs[0].shape[0]
    for k in range(4):
        at = pl.ds(pl.multiple_of((member ^ k) * rows, rows), rows)
        outs[k][...] = source_ref[at, : 2 * HS]
    for h in range(2):
        start = ((member >> 1) ^ h) * rows
        at = pl.ds(pl.multiple_of(start, rows), rows)
        outs[4 + h][:, :HS] = source_ref[at, 2 * HS :]
        at = pl.ds(pl.multiple_of(start + 2 * rows, rows), rows)
        outs[4 + h][:, HS:] = source_ref[at, 2 * HS :]


def attention_return(member, reduced):
    rows = reduced.shape[0] // 4
    *both, turned, crossed = vmem_call(
        attention_pick_kernel,
        "attention_pick",
        [jax.ShapeDtypeStruct((rows, 2 * HS), bf16)] * 6,
        member,
        reduced,
    )
    return swap_all(both) + [
        lax.ppermute(turned, PLANE, TURN),
        lax.ppermute(crossed, PLANE, CROSS_BACK),
    ]


def attention_final_kernel(member_ref, qw_ref, kw_ref, vw_ref, *refs):
    pieces = refs[:6]
    q_ref, k_ref, v_ref, o_ref, gain_ref = refs[6:]
    member = member_ref[0]
    for k in range(4):
        columns = head_columns(member ^ k)
        q_ref[:, columns] = pieces[k][:, :HS].astype(f32)
        o_ref[:, columns] = pieces[k][:, HS:].astype(f32)
    for h in range(2):
        columns = head_columns((member & 1) ^ h)
        k_ref[:, columns] = pieces[4 + h][:, :HS].astype(f32)
        v_ref[:, columns] = pieces[4 + h][:, HS:].astype(f32)

    def row_sum(weight_ref, grad_ref):
        return jnp.sum(weight_ref[...].astype(f32) * grad_ref[...], axis=1, keepdims=True)

    gain_ref[...] = row_sum(qw_ref, q_ref) + row_sum(kw_ref, k_ref) + row_sum(vw_ref, v_ref)


def attention_final(member, query_weight, key_weight, value_weight, pieces):
    rows, width = query_weight.shape
    shapes = [jax.ShapeDtypeStruct((rows, n), f32) for n in (width, width // 2, width // 2, width, 1)]
    return vmem_call(
        attention_final_kernel,
        "attention_final",
        shapes,
        member,
        query_weight,
        key_weight,
        value_weight,
        *pieces,
    )


def rms_inverse(values):
    return lax.rsqrt(jnp.mean(values * values, axis=-1, keepdims=True) + epsilon)


def rope_tables(positions):
    half_size = HS // 2
    indices = jnp.arange(half_size, dtype=f32)
    inverse = theta_base ** (-2.0 * indices / HS)
    angles = positions.astype(f32)[:, None] * inverse[None, :]
    return jnp.cos(angles), jnp.sin(angles)


def rotate(vectors, cos, sin):
    front, back = vectors[:, : HS // 2], vectors[:, HS // 2 :]
    return jnp.concatenate([front * cos - back * sin, back * cos + front * sin], axis=-1)


def unrotate(grads, cos, sin):
    front, back = grads[:, : HS // 2], grads[:, HS // 2 :]
    return jnp.concatenate([front * cos + back * sin, back * cos - front * sin], axis=-1)


def mlp_tile(width, normed, cot, weight_ref):
    both = product(normed, weight_ref[:, : 2 * width])
    d_inner = product(cot, weight_ref[:, 2 * width :])
    gate, upward = both[:, :width], both[:, width:]
    sig = 1.0 / (1.0 + jnp.exp(-gate))
    silu = gate * sig
    d_gate = d_inner * upward * sig * (1.0 + gate * (1.0 - sig))
    return (
        (silu * upward).astype(bf16),
        jnp.concatenate([d_gate, d_inner * silu], axis=1).astype(bf16),
    )


def mlp_kernel(width, normed_ref, cot_ref, weight_ref, inner_ref, grads_ref):
    inner_ref[...], grads_ref[...] = mlp_tile(
        width, normed_ref[...], cot_ref[...], weight_ref
    )


def tail_kernel(width, normed_ref, cot_ref, weight_ref, base_ref, *refs):
    inner_ref, grads_ref, front_ref, back_ref = refs[-4:]
    inner, grads = mlp_tile(width, normed_ref[...], cot_ref[...], weight_ref)
    inner_ref[...], grads_ref[...] = inner, grads
    total = times_transposed(grads, weight_ref[:, : 2 * width]) + base_ref[...]
    half = total.shape[1] // 2
    front_ref[...] = total[:, :half].astype(front_ref.dtype)
    back_ref[...] = total[:, half:].astype(back_ref.dtype)


def mlp_tail(normed, cot, weight, base, part, dtype, chained=()):
    tokens, features = normed.shape
    width = weight.shape[1] // 3
    tile, rows = 256, tokens // 2
    steps = rows // tile
    count = len(chained)
    return pl.pallas_call(
        functools.partial(tail_kernel, width),
        grid=(steps,),
        in_specs=[
            pl.BlockSpec((tile, features), lambda i: (part * steps + i, 0)),
            pl.BlockSpec((tile, features), lambda i: (part * steps + i, 0)),
            pl.BlockSpec((features, 3 * width), lambda i: (0, 0)),
            pl.BlockSpec((tile, features), lambda i: (i, 0)),
        ]
        + [pl.BlockSpec(memory_space=pl.ANY)] * count,
        out_specs=[
            pl.BlockSpec((tile, width), lambda i: (part * steps + i, 0)),
            pl.BlockSpec((tile, 2 * width), lambda i: (part * steps + i, 0)),
            pl.BlockSpec((tile, features // 2), lambda i: (i, 0)),
            pl.BlockSpec((tile, features // 2), lambda i: (i, 0)),
        ],
        out_shape=[
            jax.ShapeDtypeStruct((tokens, width), bf16),
            jax.ShapeDtypeStruct((tokens, 2 * width), bf16),
            jax.ShapeDtypeStruct((rows, features // 2), dtype),
            jax.ShapeDtypeStruct((rows, features // 2), dtype),
        ],
        input_output_aliases={4 + i: i for i in range(count)},
        cost_estimate=pl.CostEstimate(
            flops=10 * rows * features * width,
            bytes_accessed=2 * features * (5 * rows + 3 * width),
            transcendentals=rows * width,
        ),
        compiler_params=pltpu.CompilerParams(vmem_limit_bytes=VMEM_LIMIT),
        name="mlp_tail",
    )(normed, cot, weight, base, *chained)


def mlp_chunk(normed, cot, weight):
    tokens, features = normed.shape
    width = weight.shape[1] // 3
    tile = 256
    return pl.pallas_call(
        functools.partial(mlp_kernel, width),
        grid=(tokens // tile,),
        in_specs=[
            pl.BlockSpec((tile, features), lambda i: (i, 0)),
            pl.BlockSpec((tile, features), lambda i: (i, 0)),
            pl.BlockSpec((features, 3 * width), lambda i: (0, 0)),
        ],
        out_specs=[
            pl.BlockSpec((tile, width), lambda i: (i, 0)),
            pl.BlockSpec((tile, 2 * width), lambda i: (i, 0)),
        ],
        out_shape=[
            jax.ShapeDtypeStruct((tokens, width), bf16),
            jax.ShapeDtypeStruct((tokens, 2 * width), bf16),
        ],
        cost_estimate=pl.CostEstimate(
            flops=6 * tokens * features * width,
            bytes_accessed=2 * features * (2 * tokens + 3 * width),
            transcendentals=tokens * width,
        ),
        compiler_params=pltpu.CompilerParams(vmem_limit_bytes=VMEM_LIMIT),
        name="mlp_chunk",
    )(normed, cot, weight)


def sum_kernel(count, *refs):
    lefts, rights, out_ref = refs[:count], refs[count : 2 * count], refs[-1]
    total = times_transposed(lefts[0][...], rights[0][...])
    for left, right in zip(lefts[1:], rights[1:]):
        total += times_transposed(left[...], right[...])
    for base in refs[2 * count : -1]:
        total += base[...].astype(f32)
    out_ref[...] = total.astype(out_ref.dtype)


def chunk_sum(lefts, rights, column, part, half, dtype):
    count = len(lefts)
    tokens, features = lefts[0].shape[0], rights[0].shape[0]
    widths = [left.shape[1] for left in lefts]
    rows = tokens // 2
    tile = 256
    if half is not None:
        features, tile = features // 2, 512
    steps = rows // tile
    block = half or 0
    return pl.pallas_call(
        functools.partial(sum_kernel, count),
        grid=(steps,),
        in_specs=[pl.BlockSpec((tile, w), lambda i: (part * steps + i, 0)) for w in widths]
        + [pl.BlockSpec((features, w), lambda i: (block, column)) for w in widths],
        out_specs=pl.BlockSpec((tile, features), lambda i: (i, 0)),
        out_shape=jax.ShapeDtypeStruct((rows, features), dtype),
        cost_estimate=pl.CostEstimate(
            flops=2 * rows * features * sum(widths),
            bytes_accessed=2 * sum(widths) * (rows + features) + 4 * rows * features,
            transcendentals=0,
        ),
        compiler_params=pltpu.CompilerParams(vmem_limit_bytes=VMEM_LIMIT),
        name="chunk_sum",
    )(*lefts, *rights)


def grads_kernel(count, *refs):
    column = 0
    for left, right in zip(refs[:count], refs[count : 2 * count]):
        width = right.shape[1]
        refs[-1][:, column : column + width] = outer_sum(left[...], right[...]).astype(bf16)
        column += width


def weight_grads(*pairs):
    lefts = [left for left, _ in pairs]
    rights = [r if isinstance(r, tuple) else (r, r.shape[1], 0) for _, r in pairs]
    count = len(pairs)
    tokens, features = lefts[0].shape
    widths = [width for _, width, _ in rights]
    tile = 256

    def block(width, at):
        return pl.BlockSpec((tokens, width), lambda i: (0, at))

    return pl.pallas_call(
        functools.partial(grads_kernel, count),
        grid=(features // tile,),
        in_specs=[pl.BlockSpec((tokens, tile), lambda i: (0, i))] * count
        + [block(width, at) for _, width, at in rights],
        out_specs=pl.BlockSpec((tile, sum(widths)), lambda i: (i, 0)),
        out_shape=jax.ShapeDtypeStruct((features, sum(widths)), bf16),
        cost_estimate=pl.CostEstimate(
            flops=2 * tokens * features * sum(widths),
            bytes_accessed=2 * (count * tokens * features + sum(widths) * (tokens + features)),
            transcendentals=0,
        ),
        compiler_params=pltpu.CompilerParams(vmem_limit_bytes=VMEM_LIMIT),
        name="weight_grads",
    )(*lefts, *[array for array, _, _ in rights])


def project_kernel(place_ref, normed_ref, weight_ref, cos_ref, sin_ref, q_ref, k_ref, v_ref):
    step = pl.program_id(0)
    cos, sin = cos_ref[...], sin_ref[...]
    qkv = product(normed_ref[...], weight_ref[...])
    keys = rotate(qkv[:, :HS], cos, sin).astype(bf16)
    vals = qkv[:, HS : 2 * HS].astype(bf16)
    query = rotate(qkv[:, 2 * HS :], cos, sin).astype(bf16) * HS ** (-0.5)
    blocks = normed_ref.shape[0] // BLOCK
    for b in range(blocks):
        rows = pl.ds(pl.multiple_of(place_ref[step * blocks + b] * BLOCK, BLOCK), BLOCK)
        part = slice(b * BLOCK, (b + 1) * BLOCK)
        q_ref[rows, :] = query[part]
        k_ref[rows, :] = keys[part]
        v_ref[rows, :] = vals[part]


def project(place, normed, weight, cos, sin):
    tokens, features = normed.shape
    tile = 256
    whole = pl.BlockSpec((tokens, HS), lambda i, place: (0, 0))
    return pl.pallas_call(
        project_kernel,
        grid_spec=pltpu.PrefetchScalarGridSpec(
            num_scalar_prefetch=1,
            grid=(tokens // tile,),
            in_specs=[
                pl.BlockSpec((tile, features), lambda i, place: (i, 0)),
                pl.BlockSpec((features, 3 * HS), lambda i, place: (0, 0)),
                pl.BlockSpec((tile, HS // 2), lambda i, place: (i, 0)),
                pl.BlockSpec((tile, HS // 2), lambda i, place: (i, 0)),
            ],
            out_specs=[whole] * 3,
        ),
        out_shape=[jax.ShapeDtypeStruct((tokens, HS), bf16)] * 3,
        cost_estimate=pl.CostEstimate(
            flops=6 * tokens * features * HS,
            bytes_accessed=2 * features * (tokens + 3 * HS) + 10 * tokens * HS,
            transcendentals=0,
        ),
        compiler_params=pltpu.CompilerParams(vmem_limit_bytes=VMEM_LIMIT),
        name="project",
    )(place, normed, weight, cos, sin)


TILE = 256


def tile_masks():
    rows = lax.broadcasted_iota(jnp.int32, (TILE, TILE), 0)
    cols = lax.broadcasted_iota(jnp.int32, (TILE, TILE), 1)
    causal = rows >= cols
    return causal, causal & (rows // BLOCK == cols // BLOCK)


def block_rows(order_ref, index):
    return pl.ds(pl.multiple_of(order_ref[index] * BLOCK, BLOCK), BLOCK)


def forward_kernel(order_ref, q_ref, k_ref, v_ref, mixed_ref, lse_ref, peak_ref):
    causal, inside = tile_masks()
    prompt = GROUP // 2
    top = jnp.full((TILE, 1), masked_value, f32)
    for i in range(GROUP // TILE):
        rows = slice(i * TILE, (i + 1) * TILE)
        past = min(i * TILE, prompt)
        query = q_ref[rows, :]
        near = times_transposed(query, k_ref[rows, :])
        near = jnp.where(causal if i * TILE < prompt else inside, near, masked_value)
        peak = jnp.max(near, axis=1, keepdims=True)
        if past:
            far = times_transposed(query, k_ref[:past, :])
            peak = jnp.maximum(peak, jnp.max(far, axis=1, keepdims=True))
            far = jnp.exp(far - peak)
        near = jnp.exp(near - peak)
        total = jnp.sum(near, axis=1, keepdims=True)
        if past:
            total += jnp.sum(far, axis=1, keepdims=True)
        share = 1.0 / total
        mixed = product((near * share).astype(bf16), v_ref[rows, :])
        if past:
            mixed += product((far * share).astype(bf16), v_ref[:past, :])
        mixed = mixed.astype(bf16)
        for b in range(TILE // BLOCK):
            mixed_ref[block_rows(order_ref, i * (TILE // BLOCK) + b), :] = mixed[
                b * BLOCK : (b + 1) * BLOCK
            ]
        lse_ref[rows, :] = peak + jnp.log(total)
        top = jnp.maximum(top, peak)
    peak_ref[...] = jnp.full(peak_ref.shape, jnp.max(top), f32)


def attention_forward(order, query, keys, vals):
    whole = pl.BlockSpec(memory_space=pltpu.VMEM)
    return pl.pallas_call(
        forward_kernel,
        in_specs=[pl.BlockSpec(memory_space=pltpu.SMEM), whole, whole, whole],
        out_specs=[whole] * 3,
        out_shape=[
            jax.ShapeDtypeStruct((GROUP, HS), bf16),
            jax.ShapeDtypeStruct((GROUP, 1), f32),
            jax.ShapeDtypeStruct((8, 128), f32),
        ],
        cost_estimate=pl.CostEstimate(
            flops=2 * GROUP * GROUP * HS,
            bytes_accessed=8 * GROUP * HS,
            transcendentals=GROUP * GROUP // 2,
        ),
        compiler_params=pltpu.CompilerParams(vmem_limit_bytes=VMEM_LIMIT),
        name="attention_forward",
    )(order, query, keys, vals)


def backward_kernel(
    order_ref, q_ref, k_ref, v_ref, lse_ref, mixed_ref, cos_ref, sin_ref, out_ref, dk_ref, dv_ref
):
    causal, inside = tile_masks()
    prompt = GROUP // 2
    blocks = TILE // BLOCK

    def back(grad, index):
        rows = block_rows(order_ref, index)
        return rows, unrotate(grad, cos_ref[rows, :], sin_ref[rows, :]).astype(bf16)

    for i in range(GROUP // TILE):
        rows = slice(i * TILE, (i + 1) * TILE)
        past = min(i * TILE, prompt)
        query, lse = q_ref[rows, :], lse_ref[rows, :]
        d_mixed = jnp.concatenate(
            [mixed_ref[block_rows(order_ref, i * blocks + b), :] for b in range(blocks)], axis=0
        )
        near = times_transposed(query, k_ref[rows, :])
        near = jnp.where(causal if i * TILE < prompt else inside, near, masked_value)
        near = jnp.exp(near - lse)
        d_near = times_transposed(d_mixed, v_ref[rows, :])
        inner = jnp.sum(near * d_near, axis=1, keepdims=True)
        if past:
            far = jnp.exp(times_transposed(query, k_ref[:past, :]) - lse)
            d_far = times_transposed(d_mixed, v_ref[:past, :])
            inner += jnp.sum(far * d_far, axis=1, keepdims=True)
        d_near = (near * (d_near - inner)).astype(bf16)
        d_query = product(d_near, k_ref[rows, :])
        dk_ref[rows, :] = outer_sum(d_near, query)
        dv_ref[rows, :] = outer_sum(near.astype(bf16), d_mixed)
        if past:
            d_far = (far * (d_far - inner)).astype(bf16)
            d_query += product(d_far, k_ref[:past, :])
            dk_ref[:past, :] += outer_sum(d_far, query)
            dv_ref[:past, :] += outer_sum(far.astype(bf16), d_mixed)
        d_query = d_query * HS ** (-0.5)
        for b in range(blocks):
            where, grad = back(d_query[b * BLOCK : (b + 1) * BLOCK], i * blocks + b)
            out_ref[where, 2 * HS :] = grad
    for c in range(GROUP // BLOCK):
        part = slice(c * BLOCK, (c + 1) * BLOCK)
        where, grad = back(dk_ref[part, :], c)
        out_ref[where, :HS] = grad
        out_ref[where, HS : 2 * HS] = dv_ref[part, :].astype(bf16)


def attention_backward(order, query, keys, vals, lse, d_mixed, cos, sin):
    whole = pl.BlockSpec(memory_space=pltpu.VMEM)
    return pl.pallas_call(
        backward_kernel,
        in_specs=[pl.BlockSpec(memory_space=pltpu.SMEM)] + [whole] * 7,
        out_specs=whole,
        out_shape=jax.ShapeDtypeStruct((GROUP, 3 * HS), bf16),
        scratch_shapes=[pltpu.VMEM((GROUP, HS), f32), pltpu.VMEM((GROUP, HS), f32)],
        cost_estimate=pl.CostEstimate(
            flops=5 * GROUP * GROUP * HS,
            bytes_accessed=20 * GROUP * HS,
            transcendentals=GROUP * GROUP // 2,
        ),
        compiler_params=pltpu.CompilerParams(vmem_limit_bytes=VMEM_LIMIT),
        name="attention_backward",
    )(order, query, keys, vals, lse, d_mixed, cos, sin)


def local(
    tokens,
    cotangent,
    segment,
    position,
    clip_limit,
    attn_gain,
    query_weight,
    key_weight,
    value_weight,
    output_weight,
    mlp_gain,
    gate_weight,
    up_weight,
    down_weight,
):
    groups = lax.axis_size("group")
    group = lax.axis_index("group")
    core = lax.axis_index("tp")
    member = lax.axis_index(PLANE)
    token_rows = tokens.shape[0]
    own_rows, features = query_weight.shape[0], tokens.shape[1]
    hidden_own = gate_weight.shape[1] // 4
    chunks, offset = [], 0
    for part in SIXTEENTHS:
        chunks.append((offset, hidden_own * part // 16))
        offset += hidden_own * part // 16
    member_at = member.astype(jnp.int32).reshape(1)

    def own_order(array):
        parts = []
        for j in range(2):
            for k in range(4):
                start = group * GROUP + (member ^ k) * (2 * token_rows) + (core ^ j) * token_rows
                parts.append(lax.dynamic_slice_in_dim(array, start, token_rows))
        return jnp.concatenate(parts)

    def collect(blocks):
        return lax.all_gather(blocks, "group", axis=0, tiled=True)

    def mlp_exchange(some, waits):
        weights = [after(a, *waits) for a in (gate_weight, up_weight, down_weight)]
        spans = tuple((start, hidden_own, count, 0) for start, count in some for _ in range(3))
        return swap_all(split(member_at, weights * len(some), spans))

    seg, pos = own_order(segment), own_order(position)
    cos, sin = rope_tables(pos)
    seg_blocks, pos_blocks = seg[::BLOCK], pos[::BLOCK]
    half_blocks = GROUP // BLOCK // 2
    place = jnp.where(seg_blocks == 0, pos_blocks // BLOCK, half_blocks - 1 + seg_blocks)
    labels = jnp.arange(2 * half_blocks, dtype=jnp.int32)
    order = jnp.sum(jnp.where(place[None, :] == labels[:, None], labels[None, :], 0), axis=1)
    index = lax.axis_index(FSDP)
    gains = jnp.stack([attn_gain, mlp_gain])[:, None, :]
    gains = jnp.where(jnp.arange(4 * groups)[None, :, None] == index, gains, 0)
    gains, gain_rounds = combine_all(gains, groups, lambda a, b: a + b)
    gains = gains.reshape(2, features).astype(f32)
    head, pair = (0, HS, HS, 0), (0, HS, HS, 1)
    attn_pieces = swap_all(
        split(
            member_at,
            (key_weight, value_weight, query_weight, output_weight),
            (pair, pair, head, head),
        )
    )
    (attn_blocks,) = place_rows(
        member_at, attn_pieces
    )
    attn_weights = collect(attn_blocks)
    late_tokens = after(tokens, *attn_pieces[1:])
    neighbours = plane_neighbours(late_tokens)
    tokens_far = plane_far(neighbours)
    tokens_mine = [late_tokens, *neighbours, *tokens_far]
    tokens_near = [swap(piece, "tp") for piece in tokens_mine[:3]]
    normed_all = pack_normed(
        with_partner(tokens_mine, tokens_near), gains[:1], (cos, sin, place, order)
    )
    pieces_0 = mlp_exchange(chunks[:1], (*tokens_far, *tokens_near))
    (blocks_0,) = place_rows(
        member_at, [after(pieces_0[0], normed_all, *gain_rounds[-1])] + pieces_0[1:]
    )
    late_cot = after(cotangent, *pieces_0[1:])
    cot_near = plane_neighbours(late_cot)
    cot_far = plane_far(cot_near)
    query, keys, vals = project(
        place, normed_all, attn_weights, cos, sin
    )
    mixed, logsum, peak = attention_forward(
        order, after(query, *cot_near), keys, vals
    )

    head_top = jnp.where(jnp.arange(4) == member, peak[0, :4], masked_value)
    head_top, head_rounds = combine_all(head_top, groups, jnp.maximum)

    def projected(left, column, waits=(), others=()):
        lefts = (after(left, *others) if others else left, after(left, *waits) if waits else left)
        return [
            [
                chunk_sum([lefts[j]], [attn_weights], column, j, h, bf16 if j else f32)
                for j in (0, 1)
            ]
            for h in range(2)
        ]

    attn_sums = chip_sums(*projected(mixed, 3, (), cot_far))
    arrived = reduce_first(first_operands(attn_sums))
    attn_operands = reduce_operands(attn_sums, arrived)
    attn_last = last_swaps(attn_operands, *head_rounds[0])
    hidden, own_normed = add_and_norm(attn_operands, attn_last, tokens, gains[1:])
    neighbours = plane_neighbours(own_normed)
    normed_far = plane_far(neighbours, *head_rounds[-1])
    pieces_1 = mlp_exchange(chunks[1:], normed_far)
    mlp_weights = [collect(blocks_0), collect(*place_rows(member_at, pieces_1))]
    normed_mlp = pack(with_partner([own_normed, *neighbours, *normed_far]))
    cot_all = pack(with_partner([late_cot, *cot_near, *cot_far]))

    def line_sum(partial):
        return lax.psum_scatter(partial, "group", scatter_dimension=0, tiled=True)

    inner_0, both_0 = mlp_chunk(normed_mlp, cot_all, mlp_weights[0])
    grads_0 = weight_grads((normed_mlp, both_0), (cot_all, inner_0))
    sum_0 = line_sum(grads_0)
    late_both = after(both_0, grads_0)
    early = [chunk_sum([late_both], mlp_weights[:1], 0, j, None, f32) for j in range(2)]
    inner_1, both_1, front_1, back_1 = mlp_tail(
        after(normed_mlp, *early), cot_all, mlp_weights[1], early[1], 1, bf16
    )
    inner_1, both_1, front_0, back_0 = mlp_tail(
        normed_mlp, cot_all, mlp_weights[1], early[0], 0, f32, (inner_1, both_1)
    )

    mlp_sums = chip_sums((front_0, front_1), (back_0, back_1))
    operands = first_operands(mlp_sums)
    arrived = reduce_first(operands)
    inners = [after(inner, *operands) for inner in (inner_0, inner_1)]
    out_parts = [
        [chunk_sum(inners, mlp_weights, 2, j, h, bf16 if j else f32) for j in (0, 1)]
        for h in range(2)
    ]
    mlp_operands = reduce_operands(mlp_sums, arrived)
    mlp_last = last_swaps(mlp_operands, *out_parts[0], *out_parts[1])
    d_hidden, own_d = norm_back(
        mlp_operands, mlp_last, hidden, cotangent, gains[1:], (f32, bf16)
    )
    neighbours = plane_neighbours(own_d)
    late_both = after(both_1, own_d)
    grads_1 = weight_grads((normed_mlp, late_both), (cot_all, inner_1))
    sum_1 = line_sum(after(grads_1, *neighbours))
    d_far = plane_far(neighbours, grads_1)
    d_attn_all = pack(with_partner([own_d, *neighbours, *d_far]))
    out_sums = chip_sums(*out_parts)
    out_arrived = reduce_first(first_operands(out_sums), *d_far)
    out_operands = reduce_operands(out_sums, out_arrived)
    out_last = last_swaps(out_operands)

    def send_grads(sources, *waits):
        first = after(sources[0], *waits) if waits else sources[0]
        return swap_all(pick_rows(member_at, first, *sources[1:]))


    final_0 = send_grads([sum_0], *out_arrived)
    d_mixed = product(d_attn_all, attn_weights[:, 3 * HS :]).astype(bf16)
    d_qkv = attention_backward(
        order, query, keys, vals, logsum, d_mixed, cos, sin
    )
    pair_grads = weight_grads((normed_all, (after(d_qkv, *out_arrived), 2 * HS, 0)))
    half_shape = jax.ShapeDtypeStruct((features // 2, 2 * HS), bf16)
    keep, send = vmem_call(
        functools.partial(halves_kernel, own_rows),
        "halves",
        [half_shape] * 2,
        member_at,
        pair_grads,
    )
    got = swap(send, "col")
    both_grads = weight_grads(
        (normed_all, (after(d_qkv, keep), HS, 2)), (d_attn_all, mixed)
    )
    late_qkv = after(d_qkv, both_grads, *out_last, *final_0[1:])
    qkv_parts = projected(late_qkv, 0)
    (attn_grads,) = vmem_call(
        functools.partial(join_kernel, own_rows),
        "join",
        [jax.ShapeDtypeStruct((features, 3 * HS), bf16)],
        member_at,
        after(keep, *qkv_parts[0], *qkv_parts[1]),
        got,
        both_grads,
    )
    attn_sum = line_sum(attn_grads)
    qkv_sums = chip_sums(*qkv_parts)
    final_1 = send_grads([sum_1], attn_grads)
    arrived = reduce_first(first_operands(qkv_sums), *final_1[1:])
    qkv_operands = reduce_operands(qkv_sums, arrived)
    qkv_last = last_swaps(qkv_operands)
    (tokens_grad,) = norm_back(qkv_operands, qkv_last, tokens, d_hidden, gains[:1], (f32,))
    block_out = add_sum(out_operands, out_last, hidden)

    gate_grad, up_grad, down_grad, mlp_gain_row = mlp_final(
        member_at, gate_weight, up_weight, (chunks[:1], chunks[1:]), [final_0, final_1]
    )
    attn_parts = attention_return(
        member_at, after(attn_sum, *qkv_last, mlp_gain_row, block_out)
    )
    query_grad, key_grad, value_grad, output_grad, attn_gain_row = attention_final(
        member_at,
        query_weight,
        key_weight,
        value_weight,
        [after(attn_parts[0], tokens_grad)] + attn_parts[1:],
    )
    gain_grads = jnp.concatenate([attn_gain_row, mlp_gain_row], axis=1)
    gain_grads = gain_grads + swap(gain_grads, "tp")
    attn_gain_grad = gain_grads[:, 0] / attn_gain.astype(f32)
    mlp_gain_grad = gain_grads[:, 1] / mlp_gain.astype(f32)

    factor = clip_limit / jnp.maximum(head_top, clip_limit)
    query_scale = jnp.repeat(jnp.sqrt(factor), HS)
    key_factor = jnp.min(factor.reshape(2, 2), axis=1)
    key_scale = jnp.repeat(jnp.sqrt(key_factor), HS)
    query_clipped = (query_weight.astype(f32) * query_scale[None, :]).astype(bf16)
    key_clipped = (key_weight.astype(f32) * key_scale[None, :]).astype(bf16)
    return (
        block_out,
        tokens_grad,
        attn_gain_grad,
        query_grad,
        key_grad,
        value_grad,
        output_grad,
        mlp_gain_grad,
        gate_grad,
        up_grad,
        down_grad,
        head_top,
        query_clipped,
        key_clipped,
    )


def solution(mesh):
    shape = (mesh.shape["fsdp"] // 4, 2, 2, mesh.shape["tp"])
    fine = Mesh(mesh.devices.reshape(shape), ("group", "row", "col", "tp"))
    rows = P(("group", "row", "col", "tp"), None)
    weight = P(FSDP, "tp")
    gain = P(FSDP)
    heads = P("tp")
    return jax.shard_map(
        local,
        mesh=fine,
        in_specs=(
            rows, rows, P(), P(), heads, gain, weight, weight, weight, weight,
            gain, weight, weight, weight,
        ),
        out_specs=(
            rows, rows, gain, weight, weight, weight, weight, gain, weight, weight, weight,
            heads, weight, weight,
        ),
        check_vma=False,
    )
```

```python
import functools

import jax
import jax.numpy as jnp
from jax import lax
from jax.experimental import pallas as pl
from jax.experimental.pallas import tpu as pltpu
from jax.sharding import Mesh, PartitionSpec as P

HS = 256
GROUP = 2048
SIXTEENTHS = (10, 6)
BLOCK = 128

epsilon = 1e-05
theta_base = 1000042.0
masked_value = -1e30

bf16 = jnp.bfloat16
f32 = jnp.float32
PLANE = ("row", "col")
FSDP = ("group", "row", "col")
VMEM_LIMIT = 48 * 1024 * 1024


def product(left, right):
    return jnp.dot(left, right, preferred_element_type=f32)


def times_transposed(left, right):
    return lax.dot_general(left, right, (((1,), (1,)), ((), ())), preferred_element_type=f32)


def outer_sum(left, right):
    return lax.dot_general(left, right, (((0,), (0,)), ((), ())), preferred_element_type=f32)


def take(array, index, axis=0):
    return lax.dynamic_index_in_dim(array, index, axis, keepdims=False)


def swap(block, axis):
    return lax.ppermute(block, axis, [(0, 1), (1, 0)])


def swap_plane(block, distance):
    return lax.ppermute(block, PLANE, [(i, i ^ distance) for i in range(4)])


def after(value, *others):
    return lax.optimization_barrier((value,) + others)[0]


def combine_all(values, groups, combine):
    distance, count = 1, 4 * groups
    rounds = []
    while distance < count:
        arrived = []
        for step in range(1, min(4, count // distance)):
            route = [(i, i ^ step * distance) for i in range(count)]
            arrived.append(lax.ppermute(values, FSDP, route))
        for other in arrived:
            values = combine(values, other)
        rounds.append(arrived)
        distance *= 4
    return values, rounds


def pack_kernel(count, *refs):
    out_ref, sems = refs[count], refs[count + 1]
    copies, start = [], 0
    for i in range(count):
        rows = refs[i].shape[0]
        copy = pltpu.make_async_copy(refs[i], out_ref.at[pl.ds(start, rows)], sems.at[i])
        copy.start()
        copies.append(copy)
        start += rows
    for copy in copies:
        copy.wait()


def pack(pieces):
    rows, width = sum(p.shape[0] for p in pieces), pieces[0].shape[1]
    count = len(pieces)
    return pl.pallas_call(
        functools.partial(pack_kernel, count),
        in_specs=[pl.BlockSpec(memory_space=pl.ANY)] * count,
        out_specs=pl.BlockSpec(memory_space=pltpu.VMEM),
        out_shape=jax.ShapeDtypeStruct((rows, width), pieces[0].dtype),
        scratch_shapes=[pltpu.SemaphoreType.DMA((count,))],
        cost_estimate=pl.CostEstimate(
            flops=0, bytes_accessed=4 * rows * width, transcendentals=0
        ),
        compiler_params=pltpu.CompilerParams(vmem_limit_bytes=VMEM_LIMIT),
        name="pack",
    )(*pieces)


def norm_kernel(count, *refs):
    gain_ref, out_ref = refs[count], refs[-2]
    pack_kernel(count, *refs[:count], *refs[-2:])
    tile = 256

    @pl.loop(0, out_ref.shape[0] // tile)
    def _(i):
        rows = pl.ds(pl.multiple_of(i * tile, tile), tile)
        values = out_ref[rows, :].astype(f32)
        out_ref[rows, :] = (values * rms_inverse(values) * gain_ref[...]).astype(bf16)


def pack_normed(pieces, gain, early):
    rows, width = sum(p.shape[0] for p in pieces), pieces[0].shape[1]
    count = len(pieces)
    return pl.pallas_call(
        functools.partial(norm_kernel, count),
        in_specs=[pl.BlockSpec(memory_space=pl.ANY)] * count
        + [pl.BlockSpec(memory_space=pltpu.VMEM)]
        + [pl.BlockSpec(memory_space=pl.ANY)] * len(early),
        out_specs=pl.BlockSpec(memory_space=pltpu.VMEM),
        out_shape=jax.ShapeDtypeStruct((rows, width), bf16),
        scratch_shapes=[pltpu.SemaphoreType.DMA((count,))],
        cost_estimate=pl.CostEstimate(
            flops=8 * rows * width, bytes_accessed=4 * rows * width, transcendentals=0
        ),
        compiler_params=pltpu.CompilerParams(vmem_limit_bytes=VMEM_LIMIT),
        name="pack_normed",
    )(*pieces, gain, *early)


def plane_neighbours(own):
    return swap(own, "col"), swap(own, "row")


def plane_far(neighbours, *waits):
    across, along = neighbours
    half = across.shape[0] // 2
    return (
        swap(after(across[:half], *waits), "row"),
        swap(after(along[half:], *waits), "col"),
    )


def with_partner(pieces, swapped=()):
    return pieces + list(swapped) + [swap(piece, "tp") for piece in pieces[len(swapped) :]]


def chip_sums(front, back):
    pairs = []
    for own, other in (front, back):
        shape = (4, own.shape[0] // 4, own.shape[1])
        pairs.append((own.reshape(shape), swap(other, "tp").reshape(shape)))
    return pairs


def quarter(pair, k):
    return pair[0][k].astype(f32) + pair[1][k].astype(f32)


def first_operands(sums):
    front, back = sums
    return (
        jnp.concatenate([quarter(front, 1), quarter(front, 3)]).astype(bf16),
        (back[0][2:].astype(f32) + back[1][2:].astype(f32)).astype(bf16),
    )


def reduce_first(operands, *waits):
    front, back = operands
    rows = front.shape[0] // 2
    return (
        swap(after(front, *waits), "col").reshape(2, rows, -1),
        swap(after(back, *waits), "row"),
    )


def reduce_operands(sums, arrived):
    front, back = sums
    got, got_back = arrived[0].astype(f32), arrived[1].astype(f32)
    return (
        (quarter(front, 0) + got[0], (quarter(front, 2) + got[1]).astype(bf16)),
        (quarter(back, 0) + got_back[0], (quarter(back, 1) + got_back[1]).astype(bf16)),
    )


def last_swaps(operands, *waits):
    return (
        swap(after(operands[0][1], *waits), "row"),
        swap(after(operands[1][1], *waits), "col"),
    )


def joined(front_ref, front_last_ref, back_ref, back_last_ref):
    return jnp.concatenate(
        [
            front_ref[...] + front_last_ref[...].astype(f32),
            back_ref[...] + back_last_ref[...].astype(f32),
        ],
        axis=1,
    )


def hidden_kernel(front, front_last, back, back_last, tokens_ref, gain_ref, hidden_ref, normed_ref):
    hidden = tokens_ref[...].astype(f32) + joined(front, front_last, back, back_last)
    hidden_ref[...] = hidden
    normed_ref[...] = (hidden * rms_inverse(hidden) * gain_ref[...]).astype(bf16)


def add_and_norm(operands, last, tokens, gain):
    halves = [part for (keep, _), got in zip(operands, last) for part in (keep, got)]
    return pl.pallas_call(
        hidden_kernel,
        in_specs=[pl.BlockSpec(memory_space=pltpu.VMEM)] * 6,
        out_specs=[pl.BlockSpec(memory_space=pltpu.VMEM)] * 2,
        out_shape=[
            jax.ShapeDtypeStruct(tokens.shape, f32),
            jax.ShapeDtypeStruct(tokens.shape, bf16),
        ],
        cost_estimate=pl.CostEstimate(
            flops=10 * tokens.size, bytes_accessed=14 * tokens.size, transcendentals=0
        ),
        compiler_params=pltpu.CompilerParams(vmem_limit_bytes=VMEM_LIMIT),
        name="add_and_norm",
    )(*halves, tokens, gain)


def out_kernel(front, front_last, back, back_last, hidden_ref, out_ref):
    out_ref[...] = (hidden_ref[...] + joined(front, front_last, back, back_last)).astype(bf16)


def add_sum(operands, last, hidden):
    halves = [part for (keep, _), got in zip(operands, last) for part in (keep, got)]
    return pl.pallas_call(
        out_kernel,
        in_specs=[pl.BlockSpec(memory_space=pltpu.VMEM)] * 5,
        out_specs=pl.BlockSpec(memory_space=pltpu.VMEM),
        out_shape=jax.ShapeDtypeStruct(hidden.shape, bf16),
        cost_estimate=pl.CostEstimate(
            flops=2 * hidden.size, bytes_accessed=12 * hidden.size, transcendentals=0
        ),
        compiler_params=pltpu.CompilerParams(vmem_limit_bytes=VMEM_LIMIT),
        name="add_sum",
    )(*halves, hidden)


def back_kernel(front, front_last, back, back_last, values_ref, base_ref, gain_ref, *outs):
    values = values_ref[...].astype(f32)
    inverse = rms_inverse(values)
    unit = values * inverse
    scaled = joined(front, front_last, back, back_last) * gain_ref[...]
    grad = base_ref[...].astype(f32) + inverse * (
        scaled - unit * jnp.mean(scaled * unit, axis=-1, keepdims=True)
    )
    for out in outs:
        out[...] = grad.astype(out.dtype)


def norm_back(operands, last, values, base, gain, dtypes):
    halves = [part for (keep, _), got in zip(operands, last) for part in (keep, got)]
    return pl.pallas_call(
        back_kernel,
        in_specs=[pl.BlockSpec(memory_space=pltpu.VMEM)] * 7,
        out_specs=[pl.BlockSpec(memory_space=pltpu.VMEM)] * len(dtypes),
        out_shape=[jax.ShapeDtypeStruct(values.shape, dtype) for dtype in dtypes],
        cost_estimate=pl.CostEstimate(
            flops=16 * values.size, bytes_accessed=18 * values.size, transcendentals=0
        ),
        compiler_params=pltpu.CompilerParams(vmem_limit_bytes=VMEM_LIMIT),
        name="norm_back",
    )(*halves, values, base, gain)


def split_kernel(spans, member_ref, *refs):
    sources, outs = refs[: len(spans)], refs[len(spans) :]
    for k in range(4):
        target = member_ref[0] ^ k
        column = 0
        for source, (offset, stride, width, shift) in zip(sources, spans):
            start = pl.multiple_of((target >> shift) * stride + offset, 128)
            outs[k][:, column : column + width] = source[:, pl.ds(start, width)]
            column += width


def split(member, sources, spans):
    rows, width = sources[0].shape[0], sum(span[2] for span in spans)
    whole = pl.BlockSpec(memory_space=pltpu.VMEM)
    return pl.pallas_call(
        functools.partial(split_kernel, spans),
        in_specs=[pl.BlockSpec(memory_space=pltpu.SMEM)] + [whole] * len(sources),
        out_specs=[whole] * 4,
        out_shape=[jax.ShapeDtypeStruct((rows, width), bf16)] * 4,
        cost_estimate=pl.CostEstimate(
            flops=0, bytes_accessed=16 * rows * width, transcendentals=0
        ),
        compiler_params=pltpu.CompilerParams(vmem_limit_bytes=VMEM_LIMIT),
        name="split",
    )(member, *sources)


def place_kernel(member_ref, *refs):
    rows = refs[0].shape[0]
    for k in range(4):
        start = pl.multiple_of((member_ref[0] ^ k) * rows, rows)
        column = 0
        for out_ref in refs[4:]:
            width = out_ref.shape[1]
            out_ref[pl.ds(start, rows), :] = refs[k][:, column : column + width]
            column += width


def place_rows(member, pieces, *widths):
    rows, width = pieces[0].shape
    whole = pl.BlockSpec(memory_space=pltpu.VMEM)
    return pl.pallas_call(
        place_kernel,
        in_specs=[pl.BlockSpec(memory_space=pltpu.SMEM)] + [whole] * 4,
        out_specs=[whole] * len(widths or (width,)),
        out_shape=[
            jax.ShapeDtypeStruct((4 * rows, w), bf16) for w in widths or (width,)
        ],
        cost_estimate=pl.CostEstimate(
            flops=0, bytes_accessed=16 * rows * width, transcendentals=0
        ),
        compiler_params=pltpu.CompilerParams(vmem_limit_bytes=VMEM_LIMIT),
        name="place_rows",
    )(member, *pieces)


def pick_kernel(member_ref, *refs):
    sources, outs = refs[:-4], refs[-4:]
    rows = outs[0].shape[0]
    for k in range(4):
        start = pl.multiple_of((member_ref[0] ^ k) * rows, rows)
        column = 0
        for source in sources:
            width = source.shape[1]
            outs[k][:, column : column + width] = source[pl.ds(start, rows), :]
            column += width


def pick_rows(member, *sources):
    rows, width = sources[0].shape[0] // 4, sum(source.shape[1] for source in sources)
    whole = pl.BlockSpec(memory_space=pltpu.VMEM)
    return pl.pallas_call(
        pick_kernel,
        in_specs=[pl.BlockSpec(memory_space=pltpu.SMEM)] + [whole] * len(sources),
        out_specs=[whole] * 4,
        out_shape=[jax.ShapeDtypeStruct((rows, width), bf16)] * 4,
        cost_estimate=pl.CostEstimate(
            flops=0, bytes_accessed=16 * rows * width, transcendentals=0
        ),
        compiler_params=pltpu.CompilerParams(vmem_limit_bytes=VMEM_LIMIT),
        name="pick_rows",
    )(member, *sources)


def swap_all(pieces):
    return [pieces[0]] + [swap_plane(pieces[k], k) for k in (1, 2, 3)]


def mlp_final_kernel(parts, stride, member_ref, gate_w_ref, up_w_ref, *refs):
    pieces, outs, gain_ref = refs[:-4], refs[-4:-1], refs[-1]
    for n, chunks in enumerate(parts):
        for k in range(4):
            start = 0
            for offset, width in chunks:
                column = pl.multiple_of((member_ref[0] ^ k) * stride + offset, 128)
                for i in range(3):
                    part = pieces[4 * n + k][:, start : start + width]
                    outs[i][:, pl.ds(column, width)] = part.astype(f32)
                    start += width
    gain_ref[...] = jnp.sum(
        gate_w_ref[...].astype(f32) * outs[0][...] + up_w_ref[...].astype(f32) * outs[1][...],
        axis=1,
        keepdims=True,
    )


def mlp_final(member, gate_weight, up_weight, chunks, parts):
    rows, hidden = gate_weight.shape
    pieces = [piece for part in parts for piece in part]
    whole = pl.BlockSpec(memory_space=pltpu.VMEM)
    return pl.pallas_call(
        functools.partial(mlp_final_kernel, chunks, hidden // 4),
        in_specs=[pl.BlockSpec(memory_space=pltpu.SMEM)] + [whole] * (2 + len(pieces)),
        out_specs=[whole] * 4,
        out_shape=[jax.ShapeDtypeStruct((rows, hidden), f32)] * 3
        + [jax.ShapeDtypeStruct((rows, 1), f32)],
        cost_estimate=pl.CostEstimate(
            flops=4 * rows * hidden, bytes_accessed=22 * rows * hidden, transcendentals=0
        ),
        compiler_params=pltpu.CompilerParams(vmem_limit_bytes=VMEM_LIMIT),
        name="mlp_final",
    )(member, gate_weight, up_weight, *pieces)


TURN = [(0, 0), (1, 2), (2, 1), (3, 3)]
CROSS = [(0, 2), (1, 0), (2, 3), (3, 1)]
CROSS_BACK = [(2, 0), (0, 1), (3, 2), (1, 3)]


def vmem_call(kernel, name, out_shape, *operands):
    whole = pl.BlockSpec(memory_space=pltpu.VMEM)
    moved = sum(a.size * a.dtype.itemsize for a in operands)
    moved += sum(a.size * a.dtype.itemsize for a in out_shape)
    return pl.pallas_call(
        kernel,
        in_specs=[pl.BlockSpec(memory_space=pltpu.SMEM)] + [whole] * (len(operands) - 1),
        out_specs=[whole] * len(out_shape),
        out_shape=out_shape,
        cost_estimate=pl.CostEstimate(flops=0, bytes_accessed=moved, transcendentals=0),
        compiler_params=pltpu.CompilerParams(vmem_limit_bytes=VMEM_LIMIT),
        name=name,
    )(*operands)


def head_columns(index):
    return pl.ds(pl.multiple_of(index * HS, HS), HS)


def halves_kernel(rows, member_ref, grads_ref, keep_ref, send_ref):
    half = (member_ref[0] & 1) * 2 * rows
    for i, base in enumerate(range(0, grads_ref.shape[0], 4 * rows)):
        part = slice(i * 2 * rows, (i + 1) * 2 * rows)
        mine = pl.ds(pl.multiple_of(base + half, 2 * rows), 2 * rows)
        other = pl.ds(pl.multiple_of(base + 2 * rows - half, 2 * rows), 2 * rows)
        keep_ref[part, :] = grads_ref[mine, :]
        send_ref[part, :] = grads_ref[other, :]


def join_kernel(rows, member_ref, keep_ref, got_ref, both_ref, out_ref):
    out_ref[:, : 2 * HS] = both_ref[...]
    for i, base in enumerate(range(0, out_ref.shape[0], 4 * rows)):
        part = slice(i * 2 * rows, (i + 1) * 2 * rows)
        total = (keep_ref[part, :].astype(f32) + got_ref[part, :].astype(f32)).astype(bf16)
        out_ref[base : base + 2 * rows, 2 * HS :] = total[:, :HS]
        out_ref[base + 2 * rows : base + 4 * rows, 2 * HS :] = total[:, HS:]


def attention_pick_kernel(member_ref, source_ref, *outs):
    member, rows = member_ref[0], outs[0].shape[0]
    for k in range(4):
        at = pl.ds(pl.multiple_of((member ^ k) * rows, rows), rows)
        outs[k][...] = source_ref[at, : 2 * HS]
    for h in range(2):
        start = ((member >> 1) ^ h) * rows
        at = pl.ds(pl.multiple_of(start, rows), rows)
        outs[4 + h][:, :HS] = source_ref[at, 2 * HS :]
        at = pl.ds(pl.multiple_of(start + 2 * rows, rows), rows)
        outs[4 + h][:, HS:] = source_ref[at, 2 * HS :]


def attention_return(member, reduced):
    rows = reduced.shape[0] // 4
    *both, turned, crossed = vmem_call(
        attention_pick_kernel,
        "attention_pick",
        [jax.ShapeDtypeStruct((rows, 2 * HS), bf16)] * 6,
        member,
        reduced,
    )
    return swap_all(both) + [
        lax.ppermute(turned, PLANE, TURN),
        lax.ppermute(crossed, PLANE, CROSS_BACK),
    ]


def attention_final_kernel(member_ref, qw_ref, kw_ref, vw_ref, *refs):
    pieces = refs[:6]
    q_ref, k_ref, v_ref, o_ref, gain_ref = refs[6:]
    member = member_ref[0]
    for k in range(4):
        columns = head_columns(member ^ k)
        q_ref[:, columns] = pieces[k][:, :HS].astype(f32)
        o_ref[:, columns] = pieces[k][:, HS:].astype(f32)
    for h in range(2):
        columns = head_columns((member & 1) ^ h)
        k_ref[:, columns] = pieces[4 + h][:, :HS].astype(f32)
        v_ref[:, columns] = pieces[4 + h][:, HS:].astype(f32)

    def row_sum(weight_ref, grad_ref):
        return jnp.sum(weight_ref[...].astype(f32) * grad_ref[...], axis=1, keepdims=True)

    gain_ref[...] = row_sum(qw_ref, q_ref) + row_sum(kw_ref, k_ref) + row_sum(vw_ref, v_ref)


def attention_final(member, query_weight, key_weight, value_weight, pieces):
    rows, width = query_weight.shape
    shapes = [jax.ShapeDtypeStruct((rows, n), f32) for n in (width, width // 2, width // 2, width, 1)]
    return vmem_call(
        attention_final_kernel,
        "attention_final",
        shapes,
        member,
        query_weight,
        key_weight,
        value_weight,
        *pieces,
    )


def rms_inverse(values):
    return lax.rsqrt(jnp.mean(values * values, axis=-1, keepdims=True) + epsilon)


def rope_tables(positions):
    half_size = HS // 2
    indices = jnp.arange(half_size, dtype=f32)
    inverse = theta_base ** (-2.0 * indices / HS)
    angles = positions.astype(f32)[:, None] * inverse[None, :]
    return jnp.cos(angles), jnp.sin(angles)


def rotate(vectors, cos, sin):
    front, back = vectors[:, : HS // 2], vectors[:, HS // 2 :]
    return jnp.concatenate([front * cos - back * sin, back * cos + front * sin], axis=-1)


def unrotate(grads, cos, sin):
    front, back = grads[:, : HS // 2], grads[:, HS // 2 :]
    return jnp.concatenate([front * cos + back * sin, back * cos - front * sin], axis=-1)


def mlp_tile(width, normed, cot, weight_ref):
    both = product(normed, weight_ref[:, : 2 * width])
    d_inner = product(cot, weight_ref[:, 2 * width :])
    gate, upward = both[:, :width], both[:, width:]
    sig = 1.0 / (1.0 + jnp.exp(-gate))
    silu = gate * sig
    d_gate = d_inner * upward * sig * (1.0 + gate * (1.0 - sig))
    return (
        (silu * upward).astype(bf16),
        jnp.concatenate([d_gate, d_inner * silu], axis=1).astype(bf16),
    )


def mlp_kernel(width, normed_ref, cot_ref, weight_ref, inner_ref, grads_ref):
    inner_ref[...], grads_ref[...] = mlp_tile(
        width, normed_ref[...], cot_ref[...], weight_ref
    )


def tail_kernel(width, normed_ref, cot_ref, weight_ref, base_ref, *refs):
    inner_ref, grads_ref, front_ref, back_ref = refs[-4:]
    inner, grads = mlp_tile(width, normed_ref[...], cot_ref[...], weight_ref)
    inner_ref[...], grads_ref[...] = inner, grads
    total = times_transposed(grads, weight_ref[:, : 2 * width]) + base_ref[...]
    half = total.shape[1] // 2
    front_ref[...] = total[:, :half].astype(front_ref.dtype)
    back_ref[...] = total[:, half:].astype(back_ref.dtype)


def mlp_tail(normed, cot, weight, base, part, dtype, chained=()):
    tokens, features = normed.shape
    width = weight.shape[1] // 3
    tile, rows = 256, tokens // 2
    steps = rows // tile
    count = len(chained)
    return pl.pallas_call(
        functools.partial(tail_kernel, width),
        grid=(steps,),
        in_specs=[
            pl.BlockSpec((tile, features), lambda i: (part * steps + i, 0)),
            pl.BlockSpec((tile, features), lambda i: (part * steps + i, 0)),
            pl.BlockSpec((features, 3 * width), lambda i: (0, 0)),
            pl.BlockSpec((tile, features), lambda i: (i, 0)),
        ]
        + [pl.BlockSpec(memory_space=pl.ANY)] * count,
        out_specs=[
            pl.BlockSpec((tile, width), lambda i: (part * steps + i, 0)),
            pl.BlockSpec((tile, 2 * width), lambda i: (part * steps + i, 0)),
            pl.BlockSpec((tile, features // 2), lambda i: (i, 0)),
            pl.BlockSpec((tile, features // 2), lambda i: (i, 0)),
        ],
        out_shape=[
            jax.ShapeDtypeStruct((tokens, width), bf16),
            jax.ShapeDtypeStruct((tokens, 2 * width), bf16),
            jax.ShapeDtypeStruct((rows, features // 2), dtype),
            jax.ShapeDtypeStruct((rows, features // 2), dtype),
        ],
        input_output_aliases={4 + i: i for i in range(count)},
        cost_estimate=pl.CostEstimate(
            flops=10 * rows * features * width,
            bytes_accessed=2 * features * (5 * rows + 3 * width),
            transcendentals=rows * width,
        ),
        compiler_params=pltpu.CompilerParams(vmem_limit_bytes=VMEM_LIMIT),
        name="mlp_tail",
    )(normed, cot, weight, base, *chained)


def mlp_chunk(normed, cot, weight):
    tokens, features = normed.shape
    width = weight.shape[1] // 3
    tile = 256
    return pl.pallas_call(
        functools.partial(mlp_kernel, width),
        grid=(tokens // tile,),
        in_specs=[
            pl.BlockSpec((tile, features), lambda i: (i, 0)),
            pl.BlockSpec((tile, features), lambda i: (i, 0)),
            pl.BlockSpec((features, 3 * width), lambda i: (0, 0)),
        ],
        out_specs=[
            pl.BlockSpec((tile, width), lambda i: (i, 0)),
            pl.BlockSpec((tile, 2 * width), lambda i: (i, 0)),
        ],
        out_shape=[
            jax.ShapeDtypeStruct((tokens, width), bf16),
            jax.ShapeDtypeStruct((tokens, 2 * width), bf16),
        ],
        cost_estimate=pl.CostEstimate(
            flops=6 * tokens * features * width,
            bytes_accessed=2 * features * (2 * tokens + 3 * width),
            transcendentals=tokens * width,
        ),
        compiler_params=pltpu.CompilerParams(vmem_limit_bytes=VMEM_LIMIT),
        name="mlp_chunk",
    )(normed, cot, weight)


def sum_kernel(count, *refs):
    lefts, rights, out_ref = refs[:count], refs[count : 2 * count], refs[-1]
    total = times_transposed(lefts[0][...], rights[0][...])
    for left, right in zip(lefts[1:], rights[1:]):
        total += times_transposed(left[...], right[...])
    for base in refs[2 * count : -1]:
        total += base[...].astype(f32)
    out_ref[...] = total.astype(out_ref.dtype)


def chunk_sum(lefts, rights, column, part, half, dtype):
    count = len(lefts)
    tokens, features = lefts[0].shape[0], rights[0].shape[0]
    widths = [left.shape[1] for left in lefts]
    rows = tokens // 2
    tile = 256
    if half is not None:
        features, tile = features // 2, 512
    steps = rows // tile
    block = half or 0
    return pl.pallas_call(
        functools.partial(sum_kernel, count),
        grid=(steps,),
        in_specs=[pl.BlockSpec((tile, w), lambda i: (part * steps + i, 0)) for w in widths]
        + [pl.BlockSpec((features, w), lambda i: (block, column)) for w in widths],
        out_specs=pl.BlockSpec((tile, features), lambda i: (i, 0)),
        out_shape=jax.ShapeDtypeStruct((rows, features), dtype),
        cost_estimate=pl.CostEstimate(
            flops=2 * rows * features * sum(widths),
            bytes_accessed=2 * sum(widths) * (rows + features) + 4 * rows * features,
            transcendentals=0,
        ),
        compiler_params=pltpu.CompilerParams(vmem_limit_bytes=VMEM_LIMIT),
        name="chunk_sum",
    )(*lefts, *rights)


def grads_kernel(count, *refs):
    column = 0
    for left, right in zip(refs[:count], refs[count : 2 * count]):
        width = right.shape[1]
        refs[-1][:, column : column + width] = outer_sum(left[...], right[...]).astype(bf16)
        column += width


def weight_grads(*pairs):
    lefts = [left for left, _ in pairs]
    rights = [r if isinstance(r, tuple) else (r, r.shape[1], 0) for _, r in pairs]
    count = len(pairs)
    tokens, features = lefts[0].shape
    widths = [width for _, width, _ in rights]
    tile = 256

    def block(width, at):
        return pl.BlockSpec((tokens, width), lambda i: (0, at))

    return pl.pallas_call(
        functools.partial(grads_kernel, count),
        grid=(features // tile,),
        in_specs=[pl.BlockSpec((tokens, tile), lambda i: (0, i))] * count
        + [block(width, at) for _, width, at in rights],
        out_specs=pl.BlockSpec((tile, sum(widths)), lambda i: (i, 0)),
        out_shape=jax.ShapeDtypeStruct((features, sum(widths)), bf16),
        cost_estimate=pl.CostEstimate(
            flops=2 * tokens * features * sum(widths),
            bytes_accessed=2 * (count * tokens * features + sum(widths) * (tokens + features)),
            transcendentals=0,
        ),
        compiler_params=pltpu.CompilerParams(vmem_limit_bytes=VMEM_LIMIT),
        name="weight_grads",
    )(*lefts, *[array for array, _, _ in rights])


def project_kernel(place_ref, normed_ref, weight_ref, cos_ref, sin_ref, q_ref, k_ref, v_ref):
    step = pl.program_id(0)
    cos, sin = cos_ref[...], sin_ref[...]
    qkv = product(normed_ref[...], weight_ref[...])
    keys = rotate(qkv[:, :HS], cos, sin).astype(bf16)
    vals = qkv[:, HS : 2 * HS].astype(bf16)
    query = rotate(qkv[:, 2 * HS :], cos, sin).astype(bf16) * HS ** (-0.5)
    blocks = normed_ref.shape[0] // BLOCK
    for b in range(blocks):
        rows = pl.ds(pl.multiple_of(place_ref[step * blocks + b] * BLOCK, BLOCK), BLOCK)
        part = slice(b * BLOCK, (b + 1) * BLOCK)
        q_ref[rows, :] = query[part]
        k_ref[rows, :] = keys[part]
        v_ref[rows, :] = vals[part]


def project(place, normed, weight, cos, sin):
    tokens, features = normed.shape
    tile = 256
    whole = pl.BlockSpec((tokens, HS), lambda i, place: (0, 0))
    return pl.pallas_call(
        project_kernel,
        grid_spec=pltpu.PrefetchScalarGridSpec(
            num_scalar_prefetch=1,
            grid=(tokens // tile,),
            in_specs=[
                pl.BlockSpec((tile, features), lambda i, place: (i, 0)),
                pl.BlockSpec((features, 3 * HS), lambda i, place: (0, 0)),
                pl.BlockSpec((tile, HS // 2), lambda i, place: (i, 0)),
                pl.BlockSpec((tile, HS // 2), lambda i, place: (i, 0)),
            ],
            out_specs=[whole] * 3,
        ),
        out_shape=[jax.ShapeDtypeStruct((tokens, HS), bf16)] * 3,
        cost_estimate=pl.CostEstimate(
            flops=6 * tokens * features * HS,
            bytes_accessed=2 * features * (tokens + 3 * HS) + 10 * tokens * HS,
            transcendentals=0,
        ),
        compiler_params=pltpu.CompilerParams(vmem_limit_bytes=VMEM_LIMIT),
        name="project",
    )(place, normed, weight, cos, sin)


TILE = 256


def tile_masks():
    rows = lax.broadcasted_iota(jnp.int32, (TILE, TILE), 0)
    cols = lax.broadcasted_iota(jnp.int32, (TILE, TILE), 1)
    causal = rows >= cols
    return causal, causal & (rows // BLOCK == cols // BLOCK)


def block_rows(order_ref, index):
    return pl.ds(pl.multiple_of(order_ref[index] * BLOCK, BLOCK), BLOCK)


def forward_kernel(order_ref, q_ref, k_ref, v_ref, mixed_ref, lse_ref, peak_ref):
    causal, inside = tile_masks()
    prompt = GROUP // 2
    top = jnp.full((TILE, 1), masked_value, f32)
    for i in range(GROUP // TILE):
        rows = slice(i * TILE, (i + 1) * TILE)
        past = min(i * TILE, prompt)
        query = q_ref[rows, :]
        near = times_transposed(query, k_ref[rows, :])
        near = jnp.where(causal if i * TILE < prompt else inside, near, masked_value)
        peak = jnp.max(near, axis=1, keepdims=True)
        if past:
            far = times_transposed(query, k_ref[:past, :])
            peak = jnp.maximum(peak, jnp.max(far, axis=1, keepdims=True))
            far = jnp.exp(far - peak)
        near = jnp.exp(near - peak)
        total = jnp.sum(near, axis=1, keepdims=True)
        if past:
            total += jnp.sum(far, axis=1, keepdims=True)
        share = 1.0 / total
        mixed = product((near * share).astype(bf16), v_ref[rows, :])
        if past:
            mixed += product((far * share).astype(bf16), v_ref[:past, :])
        mixed = mixed.astype(bf16)
        for b in range(TILE // BLOCK):
            mixed_ref[block_rows(order_ref, i * (TILE // BLOCK) + b), :] = mixed[
                b * BLOCK : (b + 1) * BLOCK
            ]
        lse_ref[rows, :] = peak + jnp.log(total)
        top = jnp.maximum(top, peak)
    peak_ref[...] = jnp.full(peak_ref.shape, jnp.max(top), f32)


def attention_forward(order, query, keys, vals):
    whole = pl.BlockSpec(memory_space=pltpu.VMEM)
    return pl.pallas_call(
        forward_kernel,
        in_specs=[pl.BlockSpec(memory_space=pltpu.SMEM), whole, whole, whole],
        out_specs=[whole] * 3,
        out_shape=[
            jax.ShapeDtypeStruct((GROUP, HS), bf16),
            jax.ShapeDtypeStruct((GROUP, 1), f32),
            jax.ShapeDtypeStruct((8, 128), f32),
        ],
        cost_estimate=pl.CostEstimate(
            flops=2 * GROUP * GROUP * HS,
            bytes_accessed=8 * GROUP * HS,
            transcendentals=GROUP * GROUP // 2,
        ),
        compiler_params=pltpu.CompilerParams(vmem_limit_bytes=VMEM_LIMIT),
        name="attention_forward",
    )(order, query, keys, vals)


def backward_kernel(
    order_ref, q_ref, k_ref, v_ref, lse_ref, mixed_ref, cos_ref, sin_ref, out_ref, dk_ref, dv_ref
):
    causal, inside = tile_masks()
    prompt = GROUP // 2
    blocks = TILE // BLOCK

    def back(grad, index):
        rows = block_rows(order_ref, index)
        return rows, unrotate(grad, cos_ref[rows, :], sin_ref[rows, :]).astype(bf16)

    for i in range(GROUP // TILE):
        rows = slice(i * TILE, (i + 1) * TILE)
        past = min(i * TILE, prompt)
        query, lse = q_ref[rows, :], lse_ref[rows, :]
        d_mixed = jnp.concatenate(
            [mixed_ref[block_rows(order_ref, i * blocks + b), :] for b in range(blocks)], axis=0
        )
        near = times_transposed(query, k_ref[rows, :])
        near = jnp.where(causal if i * TILE < prompt else inside, near, masked_value)
        near = jnp.exp(near - lse)
        d_near = times_transposed(d_mixed, v_ref[rows, :])
        inner = jnp.sum(near * d_near, axis=1, keepdims=True)
        if past:
            far = jnp.exp(times_transposed(query, k_ref[:past, :]) - lse)
            d_far = times_transposed(d_mixed, v_ref[:past, :])
            inner += jnp.sum(far * d_far, axis=1, keepdims=True)
        d_near = (near * (d_near - inner)).astype(bf16)
        d_query = product(d_near, k_ref[rows, :])
        dk_ref[rows, :] = outer_sum(d_near, query)
        dv_ref[rows, :] = outer_sum(near.astype(bf16), d_mixed)
        if past:
            d_far = (far * (d_far - inner)).astype(bf16)
            d_query += product(d_far, k_ref[:past, :])
            dk_ref[:past, :] += outer_sum(d_far, query)
            dv_ref[:past, :] += outer_sum(far.astype(bf16), d_mixed)
        d_query = d_query * HS ** (-0.5)
        for b in range(blocks):
            where, grad = back(d_query[b * BLOCK : (b + 1) * BLOCK], i * blocks + b)
            out_ref[where, 2 * HS :] = grad
    for c in range(GROUP // BLOCK):
        part = slice(c * BLOCK, (c + 1) * BLOCK)
        where, grad = back(dk_ref[part, :], c)
        out_ref[where, :HS] = grad
        out_ref[where, HS : 2 * HS] = dv_ref[part, :].astype(bf16)


def attention_backward(order, query, keys, vals, lse, d_mixed, cos, sin):
    whole = pl.BlockSpec(memory_space=pltpu.VMEM)
    return pl.pallas_call(
        backward_kernel,
        in_specs=[pl.BlockSpec(memory_space=pltpu.SMEM)] + [whole] * 7,
        out_specs=whole,
        out_shape=jax.ShapeDtypeStruct((GROUP, 3 * HS), bf16),
        scratch_shapes=[pltpu.VMEM((GROUP, HS), f32), pltpu.VMEM((GROUP, HS), f32)],
        cost_estimate=pl.CostEstimate(
            flops=5 * GROUP * GROUP * HS,
            bytes_accessed=20 * GROUP * HS,
            transcendentals=GROUP * GROUP // 2,
        ),
        compiler_params=pltpu.CompilerParams(vmem_limit_bytes=VMEM_LIMIT),
        name="attention_backward",
    )(order, query, keys, vals, lse, d_mixed, cos, sin)


def local(
    tokens,
    cotangent,
    segment,
    position,
    clip_limit,
    attn_gain,
    query_weight,
    key_weight,
    value_weight,
    output_weight,
    mlp_gain,
    gate_weight,
    up_weight,
    down_weight,
):
    groups = lax.axis_size("group")
    group = lax.axis_index("group")
    core = lax.axis_index("tp")
    member = lax.axis_index(PLANE)
    token_rows = tokens.shape[0]
    own_rows, features = query_weight.shape[0], tokens.shape[1]
    hidden_own = gate_weight.shape[1] // 4
    chunks, offset = [], 0
    for part in SIXTEENTHS:
        chunks.append((offset, hidden_own * part // 16))
        offset += hidden_own * part // 16
    member_at = member.astype(jnp.int32).reshape(1)

    def own_order(array):
        parts = []
        for j in range(2):
            for k in range(4):
                start = group * GROUP + (member ^ k) * (2 * token_rows) + (core ^ j) * token_rows
                parts.append(lax.dynamic_slice_in_dim(array, start, token_rows))
        return jnp.concatenate(parts)

    def collect(blocks):
        return lax.all_gather(blocks, "group", axis=0, tiled=True)

    def mlp_exchange(some, waits):
        weights = [after(a, *waits) for a in (gate_weight, up_weight, down_weight)]
        spans = tuple((start, hidden_own, count, 0) for start, count in some for _ in range(3))
        return swap_all(split(member_at, weights * len(some), spans))

    seg, pos = own_order(segment), own_order(position)
    cos, sin = rope_tables(pos)
    seg_blocks, pos_blocks = seg[::BLOCK], pos[::BLOCK]
    half_blocks = GROUP // BLOCK // 2
    place = jnp.where(seg_blocks == 0, pos_blocks // BLOCK, half_blocks - 1 + seg_blocks)
    labels = jnp.arange(2 * half_blocks, dtype=jnp.int32)
    order = jnp.sum(jnp.where(place[None, :] == labels[:, None], labels[None, :], 0), axis=1)
    index = lax.axis_index(FSDP)
    gains = jnp.stack([attn_gain, mlp_gain])[:, None, :]
    gains = jnp.where(jnp.arange(4 * groups)[None, :, None] == index, gains, 0)
    gains, gain_rounds = combine_all(gains, groups, lambda a, b: a + b)
    gains = gains.reshape(2, features).astype(f32)
    head, pair = (0, HS, HS, 0), (0, HS, HS, 1)
    attn_pieces = swap_all(
        split(
            member_at,
            (key_weight, value_weight, query_weight, output_weight),
            (pair, pair, head, head),
        )
    )
    (attn_blocks,) = place_rows(
        member_at, attn_pieces
    )
    attn_weights = collect(attn_blocks)
    late_tokens = after(tokens, *attn_pieces[1:])
    neighbours = plane_neighbours(late_tokens)
    tokens_far = plane_far(neighbours)
    tokens_mine = [late_tokens, *neighbours, *tokens_far]
    tokens_near = [swap(piece, "tp") for piece in tokens_mine[:3]]
    normed_all = pack_normed(
        with_partner(tokens_mine, tokens_near), gains[:1], (cos, sin, place, order)
    )
    pieces_0 = mlp_exchange(chunks[:1], (*tokens_far, *tokens_near))
    (blocks_0,) = place_rows(
        member_at, [after(pieces_0[0], normed_all, *gain_rounds[-1])] + pieces_0[1:]
    )
    late_cot = after(cotangent, *pieces_0[1:])
    cot_near = plane_neighbours(late_cot)
    pieces_1 = mlp_exchange(chunks[1:], cot_near)
    query, keys, vals = project(
        place, normed_all, attn_weights, cos, sin
    )
    mixed, logsum, peak = attention_forward(
        order, after(query, *cot_near), keys, vals
    )

    head_top = jnp.where(jnp.arange(4) == member, peak[0, :4], masked_value)
    head_top, head_rounds = combine_all(head_top, groups, jnp.maximum)

    def projected(left, column, waits=(), others=()):
        lefts = (after(left, *others) if others else left, after(left, *waits) if waits else left)
        return [
            [
                chunk_sum([lefts[j]], [attn_weights], column, j, h, bf16 if j else f32)
                for j in (0, 1)
            ]
            for h in range(2)
        ]

    attn_sums = chip_sums(*projected(mixed, 3, pieces_1[1:]))
    arrived = reduce_first(first_operands(attn_sums))
    attn_operands = reduce_operands(attn_sums, arrived)
    attn_last = last_swaps(attn_operands, *head_rounds[0])
    hidden, own_normed = add_and_norm(attn_operands, attn_last, tokens, gains[1:])
    neighbours = plane_neighbours(own_normed)
    normed_far = plane_far(neighbours, *head_rounds[-1])
    cot_far = plane_far(cot_near, *normed_far)
    mlp_weights = [collect(blocks_0), collect(*place_rows(member_at, pieces_1))]
    normed_mlp = pack(with_partner([own_normed, *neighbours, *normed_far]))
    cot_all = pack(with_partner([late_cot, *cot_near, *cot_far]))

    def line_sum(partial):
        return lax.psum_scatter(partial, "group", scatter_dimension=0, tiled=True)

    inner_0, both_0 = mlp_chunk(normed_mlp, cot_all, mlp_weights[0])
    grads_0 = weight_grads((normed_mlp, both_0), (cot_all, inner_0))
    sum_0 = line_sum(grads_0)
    late_both = after(both_0, grads_0)
    early = [chunk_sum([late_both], mlp_weights[:1], 0, j, None, f32) for j in range(2)]
    inner_1, both_1, front_1, back_1 = mlp_tail(
        after(normed_mlp, *early), cot_all, mlp_weights[1], early[1], 1, bf16
    )
    inner_1, both_1, front_0, back_0 = mlp_tail(
        normed_mlp, cot_all, mlp_weights[1], early[0], 0, f32, (inner_1, both_1)
    )

    mlp_sums = chip_sums((front_0, front_1), (back_0, back_1))
    operands = first_operands(mlp_sums)
    arrived = reduce_first(operands)
    inners = [after(inner, *operands) for inner in (inner_0, inner_1)]
    out_parts = [
        [chunk_sum(inners, mlp_weights, 2, j, h, bf16 if j else f32) for j in (0, 1)]
        for h in range(2)
    ]
    mlp_operands = reduce_operands(mlp_sums, arrived)
    mlp_last = last_swaps(mlp_operands, *out_parts[0], *out_parts[1])
    d_hidden, own_d = norm_back(
        mlp_operands, mlp_last, hidden, cotangent, gains[1:], (f32, bf16)
    )
    neighbours = plane_neighbours(own_d)
    late_both = after(both_1, own_d)
    grads_1 = weight_grads((normed_mlp, late_both), (cot_all, inner_1))
    sum_1 = line_sum(after(grads_1, *neighbours))
    d_far = plane_far(neighbours, grads_1)
    d_attn_all = pack(with_partner([own_d, *neighbours, *d_far]))
    out_sums = chip_sums(*out_parts)
    out_arrived = reduce_first(first_operands(out_sums), *d_far)
    out_operands = reduce_operands(out_sums, out_arrived)
    out_last = last_swaps(out_operands)

    def send_grads(sources, *waits):
        first = after(sources[0], *waits) if waits else sources[0]
        return swap_all(pick_rows(member_at, first, *sources[1:]))


    final_0 = send_grads([sum_0], *out_arrived)
    d_mixed = product(d_attn_all, attn_weights[:, 3 * HS :]).astype(bf16)
    d_qkv = attention_backward(
        order, query, keys, vals, logsum, d_mixed, cos, sin
    )
    pair_grads = weight_grads((normed_all, (after(d_qkv, *out_arrived), 2 * HS, 0)))
    half_shape = jax.ShapeDtypeStruct((features // 2, 2 * HS), bf16)
    keep, send = vmem_call(
        functools.partial(halves_kernel, own_rows),
        "halves",
        [half_shape] * 2,
        member_at,
        pair_grads,
    )
    got = swap(send, "col")
    both_grads = weight_grads(
        (normed_all, (after(d_qkv, keep), HS, 2)), (d_attn_all, mixed)
    )
    late_qkv = after(d_qkv, both_grads, *out_last, *final_0[1:])
    qkv_parts = projected(late_qkv, 0)
    (attn_grads,) = vmem_call(
        functools.partial(join_kernel, own_rows),
        "join",
        [jax.ShapeDtypeStruct((features, 3 * HS), bf16)],
        member_at,
        after(keep, qkv_parts[0][1], qkv_parts[1][1]),
        got,
        both_grads,
    )
    attn_sum = line_sum(attn_grads)
    qkv_sums = chip_sums(*qkv_parts)
    final_1 = send_grads([sum_1], attn_grads)
    arrived = reduce_first(first_operands(qkv_sums), *final_1[1:])
    qkv_operands = reduce_operands(qkv_sums, arrived)
    qkv_last = last_swaps(qkv_operands)
    (tokens_grad,) = norm_back(qkv_operands, qkv_last, tokens, d_hidden, gains[:1], (f32,))
    block_out = add_sum(out_operands, out_last, hidden)

    gate_grad, up_grad, down_grad, mlp_gain_row = mlp_final(
        member_at, gate_weight, up_weight, (chunks[:1], chunks[1:]), [final_0, final_1]
    )
    attn_parts = attention_return(
        member_at, after(attn_sum, *qkv_last, mlp_gain_row, block_out)
    )
    query_grad, key_grad, value_grad, output_grad, attn_gain_row = attention_final(
        member_at,
        query_weight,
        key_weight,
        value_weight,
        [after(attn_parts[0], tokens_grad)] + attn_parts[1:],
    )
    gain_grads = jnp.concatenate([attn_gain_row, mlp_gain_row], axis=1)
    gain_grads = gain_grads + swap(gain_grads, "tp")
    attn_gain_grad = gain_grads[:, 0] / attn_gain.astype(f32)
    mlp_gain_grad = gain_grads[:, 1] / mlp_gain.astype(f32)

    factor = clip_limit / jnp.maximum(head_top, clip_limit)
    query_scale = jnp.repeat(jnp.sqrt(factor), HS)
    key_factor = jnp.min(factor.reshape(2, 2), axis=1)
    key_scale = jnp.repeat(jnp.sqrt(key_factor), HS)
    query_clipped = (query_weight.astype(f32) * query_scale[None, :]).astype(bf16)
    key_clipped = (key_weight.astype(f32) * key_scale[None, :]).astype(bf16)
    return (
        block_out,
        tokens_grad,
        attn_gain_grad,
        query_grad,
        key_grad,
        value_grad,
        output_grad,
        mlp_gain_grad,
        gate_grad,
        up_grad,
        down_grad,
        head_top,
        query_clipped,
        key_clipped,
    )


def solution(mesh):
    shape = (mesh.shape["fsdp"] // 4, 2, 2, mesh.shape["tp"])
    fine = Mesh(mesh.devices.reshape(shape), ("group", "row", "col", "tp"))
    rows = P(("group", "row", "col", "tp"), None)
    weight = P(FSDP, "tp")
    gain = P(FSDP)
    heads = P("tp")
    return jax.shard_map(
        local,
        mesh=fine,
        in_specs=(
            rows, rows, P(), P(), heads, gain, weight, weight, weight, weight,
            gain, weight, weight, weight,
        ),
        out_specs=(
            rows, rows, gain, weight, weight, weight, weight, gain, weight, weight, weight,
            heads, weight, weight,
        ),
        check_vma=False,
    )
```

```python
import functools

import jax
import jax.numpy as jnp
from jax import lax
from jax.experimental import pallas as pl
from jax.experimental.pallas import tpu as pltpu
from jax.sharding import Mesh, PartitionSpec as P

HS = 256
GROUP = 2048
SIXTEENTHS = (10, 6)
BLOCK = 128

epsilon = 1e-05
theta_base = 1000042.0
masked_value = -1e30

bf16 = jnp.bfloat16
f32 = jnp.float32
PLANE = ("row", "col")
FSDP = ("group", "row", "col")
VMEM_LIMIT = 48 * 1024 * 1024


def product(left, right):
    return jnp.dot(left, right, preferred_element_type=f32)


def times_transposed(left, right):
    return lax.dot_general(left, right, (((1,), (1,)), ((), ())), preferred_element_type=f32)


def outer_sum(left, right):
    return lax.dot_general(left, right, (((0,), (0,)), ((), ())), preferred_element_type=f32)


def take(array, index, axis=0):
    return lax.dynamic_index_in_dim(array, index, axis, keepdims=False)


def swap(block, axis):
    return lax.ppermute(block, axis, [(0, 1), (1, 0)])


def swap_plane(block, distance):
    return lax.ppermute(block, PLANE, [(i, i ^ distance) for i in range(4)])


def after(value, *others):
    return lax.optimization_barrier((value,) + others)[0]


def combine_all(values, groups, combine):
    distance, count = 1, 4 * groups
    rounds = []
    while distance < count:
        arrived = []
        for step in range(1, min(4, count // distance)):
            route = [(i, i ^ step * distance) for i in range(count)]
            arrived.append(lax.ppermute(values, FSDP, route))
        for other in arrived:
            values = combine(values, other)
        rounds.append(arrived)
        distance *= 4
    return values, rounds


def pack_kernel(count, *refs):
    out_ref, sems = refs[count], refs[count + 1]
    copies, start = [], 0
    for i in range(count):
        rows = refs[i].shape[0]
        copy = pltpu.make_async_copy(refs[i], out_ref.at[pl.ds(start, rows)], sems.at[i])
        copy.start()
        copies.append(copy)
        start += rows
    for copy in copies:
        copy.wait()


def pack(pieces):
    rows, width = sum(p.shape[0] for p in pieces), pieces[0].shape[1]
    count = len(pieces)
    return pl.pallas_call(
        functools.partial(pack_kernel, count),
        in_specs=[pl.BlockSpec(memory_space=pl.ANY)] * count,
        out_specs=pl.BlockSpec(memory_space=pltpu.VMEM),
        out_shape=jax.ShapeDtypeStruct((rows, width), pieces[0].dtype),
        scratch_shapes=[pltpu.SemaphoreType.DMA((count,))],
        cost_estimate=pl.CostEstimate(
            flops=0, bytes_accessed=4 * rows * width, transcendentals=0
        ),
        compiler_params=pltpu.CompilerParams(vmem_limit_bytes=VMEM_LIMIT),
        name="pack",
    )(*pieces)


def norm_kernel(count, *refs):
    gain_ref, out_ref = refs[count], refs[-2]
    pack_kernel(count, *refs[:count], *refs[-2:])
    tile = 256

    @pl.loop(0, out_ref.shape[0] // tile)
    def _(i):
        rows = pl.ds(pl.multiple_of(i * tile, tile), tile)
        values = out_ref[rows, :].astype(f32)
        out_ref[rows, :] = (values * rms_inverse(values) * gain_ref[...]).astype(bf16)


def pack_normed(pieces, gain, early):
    rows, width = sum(p.shape[0] for p in pieces), pieces[0].shape[1]
    count = len(pieces)
    return pl.pallas_call(
        functools.partial(norm_kernel, count),
        in_specs=[pl.BlockSpec(memory_space=pl.ANY)] * count
        + [pl.BlockSpec(memory_space=pltpu.VMEM)]
        + [pl.BlockSpec(memory_space=pl.ANY)] * len(early),
        out_specs=pl.BlockSpec(memory_space=pltpu.VMEM),
        out_shape=jax.ShapeDtypeStruct((rows, width), bf16),
        scratch_shapes=[pltpu.SemaphoreType.DMA((count,))],
        cost_estimate=pl.CostEstimate(
            flops=8 * rows * width, bytes_accessed=4 * rows * width, transcendentals=0
        ),
        compiler_params=pltpu.CompilerParams(vmem_limit_bytes=VMEM_LIMIT),
        name="pack_normed",
    )(*pieces, gain, *early)


def plane_neighbours(own):
    return swap(own, "col"), swap(own, "row")


def plane_far(neighbours, *waits):
    across, along = neighbours
    half = across.shape[0] // 2
    return (
        swap(after(across[:half], *waits), "row"),
        swap(after(along[half:], *waits), "col"),
    )


def with_partner(pieces, swapped=()):
    return pieces + list(swapped) + [swap(piece, "tp") for piece in pieces[len(swapped) :]]


def chip_sums(front, back):
    pairs = []
    for own, other in (front, back):
        shape = (4, own.shape[0] // 4, own.shape[1])
        pairs.append((own.reshape(shape), swap(other, "tp").reshape(shape)))
    return pairs


def quarter(pair, k):
    return pair[0][k].astype(f32) + pair[1][k].astype(f32)


def first_operands(sums):
    front, back = sums
    return (
        jnp.concatenate([quarter(front, 1), quarter(front, 3)]).astype(bf16),
        (back[0][2:].astype(f32) + back[1][2:].astype(f32)).astype(bf16),
    )


def reduce_first(operands, *waits):
    front, back = operands
    rows = front.shape[0] // 2
    return (
        swap(after(front, *waits), "col").reshape(2, rows, -1),
        swap(after(back, *waits), "row"),
    )


def reduce_operands(sums, arrived):
    front, back = sums
    got, got_back = arrived[0].astype(f32), arrived[1].astype(f32)
    return (
        (quarter(front, 0) + got[0], (quarter(front, 2) + got[1]).astype(bf16)),
        (quarter(back, 0) + got_back[0], (quarter(back, 1) + got_back[1]).astype(bf16)),
    )


def last_swaps(operands, *waits):
    return (
        swap(after(operands[0][1], *waits), "row"),
        swap(after(operands[1][1], *waits), "col"),
    )


def joined(front_ref, front_last_ref, back_ref, back_last_ref):
    return jnp.concatenate(
        [
            front_ref[...] + front_last_ref[...].astype(f32),
            back_ref[...] + back_last_ref[...].astype(f32),
        ],
        axis=1,
    )


def hidden_kernel(front, front_last, back, back_last, tokens_ref, gain_ref, hidden_ref, normed_ref):
    hidden = tokens_ref[...].astype(f32) + joined(front, front_last, back, back_last)
    hidden_ref[...] = hidden
    normed_ref[...] = (hidden * rms_inverse(hidden) * gain_ref[...]).astype(bf16)


def add_and_norm(operands, last, tokens, gain):
    halves = [part for (keep, _), got in zip(operands, last) for part in (keep, got)]
    return pl.pallas_call(
        hidden_kernel,
        in_specs=[pl.BlockSpec(memory_space=pltpu.VMEM)] * 6,
        out_specs=[pl.BlockSpec(memory_space=pltpu.VMEM)] * 2,
        out_shape=[
            jax.ShapeDtypeStruct(tokens.shape, f32),
            jax.ShapeDtypeStruct(tokens.shape, bf16),
        ],
        cost_estimate=pl.CostEstimate(
            flops=10 * tokens.size, bytes_accessed=14 * tokens.size, transcendentals=0
        ),
        compiler_params=pltpu.CompilerParams(vmem_limit_bytes=VMEM_LIMIT),
        name="add_and_norm",
    )(*halves, tokens, gain)


def out_kernel(front, front_last, back, back_last, hidden_ref, out_ref):
    out_ref[...] = (hidden_ref[...] + joined(front, front_last, back, back_last)).astype(bf16)


def add_sum(operands, last, hidden):
    halves = [part for (keep, _), got in zip(operands, last) for part in (keep, got)]
    return pl.pallas_call(
        out_kernel,
        in_specs=[pl.BlockSpec(memory_space=pltpu.VMEM)] * 5,
        out_specs=pl.BlockSpec(memory_space=pltpu.VMEM),
        out_shape=jax.ShapeDtypeStruct(hidden.shape, bf16),
        cost_estimate=pl.CostEstimate(
            flops=2 * hidden.size, bytes_accessed=12 * hidden.size, transcendentals=0
        ),
        compiler_params=pltpu.CompilerParams(vmem_limit_bytes=VMEM_LIMIT),
        name="add_sum",
    )(*halves, hidden)


def back_kernel(front, front_last, back, back_last, values_ref, base_ref, gain_ref, *outs):
    values = values_ref[...].astype(f32)
    inverse = rms_inverse(values)
    unit = values * inverse
    scaled = joined(front, front_last, back, back_last) * gain_ref[...]
    grad = base_ref[...].astype(f32) + inverse * (
        scaled - unit * jnp.mean(scaled * unit, axis=-1, keepdims=True)
    )
    for out in outs:
        out[...] = grad.astype(out.dtype)


def norm_back(operands, last, values, base, gain, dtypes):
    halves = [part for (keep, _), got in zip(operands, last) for part in (keep, got)]
    return pl.pallas_call(
        back_kernel,
        in_specs=[pl.BlockSpec(memory_space=pltpu.VMEM)] * 7,
        out_specs=[pl.BlockSpec(memory_space=pltpu.VMEM)] * len(dtypes),
        out_shape=[jax.ShapeDtypeStruct(values.shape, dtype) for dtype in dtypes],
        cost_estimate=pl.CostEstimate(
            flops=16 * values.size, bytes_accessed=18 * values.size, transcendentals=0
        ),
        compiler_params=pltpu.CompilerParams(vmem_limit_bytes=VMEM_LIMIT),
        name="norm_back",
    )(*halves, values, base, gain)


def split_kernel(spans, member_ref, *refs):
    sources, outs = refs[: len(spans)], refs[len(spans) :]
    for k in range(4):
        target = member_ref[0] ^ k
        column = 0
        for source, (offset, stride, width, shift) in zip(sources, spans):
            start = pl.multiple_of((target >> shift) * stride + offset, 128)
            outs[k][:, column : column + width] = source[:, pl.ds(start, width)]
            column += width


def split(member, sources, spans):
    rows, width = sources[0].shape[0], sum(span[2] for span in spans)
    whole = pl.BlockSpec(memory_space=pltpu.VMEM)
    return pl.pallas_call(
        functools.partial(split_kernel, spans),
        in_specs=[pl.BlockSpec(memory_space=pltpu.SMEM)] + [whole] * len(sources),
        out_specs=[whole] * 4,
        out_shape=[jax.ShapeDtypeStruct((rows, width), bf16)] * 4,
        cost_estimate=pl.CostEstimate(
            flops=0, bytes_accessed=16 * rows * width, transcendentals=0
        ),
        compiler_params=pltpu.CompilerParams(vmem_limit_bytes=VMEM_LIMIT),
        name="split",
    )(member, *sources)


def place_kernel(member_ref, *refs):
    rows = refs[0].shape[0]
    for k in range(4):
        start = pl.multiple_of((member_ref[0] ^ k) * rows, rows)
        column = 0
        for out_ref in refs[4:]:
            width = out_ref.shape[1]
            out_ref[pl.ds(start, rows), :] = refs[k][:, column : column + width]
            column += width


def place_rows(member, pieces, *widths):
    rows, width = pieces[0].shape
    whole = pl.BlockSpec(memory_space=pltpu.VMEM)
    return pl.pallas_call(
        place_kernel,
        in_specs=[pl.BlockSpec(memory_space=pltpu.SMEM)] + [whole] * 4,
        out_specs=[whole] * len(widths or (width,)),
        out_shape=[
            jax.ShapeDtypeStruct((4 * rows, w), bf16) for w in widths or (width,)
        ],
        cost_estimate=pl.CostEstimate(
            flops=0, bytes_accessed=16 * rows * width, transcendentals=0
        ),
        compiler_params=pltpu.CompilerParams(vmem_limit_bytes=VMEM_LIMIT),
        name="place_rows",
    )(member, *pieces)


def pick_kernel(member_ref, *refs):
    sources, outs = refs[:-4], refs[-4:]
    rows = outs[0].shape[0]
    for k in range(4):
        start = pl.multiple_of((member_ref[0] ^ k) * rows, rows)
        column = 0
        for source in sources:
            width = source.shape[1]
            outs[k][:, column : column + width] = source[pl.ds(start, rows), :]
            column += width


def pick_rows(member, *sources):
    rows, width = sources[0].shape[0] // 4, sum(source.shape[1] for source in sources)
    whole = pl.BlockSpec(memory_space=pltpu.VMEM)
    return pl.pallas_call(
        pick_kernel,
        in_specs=[pl.BlockSpec(memory_space=pltpu.SMEM)] + [whole] * len(sources),
        out_specs=[whole] * 4,
        out_shape=[jax.ShapeDtypeStruct((rows, width), bf16)] * 4,
        cost_estimate=pl.CostEstimate(
            flops=0, bytes_accessed=16 * rows * width, transcendentals=0
        ),
        compiler_params=pltpu.CompilerParams(vmem_limit_bytes=VMEM_LIMIT),
        name="pick_rows",
    )(member, *sources)


def swap_all(pieces):
    return [pieces[0]] + [swap_plane(pieces[k], k) for k in (1, 2, 3)]


def mlp_final_kernel(parts, stride, member_ref, gate_w_ref, up_w_ref, *refs):
    pieces, outs, gain_ref = refs[:-4], refs[-4:-1], refs[-1]
    for n, chunks in enumerate(parts):
        for k in range(4):
            start = 0
            for offset, width in chunks:
                column = pl.multiple_of((member_ref[0] ^ k) * stride + offset, 128)
                for i in range(3):
                    part = pieces[4 * n + k][:, start : start + width]
                    outs[i][:, pl.ds(column, width)] = part.astype(f32)
                    start += width
    gain_ref[...] = jnp.sum(
        gate_w_ref[...].astype(f32) * outs[0][...] + up_w_ref[...].astype(f32) * outs[1][...],
        axis=1,
        keepdims=True,
    )


def mlp_final(member, gate_weight, up_weight, chunks, parts):
    rows, hidden = gate_weight.shape
    pieces = [piece for part in parts for piece in part]
    whole = pl.BlockSpec(memory_space=pltpu.VMEM)
    return pl.pallas_call(
        functools.partial(mlp_final_kernel, chunks, hidden // 4),
        in_specs=[pl.BlockSpec(memory_space=pltpu.SMEM)] + [whole] * (2 + len(pieces)),
        out_specs=[whole] * 4,
        out_shape=[jax.ShapeDtypeStruct((rows, hidden), f32)] * 3
        + [jax.ShapeDtypeStruct((rows, 1), f32)],
        cost_estimate=pl.CostEstimate(
            flops=4 * rows * hidden, bytes_accessed=22 * rows * hidden, transcendentals=0
        ),
        compiler_params=pltpu.CompilerParams(vmem_limit_bytes=VMEM_LIMIT),
        name="mlp_final",
    )(member, gate_weight, up_weight, *pieces)


TURN = [(0, 0), (1, 2), (2, 1), (3, 3)]
CROSS = [(0, 2), (1, 0), (2, 3), (3, 1)]
CROSS_BACK = [(2, 0), (0, 1), (3, 2), (1, 3)]


def vmem_call(kernel, name, out_shape, *operands):
    whole = pl.BlockSpec(memory_space=pltpu.VMEM)
    moved = sum(a.size * a.dtype.itemsize for a in operands)
    moved += sum(a.size * a.dtype.itemsize for a in out_shape)
    return pl.pallas_call(
        kernel,
        in_specs=[pl.BlockSpec(memory_space=pltpu.SMEM)] + [whole] * (len(operands) - 1),
        out_specs=[whole] * len(out_shape),
        out_shape=out_shape,
        cost_estimate=pl.CostEstimate(flops=0, bytes_accessed=moved, transcendentals=0),
        compiler_params=pltpu.CompilerParams(vmem_limit_bytes=VMEM_LIMIT),
        name=name,
    )(*operands)


def head_columns(index):
    return pl.ds(pl.multiple_of(index * HS, HS), HS)


def halves_kernel(rows, member_ref, grads_ref, keep_ref, send_ref):
    half = (member_ref[0] & 1) * 2 * rows
    for i, base in enumerate(range(0, grads_ref.shape[0], 4 * rows)):
        part = slice(i * 2 * rows, (i + 1) * 2 * rows)
        mine = pl.ds(pl.multiple_of(base + half, 2 * rows), 2 * rows)
        other = pl.ds(pl.multiple_of(base + 2 * rows - half, 2 * rows), 2 * rows)
        keep_ref[part, :] = grads_ref[mine, :]
        send_ref[part, :] = grads_ref[other, :]


def join_kernel(rows, member_ref, keep_ref, got_ref, both_ref, out_ref):
    out_ref[:, : 2 * HS] = both_ref[...]
    for i, base in enumerate(range(0, out_ref.shape[0], 4 * rows)):
        part = slice(i * 2 * rows, (i + 1) * 2 * rows)
        total = (keep_ref[part, :].astype(f32) + got_ref[part, :].astype(f32)).astype(bf16)
        out_ref[base : base + 2 * rows, 2 * HS :] = total[:, :HS]
        out_ref[base + 2 * rows : base + 4 * rows, 2 * HS :] = total[:, HS:]


def attention_pick_kernel(member_ref, source_ref, *outs):
    member, rows = member_ref[0], outs[0].shape[0]
    for k in range(4):
        at = pl.ds(pl.multiple_of((member ^ k) * rows, rows), rows)
        outs[k][...] = source_ref[at, : 2 * HS]
    for h in range(2):
        start = ((member >> 1) ^ h) * rows
        at = pl.ds(pl.multiple_of(start, rows), rows)
        outs[4 + h][:, :HS] = source_ref[at, 2 * HS :]
        at = pl.ds(pl.multiple_of(start + 2 * rows, rows), rows)
        outs[4 + h][:, HS:] = source_ref[at, 2 * HS :]


def attention_return(member, reduced):
    rows = reduced.shape[0] // 4
    *both, turned, crossed = vmem_call(
        attention_pick_kernel,
        "attention_pick",
        [jax.ShapeDtypeStruct((rows, 2 * HS), bf16)] * 6,
        member,
        reduced,
    )
    return swap_all(both) + [
        lax.ppermute(turned, PLANE, TURN),
        lax.ppermute(crossed, PLANE, CROSS_BACK),
    ]


def attention_final_kernel(member_ref, qw_ref, kw_ref, vw_ref, *refs):
    pieces = refs[:6]
    q_ref, k_ref, v_ref, o_ref, gain_ref = refs[6:]
    member = member_ref[0]
    for k in range(4):
        columns = head_columns(member ^ k)
        q_ref[:, columns] = pieces[k][:, :HS].astype(f32)
        o_ref[:, columns] = pieces[k][:, HS:].astype(f32)
    for h in range(2):
        columns = head_columns((member & 1) ^ h)
        k_ref[:, columns] = pieces[4 + h][:, :HS].astype(f32)
        v_ref[:, columns] = pieces[4 + h][:, HS:].astype(f32)

    def row_sum(weight_ref, grad_ref):
        return jnp.sum(weight_ref[...].astype(f32) * grad_ref[...], axis=1, keepdims=True)

    gain_ref[...] = row_sum(qw_ref, q_ref) + row_sum(kw_ref, k_ref) + row_sum(vw_ref, v_ref)


def attention_final(member, query_weight, key_weight, value_weight, pieces):
    rows, width = query_weight.shape
    shapes = [jax.ShapeDtypeStruct((rows, n), f32) for n in (width, width // 2, width // 2, width, 1)]
    return vmem_call(
        attention_final_kernel,
        "attention_final",
        shapes,
        member,
        query_weight,
        key_weight,
        value_weight,
        *pieces,
    )


def rms_inverse(values):
    return lax.rsqrt(jnp.mean(values * values, axis=-1, keepdims=True) + epsilon)


def rope_tables(positions):
    half_size = HS // 2
    indices = jnp.arange(half_size, dtype=f32)
    inverse = theta_base ** (-2.0 * indices / HS)
    angles = positions.astype(f32)[:, None] * inverse[None, :]
    return jnp.cos(angles), jnp.sin(angles)


def rotate(vectors, cos, sin):
    front, back = vectors[:, : HS // 2], vectors[:, HS // 2 :]
    return jnp.concatenate([front * cos - back * sin, back * cos + front * sin], axis=-1)


def unrotate(grads, cos, sin):
    front, back = grads[:, : HS // 2], grads[:, HS // 2 :]
    return jnp.concatenate([front * cos + back * sin, back * cos - front * sin], axis=-1)


def mlp_tile(width, normed, cot, weight_ref):
    both = product(normed, weight_ref[:, : 2 * width])
    d_inner = product(cot, weight_ref[:, 2 * width :])
    gate, upward = both[:, :width], both[:, width:]
    sig = 1.0 / (1.0 + jnp.exp(-gate))
    silu = gate * sig
    d_gate = d_inner * upward * sig * (1.0 + gate * (1.0 - sig))
    return (
        (silu * upward).astype(bf16),
        jnp.concatenate([d_gate, d_inner * silu], axis=1).astype(bf16),
    )


def mlp_kernel(width, normed_ref, cot_ref, weight_ref, inner_ref, grads_ref):
    inner_ref[...], grads_ref[...] = mlp_tile(
        width, normed_ref[...], cot_ref[...], weight_ref
    )


def tail_kernel(width, normed_ref, cot_ref, weight_ref, base_ref, *refs):
    inner_ref, grads_ref, front_ref, back_ref = refs[-4:]
    inner, grads = mlp_tile(width, normed_ref[...], cot_ref[...], weight_ref)
    inner_ref[...], grads_ref[...] = inner, grads
    total = times_transposed(grads, weight_ref[:, : 2 * width]) + base_ref[...]
    half = total.shape[1] // 2
    front_ref[...] = total[:, :half].astype(front_ref.dtype)
    back_ref[...] = total[:, half:].astype(back_ref.dtype)


def mlp_tail(normed, cot, weight, base, part, dtype, chained=()):
    tokens, features = normed.shape
    width = weight.shape[1] // 3
    tile, rows = 256, tokens // 2
    steps = rows // tile
    count = len(chained)
    return pl.pallas_call(
        functools.partial(tail_kernel, width),
        grid=(steps,),
        in_specs=[
            pl.BlockSpec((tile, features), lambda i: (part * steps + i, 0)),
            pl.BlockSpec((tile, features), lambda i: (part * steps + i, 0)),
            pl.BlockSpec((features, 3 * width), lambda i: (0, 0)),
            pl.BlockSpec((tile, features), lambda i: (i, 0)),
        ]
        + [pl.BlockSpec(memory_space=pl.ANY)] * count,
        out_specs=[
            pl.BlockSpec((tile, width), lambda i: (part * steps + i, 0)),
            pl.BlockSpec((tile, 2 * width), lambda i: (part * steps + i, 0)),
            pl.BlockSpec((tile, features // 2), lambda i: (i, 0)),
            pl.BlockSpec((tile, features // 2), lambda i: (i, 0)),
        ],
        out_shape=[
            jax.ShapeDtypeStruct((tokens, width), bf16),
            jax.ShapeDtypeStruct((tokens, 2 * width), bf16),
            jax.ShapeDtypeStruct((rows, features // 2), dtype),
            jax.ShapeDtypeStruct((rows, features // 2), dtype),
        ],
        input_output_aliases={4 + i: i for i in range(count)},
        cost_estimate=pl.CostEstimate(
            flops=10 * rows * features * width,
            bytes_accessed=2 * features * (5 * rows + 3 * width),
            transcendentals=rows * width,
        ),
        compiler_params=pltpu.CompilerParams(vmem_limit_bytes=VMEM_LIMIT),
        name="mlp_tail",
    )(normed, cot, weight, base, *chained)


def mlp_chunk(normed, cot, weight):
    tokens, features = normed.shape
    width = weight.shape[1] // 3
    tile = 256
    return pl.pallas_call(
        functools.partial(mlp_kernel, width),
        grid=(tokens // tile,),
        in_specs=[
            pl.BlockSpec((tile, features), lambda i: (i, 0)),
            pl.BlockSpec((tile, features), lambda i: (i, 0)),
            pl.BlockSpec((features, 3 * width), lambda i: (0, 0)),
        ],
        out_specs=[
            pl.BlockSpec((tile, width), lambda i: (i, 0)),
            pl.BlockSpec((tile, 2 * width), lambda i: (i, 0)),
        ],
        out_shape=[
            jax.ShapeDtypeStruct((tokens, width), bf16),
            jax.ShapeDtypeStruct((tokens, 2 * width), bf16),
        ],
        cost_estimate=pl.CostEstimate(
            flops=6 * tokens * features * width,
            bytes_accessed=2 * features * (2 * tokens + 3 * width),
            transcendentals=tokens * width,
        ),
        compiler_params=pltpu.CompilerParams(vmem_limit_bytes=VMEM_LIMIT),
        name="mlp_chunk",
    )(normed, cot, weight)


def sum_kernel(count, *refs):
    lefts, rights, out_ref = refs[:count], refs[count : 2 * count], refs[-1]
    total = times_transposed(lefts[0][...], rights[0][...])
    for left, right in zip(lefts[1:], rights[1:]):
        total += times_transposed(left[...], right[...])
    for base in refs[2 * count : -1]:
        total += base[...].astype(f32)
    out_ref[...] = total.astype(out_ref.dtype)


def chunk_sum(lefts, rights, column, part, half, dtype):
    count = len(lefts)
    tokens, features = lefts[0].shape[0], rights[0].shape[0]
    widths = [left.shape[1] for left in lefts]
    rows = tokens // 2
    tile = 256
    if half is not None:
        features, tile = features // 2, 512
    steps = rows // tile
    block = half or 0
    return pl.pallas_call(
        functools.partial(sum_kernel, count),
        grid=(steps,),
        in_specs=[pl.BlockSpec((tile, w), lambda i: (part * steps + i, 0)) for w in widths]
        + [pl.BlockSpec((features, w), lambda i: (block, column)) for w in widths],
        out_specs=pl.BlockSpec((tile, features), lambda i: (i, 0)),
        out_shape=jax.ShapeDtypeStruct((rows, features), dtype),
        cost_estimate=pl.CostEstimate(
            flops=2 * rows * features * sum(widths),
            bytes_accessed=2 * sum(widths) * (rows + features) + 4 * rows * features,
            transcendentals=0,
        ),
        compiler_params=pltpu.CompilerParams(vmem_limit_bytes=VMEM_LIMIT),
        name="chunk_sum",
    )(*lefts, *rights)


def grads_kernel(count, *refs):
    column = 0
    for left, right in zip(refs[:count], refs[count : 2 * count]):
        width = right.shape[1]
        refs[-1][:, column : column + width] = outer_sum(left[...], right[...]).astype(bf16)
        column += width


def weight_grads(*pairs):
    lefts = [left for left, _ in pairs]
    rights = [r if isinstance(r, tuple) else (r, r.shape[1], 0) for _, r in pairs]
    count = len(pairs)
    tokens, features = lefts[0].shape
    widths = [width for _, width, _ in rights]
    tile = 256

    def block(width, at):
        return pl.BlockSpec((tokens, width), lambda i: (0, at))

    return pl.pallas_call(
        functools.partial(grads_kernel, count),
        grid=(features // tile,),
        in_specs=[pl.BlockSpec((tokens, tile), lambda i: (0, i))] * count
        + [block(width, at) for _, width, at in rights],
        out_specs=pl.BlockSpec((tile, sum(widths)), lambda i: (i, 0)),
        out_shape=jax.ShapeDtypeStruct((features, sum(widths)), bf16),
        cost_estimate=pl.CostEstimate(
            flops=2 * tokens * features * sum(widths),
            bytes_accessed=2 * (count * tokens * features + sum(widths) * (tokens + features)),
            transcendentals=0,
        ),
        compiler_params=pltpu.CompilerParams(vmem_limit_bytes=VMEM_LIMIT),
        name="weight_grads",
    )(*lefts, *[array for array, _, _ in rights])


def project_kernel(place_ref, normed_ref, weight_ref, cos_ref, sin_ref, q_ref, k_ref, v_ref):
    step = pl.program_id(0)
    cos, sin = cos_ref[...], sin_ref[...]
    qkv = product(normed_ref[...], weight_ref[...])
    keys = rotate(qkv[:, :HS], cos, sin).astype(bf16)
    vals = qkv[:, HS : 2 * HS].astype(bf16)
    query = rotate(qkv[:, 2 * HS :], cos, sin).astype(bf16) * HS ** (-0.5)
    blocks = normed_ref.shape[0] // BLOCK
    for b in range(blocks):
        rows = pl.ds(pl.multiple_of(place_ref[step * blocks + b] * BLOCK, BLOCK), BLOCK)
        part = slice(b * BLOCK, (b + 1) * BLOCK)
        q_ref[rows, :] = query[part]
        k_ref[rows, :] = keys[part]
        v_ref[rows, :] = vals[part]


def project(place, normed, weight, cos, sin):
    tokens, features = normed.shape
    tile = 256
    whole = pl.BlockSpec((tokens, HS), lambda i, place: (0, 0))
    return pl.pallas_call(
        project_kernel,
        grid_spec=pltpu.PrefetchScalarGridSpec(
            num_scalar_prefetch=1,
            grid=(tokens // tile,),
            in_specs=[
                pl.BlockSpec((tile, features), lambda i, place: (i, 0)),
                pl.BlockSpec((features, 3 * HS), lambda i, place: (0, 0)),
                pl.BlockSpec((tile, HS // 2), lambda i, place: (i, 0)),
                pl.BlockSpec((tile, HS // 2), lambda i, place: (i, 0)),
            ],
            out_specs=[whole] * 3,
        ),
        out_shape=[jax.ShapeDtypeStruct((tokens, HS), bf16)] * 3,
        cost_estimate=pl.CostEstimate(
            flops=6 * tokens * features * HS,
            bytes_accessed=2 * features * (tokens + 3 * HS) + 10 * tokens * HS,
            transcendentals=0,
        ),
        compiler_params=pltpu.CompilerParams(vmem_limit_bytes=VMEM_LIMIT),
        name="project",
    )(place, normed, weight, cos, sin)


TILE = 256


def tile_masks():
    rows = lax.broadcasted_iota(jnp.int32, (TILE, TILE), 0)
    cols = lax.broadcasted_iota(jnp.int32, (TILE, TILE), 1)
    causal = rows >= cols
    return causal, causal & (rows // BLOCK == cols // BLOCK)


def block_rows(order_ref, index):
    return pl.ds(pl.multiple_of(order_ref[index] * BLOCK, BLOCK), BLOCK)


def forward_kernel(order_ref, q_ref, k_ref, v_ref, mixed_ref, lse_ref, peak_ref):
    causal, inside = tile_masks()
    prompt = GROUP // 2
    top = jnp.full((TILE, 1), masked_value, f32)
    for i in range(GROUP // TILE):
        rows = slice(i * TILE, (i + 1) * TILE)
        past = min(i * TILE, prompt)
        query = q_ref[rows, :]
        near = times_transposed(query, k_ref[rows, :])
        near = jnp.where(causal if i * TILE < prompt else inside, near, masked_value)
        peak = jnp.max(near, axis=1, keepdims=True)
        if past:
            far = times_transposed(query, k_ref[:past, :])
            peak = jnp.maximum(peak, jnp.max(far, axis=1, keepdims=True))
            far = jnp.exp(far - peak)
        near = jnp.exp(near - peak)
        total = jnp.sum(near, axis=1, keepdims=True)
        if past:
            total += jnp.sum(far, axis=1, keepdims=True)
        share = 1.0 / total
        mixed = product((near * share).astype(bf16), v_ref[rows, :])
        if past:
            mixed += product((far * share).astype(bf16), v_ref[:past, :])
        mixed = mixed.astype(bf16)
        for b in range(TILE // BLOCK):
            mixed_ref[block_rows(order_ref, i * (TILE // BLOCK) + b), :] = mixed[
                b * BLOCK : (b + 1) * BLOCK
            ]
        lse_ref[rows, :] = peak + jnp.log(total)
        top = jnp.maximum(top, peak)
    peak_ref[...] = jnp.full(peak_ref.shape, jnp.max(top), f32)


def attention_forward(order, query, keys, vals):
    whole = pl.BlockSpec(memory_space=pltpu.VMEM)
    return pl.pallas_call(
        forward_kernel,
        in_specs=[pl.BlockSpec(memory_space=pltpu.SMEM), whole, whole, whole],
        out_specs=[whole] * 3,
        out_shape=[
            jax.ShapeDtypeStruct((GROUP, HS), bf16),
            jax.ShapeDtypeStruct((GROUP, 1), f32),
            jax.ShapeDtypeStruct((8, 128), f32),
        ],
        cost_estimate=pl.CostEstimate(
            flops=2 * GROUP * GROUP * HS,
            bytes_accessed=8 * GROUP * HS,
            transcendentals=GROUP * GROUP // 2,
        ),
        compiler_params=pltpu.CompilerParams(vmem_limit_bytes=VMEM_LIMIT),
        name="attention_forward",
    )(order, query, keys, vals)


def backward_kernel(
    order_ref, q_ref, k_ref, v_ref, lse_ref, mixed_ref, cos_ref, sin_ref, out_ref, dk_ref, dv_ref
):
    causal, inside = tile_masks()
    prompt = GROUP // 2
    blocks = TILE // BLOCK

    def back(grad, index):
        rows = block_rows(order_ref, index)
        return rows, unrotate(grad, cos_ref[rows, :], sin_ref[rows, :]).astype(bf16)

    for i in range(GROUP // TILE):
        rows = slice(i * TILE, (i + 1) * TILE)
        past = min(i * TILE, prompt)
        query, lse = q_ref[rows, :], lse_ref[rows, :]
        d_mixed = jnp.concatenate(
            [mixed_ref[block_rows(order_ref, i * blocks + b), :] for b in range(blocks)], axis=0
        )
        near = times_transposed(query, k_ref[rows, :])
        near = jnp.where(causal if i * TILE < prompt else inside, near, masked_value)
        near = jnp.exp(near - lse)
        d_near = times_transposed(d_mixed, v_ref[rows, :])
        inner = jnp.sum(near * d_near, axis=1, keepdims=True)
        if past:
            far = jnp.exp(times_transposed(query, k_ref[:past, :]) - lse)
            d_far = times_transposed(d_mixed, v_ref[:past, :])
            inner += jnp.sum(far * d_far, axis=1, keepdims=True)
        d_near = (near * (d_near - inner)).astype(bf16)
        d_query = product(d_near, k_ref[rows, :])
        dk_ref[rows, :] = outer_sum(d_near, query)
        dv_ref[rows, :] = outer_sum(near.astype(bf16), d_mixed)
        if past:
            d_far = (far * (d_far - inner)).astype(bf16)
            d_query += product(d_far, k_ref[:past, :])
            dk_ref[:past, :] += outer_sum(d_far, query)
            dv_ref[:past, :] += outer_sum(far.astype(bf16), d_mixed)
        d_query = d_query * HS ** (-0.5)
        for b in range(blocks):
            where, grad = back(d_query[b * BLOCK : (b + 1) * BLOCK], i * blocks + b)
            out_ref[where, 2 * HS :] = grad
    for c in range(GROUP // BLOCK):
        part = slice(c * BLOCK, (c + 1) * BLOCK)
        where, grad = back(dk_ref[part, :], c)
        out_ref[where, :HS] = grad
        out_ref[where, HS : 2 * HS] = dv_ref[part, :].astype(bf16)


def attention_backward(order, query, keys, vals, lse, d_mixed, cos, sin):
    whole = pl.BlockSpec(memory_space=pltpu.VMEM)
    return pl.pallas_call(
        backward_kernel,
        in_specs=[pl.BlockSpec(memory_space=pltpu.SMEM)] + [whole] * 7,
        out_specs=whole,
        out_shape=jax.ShapeDtypeStruct((GROUP, 3 * HS), bf16),
        scratch_shapes=[pltpu.VMEM((GROUP, HS), f32), pltpu.VMEM((GROUP, HS), f32)],
        cost_estimate=pl.CostEstimate(
            flops=5 * GROUP * GROUP * HS,
            bytes_accessed=20 * GROUP * HS,
            transcendentals=GROUP * GROUP // 2,
        ),
        compiler_params=pltpu.CompilerParams(vmem_limit_bytes=VMEM_LIMIT),
        name="attention_backward",
    )(order, query, keys, vals, lse, d_mixed, cos, sin)


def local(
    tokens,
    cotangent,
    segment,
    position,
    clip_limit,
    attn_gain,
    query_weight,
    key_weight,
    value_weight,
    output_weight,
    mlp_gain,
    gate_weight,
    up_weight,
    down_weight,
):
    groups = lax.axis_size("group")
    group = lax.axis_index("group")
    core = lax.axis_index("tp")
    member = lax.axis_index(PLANE)
    token_rows = tokens.shape[0]
    own_rows, features = query_weight.shape[0], tokens.shape[1]
    hidden_own = gate_weight.shape[1] // 4
    chunks, offset = [], 0
    for part in SIXTEENTHS:
        chunks.append((offset, hidden_own * part // 16))
        offset += hidden_own * part // 16
    member_at = member.astype(jnp.int32).reshape(1)

    def own_order(array):
        parts = []
        for j in range(2):
            for k in range(4):
                start = group * GROUP + (member ^ k) * (2 * token_rows) + (core ^ j) * token_rows
                parts.append(lax.dynamic_slice_in_dim(array, start, token_rows))
        return jnp.concatenate(parts)

    def collect(blocks):
        return lax.all_gather(blocks, "group", axis=0, tiled=True)

    def mlp_exchange(some, waits):
        weights = [after(a, *waits) for a in (gate_weight, up_weight, down_weight)]
        spans = tuple((start, hidden_own, count, 0) for start, count in some for _ in range(3))
        return swap_all(split(member_at, weights * len(some), spans))

    seg, pos = own_order(segment), own_order(position)
    cos, sin = rope_tables(pos)
    seg_blocks, pos_blocks = seg[::BLOCK], pos[::BLOCK]
    half_blocks = GROUP // BLOCK // 2
    place = jnp.where(seg_blocks == 0, pos_blocks // BLOCK, half_blocks - 1 + seg_blocks)
    labels = jnp.arange(2 * half_blocks, dtype=jnp.int32)
    order = jnp.sum(jnp.where(place[None, :] == labels[:, None], labels[None, :], 0), axis=1)
    index = lax.axis_index(FSDP)
    gains = jnp.stack([attn_gain, mlp_gain])[:, None, :]
    gains = jnp.where(jnp.arange(4 * groups)[None, :, None] == index, gains, 0)
    gains, gain_rounds = combine_all(gains, groups, lambda a, b: a + b)
    gains = gains.reshape(2, features).astype(f32)
    head, pair = (0, HS, HS, 0), (0, HS, HS, 1)
    attn_pieces = swap_all(
        split(
            member_at,
            (key_weight, value_weight, query_weight, output_weight),
            (pair, pair, head, head),
        )
    )
    (attn_blocks,) = place_rows(
        member_at, attn_pieces
    )
    attn_weights = collect(attn_blocks)
    late_tokens = after(tokens, *attn_pieces[1:])
    neighbours = plane_neighbours(late_tokens)
    tokens_far = plane_far(neighbours)
    tokens_mine = [late_tokens, *neighbours, *tokens_far]
    tokens_near = [swap(piece, "tp") for piece in tokens_mine[:3]]
    normed_all = pack_normed(
        with_partner(tokens_mine, tokens_near), gains[:1], (cos, sin, place, order)
    )
    pieces_0 = mlp_exchange(chunks[:1], (*tokens_far, *tokens_near))
    (blocks_0,) = place_rows(
        member_at, [after(pieces_0[0], normed_all, *gain_rounds[-1])] + pieces_0[1:]
    )
    late_cot = after(cotangent, *pieces_0[1:])
    cot_near = plane_neighbours(late_cot)
    pieces_1 = mlp_exchange(chunks[1:], cot_near)
    query, keys, vals = project(
        place, normed_all, attn_weights, cos, sin
    )
    mixed, logsum, peak = attention_forward(
        order, after(query, *cot_near), keys, vals
    )

    head_top = jnp.where(jnp.arange(4) == member, peak[0, :4], masked_value)
    head_top, head_rounds = combine_all(head_top, groups, jnp.maximum)

    def projected(left, column, waits=(), others=()):
        lefts = (after(left, *others) if others else left, after(left, *waits) if waits else left)
        return [
            [
                chunk_sum([lefts[j]], [attn_weights], column, j, h, bf16 if j else f32)
                for j in (0, 1)
            ]
            for h in range(2)
        ]

    attn_sums = chip_sums(*projected(mixed, 3, pieces_1[1:]))
    arrived = reduce_first(first_operands(attn_sums))
    attn_operands = reduce_operands(attn_sums, arrived)
    attn_last = last_swaps(attn_operands, *head_rounds[0])
    hidden, own_normed = add_and_norm(attn_operands, attn_last, tokens, gains[1:])
    neighbours = plane_neighbours(own_normed)
    normed_far = plane_far(neighbours, *head_rounds[-1])
    cot_far = plane_far(cot_near, *normed_far)
    mlp_weights = [collect(blocks_0), collect(*place_rows(member_at, pieces_1))]
    normed_mlp = pack(with_partner([own_normed, *neighbours, *normed_far]))
    cot_all = pack(with_partner([late_cot, *cot_near, *cot_far]))

    def line_sum(partial):
        return lax.psum_scatter(partial, "group", scatter_dimension=0, tiled=True)

    inner_0, both_0 = mlp_chunk(normed_mlp, cot_all, mlp_weights[0])
    grads_0 = weight_grads((normed_mlp, both_0), (cot_all, inner_0))
    sum_0 = line_sum(grads_0)
    late_both = after(both_0, grads_0)
    early = [chunk_sum([late_both], mlp_weights[:1], 0, j, None, f32) for j in range(2)]
    inner_1, both_1, front_1, back_1 = mlp_tail(
        after(normed_mlp, *early), cot_all, mlp_weights[1], early[1], 1, bf16
    )
    inner_1, both_1, front_0, back_0 = mlp_tail(
        normed_mlp, cot_all, mlp_weights[1], early[0], 0, f32, (inner_1, both_1)
    )

    mlp_sums = chip_sums((front_0, front_1), (back_0, back_1))
    operands = first_operands(mlp_sums)
    arrived = reduce_first(operands)
    inners = [after(inner, *operands) for inner in (inner_0, inner_1)]
    out_parts = [
        [chunk_sum(inners, mlp_weights, 2, j, h, bf16 if j else f32) for j in (0, 1)]
        for h in range(2)
    ]
    mlp_operands = reduce_operands(mlp_sums, arrived)
    mlp_last = last_swaps(mlp_operands, *out_parts[0], *out_parts[1])
    d_hidden, own_d = norm_back(
        mlp_operands, mlp_last, hidden, cotangent, gains[1:], (f32, bf16)
    )
    neighbours = plane_neighbours(own_d)
    late_both = after(both_1, own_d)
    grads_1 = weight_grads((normed_mlp, late_both), (cot_all, inner_1))
    sum_1 = line_sum(after(grads_1, *neighbours))
    d_far = plane_far(neighbours, grads_1)
    d_attn_all = pack(with_partner([own_d, *neighbours, *d_far]))
    out_sums = chip_sums(*out_parts)
    def send_grads(sources, *waits):
        first = after(sources[0], *waits) if waits else sources[0]
        return swap_all(pick_rows(member_at, first, *sources[1:]))


    final_0 = send_grads([sum_0], *d_far)
    out_arrived = reduce_first(first_operands(out_sums), *final_0[1:])
    out_operands = reduce_operands(out_sums, out_arrived)
    out_last = last_swaps(out_operands)

    d_mixed = product(d_attn_all, attn_weights[:, 3 * HS :]).astype(bf16)
    d_qkv = attention_backward(
        order, after(query, *final_0[1:]), keys, vals, logsum, d_mixed, cos, sin
    )
    pair_grads = weight_grads((normed_all, (d_qkv, 2 * HS, 0)))
    half_shape = jax.ShapeDtypeStruct((features // 2, 2 * HS), bf16)
    keep, send = vmem_call(
        functools.partial(halves_kernel, own_rows),
        "halves",
        [half_shape] * 2,
        member_at,
        pair_grads,
    )
    got = swap(send, "col")
    both_grads = weight_grads(
        (normed_all, (after(d_qkv, keep, *out_arrived), HS, 2)), (d_attn_all, mixed)
    )
    late_qkv = after(d_qkv, both_grads)
    qkv_parts = projected(late_qkv, 0, (), out_last)
    (attn_grads,) = vmem_call(
        functools.partial(join_kernel, own_rows),
        "join",
        [jax.ShapeDtypeStruct((features, 3 * HS), bf16)],
        member_at,
        after(keep, qkv_parts[0][1], qkv_parts[1][1]),
        got,
        both_grads,
    )
    attn_sum = line_sum(attn_grads)
    qkv_sums = chip_sums(*qkv_parts)
    final_1 = send_grads([sum_1], attn_grads)
    arrived = reduce_first(first_operands(qkv_sums), *final_1[1:])
    qkv_operands = reduce_operands(qkv_sums, arrived)
    qkv_last = last_swaps(qkv_operands)
    (tokens_grad,) = norm_back(qkv_operands, qkv_last, tokens, d_hidden, gains[:1], (f32,))
    block_out = add_sum(out_operands, out_last, hidden)

    gate_grad, up_grad, down_grad, mlp_gain_row = mlp_final(
        member_at, gate_weight, up_weight, (chunks[:1], chunks[1:]), [final_0, final_1]
    )
    attn_parts = attention_return(
        member_at, after(attn_sum, *qkv_last, mlp_gain_row, block_out)
    )
    query_grad, key_grad, value_grad, output_grad, attn_gain_row = attention_final(
        member_at,
        query_weight,
        key_weight,
        value_weight,
        [after(attn_parts[0], tokens_grad)] + attn_parts[1:],
    )
    gain_grads = jnp.concatenate([attn_gain_row, mlp_gain_row], axis=1)
    gain_grads = gain_grads + swap(gain_grads, "tp")
    attn_gain_grad = gain_grads[:, 0] / attn_gain.astype(f32)
    mlp_gain_grad = gain_grads[:, 1] / mlp_gain.astype(f32)

    factor = clip_limit / jnp.maximum(head_top, clip_limit)
    query_scale = jnp.repeat(jnp.sqrt(factor), HS)
    key_factor = jnp.min(factor.reshape(2, 2), axis=1)
    key_scale = jnp.repeat(jnp.sqrt(key_factor), HS)
    query_clipped = (query_weight.astype(f32) * query_scale[None, :]).astype(bf16)
    key_clipped = (key_weight.astype(f32) * key_scale[None, :]).astype(bf16)
    return (
        block_out,
        tokens_grad,
        attn_gain_grad,
        query_grad,
        key_grad,
        value_grad,
        output_grad,
        mlp_gain_grad,
        gate_grad,
        up_grad,
        down_grad,
        head_top,
        query_clipped,
        key_clipped,
    )


def solution(mesh):
    shape = (mesh.shape["fsdp"] // 4, 2, 2, mesh.shape["tp"])
    fine = Mesh(mesh.devices.reshape(shape), ("group", "row", "col", "tp"))
    rows = P(("group", "row", "col", "tp"), None)
    weight = P(FSDP, "tp")
    gain = P(FSDP)
    heads = P("tp")
    return jax.shard_map(
        local,
        mesh=fine,
        in_specs=(
            rows, rows, P(), P(), heads, gain, weight, weight, weight, weight,
            gain, weight, weight, weight,
        ),
        out_specs=(
            rows, rows, gain, weight, weight, weight, weight, gain, weight, weight, weight,
            heads, weight, weight,
        ),
        check_vma=False,
    )
```
